32 devices in a mesh: row: 8 (over z, y), col: 4 (over x, core).
Axes of the slice: x: 2, y: 2, z: 4, core: 2. Of those that a mesh axis runs over, the one named last changes fastest.
Arguments:
- rhs: float32 [32, 65536], P(None, ('row', 'col')), may hold values from -5 to 7
- coords: float32 [3, 65536], P(None, ('row', 'col')), may hold values from 0 to 8, as said below
- nugget: float32 [65536], P(('row', 'col')), may hold values from 1.5 to 3
- near_ids: int32 [128, 3], P(('row', 'col')), may hold values from -1 to 127, as said below
- basis: float32 [7, 128, 65536], P(None, None, ('row', 'col')), may hold values from -6 to 6
Outputs:
- solution: float32 [32, 65536], P(None, ('row', 'col'))
- residual: float32 [32, 65536], P(None, ('row', 'col'))
The draws below stay inside these ranges and needn't reach their ends.
Inputs may be any that keep to these rules, and one draw needn't show every extreme that they name: `near_ids`: row i lists leaf i and some of the leaves i - 1 to i + 1 inside the range, each at most once, in any order; the other slots hold -1; the first and last leaf of each device's block of 4 list all such leaves inside the range. `coords`: each leaf's points lie in a unit box with an integer corner; consecutive leaves lie in boxes that share a face.
All inputs are finite; a program needn't handle non-finite values.
Results may differ from the reference program's by a relative error of at most 0.0003.
Values sent between devices are 32-bit elements; how exact they have to be, the bound alone decides.
No kernel may reach another device: no remote copies, remote signals or barrier semaphores. Data moves between devices by JAX's collectives and lax.ppermute only.
A program may use at most 128 MiB of HBM per device.

```python
import jax
import jax.numpy as jnp
from jax import lax

LEAF = 512
RANK = 128
NRHS = 32
ITERS = 4
REACH = 1
LEAF_DEV = 4
WIN = 3
NLEAF = 128
NPTS = 65536
LEAF_BITS = 2
DEV_BITS = 5
LEVELS = 7


def snake_corner(leaf):
    total_bits = DEV_BITS + LEAF_BITS
    side = 2 ** (total_bits // 3)
    first = leaf % side
    line = leaf // side
    second_raw = line % side
    plane = line // side
    first = jnp.where(line % 2 == 0, first, side - 1 - first)
    second = jnp.where(plane % 2 == 0, second_raw, side - 1 - second_raw)
    return jnp.stack([first, second, plane])


def draw_coords(key, part):
    key = jax.random.fold_in(key, 11)
    leaf = jnp.arange(NPTS, dtype=jnp.int32) // LEAF
    corner = snake_corner(leaf).astype(jnp.float32)
    jitter = jax.random.uniform(key, (3, NPTS), jnp.float32)
    return corner + jitter


def draw_rhs(key, part):
    key = jax.random.fold_in(key, 23)
    rough_key, mean_key = jax.random.split(key)
    rough = jnp.clip(jax.random.normal(rough_key, (NRHS, NPTS), jnp.float32), -5.0, 5.0)
    offset = jax.random.uniform(mean_key, (NRHS, NLEAF, 1), jnp.float32, 0.0, 1.5)
    return (rough.reshape(NRHS, NLEAF, LEAF) + offset).reshape(NRHS, NPTS)


def draw_near_ids(key, part):
    key = jax.random.fold_in(key, 37)
    rate_key, roll_key, order_key = jax.random.split(key, 3)
    leaf = jnp.arange(NLEAF, dtype=jnp.int32)[:, None]
    offsets = jnp.arange(WIN, dtype=jnp.int32)[None, :] - REACH
    target = leaf + offsets
    inside = (target >= 0) & (target < NLEAF)
    rates = jnp.repeat(jax.random.randint(rate_key, (NLEAF // 8,), 10, 100), 8)[:, None]
    rolls = jax.random.randint(roll_key, (NLEAF, WIN), 0, 100)
    edge = (leaf % LEAF_DEV == 0) | (leaf % LEAF_DEV == LEAF_DEV - 1)
    keep = inside & ((rolls < rates) | (offsets == 0) | edge)
    listed = jnp.where(keep, target, -1)
    scores = jax.random.randint(order_key, (NLEAF, WIN), 0, 2 ** 20) * WIN + jnp.arange(WIN, dtype=jnp.int32)[None, :]
    order = jnp.argsort(scores, axis=1)
    return jnp.take_along_axis(listed, order, axis=1).astype(jnp.int32)


def block_levels(own_key, dims, cuts, low, high):
    loudness = 1.0
    for dim, shards_of in cuts:
        draws = jax.random.uniform(jax.random.fold_in(jax.random.fold_in(own_key, 6), dim), (shards_of,), jnp.float32, low / len(cuts), high / len(cuts))
        loudness = loudness * jnp.repeat(jnp.exp(draws), dims[dim] // shards_of).reshape((-1,) + (1,) * (len(dims) - 1 - dim))
    return loudness


def scatter_about(rng, extent, scale, limit, cuts=(), kind=jnp.bfloat16):
    values = jax.random.normal(rng, extent, jnp.float32) * scale
    if len(cuts) > 0:
        values = block_levels(rng, extent, cuts, -0.22, 0.18) * values
    return jnp.clip(values, min=-limit, max=limit).astype(kind)


def setup_inputs(seed: int = 0) -> dict:
    arg_keys = jax.random.split(jax.random.key(seed), 6)
    rhs = draw_rhs(jax.random.fold_in(arg_keys[5], 71), 0)
    coords = draw_coords(jax.random.fold_in(arg_keys[5], 71), 0)
    nugget = jnp.clip(1.5 + 1.5 * jax.random.uniform(arg_keys[2], (NPTS,), jnp.float32) ** block_levels(arg_keys[2], (NPTS,), ((0, 32),), -0.2, 0.2), 1.5, 3.0)
    near_ids = draw_near_ids(jax.random.fold_in(arg_keys[5], 71), 0)
    basis = scatter_about(arg_keys[4], (LEVELS, RANK, NPTS), 1.0, 6.0, ((2, 32),), jnp.float32)
    return {"rhs": rhs, "coords": coords, "nugget": nugget, "near_ids": near_ids, "basis": basis}


root_three = 1.7320508075688772
spacing_factor = 1.6

def matern(square_dist):
    length = spacing_factor * LEAF ** (-1.0 / 3.0)
    scaled = root_three * jnp.sqrt(square_dist) / length
    return (1.0 + scaled) * jnp.exp(-scaled)

def window_mask(near_ids, first_leaf, count):
    leaves = first_leaf + jnp.arange(count, dtype=jnp.int32)
    offsets = jnp.arange(WIN, dtype=jnp.int32) - REACH
    target = leaves[None, :] + offsets[:, None]
    matches = near_ids.T[None, :, :] == target[:, None, :]
    return jnp.any(matches, axis=1).astype(jnp.float32)

def tile_block(own_coords, far_coords, weight):
    spread = own_coords[:, :, :, None] - far_coords[:, :, None, :]
    square_dist = lax.optimization_barrier(jnp.sum(spread * spread, axis=0))
    return matern(square_dist) * (weight / (16 * WIN))[:, None, None]

def near_field(field, coords, mask):
    margin = REACH * LEAF
    blocks = NLEAF // LEAF_DEV
    field_pad = jnp.pad(field, ((0, 0), (margin, margin)))
    coord_pad = jnp.pad(coords, ((0, 0), (margin, margin)))
    own = coords.reshape(3, blocks, LEAF_DEV, LEAF).transpose(1, 0, 2, 3)
    total = jnp.zeros((NRHS, NPTS), jnp.float32)
    for offset in range(WIN):
        far = coord_pad[:, offset * LEAF:offset * LEAF + NPTS].reshape(3, blocks, LEAF_DEV, LEAF).transpose(1, 0, 2, 3)
        segment = field_pad[:, offset * LEAF:offset * LEAF + NPTS].reshape(NRHS, blocks, LEAF_DEV, LEAF).transpose(1, 0, 2, 3)
        weight = mask[offset].reshape(blocks, LEAF_DEV)

        def one_block(inputs):
            own_block, far_block, seg_block, wgt_block = inputs
            tile_set = tile_block(own_block, far_block, wgt_block)
            return jnp.einsum('bij,rbj->rbi', tile_set, seg_block, precision=lax.Precision.HIGHEST)
        part_sum = lax.map(one_block, (own, far, segment, weight))
        total = total + part_sum.transpose(1, 0, 2, 3).reshape(NRHS, NPTS)
    return total

def far_field(field, basis):
    total = jnp.zeros((NRHS, NPTS), jnp.float32)
    for level in range(LEVELS):
        cluster = LEAF * 2 ** (level + 1)
        grouped = basis[level].reshape(RANK, NPTS // cluster, cluster)
        values = field.reshape(NRHS, NPTS // cluster, cluster)
        skeleton = jnp.einsum('kcs,rcs->crk', grouped, values, precision=lax.Precision.HIGHEST)
        spread_back = jnp.einsum('kcs,crk->rcs', grouped, skeleton, precision=lax.Precision.HIGHEST)
        total = total + spread_back.reshape(NRHS, NPTS) / cluster
    return total

def reference(rhs, coords, nugget, near_ids, basis):
    mask = window_mask(near_ids, jnp.int32(0), NLEAF)

    def operate(field):
        return nugget[None, :] * field + near_field(field, coords, mask) + far_field(field, basis)
    solution = jnp.zeros((NRHS, NPTS), jnp.float32)
    residual = rhs
    direction = rhs
    norm_now = lax.optimization_barrier(jnp.sum(residual * residual, axis=1))
    for step in range(ITERS):
        image = operate(direction)
        step_size = norm_now / lax.optimization_barrier(jnp.sum(direction * image, axis=1))
        solution = solution + step_size[:, None] * direction
        residual = residual - step_size[:, None] * image
        norm_next = lax.optimization_barrier(jnp.sum(residual * residual, axis=1))
        direction = residual + (norm_next / norm_now)[:, None] * direction
        norm_now = norm_next
    return (solution, residual)
```

```python
import functools

import jax
import jax.numpy as jnp
from jax import lax
from jax.experimental import pallas as pl
from jax.experimental.pallas import tpu as pltpu
from jax.sharding import PartitionSpec as P

LEAF = 512
ITERS = 4
REACH = 1
WIN = 3
LANES = 128
LOCAL = 3
CHUNK = 64

root_three = 1.7320508075688772
spacing_factor = 1.6
matern_scale = root_three / (spacing_factor * LEAF ** (-1.0 / 3.0))

BOTH = ("row", "col")
ROWS_COLS = (((1,), (0,)), ((), ()))
ROWS_ROWS = (((1,), (1,)), ((), ()))


def halves(values):
    high = values.astype(jnp.bfloat16)
    low = (values - high.astype(jnp.float32)).astype(jnp.bfloat16)
    return high, low


def stacked(values):
    return jnp.concatenate(halves(values), axis=0)


def product(stack, high, low, dims):
    rows = stack.shape[0] // 2
    main = lax.dot_general(stack, high, dims, preferred_element_type=jnp.float32)
    rest = lax.dot_general(stack[:rows], low, dims, preferred_element_type=jnp.float32)
    return main[:rows] + (main[rows:] + rest)


def row_sum(values):
    return jnp.sum(values, axis=1, keepdims=True)


def in_lanes(columns, shape):
    lane = lax.broadcasted_iota(jnp.int32, shape, 1)
    block = jnp.zeros(shape, jnp.float32)
    for index, column in enumerate(columns):
        block = jnp.where(lane == index, column, block)
    return block


def whole(memory=pltpu.VMEM):
    return pl.BlockSpec(memory_space=memory)


def call(body, outs, *args, specs=None, flops=0, limit=32, **extra):
    return pl.pallas_call(
        body,
        out_shape=outs,
        in_specs=specs or [whole()] * len(args),
        out_specs=[whole()] * len(outs),
        compiler_params=pltpu.CompilerParams(vmem_limit_bytes=limit * 2**20),
        cost_estimate=pl.CostEstimate(flops=flops, bytes_accessed=2**20, transcendentals=0),
        **extra,
    )(*args)


def f32(*shape):
    return jax.ShapeDtypeStruct(shape, jnp.float32)


def bf16(*shape):
    return jax.ShapeDtypeStruct(shape, jnp.bfloat16)


def split_kernel(basis_ref, high_ref, low_ref):
    high_ref[...], low_ref[...] = halves(basis_ref[0])


def split_basis(basis):
    levels, rank, width = basis.shape
    return pl.pallas_call(
        split_kernel,
        out_shape=[bf16(levels * rank, width)] * 2,
        grid=(levels,),
        in_specs=[pl.BlockSpec((1, rank, width), lambda level: (level, 0, 0))],
        out_specs=[pl.BlockSpec((rank, width), lambda level: (level, 0))] * 2,
        compiler_params=pltpu.CompilerParams(vmem_limit_bytes=16 * 2**20),
    )(basis)


def kernel_matrices(lane_ref, sub_ref, high_ref, low_ref):
    leaves = lane_ref.shape[1] // LEAF - 2
    parts = LEAF // CHUNK

    def one(step, carry):
        matrix = step // parts
        part = step % parts
        pair = matrix >= leaves
        row_leaf = jnp.where(pair, matrix - leaves, matrix + 1)
        col_leaf = jnp.where(pair, matrix - leaves + 1, matrix + 1)
        row_at = pl.multiple_of(row_leaf * LEAF + part * CHUNK, CHUNK)
        col_at = pl.multiple_of(col_leaf * LEAF, LEAF)
        square = None
        for axis in range(3):
            spread = sub_ref[pl.ds(row_at, CHUNK), axis : axis + 1] - lane_ref[axis : axis + 1, pl.ds(col_at, LEAF)]
            square = spread * spread if square is None else square + spread * spread
        square = square * (matern_scale * matern_scale)
        scaled = square * lax.rsqrt(jnp.maximum(square, 1e-30))
        values = (1.0 + scaled) * jnp.exp(-scaled)
        out_at = pl.ds(pl.multiple_of(part * CHUNK, CHUNK), CHUNK)
        high_ref[matrix, out_at], low_ref[matrix, out_at] = halves(values)
        return carry

    lax.fori_loop(0, (2 * leaves + 1) * parts, one, 0)


def down_kernel(field_ref, high_ref, low_ref, out_ref):
    rank = LANES
    half = field_ref.shape[1] // 2
    stack = stacked(field_ref[...])
    for part in range(2):
        points = slice(part * half, (part + 1) * half)
        out_ref[:, part * rank : (part + 1) * rank] = product(
            stack[:, points], high_ref[:rank, points], low_ref[:rank, points], ROWS_ROWS
        )
    out_ref[:, 2 * rank :] = product(stack, high_ref[rank:], low_ref[rank:], ROWS_ROWS)


def near_kernel(first, *refs):
    (place_ref, ids_ref, field_ref, before_ref, after_ref, nugget_ref, high_ref, low_ref, skel_ref) = refs[:9]
    if first:
        out_ref, message_ref = refs[9:]
    else:
        direction_ref, image_ref, old_skel_ref, out_ref, message_ref = refs[9:]
    rows, width = field_ref.shape
    leaves = width // LEAF

    def weight(leaf, offset):
        target = place_ref[0] * leaves + leaf + offset
        found = ids_ref[leaf, 0] == target
        for slot in range(1, WIN):
            found = jnp.logical_or(found, ids_ref[leaf, slot] == target)
        return jnp.where(found, 1.0 / (16 * WIN), 0.0)

    def own(ref, leaf):
        return ref[:, leaf * LEAF : (leaf + 1) * LEAF]

    pieces = [stacked(before_ref[...])] + [stacked(own(field_ref, leaf)) for leaf in range(leaves)]
    pieces = pieces + [stacked(after_ref[...])]
    square = with_image = cross = 0.0
    for leaf in range(leaves):
        field = own(field_ref, leaf)
        before = product(pieces[leaf], high_ref[leaves + leaf], low_ref[leaves + leaf], ROWS_COLS)
        inside = product(pieces[leaf + 1], high_ref[leaf], low_ref[leaf], ROWS_COLS)
        after = product(pieces[leaf + 2], high_ref[leaves + leaf + 1], low_ref[leaves + leaf + 1], ROWS_ROWS)
        total = own(nugget_ref, leaf) * field + weight(leaf, 0) * inside
        total = total + weight(leaf, -1) * before + weight(leaf, 1) * after
        out_ref[:, leaf * LEAF : (leaf + 1) * LEAF] = total
        square = square + row_sum(field * field)
        with_image = with_image + row_sum(field * total)
        if not first:
            cross = cross + row_sum(field * own(image_ref, leaf) + own(direction_ref, leaf) * total)
    for block in range(LOCAL):
        scale = 1.0 / (LEAF * (2 if block < 2 else 4))
        here = slice(block * LANES, (block + 1) * LANES)
        with_image = with_image + scale * row_sum(skel_ref[:, here] * skel_ref[:, here])
        if not first:
            cross = cross + scale * row_sum(skel_ref[:, here] * old_skel_ref[:, here])
    wide = message_ref.shape[1] - LANES
    message_ref[:, :wide] = skel_ref[:, LOCAL * LANES :]
    message_ref[:, wide:] = in_lanes([square, with_image, cross], (rows, LANES))


def combine_kernel(first, cluster, *refs):
    if first:
        mine_ref, other_ref, next_ref, level_ref = refs
    else:
        mine_ref, other_ref, old_ref, next_ref, level_ref = refs
    total = mine_ref[...] + other_ref[...]
    level = total[:, :LANES]
    level_ref[...] = level
    columns = [0.0, row_sum(level * level) * (1.0 / cluster)]
    if not first:
        columns.append(row_sum(level * old_ref[...]) * (1.0 / cluster))
    wide = total.shape[1] - 2 * LANES
    if wide:
        next_ref[:, :wide] = total[:, LANES : LANES + wide]
    next_ref[:, wide:] = total[:, LANES + wide :] + in_lanes(columns, level.shape)


def up_kernel(first, last, crossing, *refs):
    refs = list(refs)
    high_ref, low_ref, near_ref, field_ref, sums_ref, skel_ref = refs[:6]
    level_refs = refs[6 : 6 + crossing]
    refs = refs[6 + crossing :]
    if not first:
        solution_ref, direction_ref, image_ref, old_skel_ref, state_ref = refs[:5]
        refs = refs[5:]
    if last:
        new_solution_ref, new_field_ref = refs
    else:
        (
            new_solution_ref,
            new_field_ref,
            new_direction_ref,
            new_image_ref,
            new_skel_ref,
            new_state_ref,
            head_ref,
            tail_ref,
        ) = refs
    rows, width = field_ref.shape
    half = width // 2
    norm = sums_ref[:, 0:1]
    curve = sums_ref[:, 1:2]
    if not first:
        ratio = norm / state_ref[:, 0:1]
        curve = curve + ratio * (sums_ref[:, 2:3] + ratio * state_ref[:, 1:2])
    step = norm / curve
    blocks = [skel_ref[:, block * LANES : (block + 1) * LANES] for block in range(LOCAL)]
    blocks = blocks + [ref[...] for ref in level_refs]
    scaled = [block * (1.0 / (LEAF * (2 ** max(index, 1)))) for index, block in enumerate(blocks)]
    for part in range(2):
        points = slice(part * half, (part + 1) * half)
        stack = stacked(jnp.concatenate([scaled[part]] + scaled[2:], axis=1))
        image = near_ref[:, points] + product(stack, high_ref[:, points], low_ref[:, points], ROWS_COLS)
        direction = field_ref[:, points]
        if not first:
            image = image + ratio * image_ref[:, points]
            direction = direction + ratio * direction_ref[:, points]
        moved = step * direction
        new_solution_ref[:, points] = moved if first else solution_ref[:, points] + moved
        new_field_ref[:, points] = field_ref[:, points] - step * image
        if not last:
            new_direction_ref[:, points] = direction
            new_image_ref[:, points] = image
    if not last:
        head_ref[...] = new_field_ref[:, :LEAF]
        tail_ref[...] = new_field_ref[:, width - LEAF :]
        for index, block in enumerate(blocks):
            here = slice(index * LANES, (index + 1) * LANES)
            new_skel_ref[:, here] = block if first else block + ratio * old_skel_ref[:, here]
        new_state_ref[...] = in_lanes([norm, curve], (rows, LANES))


def per_device(rhs, coords, nugget, near_ids, basis):
    rows, width = rhs.shape
    levels, rank, _ = basis.shape
    leaves = width // LEAF
    crossing = levels - (leaves.bit_length() - 1)
    blocks = LOCAL + crossing
    devices = lax.axis_size("row") * lax.axis_size("col")
    place = jnp.reshape(lax.axis_index(BOTH), (1,))
    upward = [(index, index + 1) for index in range(devices - 1)]
    downward = [(index + 1, index) for index in range(devices - 1)]

    def halo(head, tail):
        return lax.ppermute(tail, BOTH, upward), lax.ppermute(head, BOTH, downward)

    before, after = halo(coords[:, :LEAF], coords[:, width - LEAF :])
    wide = jnp.concatenate([before, coords, after], axis=1)
    near_high, near_low = call(kernel_matrices, [bf16(2 * leaves + 1, LEAF, LEAF)] * 2, wide, wide.T)
    high, low = split_basis(basis)
    nugget = nugget[None, :]
    scalars = [whole(pltpu.SMEM), whole(pltpu.SMEM)]

    solution, field, edges, carried = None, rhs, (rhs[:, :LEAF], rhs[:, width - LEAF :]), None
    for step in range(ITERS):
        first, last = step == 0, step == ITERS - 1
        before, after = halo(*edges)
        (skel,) = call(down_kernel, [f32(rows, blocks * LANES)], field, high, low)
        extra = [] if first else [carried[0], carried[1], carried[2]]
        args = [place, near_ids, field, before, after, nugget, near_high, near_low, skel] + extra
        near, message = call(
            functools.partial(near_kernel, first),
            [f32(rows, width), f32(rows, (crossing + 1) * LANES)],
            *args,
            specs=scalars + [whole()] * (len(args) - 2),
        )
        summed = []
        for bit in range(crossing):
            pairs = [(source, source ^ 2**bit) for source in range(devices)]
            args = [message, lax.ppermute(message, BOTH, pairs)]
            if not first:
                block = (LOCAL + bit) * LANES
                args.append(carried[2][:, block : block + LANES])
            message, level = call(
                functools.partial(combine_kernel, first, LEAF * leaves * 2 ** (bit + 1)),
                [f32(rows, (crossing - bit) * LANES), f32(rows, LANES)],
                *args,
            )
            summed.append(level)
        args = [high, low, near, field, message, skel] + summed
        if not first:
            args = args + [solution, *carried]
        outs = [f32(rows, width)] * 2
        if not last:
            outs = outs + [f32(rows, width)] * 2 + [f32(rows, blocks * LANES), f32(rows, LANES)] + [f32(rows, LEAF)] * 2
        out = call(functools.partial(up_kernel, first, last, crossing), outs, *args)
        solution, field = out[:2]
        if not last:
            carried = out[2:6]
            edges = out[6:8]
    return (solution, field)


def solution(mesh):
    placed = (
        P(None, BOTH),
        P(None, BOTH),
        P(BOTH),
        P(BOTH, None),
        P(None, None, BOTH),
    )
    return jax.shard_map(
        per_device,
        mesh=mesh,
        in_specs=placed,
        out_specs=(P(None, BOTH), P(None, BOTH)),
        check_vma=False,
    )
```

```python
import functools

import jax
import jax.numpy as jnp
from jax import lax
from jax.experimental import pallas as pl
from jax.experimental.pallas import tpu as pltpu
from jax.sharding import PartitionSpec as P

LEAF = 512
ITERS = 4
REACH = 1
WIN = 3
LANES = 128
LOCAL = 3
CHUNK = 64

root_three = 1.7320508075688772
spacing_factor = 1.6
matern_scale = root_three / (spacing_factor * LEAF ** (-1.0 / 3.0))

BOTH = ("row", "col")
ROWS_COLS = (((1,), (0,)), ((), ()))
ROWS_ROWS = (((1,), (1,)), ((), ()))


def halves(values):
    high = values.astype(jnp.bfloat16)
    low = (values - high.astype(jnp.float32)).astype(jnp.bfloat16)
    return high, low


def stacked(values):
    return jnp.concatenate(halves(values), axis=0)


def product(stack, high, low, dims):
    rows = stack.shape[0] // 2
    main = lax.dot_general(stack, high, dims, preferred_element_type=jnp.float32)
    rest = lax.dot_general(stack[:rows], low, dims, preferred_element_type=jnp.float32)
    return main[:rows] + (main[rows:] + rest)


def row_sum(values):
    return jnp.sum(values, axis=1, keepdims=True)


def in_lanes(columns, shape):
    lane = lax.broadcasted_iota(jnp.int32, shape, 1)
    block = jnp.zeros(shape, jnp.float32)
    for index, column in enumerate(columns):
        block = jnp.where(lane == index, column, block)
    return block


def whole(memory=pltpu.VMEM):
    return pl.BlockSpec(memory_space=memory)


def call(body, outs, *args, specs=None, flops=0, limit=32, **extra):
    return pl.pallas_call(
        body,
        out_shape=outs,
        in_specs=specs or [whole()] * len(args),
        out_specs=[whole()] * len(outs),
        compiler_params=pltpu.CompilerParams(vmem_limit_bytes=limit * 2**20),
        cost_estimate=pl.CostEstimate(flops=flops, bytes_accessed=2**20, transcendentals=0),
        **extra,
    )(*args)


def f32(*shape):
    return jax.ShapeDtypeStruct(shape, jnp.float32)


def bf16(*shape):
    return jax.ShapeDtypeStruct(shape, jnp.bfloat16)


def split_kernel(basis_ref, high_ref, low_ref):
    high_ref[...], low_ref[...] = halves(basis_ref[0])


def split_basis(basis):
    levels, rank, width = basis.shape
    return pl.pallas_call(
        split_kernel,
        out_shape=[bf16(levels * rank, width)] * 2,
        grid=(levels,),
        in_specs=[pl.BlockSpec((1, rank, width), lambda level: (level, 0, 0))],
        out_specs=[pl.BlockSpec((rank, width), lambda level: (level, 0))] * 2,
        compiler_params=pltpu.CompilerParams(vmem_limit_bytes=16 * 2**20),
    )(basis)


def kernel_matrices(lane_ref, sub_ref, high_ref, low_ref):
    leaves = lane_ref.shape[1] // LEAF - 2
    parts = LEAF // CHUNK

    def one(step, carry):
        matrix = step // parts
        part = step % parts
        pair = matrix >= leaves
        row_leaf = jnp.where(pair, matrix - leaves, matrix + 1)
        col_leaf = jnp.where(pair, matrix - leaves + 1, matrix + 1)
        row_at = pl.multiple_of(row_leaf * LEAF + part * CHUNK, CHUNK)
        col_at = pl.multiple_of(col_leaf * LEAF, LEAF)
        square = None
        for axis in range(3):
            spread = sub_ref[pl.ds(row_at, CHUNK), axis : axis + 1] - lane_ref[axis : axis + 1, pl.ds(col_at, LEAF)]
            square = spread * spread if square is None else square + spread * spread
        square = square * (matern_scale * matern_scale)
        scaled = square * lax.rsqrt(jnp.maximum(square, 1e-30))
        values = (1.0 + scaled) * jnp.exp(-scaled)
        out_at = pl.ds(pl.multiple_of(part * CHUNK, CHUNK), CHUNK)
        high_ref[matrix, out_at], low_ref[matrix, out_at] = halves(values)
        return carry

    lax.fori_loop(0, (2 * leaves + 1) * parts, one, 0)


def down_kernel(field_ref, high_ref, low_ref, local_ref, out_ref):
    rank = LANES
    half = field_ref.shape[1] // 2
    stack = stacked(field_ref[...])
    for part in range(2):
        points = slice(part * half, (part + 1) * half)
        local_ref[:, part * rank : (part + 1) * rank] = product(
            stack[:, points], high_ref[:rank, points], low_ref[:rank, points], ROWS_ROWS
        )
    whole_width = product(stack, high_ref[rank:], low_ref[rank:], ROWS_ROWS)
    local_ref[:, 2 * rank :] = whole_width[:, :rank]
    out_ref[...] = jnp.zeros(out_ref.shape, jnp.float32)
    for bit in range(whole_width.shape[1] // rank - 1):
        out_ref[:, bit, :] = whole_width[:, (bit + 1) * rank : (bit + 2) * rank]


def near_kernel(first, *refs):
    (place_ref, ids_ref, field_ref, before_ref, after_ref, nugget_ref, high_ref, low_ref, skel_ref) = refs[:9]
    if first:
        out_ref, sums_ref = refs[9:]
    else:
        direction_ref, image_ref, old_skel_ref, out_ref, sums_ref = refs[9:]
    rows, width = field_ref.shape
    leaves = width // LEAF

    def weight(leaf, offset):
        target = place_ref[0] * leaves + leaf + offset
        found = ids_ref[leaf, 0] == target
        for slot in range(1, WIN):
            found = jnp.logical_or(found, ids_ref[leaf, slot] == target)
        return jnp.where(found, 1.0 / (16 * WIN), 0.0)

    def own(ref, leaf):
        return ref[:, leaf * LEAF : (leaf + 1) * LEAF]

    pieces = [stacked(before_ref[...])] + [stacked(own(field_ref, leaf)) for leaf in range(leaves)]
    pieces = pieces + [stacked(after_ref[...])]
    square = with_image = cross = jnp.zeros((rows, 1), jnp.float32)
    for leaf in range(leaves):
        field = own(field_ref, leaf)
        before = product(pieces[leaf], high_ref[leaves + leaf], low_ref[leaves + leaf], ROWS_COLS)
        inside = product(pieces[leaf + 1], high_ref[leaf], low_ref[leaf], ROWS_COLS)
        after = product(pieces[leaf + 2], high_ref[leaves + leaf + 1], low_ref[leaves + leaf + 1], ROWS_ROWS)
        total = own(nugget_ref, leaf) * field + weight(leaf, 0) * inside
        total = total + weight(leaf, -1) * before + weight(leaf, 1) * after
        out_ref[:, leaf * LEAF : (leaf + 1) * LEAF] = total
        square = square + row_sum(field * field)
        with_image = with_image + row_sum(field * total)
        if not first:
            cross = cross + row_sum(field * own(image_ref, leaf) + own(direction_ref, leaf) * total)
    for block in range(LOCAL):
        scale = 1.0 / (LEAF * (2 if block < 2 else 4))
        here = slice(block * LANES, (block + 1) * LANES)
        with_image = with_image + scale * row_sum(skel_ref[:, here] * skel_ref[:, here])
        if not first:
            cross = cross + scale * row_sum(skel_ref[:, here] * old_skel_ref[:, here])
    sums_ref[...] = in_lanes([square, with_image, cross], (rows, LANES))


def middle_kernel(step, crossing, parts, cluster, *refs):
    refs = list(refs)
    place_ref, gathered_ref, sums_ref = refs[:3]
    previous_ref = refs[3] if step >= 1 else None
    older_ref, state_ref = refs[4:6] if step >= 2 else (None, None)
    outs = refs[3 + (step >= 1) + 2 * (step >= 2) :]
    out_ref = outs[0]
    devices, depth, _ = gathered_ref.shape
    shape = (1, depth, LANES)
    level = lax.broadcasted_iota(jnp.int32, shape, 1)
    lane = lax.broadcasted_iota(jnp.int32, shape, 2)
    mine = place_ref[0] // parts
    sums = gathered_ref[...]
    spread = jnp.zeros(sums.shape, jnp.float32)
    weight = jnp.zeros(shape, jnp.float32)
    for bit in range(crossing):
        pair = sums.reshape(devices >> (bit + 1), 2, depth, LANES)
        sums = pair[:, 0] + pair[:, 1]
        copies = jnp.broadcast_to(sums[:, None], (devices >> (bit + 1), 2 << bit, depth, LANES))
        spread = jnp.where(level == bit, copies.reshape(devices, depth, LANES), spread)
        weight = jnp.where(level == bit, 1.0 / (cluster * (2 << bit) * (2 << bit)), weight)

    def whole_sum(values):
        return jnp.sum(jnp.sum(values, axis=0), keepdims=True)[None]

    with_image = whole_sum(spread * spread * weight)
    cross = jnp.zeros((1, 1, 1), jnp.float32)
    if step >= 1:
        old = previous_ref[...]
        if step >= 2:
            old = old + state_ref[pl.ds(mine, 1), 2:3][None] * older_ref[...]
        cross = whole_sum(spread * old * weight)
        if len(outs) == 2:
            outs[1][...] = old
    here = jnp.zeros((sums_ref.shape[0], LANES), jnp.float32)
    lanes = lax.broadcasted_iota(jnp.int32, here.shape, 1)
    for index in range(3):
        here = jnp.where(lanes == crossing + index, sums_ref[:, index : index + 1], here)
    turned = here.T[:depth]
    turned = jnp.concatenate([turned, jnp.zeros((depth, LANES - turned.shape[1]), jnp.float32)], axis=1)[None]
    extra = jnp.where(level == crossing + 1, with_image, jnp.where(level == crossing + 2, cross, 0.0))
    turned = turned + jnp.where(lane == mine, extra, 0.0)
    out_ref[...] = jnp.where(level < crossing, spread, turned)


def up_kernel(first, last, crossing, *refs):
    refs = list(refs)
    high_ref, low_ref, near_ref, field_ref, spread_ref, skel_ref = refs[:6]
    refs = refs[6:]
    if not first:
        solution_ref, direction_ref, image_ref, old_skel_ref, state_ref = refs[:5]
        refs = refs[5:]
    if last:
        new_solution_ref, new_field_ref = refs
    else:
        (
            new_solution_ref,
            new_field_ref,
            new_direction_ref,
            new_image_ref,
            new_skel_ref,
            new_state_ref,
            head_ref,
            tail_ref,
        ) = refs
    rows, width = field_ref.shape
    half = width // 2
    sums = jnp.sum(spread_ref[...], axis=0).T[:rows]
    norm = sums[:, crossing : crossing + 1]
    curve = sums[:, crossing + 1 : crossing + 2]
    ratio = jnp.zeros_like(norm)
    if not first:
        ratio = norm / state_ref[:, 0:1]
        curve = curve + ratio * (sums[:, crossing + 2 : crossing + 3] + ratio * state_ref[:, 1:2])
    step = norm / curve
    blocks = [skel_ref[:, block * LANES : (block + 1) * LANES] for block in range(LOCAL)]
    blocks = blocks + [spread_ref[:, bit, :] for bit in range(crossing)]
    scaled = [block * (1.0 / (LEAF * (2 ** max(index, 1)))) for index, block in enumerate(blocks)]
    for part in range(2):
        points = slice(part * half, (part + 1) * half)
        stack = stacked(jnp.concatenate([scaled[part]] + scaled[2:], axis=1))
        image = near_ref[:, points] + product(stack, high_ref[:, points], low_ref[:, points], ROWS_COLS)
        direction = field_ref[:, points]
        if not first:
            image = image + ratio * image_ref[:, points]
            direction = direction + ratio * direction_ref[:, points]
        moved = step * direction
        new_solution_ref[:, points] = moved if first else solution_ref[:, points] + moved
        new_field_ref[:, points] = field_ref[:, points] - step * image
        if not last:
            new_direction_ref[:, points] = direction
            new_image_ref[:, points] = image
    if not last:
        head_ref[...] = new_field_ref[:, :LEAF]
        tail_ref[...] = new_field_ref[:, width - LEAF :]
        for index in range(LOCAL):
            here = slice(index * LANES, (index + 1) * LANES)
            new_skel_ref[:, here] = blocks[index] if first else blocks[index] + ratio * old_skel_ref[:, here]
        new_state_ref[...] = in_lanes([norm, curve, ratio], (rows, LANES))


def per_device(rhs, coords, nugget, near_ids, basis):
    rows, width = rhs.shape
    levels, rank, _ = basis.shape
    leaves = width // LEAF
    crossing = levels - (leaves.bit_length() - 1)
    depth = (crossing + 3 + 7) // 8 * 8
    devices = lax.axis_size("row") * lax.axis_size("col")
    parts = devices // rows
    place = jnp.reshape(lax.axis_index(BOTH), (1,))
    upward = [(index, index + 1) for index in range(devices - 1)]
    downward = [(index + 1, index) for index in range(devices - 1)]

    def halo(head, tail):
        return lax.ppermute(tail, BOTH, upward), lax.ppermute(head, BOTH, downward)

    def exchange(blocks):
        return lax.all_to_all(blocks, BOTH, 0, 0, tiled=True)

    def to_owners(partial):
        if parts == 1:
            return exchange(partial)
        cut = partial.reshape(rows, depth, parts, LANES // parts).transpose(0, 2, 1, 3)
        got = exchange(cut.reshape(devices, depth, LANES // parts))
        return jnp.pad(got, ((0, 0), (0, 0), (0, LANES - LANES // parts)))

    def from_owners(spread):
        got = exchange(spread)
        if parts == 1:
            return got
        got = got.reshape(rows, parts, depth, LANES)
        skeletons = got[:, :, :crossing, : LANES // parts].transpose(0, 2, 1, 3).reshape(rows, crossing, LANES)
        return jnp.concatenate([skeletons, jnp.sum(got[:, :, crossing:], axis=1)], axis=1)

    before, after = halo(coords[:, :LEAF], coords[:, width - LEAF :])
    wide = jnp.concatenate([before, coords, after], axis=1)
    near_high, near_low = call(kernel_matrices, [bf16(2 * leaves + 1, LEAF, LEAF)] * 2, wide, wide.T)
    high, low = split_basis(basis)
    nugget = nugget[None, :]
    smem = whole(pltpu.SMEM)

    solution, field, edges, carried = None, rhs, (rhs[:, :LEAF], rhs[:, width - LEAF :]), None
    for step in range(ITERS):
        first, last = step == 0, step == ITERS - 1
        before, after = halo(*edges)
        local, partial = call(down_kernel, [f32(rows, LOCAL * LANES), f32(rows, depth, LANES)], field, high, low)
        gathered = to_owners(partial)
        extra = [] if first else [carried[0], carried[1], carried[2]]
        args = [place, near_ids, field, before, after, nugget, near_high, near_low, local] + extra
        near, sums = call(
            functools.partial(near_kernel, first),
            [f32(rows, width), f32(rows, LANES)],
            *args,
            specs=[smem, smem] + [whole()] * (len(args) - 2),
            flops=2 * 12 * LEAF * LEAF * rows * 8,
        )
        args = [place, gathered, sums] + ([spread] if step >= 1 else []) + ([older, carried[3]] if step >= 2 else [])
        kept = 1 <= step < ITERS - 1
        spread, *rest = call(
            functools.partial(middle_kernel, step, crossing, parts, LEAF * leaves),
            [f32(devices, depth, LANES)] * (2 if kept else 1),
            *args,
            specs=[smem] + [whole()] * (len(args) - 1),
        )
        older = rest[0] if kept else None
        args = [high, low, near, field, from_owners(spread), local]
        if not first:
            args = args + [solution, *carried]
        outs = [f32(rows, width)] * 2
        if not last:
            outs = outs + [f32(rows, width)] * 2 + [f32(rows, LOCAL * LANES), f32(rows, LANES)] + [f32(rows, LEAF)] * 2
        out = call(functools.partial(up_kernel, first, last, crossing), outs, *args)
        solution, field = out[:2]
        if not last:
            carried = out[2:6]
            edges = out[6:8]
    return (solution, field)


def solution(mesh):
    placed = (
        P(None, BOTH),
        P(None, BOTH),
        P(BOTH),
        P(BOTH, None),
        P(None, None, BOTH),
    )
    return jax.shard_map(
        per_device,
        mesh=mesh,
        in_specs=placed,
        out_specs=(P(None, BOTH), P(None, BOTH)),
        check_vma=False,
    )
```

```python
import functools

import jax
import jax.numpy as jnp
from jax import lax
from jax.experimental import pallas as pl
from jax.experimental.pallas import tpu as pltpu
from jax.sharding import PartitionSpec as P

LEAF = 512
ITERS = 4
REACH = 1
WIN = 3
LANES = 128
LOCAL = 3
CHUNK = 64
FLOPS = 3 * 10**9

root_three = 1.7320508075688772
spacing_factor = 1.6
matern_scale = root_three / (spacing_factor * LEAF ** (-1.0 / 3.0))

BOTH = ("row", "col")
ROWS_COLS = (((1,), (0,)), ((), ()))
ROWS_ROWS = (((1,), (1,)), ((), ()))


def halves(values):
    high = values.astype(jnp.bfloat16)
    low = (values - high.astype(jnp.float32)).astype(jnp.bfloat16)
    return high, low


def stacked(values):
    return jnp.concatenate(halves(values), axis=0)


def product(stack, high, low, dims):
    rows = stack.shape[0] // 2
    main = lax.dot_general(stack, high, dims, preferred_element_type=jnp.float32)
    rest = lax.dot_general(stack[:rows], low, dims, preferred_element_type=jnp.float32)
    return main[:rows] + (main[rows:] + rest)


def row_sum(values):
    return jnp.sum(values, axis=1, keepdims=True)


def in_lanes(columns, shape):
    lane = lax.broadcasted_iota(jnp.int32, shape, 1)
    block = jnp.zeros(shape, jnp.float32)
    for index, column in enumerate(columns):
        block = jnp.where(lane == index, column, block)
    return block


def whole(memory=pltpu.VMEM):
    return pl.BlockSpec(memory_space=memory)


def call(body, outs, *args, specs=None, flops=0, limit=32, **extra):
    return pl.pallas_call(
        body,
        out_shape=outs,
        in_specs=specs or [whole()] * len(args),
        out_specs=[whole()] * len(outs),
        compiler_params=pltpu.CompilerParams(vmem_limit_bytes=limit * 2**20),
        cost_estimate=pl.CostEstimate(flops=flops, bytes_accessed=2**20, transcendentals=0),
        **extra,
    )(*args)


def f32(*shape):
    return jax.ShapeDtypeStruct(shape, jnp.float32)


def bf16(*shape):
    return jax.ShapeDtypeStruct(shape, jnp.bfloat16)


def split_kernel(basis_ref, high_ref, low_ref):
    high_ref[...], low_ref[...] = halves(basis_ref[0])


def split_basis(basis):
    levels, rank, width = basis.shape
    return pl.pallas_call(
        split_kernel,
        out_shape=[bf16(levels * rank, width)] * 2,
        grid=(levels,),
        in_specs=[pl.BlockSpec((1, rank, width), lambda level: (level, 0, 0))],
        out_specs=[pl.BlockSpec((rank, width), lambda level: (level, 0))] * 2,
        compiler_params=pltpu.CompilerParams(vmem_limit_bytes=16 * 2**20),
    )(basis)


def kernel_matrices(lane_ref, sub_ref, high_ref, low_ref):
    leaves = lane_ref.shape[1] // LEAF - 2
    parts = LEAF // CHUNK

    def one(step, carry):
        matrix = step // parts
        part = step % parts
        pair = matrix >= leaves
        row_leaf = jnp.where(pair, matrix - leaves, matrix + 1)
        col_leaf = jnp.where(pair, matrix - leaves + 1, matrix + 1)
        row_at = pl.multiple_of(row_leaf * LEAF + part * CHUNK, CHUNK)
        col_at = pl.multiple_of(col_leaf * LEAF, LEAF)
        square = None
        for axis in range(3):
            spread = sub_ref[pl.ds(row_at, CHUNK), axis : axis + 1] - lane_ref[axis : axis + 1, pl.ds(col_at, LEAF)]
            square = spread * spread if square is None else square + spread * spread
        square = square * (matern_scale * matern_scale)
        scaled = square * lax.rsqrt(jnp.maximum(square, 1e-30))
        values = (1.0 + scaled) * jnp.exp(-scaled)
        out_at = pl.ds(pl.multiple_of(part * CHUNK, CHUNK), CHUNK)
        high_ref[matrix, out_at], low_ref[matrix, out_at] = halves(values)
        return carry

    lax.fori_loop(0, (2 * leaves + 1) * parts, one, 0)


def down_kernel(field_ref, high_ref, low_ref, local_ref, out_ref):
    rank = LANES
    half = field_ref.shape[1] // 2
    stack = stacked(field_ref[...])
    for part in range(2):
        points = slice(part * half, (part + 1) * half)
        local_ref[:, part * rank : (part + 1) * rank] = product(
            stack[:, points], high_ref[:rank, points], low_ref[:rank, points], ROWS_ROWS
        )
    whole_width = product(stack, high_ref[rank:], low_ref[rank:], ROWS_ROWS)
    local_ref[:, 2 * rank :] = whole_width[:, :rank]
    out_ref[...] = jnp.zeros(out_ref.shape, jnp.float32)
    for bit in range(whole_width.shape[1] // rank - 1):
        out_ref[:, bit, :] = whole_width[:, (bit + 1) * rank : (bit + 2) * rank]


def near_kernel(first, *refs):
    (place_ref, ids_ref, field_ref, before_ref, after_ref, nugget_ref, high_ref, low_ref, skel_ref) = refs[:9]
    if first:
        out_ref, sums_ref = refs[9:]
    else:
        direction_ref, image_ref, old_skel_ref, out_ref, sums_ref = refs[9:]
    rows, width = field_ref.shape
    leaves = width // LEAF

    def weight(leaf, offset):
        target = place_ref[0] * leaves + leaf + offset
        found = ids_ref[leaf, 0] == target
        for slot in range(1, WIN):
            found = jnp.logical_or(found, ids_ref[leaf, slot] == target)
        return jnp.where(found, 1.0 / (16 * WIN), 0.0)

    def own(ref, leaf):
        return ref[:, leaf * LEAF : (leaf + 1) * LEAF]

    pieces = [stacked(before_ref[...])] + [stacked(own(field_ref, leaf)) for leaf in range(leaves)]
    pieces = pieces + [stacked(after_ref[...])]
    square = with_image = cross = jnp.zeros((rows, 1), jnp.float32)
    for leaf in range(leaves):
        field = own(field_ref, leaf)
        before = product(pieces[leaf], high_ref[leaves + leaf], low_ref[leaves + leaf], ROWS_COLS)
        inside = product(pieces[leaf + 1], high_ref[leaf], low_ref[leaf], ROWS_COLS)
        after = product(pieces[leaf + 2], high_ref[leaves + leaf + 1], low_ref[leaves + leaf + 1], ROWS_ROWS)
        total = own(nugget_ref, leaf) * field + weight(leaf, 0) * inside
        total = total + weight(leaf, -1) * before + weight(leaf, 1) * after
        out_ref[:, leaf * LEAF : (leaf + 1) * LEAF] = total
        square = square + row_sum(field * field)
        with_image = with_image + row_sum(field * total)
        if not first:
            cross = cross + row_sum(field * own(image_ref, leaf) + own(direction_ref, leaf) * total)
    for block in range(LOCAL):
        scale = 1.0 / (LEAF * (2 if block < 2 else 4))
        here = slice(block * LANES, (block + 1) * LANES)
        with_image = with_image + scale * row_sum(skel_ref[:, here] * skel_ref[:, here])
        if not first:
            cross = cross + scale * row_sum(skel_ref[:, here] * old_skel_ref[:, here])
    sums_ref[...] = in_lanes([square, with_image, cross], (rows, LANES))


def middle_kernel(step, crossing, parts, cluster, *refs):
    refs = list(refs)
    place_ref, gathered_ref, sums_ref = refs[:3]
    previous_ref = refs[3] if step >= 1 else None
    older_ref, state_ref = refs[4:6] if step >= 2 else (None, None)
    outs = refs[3 + (step >= 1) + 2 * (step >= 2) :]
    out_ref = outs[0]
    devices, depth, _ = gathered_ref.shape
    shape = (1, depth, LANES)
    level = lax.broadcasted_iota(jnp.int32, shape, 1)
    lane = lax.broadcasted_iota(jnp.int32, shape, 2)
    mine = place_ref[0] // parts
    sums = gathered_ref[...]
    spread = jnp.zeros(sums.shape, jnp.float32)
    weight = jnp.zeros(shape, jnp.float32)
    for bit in range(crossing):
        pair = sums.reshape(devices >> (bit + 1), 2, depth, LANES)
        sums = pair[:, 0] + pair[:, 1]
        copies = jnp.broadcast_to(sums[:, None], (devices >> (bit + 1), 2 << bit, depth, LANES))
        spread = jnp.where(level == bit, copies.reshape(devices, depth, LANES), spread)
        weight = jnp.where(level == bit, 1.0 / (cluster * (2 << bit) * (2 << bit)), weight)

    def whole_sum(values):
        return jnp.sum(jnp.sum(values, axis=0), keepdims=True)[None]

    with_image = whole_sum(spread * spread * weight)
    cross = jnp.zeros((1, 1, 1), jnp.float32)
    if step >= 1:
        old = previous_ref[...]
        if step >= 2:
            old = old + state_ref[pl.ds(mine, 1), 2:3][None] * older_ref[...]
        cross = whole_sum(spread * old * weight)
        if len(outs) == 2:
            outs[1][...] = old
    here = jnp.zeros((sums_ref.shape[0], LANES), jnp.float32)
    lanes = lax.broadcasted_iota(jnp.int32, here.shape, 1)
    for index in range(3):
        here = jnp.where(lanes == crossing + index, sums_ref[:, index : index + 1], here)
    turned = here.T[:depth]
    turned = jnp.concatenate([turned, jnp.zeros((depth, LANES - turned.shape[1]), jnp.float32)], axis=1)[None]
    extra = jnp.where(level == crossing + 1, with_image, jnp.where(level == crossing + 2, cross, 0.0))
    turned = turned + jnp.where(lane == mine, extra, 0.0)
    out_ref[...] = jnp.where(level < crossing, spread, turned)


def local_up_kernel(high_ref, low_ref, near_ref, skel_ref, out_ref):
    half = near_ref.shape[1] // 2
    for part in range(2):
        points = slice(part * half, (part + 1) * half)
        one = skel_ref[:, part * LANES : (part + 1) * LANES] * (1.0 / (2 * LEAF))
        two = skel_ref[:, 2 * LANES :] * (1.0 / (4 * LEAF))
        stack = stacked(jnp.concatenate([one, two], axis=1))
        out_ref[:, points] = near_ref[:, points] + product(
            stack, high_ref[: 2 * LANES, points], low_ref[: 2 * LANES, points], ROWS_COLS
        )


def up_kernel(first, last, crossing, *refs):
    refs = list(refs)
    high_ref, low_ref, near_ref, field_ref, spread_ref, skel_ref = refs[:6]
    refs = refs[6:]
    if not first:
        solution_ref, direction_ref, image_ref, old_skel_ref, state_ref = refs[:5]
        refs = refs[5:]
    if last:
        new_solution_ref, new_field_ref = refs
    else:
        (
            new_solution_ref,
            new_field_ref,
            new_direction_ref,
            new_image_ref,
            new_skel_ref,
            new_state_ref,
            head_ref,
            tail_ref,
        ) = refs
    rows, width = field_ref.shape
    half = width // 2
    sums = jnp.sum(spread_ref[...], axis=0).T[:rows]
    norm = sums[:, crossing : crossing + 1]
    curve = sums[:, crossing + 1 : crossing + 2]
    ratio = jnp.zeros_like(norm)
    if not first:
        ratio = norm / state_ref[:, 0:1]
        curve = curve + ratio * (sums[:, crossing + 2 : crossing + 3] + ratio * state_ref[:, 1:2])
    step = norm / curve
    scaled = [spread_ref[:, bit, :] * (1.0 / (width * (2 << bit))) for bit in range(crossing)]
    stack = stacked(jnp.concatenate(scaled, axis=1))
    for part in range(2):
        points = slice(part * half, (part + 1) * half)
        image = near_ref[:, points] + product(
            stack, high_ref[2 * LANES :, points], low_ref[2 * LANES :, points], ROWS_COLS
        )
        direction = field_ref[:, points]
        if not first:
            image = image + ratio * image_ref[:, points]
            direction = direction + ratio * direction_ref[:, points]
        moved = step * direction
        new_solution_ref[:, points] = moved if first else solution_ref[:, points] + moved
        new_field_ref[:, points] = field_ref[:, points] - step * image
        if not last:
            new_direction_ref[:, points] = direction
            new_image_ref[:, points] = image
    if not last:
        head_ref[...] = new_field_ref[:, :LEAF]
        tail_ref[...] = new_field_ref[:, width - LEAF :]
        new_skel_ref[...] = skel_ref[...] if first else skel_ref[...] + ratio * old_skel_ref[...]
        new_state_ref[...] = in_lanes([norm, curve, ratio], (rows, LANES))


def per_device(rhs, coords, nugget, near_ids, basis):
    rows, width = rhs.shape
    levels, rank, _ = basis.shape
    leaves = width // LEAF
    crossing = levels - (leaves.bit_length() - 1)
    depth = (crossing + 3 + 7) // 8 * 8
    devices = lax.axis_size("row") * lax.axis_size("col")
    parts = devices // rows
    place = jnp.reshape(lax.axis_index(BOTH), (1,))
    upward = [(index, index + 1) for index in range(devices - 1)]
    downward = [(index + 1, index) for index in range(devices - 1)]

    def halo(head, tail):
        return lax.ppermute(tail, BOTH, upward), lax.ppermute(head, BOTH, downward)

    def exchange(blocks):
        return lax.all_to_all(blocks, BOTH, 0, 0, tiled=True)

    def to_owners(partial):
        if parts == 1:
            return exchange(partial)
        cut = partial.reshape(rows, depth, parts, LANES // parts).transpose(0, 2, 1, 3)
        got = exchange(cut.reshape(devices, depth, LANES // parts))
        return jnp.pad(got, ((0, 0), (0, 0), (0, LANES - LANES // parts)))

    def from_owners(spread):
        got = exchange(spread)
        if parts == 1:
            return got
        got = got.reshape(rows, parts, depth, LANES)
        skeletons = got[:, :, :crossing, : LANES // parts].transpose(0, 2, 1, 3).reshape(rows, crossing, LANES)
        return jnp.concatenate([skeletons, jnp.sum(got[:, :, crossing:], axis=1)], axis=1)

    before, after = halo(coords[:, :LEAF], coords[:, width - LEAF :])
    wide = jnp.concatenate([before, coords, after], axis=1)
    near_high, near_low = call(kernel_matrices, [bf16(2 * leaves + 1, LEAF, LEAF)] * 2, wide, wide.T)
    high, low = split_basis(basis)
    nugget = nugget[None, :]
    smem = whole(pltpu.SMEM)

    solution, field, edges, carried = None, rhs, (rhs[:, :LEAF], rhs[:, width - LEAF :]), None
    for step in range(ITERS):
        first, last = step == 0, step == ITERS - 1
        before, after = halo(*edges)
        local, partial = call(down_kernel, [f32(rows, LOCAL * LANES), f32(rows, depth, LANES)], field, high, low, flops=FLOPS)
        gathered = to_owners(partial)
        extra = [] if first else [carried[0], carried[1], carried[2]]
        args = [place, near_ids, field, before, after, nugget, near_high, near_low, local] + extra
        near, sums = call(
            functools.partial(near_kernel, first),
            [f32(rows, width), f32(rows, LANES)],
            *args,
            specs=[smem, smem] + [whole()] * (len(args) - 2),
            flops=FLOPS,
        )
        args = [place, gathered, sums] + ([spread] if step >= 1 else []) + ([older, carried[3]] if step >= 2 else [])
        kept = 1 <= step < ITERS - 1
        spread, *rest = call(
            functools.partial(middle_kernel, step, crossing, parts, LEAF * leaves),
            [f32(devices, depth, LANES)] * (2 if kept else 1),
            *args,
            specs=[smem] + [whole()] * (len(args) - 1),
        )
        older = rest[0] if kept else None
        near, spread = lax.optimization_barrier((near, spread))
        summed = from_owners(spread)
        (near,) = call(local_up_kernel, [f32(rows, width)], high, low, near, local, flops=FLOPS // 4)
        args = [high, low, near, field, summed, local]
        if not first:
            args = args + [solution, *carried]
        outs = [f32(rows, width)] * 2
        if not last:
            outs = outs + [f32(rows, width)] * 2 + [f32(rows, LOCAL * LANES), f32(rows, LANES)] + [f32(rows, LEAF)] * 2
        out = call(functools.partial(up_kernel, first, last, crossing), outs, *args, flops=FLOPS // 2)
        solution, field = out[:2]
        if not last:
            carried = out[2:6]
            edges = out[6:8]
    return (solution, field)


def solution(mesh):
    placed = (
        P(None, BOTH),
        P(None, BOTH),
        P(BOTH),
        P(BOTH, None),
        P(None, None, BOTH),
    )
    return jax.shard_map(
        per_device,
        mesh=mesh,
        in_specs=placed,
        out_specs=(P(None, BOTH), P(None, BOTH)),
        check_vma=False,
    )
```

```python
import functools

import jax
import jax.numpy as jnp
from jax import lax
from jax.experimental import pallas as pl
from jax.experimental.pallas import tpu as pltpu
from jax.sharding import PartitionSpec as P

LEAF = 512
ITERS = 4
WIN = 3
LANES = 128
TILE = 8
LOCAL = 3
CHUNK = 16
FLOPS = 3 * 10**9

root_three = 1.7320508075688772
spacing_factor = 1.6
matern_scale = root_three / (spacing_factor * LEAF ** (-1.0 / 3.0))

BOTH = ("row", "col")
ROWS_COLS = (((1,), (0,)), ((), ()))
ROWS_ROWS = (((1,), (1,)), ((), ()))


def halves(values):
    high = values.astype(jnp.bfloat16)
    low = (values - high.astype(jnp.float32)).astype(jnp.bfloat16)
    return high, low


def stacked(values):
    return jnp.concatenate(halves(values), axis=0)


def product(stack, high, low, dims):
    rows = stack.shape[0] // 2
    main = lax.dot_general(stack, high, dims, preferred_element_type=jnp.float32)
    rest = lax.dot_general(stack[:rows], low, dims, preferred_element_type=jnp.float32)
    return main[:rows] + (main[rows:] + rest)


def row_sum(values):
    return jnp.sum(values, axis=1, keepdims=True)


def in_lanes(columns, shape):
    lane = lax.broadcasted_iota(jnp.int32, shape, 1)
    block = jnp.zeros(shape, jnp.float32)
    for index, column in enumerate(columns):
        block = jnp.where(lane == index, column, block)
    return block


def sums_tile(columns, rows):
    turned = in_lanes(columns, (rows, LANES)).T[:TILE]
    return jnp.concatenate([turned, jnp.zeros((TILE, LANES - rows), jnp.float32)], axis=1)


def level_terms(core, columns, rows):
    twice = [jnp.concatenate([column, column], axis=0) for column in columns]
    tile = sums_tile([jnp.zeros((rows, 1), jnp.float32)] + twice, rows)
    lane = lax.broadcasted_iota(jnp.int32, tile.shape, 1)
    return jnp.where(lane // (rows // 2) == core, tile, 0.0)


def chosen(core, odd, even):
    return jnp.where(core == 1, odd, even)


def whole(memory=pltpu.VMEM):
    return pl.BlockSpec(memory_space=memory)


def call(body, outs, *args, scalars=0, flops=0, limit=32):
    return pl.pallas_call(
        body,
        out_shape=outs,
        in_specs=[whole(pltpu.SMEM)] * scalars + [whole()] * (len(args) - scalars),
        out_specs=[whole()] * len(outs),
        compiler_params=pltpu.CompilerParams(vmem_limit_bytes=limit * 2**20),
        cost_estimate=pl.CostEstimate(flops=flops, bytes_accessed=2**20, transcendentals=0),
    )(*args)


def f32(*shape):
    return jax.ShapeDtypeStruct(shape, jnp.float32)


def bf16(*shape):
    return jax.ShapeDtypeStruct(shape, jnp.bfloat16)


def split_kernel(basis_ref, high_ref, low_ref):
    high_ref[...], low_ref[...] = halves(basis_ref[0])


def split_basis(basis):
    levels, rank, width = basis.shape
    return pl.pallas_call(
        split_kernel,
        out_shape=[bf16(levels * rank, width)] * 2,
        grid=(levels,),
        in_specs=[pl.BlockSpec((1, rank, width), lambda level: (level, 0, 0))],
        out_specs=[pl.BlockSpec((rank, width), lambda level: (level, 0))] * 2,
        compiler_params=pltpu.CompilerParams(vmem_limit_bytes=16 * 2**20),
    )(basis)


def matrix_rows(rows, lanes):
    square = None
    for axis in range(3):
        spread = rows[:, axis : axis + 1] - lanes[axis : axis + 1]
        square = spread * spread if square is None else square + spread * spread
    square = square * (matern_scale * matern_scale)
    scaled = square * lax.rsqrt(jnp.maximum(square, 1e-30))
    return halves((1.0 + scaled) * jnp.exp(-scaled))


def inner_matrices(lane_ref, sub_ref, high_ref, low_ref):
    leaves = lane_ref.shape[1] // LEAF
    parts = LEAF // CHUNK

    def one(step, carry):
        matrix = step // parts
        part = step % parts
        pair = matrix >= leaves
        row_leaf = jnp.where(pair, matrix - leaves, matrix)
        col_leaf = jnp.where(pair, matrix - leaves + 1, matrix)
        row_at = pl.multiple_of(row_leaf * LEAF + part * CHUNK, CHUNK)
        col_at = pl.multiple_of(col_leaf * LEAF, LEAF)
        out_at = pl.ds(pl.multiple_of(part * CHUNK, CHUNK), CHUNK)
        values = matrix_rows(sub_ref[pl.ds(row_at, CHUNK)], lane_ref[:, pl.ds(col_at, LEAF)])
        high_ref[matrix, out_at], low_ref[matrix, out_at] = values
        return carry

    lax.fori_loop(0, (2 * leaves - 1) * parts, one, 0, unroll=4)


def edge_matrices(core_ref, rows, sub_ref, paired_ref, other_ref, high_ref, low_ref):
    core = core_ref[0]
    leaves = sub_ref.shape[0] // LEAF
    here = slice(rows, rows + 3)
    lanes = [
        chosen(core, paired_ref[here], other_ref[here]),
        chosen(core, other_ref[here], paired_ref[here]),
    ]

    for side in range(2):
        first_row = side * (leaves - 1) * LEAF

        def one(part, carry):
            row_at = pl.multiple_of(first_row + part * CHUNK, CHUNK)
            out_at = pl.ds(pl.multiple_of(part * CHUNK, CHUNK), CHUNK)
            values = matrix_rows(sub_ref[pl.ds(row_at, CHUNK)], lanes[side])
            high_ref[side, out_at], low_ref[side, out_at] = values
            return carry

        lax.fori_loop(0, LEAF // CHUNK, one, 0, unroll=4)


def edges_kernel(core_ref, field_ref, coords_ref, paired_ref, other_ref):
    core = core_ref[0]
    rows, width = field_ref.shape
    pad = jnp.zeros((TILE - 3, LEAF), jnp.float32)
    head = jnp.concatenate([field_ref[:, :LEAF], coords_ref[:, :LEAF], pad], axis=0)
    tail = jnp.concatenate([field_ref[:, width - LEAF :], coords_ref[:, width - LEAF :], pad], axis=0)
    paired_ref[...] = chosen(core, head, tail)
    other_ref[...] = chosen(core, tail, head)


def down_kernel(core_ref, field_ref, high_ref, low_ref, local_ref, keep_ref, send_ref):
    core = core_ref[0]
    rank = LANES
    rows, width = field_ref.shape
    half = width // 2
    stack = stacked(field_ref[...])
    for part in range(2):
        points = slice(part * half, (part + 1) * half)
        local_ref[:, part * rank : (part + 1) * rank] = product(
            stack[:, points], high_ref[:rank, points], low_ref[:rank, points], ROWS_ROWS
        )
    all_points = product(stack, high_ref[rank:], low_ref[rank:], ROWS_ROWS)
    local_ref[:, 2 * rank :] = all_points[:, :rank]
    own = rows // 2
    for bit in range(all_points.shape[1] // rank - 1):
        block = all_points[:, (bit + 1) * rank : (bit + 2) * rank]
        keep_ref[bit * own : (bit + 1) * own] = chosen(core, block[own:], block[:own])
        send_ref[bit * own : (bit + 1) * own] = chosen(core, block[:own], block[own:])


def leaf_of(ref, leaf):
    return ref[:, leaf * LEAF : (leaf + 1) * LEAF]


def weight_of(place_ref, ids_ref, leaf, offset):
    target = place_ref[0] * ids_ref.shape[0] + leaf + offset
    found = ids_ref[leaf, 0] == target
    for slot in range(1, WIN):
        found = jnp.logical_or(found, ids_ref[leaf, slot] == target)
    return jnp.where(found, 1.0 / (16 * WIN), 0.0)


def inner_kernel(place_ref, ids_ref, field_ref, nugget_ref, high_ref, low_ref, out_ref):
    leaves = ids_ref.shape[0]
    pieces = [stacked(leaf_of(field_ref, leaf)) for leaf in range(leaves)]
    for leaf in range(leaves):
        inside = product(pieces[leaf], high_ref[leaf], low_ref[leaf], ROWS_COLS)
        total = leaf_of(nugget_ref, leaf) * leaf_of(field_ref, leaf) + weight_of(place_ref, ids_ref, leaf, 0) * inside
        if leaf > 0:
            at = leaves + leaf - 1
            before = product(pieces[leaf - 1], high_ref[at], low_ref[at], ROWS_COLS)
            total = total + weight_of(place_ref, ids_ref, leaf, -1) * before
        if leaf < leaves - 1:
            at = leaves + leaf
            after = product(pieces[leaf + 1], high_ref[at], low_ref[at], ROWS_ROWS)
            total = total + weight_of(place_ref, ids_ref, leaf, 1) * after
        out_ref[:, leaf * LEAF : (leaf + 1) * LEAF] = total


def edge_kernel(first, cluster, *refs):
    place_ref, core_ref, ids_ref, field_ref, paired_ref, other_ref, high_ref, low_ref, inner_ref = refs[:9]
    local_ref, keep_ref, got_ref = refs[9:12]
    refs = refs[12:]
    if not first:
        direction_ref, image_ref, old_local_ref, old_ref = refs[:4]
        refs = refs[4:]
    out_ref, message_ref, level_ref = refs
    core = core_ref[0]
    leaves = ids_ref.shape[0]
    rows, width = field_ref.shape
    own = rows // 2
    before = chosen(core, paired_ref[:rows], other_ref[:rows])
    after = chosen(core, other_ref[:rows], paired_ref[:rows])
    square = with_image = cross = jnp.zeros((rows, 1), jnp.float32)
    for leaf in range(leaves):
        field = leaf_of(field_ref, leaf)
        total = leaf_of(inner_ref, leaf)
        if leaf == 0:
            part = product(stacked(before), high_ref[0], low_ref[0], ROWS_ROWS)
            total = total + weight_of(place_ref, ids_ref, leaf, -1) * part
        if leaf == leaves - 1:
            part = product(stacked(after), high_ref[1], low_ref[1], ROWS_ROWS)
            total = total + weight_of(place_ref, ids_ref, leaf, 1) * part
        out_ref[:, leaf * LEAF : (leaf + 1) * LEAF] = total
        square = square + row_sum(field * field)
        with_image = with_image + row_sum(field * total)
        if not first:
            cross = cross + row_sum(field * leaf_of(image_ref, leaf) + leaf_of(direction_ref, leaf) * total)
    for block in range(LOCAL):
        scale = 1.0 / (LEAF * (2 if block < 2 else 4))
        here = slice(block * LANES, (block + 1) * LANES)
        with_image = with_image + scale * row_sum(local_ref[:, here] * local_ref[:, here])
        if not first:
            cross = cross + scale * row_sum(local_ref[:, here] * old_local_ref[:, here])
    total = keep_ref[...] + got_ref[...]
    level = total[:own]
    level_ref[...] = level
    columns = [row_sum(level * level) * (1.0 / cluster)]
    if not first:
        columns.append(row_sum(level * old_ref[:own]) * (1.0 / cluster))
    left = total.shape[0] - own
    if left:
        message_ref[:left] = total[own:]
    message_ref[left:] = sums_tile([square, with_image, cross], rows) + level_terms(core, columns, rows)


def combine_kernel(first, bit, cluster, *refs):
    refs = list(refs)
    core_ref, mine_ref, other_ref = refs[:3]
    refs = refs[3:]
    if not first:
        old_ref = refs.pop(0)
    *level_refs, next_ref, level_ref = refs
    own = level_ref.shape[0]
    total = mine_ref[...] + other_ref[...]
    level = total[:own]
    level_ref[...] = level
    columns = [row_sum(level * level) * (1.0 / cluster)]
    if not first:
        columns.append(row_sum(level * old_ref[bit * own : (bit + 1) * own]) * (1.0 / cluster))
    tile = total[total.shape[0] - TILE :] + level_terms(core_ref[0], columns, 2 * own)
    left = total.shape[0] - TILE - own
    if left:
        next_ref[:left] = total[own : own + left]
        next_ref[left:] = tile
    else:
        for index, ref in enumerate(level_refs):
            next_ref[index * own : (index + 1) * own] = ref[...]
        next_ref[bit * own : (bit + 1) * own] = level
        next_ref[(bit + 1) * own :] = tile


def up_kernel(first, last, *refs):
    core_ref, high_ref, low_ref, near_ref, field_ref, mine_ref, other_ref, local_ref = refs[:8]
    refs = refs[8:]
    if not first:
        solution_ref, direction_ref, image_ref, old_local_ref, old_ref, state_ref = refs[:6]
        refs = refs[6:]
    new_solution_ref, new_field_ref = refs[:2]
    if not last:
        new_direction_ref, new_image_ref, new_local_ref, new_old_ref, new_state_ref, paired_ref, send_ref = refs[2:]
    core = core_ref[0]
    rows, width = field_ref.shape
    own = rows // 2
    half = width // 2
    crossing = (mine_ref.shape[0] - TILE) // own
    sums = (mine_ref[crossing * own :] + other_ref[crossing * own :]).T[:rows]
    norm = sums[:, 0:1]
    curve = sums[:, 1:2]
    ratio = jnp.zeros_like(norm)
    if not first:
        ratio = norm / state_ref[:, 0:1]
        curve = curve + ratio * (sums[:, 2:3] + ratio * state_ref[:, 1:2])
    step = norm / curve
    scaled = []
    for bit in range(crossing):
        here = slice(bit * own, (bit + 1) * own)
        low_rows = chosen(core, other_ref[here], mine_ref[here])
        high_rows = chosen(core, mine_ref[here], other_ref[here])
        scaled.append(jnp.concatenate([low_rows, high_rows], axis=0) * (1.0 / (width * (2 << bit))))
    one = [local_ref[:, part * LANES : (part + 1) * LANES] * (1.0 / (2 * LEAF)) for part in range(2)]
    two = local_ref[:, 2 * LANES :] * (1.0 / (4 * LEAF))
    for part in range(2):
        points = slice(part * half, (part + 1) * half)
        stack = stacked(jnp.concatenate([one[part], two] + scaled, axis=1))
        image = near_ref[:, points] + product(stack, high_ref[:, points], low_ref[:, points], ROWS_COLS)
        direction = field_ref[:, points]
        if not first:
            image = image + ratio * image_ref[:, points]
            direction = direction + ratio * direction_ref[:, points]
        moved = step * direction
        new_solution_ref[:, points] = moved if first else solution_ref[:, points] + moved
        new_field_ref[:, points] = field_ref[:, points] - step * image
        if not last:
            new_direction_ref[:, points] = direction
            new_image_ref[:, points] = image
    if not last:
        head = new_field_ref[:, :LEAF]
        tail = new_field_ref[:, width - LEAF :]
        paired_ref[...] = chosen(core, head, tail)
        send_ref[...] = chosen(core, tail, head)
        skeletons = mine_ref[: crossing * own]
        if first:
            new_local_ref[...] = local_ref[...]
            new_old_ref[...] = skeletons
        else:
            new_local_ref[...] = local_ref[...] + ratio * old_local_ref[...]
            own_ratio = chosen(core, ratio[own:], ratio[:own])
            own_ratio = jnp.concatenate([own_ratio] * crossing, axis=0)
            new_old_ref[...] = skeletons + own_ratio * old_ref[...]
        new_state_ref[...] = in_lanes([norm, curve], (rows, LANES))


def per_device(rhs, coords, nugget, near_ids, basis):
    rows, width = rhs.shape
    levels = basis.shape[0]
    leaves = width // LEAF
    own = rows // 2
    crossing = levels - (leaves.bit_length() - 1)
    devices = lax.axis_size("row") * lax.axis_size("col")
    place = jnp.reshape(lax.axis_index(BOTH), (1,))
    core = place % 2

    def swap(value, bit):
        return lax.ppermute(value, BOTH, [(source, source ^ (1 << bit)) for source in range(devices)])

    def halo(paired, other):
        outward = [(index, index + 1) for index in range(1, devices - 1, 2)]
        pairs = outward + [(target, source) for source, target in outward]
        return swap(paired, 0), lax.ppermute(other, BOTH, pairs)

    edges = call(edges_kernel, [f32(rows + TILE, LEAF)] * 2, core, rhs, coords, scalars=1)
    edges = halo(*edges)
    turned = coords.T
    inner_pair = call(inner_matrices, [bf16(2 * leaves - 1, LEAF, LEAF)] * 2, coords, turned, flops=4 * FLOPS)
    high, low = split_basis(basis)
    edge_pair = call(
        lambda core_ref, *refs: edge_matrices(core_ref, rows, *refs),
        [bf16(2, LEAF, LEAF)] * 2,
        core,
        turned,
        *edges,
        scalars=1,
        flops=FLOPS,
    )
    nugget = nugget[None, :]

    solution, field, carried = None, rhs, None
    for step in range(ITERS):
        first, last = step == 0, step == ITERS - 1
        local, keep, send = call(
            down_kernel,
            [f32(rows, LOCAL * LANES)] + [f32(crossing * own, LANES)] * 2,
            core,
            field,
            high,
            low,
            scalars=1,
            flops=FLOPS,
        )
        got = swap(send, 0)
        (inner,) = call(
            inner_kernel, [f32(rows, width)], place, near_ids, field, nugget, *inner_pair, scalars=2, flops=FLOPS
        )
        args = [place, core, near_ids, field, *edges, *edge_pair, inner, local, keep, got]
        near, message, level = call(
            functools.partial(edge_kernel, first, 2 * width),
            [f32(rows, width), f32((crossing - 1) * own + TILE, LANES), f32(own, LANES)],
            *args,
            *([] if first else carried[:4]),
            scalars=3,
            flops=FLOPS // 4,
        )
        done = [level]
        for bit in range(1, crossing):
            left = crossing - bit - 1
            args = [core, message, swap(message, bit)] + ([] if first else [carried[3]]) + (done if left == 0 else [])
            message, level = call(
                functools.partial(combine_kernel, first, bit, width * (2 << bit)),
                [f32((left or crossing) * own + TILE, LANES), f32(own, LANES)],
                *args,
                scalars=1,
            )
            done.append(level)
        args = [core, high, low, near, field, message, swap(message, 0), local]
        if not first:
            args = args + [solution, *carried]
        outs = [f32(rows, width)] * 2
        if not last:
            outs = outs + [f32(rows, width)] * 2 + [f32(rows, LOCAL * LANES), f32(crossing * own, LANES)]
            outs = outs + [f32(rows, LANES)] + [f32(rows, LEAF)] * 2
        out = call(functools.partial(up_kernel, first, last), outs, *args, scalars=1, flops=FLOPS // 2)
        solution, field = out[:2]
        if not last:
            carried = out[2:7]
            edges = halo(*out[7:9])
    return (solution, field)


def solution(mesh):
    placed = (
        P(None, BOTH),
        P(None, BOTH),
        P(BOTH),
        P(BOTH, None),
        P(None, None, BOTH),
    )
    return jax.shard_map(
        per_device,
        mesh=mesh,
        in_specs=placed,
        out_specs=(P(None, BOTH), P(None, BOTH)),
        check_vma=False,
    )
```

```python
import functools

import jax
import jax.numpy as jnp
from jax import lax
from jax.experimental import pallas as pl
from jax.experimental.pallas import tpu as pltpu
from jax.sharding import PartitionSpec as P

LEAF = 512
ITERS = 4
WIN = 3
LANES = 128
TILE = 8
LOCAL = 3
CHUNK = 16
FLOPS = 3 * 10**9

root_three = 1.7320508075688772
spacing_factor = 1.6
matern_scale = root_three / (spacing_factor * LEAF ** (-1.0 / 3.0))

BOTH = ("row", "col")
ROWS_COLS = (((1,), (0,)), ((), ()))
ROWS_ROWS = (((1,), (1,)), ((), ()))


def halves(values):
    high = values.astype(jnp.bfloat16)
    low = (values - high.astype(jnp.float32)).astype(jnp.bfloat16)
    return high, low


def stacked(values):
    return jnp.concatenate(halves(values), axis=0)


def product(stack, high, low, dims):
    rows = stack.shape[0] // 2
    main = lax.dot_general(stack, high, dims, preferred_element_type=jnp.float32)
    rest = lax.dot_general(stack[:rows], low, dims, preferred_element_type=jnp.float32)
    return main[:rows] + (main[rows:] + rest)


def row_sum(values):
    return jnp.sum(values, axis=1, keepdims=True)


def in_lanes(columns, shape):
    lane = lax.broadcasted_iota(jnp.int32, shape, 1)
    block = jnp.zeros(shape, jnp.float32)
    for index, column in enumerate(columns):
        block = jnp.where(lane == index, column, block)
    return block


def sums_tile(columns, rows):
    turned = in_lanes(columns, (rows, LANES)).T[:TILE]
    return jnp.concatenate([turned, jnp.zeros((TILE, LANES - rows), jnp.float32)], axis=1)


def level_terms(level, old, cluster):
    columns = [jnp.zeros((level.shape[0], 1), jnp.float32), row_sum(level * level) * (1.0 / cluster)]
    if old is not None:
        columns.append(row_sum(level * old) * (1.0 / cluster))
    return sums_tile(columns, level.shape[0])


def chosen(core, odd, even):
    return jnp.where(core == 1, odd, even)


def whole(memory=pltpu.VMEM):
    return pl.BlockSpec(memory_space=memory)


def call(body, outs, *args, scalars=0, flops=0, limit=32):
    return pl.pallas_call(
        body,
        out_shape=outs,
        in_specs=[whole(pltpu.SMEM)] * scalars + [whole()] * (len(args) - scalars),
        out_specs=[whole()] * len(outs),
        compiler_params=pltpu.CompilerParams(vmem_limit_bytes=limit * 2**20),
        cost_estimate=pl.CostEstimate(flops=flops, bytes_accessed=2**20, transcendentals=0),
    )(*args)


def f32(*shape):
    return jax.ShapeDtypeStruct(shape, jnp.float32)


def bf16(*shape):
    return jax.ShapeDtypeStruct(shape, jnp.bfloat16)


def matrix_rows(rows, lanes):
    square = None
    for axis in range(3):
        spread = rows[:, axis : axis + 1] - lanes[axis : axis + 1]
        square = spread * spread if square is None else square + spread * spread
    square = square * (matern_scale * matern_scale)
    scaled = square * lax.rsqrt(jnp.maximum(square, 1e-30))
    return halves((1.0 + scaled) * jnp.exp(-scaled))


def setup_kernel(lane_ref, sub_ref, basis_ref, high_ref, low_ref, basis_high_ref, basis_low_ref, raw_ref, sem_ref):
    levels, rank, _ = basis_ref.shape
    copies = [pltpu.make_async_copy(basis_ref.at[at], raw_ref.at[at], sem_ref.at[at]) for at in range(levels)]
    for copy in copies:
        copy.start()
    leaves = lane_ref.shape[1] // LEAF
    parts = LEAF // CHUNK

    def one(step, carry):
        matrix = step // parts
        part = step % parts
        pair = matrix >= leaves
        row_leaf = jnp.where(pair, matrix - leaves, matrix)
        col_leaf = jnp.where(pair, matrix - leaves + 1, matrix)
        row_at = pl.multiple_of(row_leaf * LEAF + part * CHUNK, CHUNK)
        col_at = pl.multiple_of(col_leaf * LEAF, LEAF)
        out_at = pl.ds(pl.multiple_of(part * CHUNK, CHUNK), CHUNK)
        values = matrix_rows(sub_ref[pl.ds(row_at, CHUNK)], lane_ref[:, pl.ds(col_at, LEAF)])
        high_ref[matrix, out_at], low_ref[matrix, out_at] = values
        return carry

    lax.fori_loop(0, (2 * leaves - 1) * parts, one, 0, unroll=4)
    for at, copy in enumerate(copies):
        copy.wait()
        here = slice(at * rank, (at + 1) * rank)
        basis_high_ref[here], basis_low_ref[here] = halves(raw_ref[at])


def edge_matrices(core_ref, rows, sub_ref, paired_ref, other_ref, high_ref, low_ref):
    core = core_ref[0]
    leaves = sub_ref.shape[0] // LEAF
    here = slice(rows, rows + 3)
    lanes = [
        chosen(core, paired_ref[here], other_ref[here]),
        chosen(core, other_ref[here], paired_ref[here]),
    ]

    for side in range(2):
        first_row = side * (leaves - 1) * LEAF

        def one(part, carry):
            row_at = pl.multiple_of(first_row + part * CHUNK, CHUNK)
            out_at = pl.ds(pl.multiple_of(part * CHUNK, CHUNK), CHUNK)
            values = matrix_rows(sub_ref[pl.ds(row_at, CHUNK)], lanes[side])
            high_ref[side, out_at], low_ref[side, out_at] = values
            return carry

        lax.fori_loop(0, LEAF // CHUNK, one, 0, unroll=4)


def edges_kernel(core_ref, field_ref, coords_ref, paired_ref, other_ref):
    core = core_ref[0]
    rows, width = field_ref.shape
    pad = jnp.zeros((TILE - 3, LEAF), jnp.float32)
    head = jnp.concatenate([field_ref[:, :LEAF], coords_ref[:, :LEAF], pad], axis=0)
    tail = jnp.concatenate([field_ref[:, width - LEAF :], coords_ref[:, width - LEAF :], pad], axis=0)
    paired_ref[...] = chosen(core, head, tail)
    other_ref[...] = chosen(core, tail, head)


def down_kernel(field_ref, high_ref, low_ref, local_ref, part_ref):
    rank = LANES
    rows, width = field_ref.shape
    half = width // 2
    stack = stacked(field_ref[...])
    for part in range(2):
        points = slice(part * half, (part + 1) * half)
        local_ref[:, part * rank : (part + 1) * rank] = product(
            stack[:, points], high_ref[:rank, points], low_ref[:rank, points], ROWS_ROWS
        )
    all_points = product(stack, high_ref[rank:], low_ref[rank:], ROWS_ROWS)
    local_ref[:, 2 * rank :] = all_points[:, :rank]
    for bit in range(all_points.shape[1] // rank - 1):
        part_ref[bit * rows : (bit + 1) * rows] = all_points[:, (bit + 1) * rank : (bit + 2) * rank]


def leaf_of(ref, leaf):
    return ref[:, leaf * LEAF : (leaf + 1) * LEAF]


def weight_of(place_ref, ids_ref, leaf, offset):
    target = place_ref[0] * ids_ref.shape[0] + leaf + offset
    found = ids_ref[leaf, 0] == target
    for slot in range(1, WIN):
        found = jnp.logical_or(found, ids_ref[leaf, slot] == target)
    return jnp.where(found, 1.0 / (16 * WIN), 0.0)


def inner_kernel(place_ref, ids_ref, field_ref, nugget_ref, high_ref, low_ref, out_ref):
    leaves = ids_ref.shape[0]
    pieces = [stacked(leaf_of(field_ref, leaf)) for leaf in range(leaves)]
    for leaf in range(leaves):
        inside = product(pieces[leaf], high_ref[leaf], low_ref[leaf], ROWS_COLS)
        total = leaf_of(nugget_ref, leaf) * leaf_of(field_ref, leaf) + weight_of(place_ref, ids_ref, leaf, 0) * inside
        if leaf > 0:
            at = leaves + leaf - 1
            before = product(pieces[leaf - 1], high_ref[at], low_ref[at], ROWS_COLS)
            total = total + weight_of(place_ref, ids_ref, leaf, -1) * before
        if leaf < leaves - 1:
            at = leaves + leaf
            after = product(pieces[leaf + 1], high_ref[at], low_ref[at], ROWS_ROWS)
            total = total + weight_of(place_ref, ids_ref, leaf, 1) * after
        out_ref[:, leaf * LEAF : (leaf + 1) * LEAF] = total


def edge_kernel(first, *refs):
    place_ref, core_ref, ids_ref, field_ref, paired_ref, other_ref, high_ref, low_ref, inner_ref = refs[:9]
    local_ref, part_ref = refs[9:11]
    refs = refs[11:]
    if not first:
        direction_ref, image_ref, old_local_ref = refs[:3]
        refs = refs[3:]
    out_ref, message_ref = refs
    core = core_ref[0]
    leaves = ids_ref.shape[0]
    rows, width = field_ref.shape
    before = chosen(core, paired_ref[:rows], other_ref[:rows])
    after = chosen(core, other_ref[:rows], paired_ref[:rows])
    square = with_image = cross = jnp.zeros((rows, 1), jnp.float32)
    for leaf in range(leaves):
        field = leaf_of(field_ref, leaf)
        total = leaf_of(inner_ref, leaf)
        if leaf == 0:
            part = product(stacked(before), high_ref[0], low_ref[0], ROWS_ROWS)
            total = total + weight_of(place_ref, ids_ref, leaf, -1) * part
        if leaf == leaves - 1:
            part = product(stacked(after), high_ref[1], low_ref[1], ROWS_ROWS)
            total = total + weight_of(place_ref, ids_ref, leaf, 1) * part
        out_ref[:, leaf * LEAF : (leaf + 1) * LEAF] = total
        square = square + row_sum(field * field)
        with_image = with_image + row_sum(field * total)
        if not first:
            cross = cross + row_sum(field * leaf_of(image_ref, leaf) + leaf_of(direction_ref, leaf) * total)
    for block in range(LOCAL):
        scale = 1.0 / (LEAF * (2 if block < 2 else 4))
        here = slice(block * LANES, (block + 1) * LANES)
        with_image = with_image + scale * row_sum(local_ref[:, here] * local_ref[:, here])
        if not first:
            cross = cross + scale * row_sum(local_ref[:, here] * old_local_ref[:, here])
    left = part_ref.shape[0]
    message_ref[:left] = part_ref[...]
    message_ref[left:] = sums_tile([square, with_image, cross], rows)


def combine_kernel(first, bit, cluster, *refs):
    refs = list(refs)
    mine_ref, other_ref = refs[:2]
    refs = refs[2:]
    old_ref = None if first else refs.pop(0)
    *level_refs, next_ref, level_ref = refs
    rows = level_ref.shape[0]
    total = mine_ref[...] + other_ref[...]
    level = total[:rows]
    level_ref[...] = level
    old = None if first else old_ref[bit * rows : (bit + 1) * rows]
    tile = total[total.shape[0] - TILE :] + level_terms(level, old, cluster)
    left = total.shape[0] - TILE - rows
    if left:
        next_ref[:left] = total[rows : rows + left]
        next_ref[left:] = tile
    else:
        for index, ref in enumerate(level_refs):
            next_ref[index * rows : (index + 1) * rows] = ref[...]
        next_ref[bit * rows : (bit + 1) * rows] = level
        next_ref[(bit + 1) * rows :] = tile


def up_kernel(first, last, *refs):
    core_ref, high_ref, low_ref, near_ref, field_ref, mine_ref, other_ref, local_ref = refs[:8]
    refs = refs[8:]
    if not first:
        solution_ref, direction_ref, image_ref, old_local_ref, old_ref, state_ref = refs[:6]
        refs = refs[6:]
    new_solution_ref, new_field_ref = refs[:2]
    if not last:
        new_direction_ref, new_image_ref, new_local_ref, new_old_ref, new_state_ref, paired_ref, send_ref = refs[2:]
    core = core_ref[0]
    rows, width = field_ref.shape
    half = width // 2
    crossing = (mine_ref.shape[0] - TILE) // rows
    whole_sums = chosen(core, mine_ref[...], other_ref[...])
    sums = whole_sums[crossing * rows :].T[:rows]
    norm = sums[:, 0:1]
    curve = sums[:, 1:2]
    ratio = jnp.zeros_like(norm)
    if not first:
        ratio = norm / state_ref[:, 0:1]
        curve = curve + ratio * (sums[:, 2:3] + ratio * state_ref[:, 1:2])
    step = norm / curve
    scaled = []
    for bit in range(crossing):
        scaled.append(whole_sums[bit * rows : (bit + 1) * rows] * (1.0 / (width * (2 << bit))))
    one = [local_ref[:, part * LANES : (part + 1) * LANES] * (1.0 / (2 * LEAF)) for part in range(2)]
    two = local_ref[:, 2 * LANES :] * (1.0 / (4 * LEAF))
    for part in range(2):
        points = slice(part * half, (part + 1) * half)
        stack = stacked(jnp.concatenate([one[part], two] + scaled, axis=1))
        image = near_ref[:, points] + product(stack, high_ref[:, points], low_ref[:, points], ROWS_COLS)
        direction = field_ref[:, points]
        if not first:
            image = image + ratio * image_ref[:, points]
            direction = direction + ratio * direction_ref[:, points]
        moved = step * direction
        new_solution_ref[:, points] = moved if first else solution_ref[:, points] + moved
        new_field_ref[:, points] = field_ref[:, points] - step * image
        if not last:
            new_direction_ref[:, points] = direction
            new_image_ref[:, points] = image
    if not last:
        head = new_field_ref[:, :LEAF]
        tail = new_field_ref[:, width - LEAF :]
        paired_ref[...] = chosen(core, head, tail)
        send_ref[...] = chosen(core, tail, head)
        skeletons = whole_sums[: crossing * rows]
        if first:
            new_local_ref[...] = local_ref[...]
            new_old_ref[...] = skeletons
        else:
            new_local_ref[...] = local_ref[...] + ratio * old_local_ref[...]
            new_old_ref[...] = skeletons + jnp.concatenate([ratio] * crossing, axis=0) * old_ref[...]
        new_state_ref[...] = in_lanes([norm, curve], (rows, LANES))


def per_device(rhs, coords, nugget, near_ids, basis):
    rows, width = rhs.shape
    levels = basis.shape[0]
    leaves = width // LEAF
    crossing = levels - (leaves.bit_length() - 1)
    devices = lax.axis_size("row") * lax.axis_size("col")
    place = jnp.reshape(lax.axis_index(BOTH), (1,))
    core = place % 2

    even = range(0, devices, 2)

    def send(value, pairs):
        return lax.ppermute(value, BOTH, pairs)

    def halo(paired, other):
        outward = [(index, index + 1) for index in range(1, devices - 1, 2)]
        inside = [(index, index ^ 1) for index in range(devices)]
        return send(paired, inside), send(other, outward + [(target, source) for source, target in outward])

    edges = call(edges_kernel, [f32(rows + TILE, LEAF)] * 2, core, rhs, coords, scalars=1)
    edges = halo(*edges)
    turned = coords.T
    *inner_pair, high, low = pl.pallas_call(
        setup_kernel,
        out_shape=[bf16(2 * leaves - 1, LEAF, LEAF)] * 2 + [bf16(levels * LANES, width)] * 2,
        in_specs=[whole(), whole(), whole(pltpu.HBM)],
        out_specs=[whole()] * 4,
        scratch_shapes=[pltpu.VMEM(basis.shape, jnp.float32), pltpu.SemaphoreType.DMA((levels,))],
        compiler_params=pltpu.CompilerParams(vmem_limit_bytes=40 * 2**20),
        cost_estimate=pl.CostEstimate(flops=4 * FLOPS, bytes_accessed=2**20, transcendentals=0),
    )(coords, turned, basis)
    edge_pair = call(
        lambda core_ref, *refs: edge_matrices(core_ref, rows, *refs),
        [bf16(2, LEAF, LEAF)] * 2,
        core,
        turned,
        *edges,
        scalars=1,
        flops=FLOPS,
    )
    nugget = nugget[None, :]

    solution, field, carried = None, rhs, None
    for step in range(ITERS):
        first, last = step == 0, step == ITERS - 1
        local, part = call(
            down_kernel,
            [f32(rows, LOCAL * LANES), f32(crossing * rows, LANES)],
            field,
            high,
            low,
            flops=FLOPS,
        )
        (inner,) = call(
            inner_kernel, [f32(rows, width)], place, near_ids, field, nugget, *inner_pair, scalars=2, flops=FLOPS
        )
        args = [place, core, near_ids, field, *edges, *edge_pair, inner, local, part]
        near, message = call(
            functools.partial(edge_kernel, first),
            [f32(rows, width), f32(crossing * rows + TILE, LANES)],
            *args,
            *([] if first else carried[:3]),
            scalars=3,
            flops=FLOPS // 4,
        )
        done = []
        for bit in range(crossing):
            left = crossing - bit - 1
            if bit == 0:
                got = send(message, [(index, index + 1) for index in even])
            else:
                got = send(message, [(index + 1, (index + 1) ^ (1 << bit)) for index in even])
            args = [message, got] + ([] if first else [carried[3]]) + (done if left == 0 else [])
            message, level = call(
                functools.partial(combine_kernel, first, bit, width * (2 << bit)),
                [f32((left or crossing) * rows + TILE, LANES), f32(rows, LANES)],
                *args,
            )
            done.append(level)
        got = send(message, [(index + 1, index) for index in even])
        args = [core, high, low, near, field, message, got, local]
        if not first:
            args = args + [solution, *carried]
        outs = [f32(rows, width)] * 2
        if not last:
            outs = outs + [f32(rows, width)] * 2 + [f32(rows, LOCAL * LANES), f32(crossing * rows, LANES)]
            outs = outs + [f32(rows, LANES)] + [f32(rows, LEAF)] * 2
        out = call(functools.partial(up_kernel, first, last), outs, *args, scalars=1, flops=FLOPS // 2)
        solution, field = out[:2]
        if not last:
            carried = out[2:7]
            edges = halo(*out[7:9])
    return (solution, field)


def solution(mesh):
    placed = (
        P(None, BOTH),
        P(None, BOTH),
        P(BOTH),
        P(BOTH, None),
        P(None, None, BOTH),
    )
    return jax.shard_map(
        per_device,
        mesh=mesh,
        in_specs=placed,
        out_specs=(P(None, BOTH), P(None, BOTH)),
        check_vma=False,
    )
```

```python
import functools

import jax
import jax.numpy as jnp
from jax import lax
from jax.experimental import pallas as pl
from jax.experimental.pallas import tpu as pltpu
from jax.sharding import PartitionSpec as P

LEAF = 512
ITERS = 4
WIN = 3
LANES = 128
TILE = 8
LOCAL = 3
CHUNK = 16
FLOPS = 3 * 10**9

root_three = 1.7320508075688772
spacing_factor = 1.6
matern_scale = root_three / (spacing_factor * LEAF ** (-1.0 / 3.0))

BOTH = ("row", "col")
ROWS_COLS = (((1,), (0,)), ((), ()))
ROWS_ROWS = (((1,), (1,)), ((), ()))


def halves(values):
    high = values.astype(jnp.bfloat16)
    low = (values - high.astype(jnp.float32)).astype(jnp.bfloat16)
    return high, low


def stacked(values):
    return jnp.concatenate(halves(values), axis=0)


def product(stack, high, low, dims):
    rows = stack.shape[0] // 2
    main = lax.dot_general(stack, high, dims, preferred_element_type=jnp.float32)
    rest = lax.dot_general(stack[:rows], low, dims, preferred_element_type=jnp.float32)
    return main[:rows] + (main[rows:] + rest)


def row_sum(values):
    return jnp.sum(values, axis=1, keepdims=True)


def in_lanes(columns, shape):
    lane = lax.broadcasted_iota(jnp.int32, shape, 1)
    block = jnp.zeros(shape, jnp.float32)
    for index, column in enumerate(columns):
        block = jnp.where(lane == index, column, block)
    return block


def sums_tile(columns, rows):
    turned = in_lanes(columns, (rows, LANES)).T[:TILE]
    return jnp.concatenate([turned, jnp.zeros((TILE, LANES - rows), jnp.float32)], axis=1)


def level_terms(level, old, cluster):
    columns = [jnp.zeros((level.shape[0], 1), jnp.float32), row_sum(level * level) * (1.0 / cluster)]
    if old is not None:
        columns.append(row_sum(level * old) * (1.0 / cluster))
    return sums_tile(columns, level.shape[0])


def chosen(core, odd, even):
    return jnp.where(core == 1, odd, even)


def whole(memory=pltpu.VMEM):
    return pl.BlockSpec(memory_space=memory)


def call(body, outs, *args, scalars=0, flops=0, limit=16):
    return pl.pallas_call(
        body,
        out_shape=outs,
        in_specs=[whole(pltpu.SMEM)] * scalars + [whole()] * (len(args) - scalars),
        out_specs=[whole()] * len(outs),
        compiler_params=pltpu.CompilerParams(vmem_limit_bytes=limit * 2**20),
        cost_estimate=pl.CostEstimate(flops=flops, bytes_accessed=2**20, transcendentals=0),
    )(*args)


def f32(*shape):
    return jax.ShapeDtypeStruct(shape, jnp.float32)


def bf16(*shape):
    return jax.ShapeDtypeStruct(shape, jnp.bfloat16)


def matrix_rows(rows, lanes):
    square = None
    for axis in range(3):
        spread = rows[:, axis : axis + 1] - lanes[axis : axis + 1]
        square = spread * spread if square is None else square + spread * spread
    square = square * (matern_scale * matern_scale)
    scaled = square * lax.rsqrt(jnp.maximum(square, 1e-30))
    return halves((1.0 + scaled) * jnp.exp(-scaled))


def setup_kernel(lane_ref, sub_ref, basis_ref, high_ref, low_ref, basis_high_ref, basis_low_ref, raw_ref, sem_ref):
    levels, rank, _ = basis_ref.shape
    copies = [pltpu.make_async_copy(basis_ref.at[at], raw_ref.at[at], sem_ref.at[at]) for at in range(levels)]
    for copy in copies:
        copy.start()
    leaves = lane_ref.shape[1] // LEAF
    parts = LEAF // CHUNK

    def one(step, carry):
        matrix = step // parts
        part = step % parts
        pair = matrix >= leaves
        row_leaf = jnp.where(pair, matrix - leaves, matrix)
        col_leaf = jnp.where(pair, matrix - leaves + 1, matrix)
        row_at = pl.multiple_of(row_leaf * LEAF + part * CHUNK, CHUNK)
        col_at = pl.multiple_of(col_leaf * LEAF, LEAF)
        out_at = pl.ds(pl.multiple_of(part * CHUNK, CHUNK), CHUNK)
        values = matrix_rows(sub_ref[pl.ds(row_at, CHUNK)], lane_ref[:, pl.ds(col_at, LEAF)])
        high_ref[matrix, out_at], low_ref[matrix, out_at] = values
        return carry

    lax.fori_loop(0, (2 * leaves - 1) * parts, one, 0, unroll=4)
    for at, copy in enumerate(copies):
        copy.wait()
        here = slice(at * rank, (at + 1) * rank)
        basis_high_ref[here], basis_low_ref[here] = halves(raw_ref[at])


def edge_matrices(core_ref, rows, sub_ref, paired_ref, other_ref, high_ref, low_ref):
    core = core_ref[0]
    leaves = sub_ref.shape[0] // LEAF
    here = slice(rows, rows + 3)
    lanes = [
        chosen(core, paired_ref[here], other_ref[here]),
        chosen(core, other_ref[here], paired_ref[here]),
    ]

    for side in range(2):
        first_row = side * (leaves - 1) * LEAF

        def one(part, carry):
            row_at = pl.multiple_of(first_row + part * CHUNK, CHUNK)
            out_at = pl.ds(pl.multiple_of(part * CHUNK, CHUNK), CHUNK)
            values = matrix_rows(sub_ref[pl.ds(row_at, CHUNK)], lanes[side])
            high_ref[side, out_at], low_ref[side, out_at] = values
            return carry

        lax.fori_loop(0, LEAF // CHUNK, one, 0, unroll=4)


def edges_kernel(core_ref, field_ref, coords_ref, paired_ref, other_ref):
    core = core_ref[0]
    rows, width = field_ref.shape
    pad = jnp.zeros((TILE - 3, LEAF), jnp.float32)
    head = jnp.concatenate([field_ref[:, :LEAF], coords_ref[:, :LEAF], pad], axis=0)
    tail = jnp.concatenate([field_ref[:, width - LEAF :], coords_ref[:, width - LEAF :], pad], axis=0)
    paired_ref[...] = chosen(core, head, tail)
    other_ref[...] = chosen(core, tail, head)


def down_kernel(field_ref, high_ref, low_ref, local_ref, part_ref):
    rank = LANES
    rows, width = field_ref.shape
    half = width // 2
    stack = stacked(field_ref[...])
    for part in range(2):
        points = slice(part * half, (part + 1) * half)
        local_ref[:, part * rank : (part + 1) * rank] = product(
            stack[:, points], high_ref[:rank, points], low_ref[:rank, points], ROWS_ROWS
        )
    all_points = product(stack, high_ref[rank:], low_ref[rank:], ROWS_ROWS)
    local_ref[:, 2 * rank :] = all_points[:, :rank]
    for bit in range(all_points.shape[1] // rank - 1):
        part_ref[bit * rows : (bit + 1) * rows] = all_points[:, (bit + 1) * rank : (bit + 2) * rank]


def leaf_of(ref, leaf):
    return ref[:, leaf * LEAF : (leaf + 1) * LEAF]


def weight_of(place_ref, ids_ref, leaf, offset):
    target = place_ref[0] * ids_ref.shape[0] + leaf + offset
    found = ids_ref[leaf, 0] == target
    for slot in range(1, WIN):
        found = jnp.logical_or(found, ids_ref[leaf, slot] == target)
    return jnp.where(jnp.logical_and(found, target >= 0), 1.0 / (16 * WIN), 0.0)


def inner_kernel(place_ref, ids_ref, field_ref, nugget_ref, high_ref, low_ref, out_ref):
    leaves = ids_ref.shape[0]
    pieces = [stacked(leaf_of(field_ref, leaf)) for leaf in range(leaves)]
    for leaf in range(leaves):
        inside = product(pieces[leaf], high_ref[leaf], low_ref[leaf], ROWS_COLS)
        total = leaf_of(nugget_ref, leaf) * leaf_of(field_ref, leaf) + weight_of(place_ref, ids_ref, leaf, 0) * inside
        if leaf > 0:
            at = leaves + leaf - 1
            before = product(pieces[leaf - 1], high_ref[at], low_ref[at], ROWS_COLS)
            total = total + weight_of(place_ref, ids_ref, leaf, -1) * before
        if leaf < leaves - 1:
            at = leaves + leaf
            after = product(pieces[leaf + 1], high_ref[at], low_ref[at], ROWS_ROWS)
            total = total + weight_of(place_ref, ids_ref, leaf, 1) * after
        out_ref[:, leaf * LEAF : (leaf + 1) * LEAF] = total


def edge_kernel(first, *refs):
    place_ref, core_ref, ids_ref, field_ref, paired_ref, other_ref, high_ref, low_ref, inner_ref = refs[:9]
    local_ref, part_ref = refs[9:11]
    refs = refs[11:]
    if not first:
        direction_ref, image_ref, old_local_ref = refs[:3]
        refs = refs[3:]
    out_ref, message_ref = refs
    core = core_ref[0]
    leaves = ids_ref.shape[0]
    rows, width = field_ref.shape
    before = chosen(core, paired_ref[:rows], other_ref[:rows])
    after = chosen(core, other_ref[:rows], paired_ref[:rows])
    square = with_image = cross = jnp.zeros((rows, 1), jnp.float32)
    for leaf in range(leaves):
        field = leaf_of(field_ref, leaf)
        total = leaf_of(inner_ref, leaf)
        if leaf == 0:
            part = product(stacked(before), high_ref[0], low_ref[0], ROWS_ROWS)
            total = total + weight_of(place_ref, ids_ref, leaf, -1) * part
        if leaf == leaves - 1:
            part = product(stacked(after), high_ref[1], low_ref[1], ROWS_ROWS)
            total = total + weight_of(place_ref, ids_ref, leaf, 1) * part
        out_ref[:, leaf * LEAF : (leaf + 1) * LEAF] = total
        square = square + row_sum(field * field)
        with_image = with_image + row_sum(field * total)
        if not first:
            cross = cross + row_sum(field * leaf_of(image_ref, leaf) + leaf_of(direction_ref, leaf) * total)
    for block in range(LOCAL):
        scale = 1.0 / (LEAF * (2 if block < 2 else 4))
        here = slice(block * LANES, (block + 1) * LANES)
        with_image = with_image + scale * row_sum(local_ref[:, here] * local_ref[:, here])
        if not first:
            cross = cross + scale * row_sum(local_ref[:, here] * old_local_ref[:, here])
    left = part_ref.shape[0]
    message_ref[:left] = part_ref[...]
    message_ref[left:] = sums_tile([square, with_image, cross], rows)


def combine_kernel(first, bit, cluster, *refs):
    refs = list(refs)
    mine_ref, other_ref = refs[:2]
    refs = refs[2:]
    old_ref = None if first else refs.pop(0)
    *level_refs, next_ref, level_ref = refs
    rows = level_ref.shape[0]
    total = mine_ref[...] + other_ref[...]
    level = total[:rows]
    level_ref[...] = level
    old = None if first else old_ref[bit * rows : (bit + 1) * rows]
    tile = total[total.shape[0] - TILE :] + level_terms(level, old, cluster)
    left = total.shape[0] - TILE - rows
    if left:
        next_ref[:left] = total[rows : rows + left]
        next_ref[left:] = tile
    else:
        for index, ref in enumerate(level_refs):
            next_ref[index * rows : (index + 1) * rows] = ref[...]
        next_ref[bit * rows : (bit + 1) * rows] = level
        next_ref[(bit + 1) * rows :] = tile


def up_kernel(first, last, *refs):
    core_ref, high_ref, low_ref, near_ref, field_ref, mine_ref, other_ref, local_ref = refs[:8]
    refs = refs[8:]
    if not first:
        solution_ref, direction_ref, image_ref, old_local_ref, old_ref, state_ref = refs[:6]
        refs = refs[6:]
    new_solution_ref, new_field_ref = refs[:2]
    if not last:
        new_direction_ref, new_image_ref, new_local_ref, new_old_ref, new_state_ref, paired_ref, send_ref = refs[2:]
    core = core_ref[0]
    rows, width = field_ref.shape
    half = width // 2
    crossing = (mine_ref.shape[0] - TILE) // rows
    whole_sums = chosen(core, mine_ref[...], other_ref[...])
    sums = whole_sums[crossing * rows :].T[:rows]
    norm = sums[:, 0:1]
    curve = sums[:, 1:2]
    ratio = jnp.zeros_like(norm)
    if not first:
        ratio = norm / state_ref[:, 0:1]
        curve = curve + ratio * (sums[:, 2:3] + ratio * state_ref[:, 1:2])
    step = norm / curve
    scaled = []
    for bit in range(crossing):
        scaled.append(whole_sums[bit * rows : (bit + 1) * rows] * (1.0 / (width * (2 << bit))))
    one = [local_ref[:, part * LANES : (part + 1) * LANES] * (1.0 / (2 * LEAF)) for part in range(2)]
    two = local_ref[:, 2 * LANES :] * (1.0 / (4 * LEAF))
    for part in range(2):
        points = slice(part * half, (part + 1) * half)
        stack = stacked(jnp.concatenate([one[part], two] + scaled, axis=1))
        image = near_ref[:, points] + product(stack, high_ref[:, points], low_ref[:, points], ROWS_COLS)
        direction = field_ref[:, points]
        if not first:
            image = image + ratio * image_ref[:, points]
            direction = direction + ratio * direction_ref[:, points]
        moved = step * direction
        new_solution_ref[:, points] = moved if first else solution_ref[:, points] + moved
        new_field_ref[:, points] = field_ref[:, points] - step * image
        if not last:
            new_direction_ref[:, points] = direction
            new_image_ref[:, points] = image
    if not last:
        head = new_field_ref[:, :LEAF]
        tail = new_field_ref[:, width - LEAF :]
        paired_ref[...] = chosen(core, head, tail)
        send_ref[...] = chosen(core, tail, head)
        skeletons = whole_sums[: crossing * rows]
        if first:
            new_local_ref[...] = local_ref[...]
            new_old_ref[...] = skeletons
        else:
            new_local_ref[...] = local_ref[...] + ratio * old_local_ref[...]
            new_old_ref[...] = skeletons + jnp.concatenate([ratio] * crossing, axis=0) * old_ref[...]
        new_state_ref[...] = in_lanes([norm, curve], (rows, LANES))


def per_device(rhs, coords, nugget, near_ids, basis):
    rows, width = rhs.shape
    levels = basis.shape[0]
    leaves = width // LEAF
    crossing = levels - (leaves.bit_length() - 1)
    devices = lax.axis_size("row") * lax.axis_size("col")
    place = jnp.reshape(lax.axis_index(BOTH), (1,))
    core = place % 2

    even = range(0, devices, 2)
    inside = [(index, index ^ 1) for index in range(devices)]

    def send(value, pairs):
        return lax.ppermute(value, BOTH, pairs)

    def halo(paired, other):
        outward = [(index, index + 1) for index in range(1, devices - 1, 2)]
        ends = [(0, 0), (devices - 1, devices - 1)]
        return send(paired, inside), send(other, outward + [(target, source) for source, target in outward] + ends)

    edges = call(edges_kernel, [f32(rows + TILE, LEAF)] * 2, core, rhs, coords, scalars=1)
    edges = halo(*edges)
    turned = coords.T
    *inner_pair, high, low = pl.pallas_call(
        setup_kernel,
        out_shape=[bf16(2 * leaves - 1, LEAF, LEAF)] * 2 + [bf16(levels * LANES, width)] * 2,
        in_specs=[whole(), whole(), whole(pltpu.HBM)],
        out_specs=[whole()] * 4,
        scratch_shapes=[pltpu.VMEM(basis.shape, jnp.float32), pltpu.SemaphoreType.DMA((levels,))],
        compiler_params=pltpu.CompilerParams(vmem_limit_bytes=24 * 2**20),
        cost_estimate=pl.CostEstimate(flops=4 * FLOPS, bytes_accessed=2**20, transcendentals=0),
    )(coords, turned, basis)
    edge_pair = call(
        lambda core_ref, *refs: edge_matrices(core_ref, rows, *refs),
        [bf16(2, LEAF, LEAF)] * 2,
        core,
        turned,
        *edges,
        scalars=1,
        flops=FLOPS,
    )
    nugget = nugget[None, :]

    solution, field, carried = None, rhs, None
    for step in range(ITERS):
        first, last = step == 0, step == ITERS - 1
        local, part = call(
            down_kernel,
            [f32(rows, LOCAL * LANES), f32(crossing * rows, LANES)],
            field,
            high,
            low,
            flops=FLOPS,
        )
        (inner,) = call(
            inner_kernel, [f32(rows, width)], place, near_ids, field, nugget, *inner_pair, scalars=2, flops=FLOPS
        )
        args = [place, core, near_ids, field, *edges, *edge_pair, inner, local, part]
        near, message = call(
            functools.partial(edge_kernel, first),
            [f32(rows, width), f32(crossing * rows + TILE, LANES)],
            *args,
            *([] if first else carried[:3]),
            scalars=3,
            flops=FLOPS // 4,
        )
        done = []
        for bit in range(crossing):
            left = crossing - bit - 1
            if bit == 0:
                got = send(message, inside)
            else:
                outside = [(index + 1, (index + 1) ^ (1 << bit)) for index in even]
                got = send(message, outside + [(index, index) for index in even])
            args = [message, got] + ([] if first else [carried[3]]) + (done if left == 0 else [])
            message, level = call(
                functools.partial(combine_kernel, first, bit, width * (2 << bit)),
                [f32((left or crossing) * rows + TILE, LANES), f32(rows, LANES)],
                *args,
            )
            done.append(level)
        got = send(message, inside)
        args = [core, high, low, near, field, message, got, local]
        if not first:
            args = args + [solution, *carried]
        outs = [f32(rows, width)] * 2
        if not last:
            outs = outs + [f32(rows, width)] * 2 + [f32(rows, LOCAL * LANES), f32(crossing * rows, LANES)]
            outs = outs + [f32(rows, LANES)] + [f32(rows, LEAF)] * 2
        out = call(functools.partial(up_kernel, first, last), outs, *args, scalars=1, flops=FLOPS // 2)
        solution, field = out[:2]
        if not last:
            carried = out[2:7]
            edges = halo(*out[7:9])
    return (solution, field)


def solution(mesh):
    placed = (
        P(None, BOTH),
        P(None, BOTH),
        P(BOTH),
        P(BOTH, None),
        P(None, None, BOTH),
    )
    return jax.shard_map(
        per_device,
        mesh=mesh,
        in_specs=placed,
        out_specs=(P(None, BOTH), P(None, BOTH)),
        check_vma=False,
    )
```

```python
import functools

import jax
import jax.numpy as jnp
from jax import lax
from jax.experimental import pallas as pl
from jax.experimental.pallas import tpu as pltpu
from jax.sharding import PartitionSpec as P

LEAF = 512
ITERS = 4
WIN = 3
LANES = 128
LOCAL = 3
CHUNK = 16
NORM_TILE = 8
PRODUCTS_TILE = 16
FLOPS = 3 * 10**9

root_three = 1.7320508075688772
spacing_factor = 1.6
matern_scale = root_three / (spacing_factor * LEAF ** (-1.0 / 3.0))

BOTH = ("row", "col")
ROWS_COLS = (((1,), (0,)), ((), ()))
ROWS_ROWS = (((1,), (1,)), ((), ()))

PAIRS = ("dq", "rq", "qq", "rw", "qw", "dw", "rz", "qz", "dz")


def halves(values):
    high = values.astype(jnp.bfloat16)
    low = (values - high.astype(jnp.float32)).astype(jnp.bfloat16)
    return high, low


def stacked(values):
    return jnp.concatenate(halves(values), axis=0)


def product(stack, high, low, dims):
    rows = stack.shape[0] // 2
    main = lax.dot_general(stack, high, dims, preferred_element_type=jnp.float32)
    rest = lax.dot_general(stack[:rows], low, dims, preferred_element_type=jnp.float32)
    return main[:rows] + (main[rows:] + rest)


def row_sum(values):
    return jnp.sum(values, axis=1, keepdims=True)


def in_lanes(columns, shape):
    lane = lax.broadcasted_iota(jnp.int32, shape, 1)
    block = jnp.zeros(shape, jnp.float32)
    for index, column in enumerate(columns):
        block = jnp.where(lane == index, column, block)
    return block


def sums_tile(columns, rows, depth):
    turned = in_lanes(columns, (rows, LANES)).T[:depth]
    return jnp.concatenate([turned, jnp.zeros((depth, LANES - rows), jnp.float32)], axis=1)


def level_terms(core, columns, rows, depth):
    twice = [jnp.concatenate([column, column], axis=0) for column in columns]
    zero = jnp.zeros((rows, 1), jnp.float32)
    tile = sums_tile([zero] * (len(PAIRS) - len(columns)) + twice, rows, depth)
    lane = lax.broadcasted_iota(jnp.int32, tile.shape, 1)
    return jnp.where(lane // (rows // 2) == core, tile, 0.0)


def chosen(core, odd, even):
    return jnp.where(core == 1, odd, even)


def whole(memory=pltpu.VMEM):
    return pl.BlockSpec(memory_space=memory)


def call(body, outs, *args, scalars=0, flops=0, limit=32):
    return pl.pallas_call(
        body,
        out_shape=outs,
        in_specs=[whole(pltpu.SMEM)] * scalars + [whole()] * (len(args) - scalars),
        out_specs=[whole()] * len(outs),
        compiler_params=pltpu.CompilerParams(vmem_limit_bytes=limit * 2**20),
        cost_estimate=pl.CostEstimate(flops=flops, bytes_accessed=2**20, transcendentals=0),
    )(*args)


def f32(*shape):
    return jax.ShapeDtypeStruct(shape, jnp.float32)


def bf16(*shape):
    return jax.ShapeDtypeStruct(shape, jnp.bfloat16)


def matrix_rows(rows, lanes):
    square = None
    for axis in range(3):
        spread = rows[:, axis : axis + 1] - lanes[axis : axis + 1]
        square = spread * spread if square is None else square + spread * spread
    square = square * (matern_scale * matern_scale)
    scaled = square * lax.rsqrt(jnp.maximum(square, 1e-30))
    return halves((1.0 + scaled) * jnp.exp(-scaled))


def fill_matrices(pairs, lane_ref, sub_ref, high_ref, low_ref):
    for matrix, (row_leaf, col_leaf) in enumerate(pairs):
        lanes = lane_ref[:, col_leaf * LEAF : (col_leaf + 1) * LEAF]

        def one(part, carry):
            row_at = pl.multiple_of(row_leaf * LEAF + part * CHUNK, CHUNK)
            out_at = pl.ds(pl.multiple_of(part * CHUNK, CHUNK), CHUNK)
            values = matrix_rows(sub_ref[pl.ds(row_at, CHUNK)], lanes)
            high_ref[matrix, out_at], low_ref[matrix, out_at] = values
            return carry

        lax.fori_loop(0, LEAF // CHUNK, one, 0, unroll=4)


def setup_kernel(pairs, lane_ref, sub_ref, basis_ref, high_ref, low_ref, basis_high_ref, basis_low_ref, raw_ref, sem_ref):
    levels, rank, _ = basis_ref.shape
    copies = [pltpu.make_async_copy(basis_ref.at[at], raw_ref.at[at], sem_ref.at[at]) for at in range(levels)]
    for copy in copies:
        copy.start()
    fill_matrices(pairs, lane_ref, sub_ref, high_ref, low_ref)
    for at, copy in enumerate(copies):
        copy.wait()
        here = slice(at * rank, (at + 1) * rank)
        basis_high_ref[here], basis_low_ref[here] = halves(raw_ref[at])


def edge_matrices(core_ref, rows, sub_ref, paired_ref, other_ref, high_ref, low_ref):
    core = core_ref[0]
    leaves = sub_ref.shape[0] // LEAF
    here = slice(rows, rows + 3)
    lanes = [
        chosen(core, paired_ref[here], other_ref[here]),
        chosen(core, other_ref[here], paired_ref[here]),
    ]

    for side in range(2):
        first_row = side * (leaves - 1) * LEAF

        def one(part, carry):
            row_at = pl.multiple_of(first_row + part * CHUNK, CHUNK)
            out_at = pl.ds(pl.multiple_of(part * CHUNK, CHUNK), CHUNK)
            values = matrix_rows(sub_ref[pl.ds(row_at, CHUNK)], lanes[side])
            high_ref[side, out_at], low_ref[side, out_at] = values
            return carry

        lax.fori_loop(0, LEAF // CHUNK, one, 0, unroll=4)


def edges_kernel(core_ref, field_ref, coords_ref, paired_ref, other_ref):
    core = core_ref[0]
    rows, width = field_ref.shape
    pad = jnp.zeros((8 - 3, LEAF), jnp.float32)
    head = jnp.concatenate([field_ref[:, :LEAF], coords_ref[:, :LEAF], pad], axis=0)
    tail = jnp.concatenate([field_ref[:, width - LEAF :], coords_ref[:, width - LEAF :], pad], axis=0)
    paired_ref[...] = chosen(core, head, tail)
    other_ref[...] = chosen(core, tail, head)


def down_kernel(core_ref, field_ref, high_ref, low_ref, local_ref, keep_ref, send_ref, tile_ref):
    core = core_ref[0]
    rank = LANES
    rows, width = field_ref.shape
    half = width // 2
    stack = stacked(field_ref[...])
    for part in range(2):
        points = slice(part * half, (part + 1) * half)
        local_ref[:, part * rank : (part + 1) * rank] = product(
            stack[:, points], high_ref[:rank, points], low_ref[:rank, points], ROWS_ROWS
        )
    all_points = product(stack, high_ref[rank:], low_ref[rank:], ROWS_ROWS)
    local_ref[:, 2 * rank :] = all_points[:, :rank]
    own = rows // 2
    for bit in range(all_points.shape[1] // rank - 1):
        block = all_points[:, (bit + 1) * rank : (bit + 2) * rank]
        keep_ref[bit * own : (bit + 1) * own] = chosen(core, block[own:], block[:own])
        send_ref[bit * own : (bit + 1) * own] = chosen(core, block[:own], block[own:])
    tile_ref[...] = sums_tile([row_sum(field_ref[...] * field_ref[...])], rows, NORM_TILE)


def leaf_of(ref, leaf):
    return ref[:, leaf * LEAF : (leaf + 1) * LEAF]


def weight_of(place_ref, ids_ref, leaf, offset):
    target = place_ref[0] * ids_ref.shape[0] + leaf + offset
    found = ids_ref[leaf, 0] == target
    for slot in range(1, WIN):
        found = jnp.logical_or(found, ids_ref[leaf, slot] == target)
    return jnp.where(jnp.logical_and(found, target >= 0), 1.0 / (16 * WIN), 0.0)


def inner_kernel(half, place_ref, ids_ref, field_ref, nugget_ref, high_ref, low_ref, pair_high_ref, pair_low_ref, out_ref):
    leaves = ids_ref.shape[0]
    start = half * (leaves // 2)
    stop = start + leaves // 2
    pieces = {leaf: stacked(leaf_of(field_ref, leaf)) for leaf in range(max(start - 1, 0), min(stop + 1, leaves))}
    for leaf in range(start, stop):
        at = leaf - start
        inside = product(pieces[leaf], high_ref[at], low_ref[at], ROWS_COLS)
        total = leaf_of(nugget_ref, leaf) * leaf_of(field_ref, leaf) + weight_of(place_ref, ids_ref, leaf, 0) * inside
        if leaf > 0:
            before = product(pieces[leaf - 1], pair_high_ref[leaf - 1], pair_low_ref[leaf - 1], ROWS_COLS)
            total = total + weight_of(place_ref, ids_ref, leaf, -1) * before
        if leaf < leaves - 1:
            after = product(pieces[leaf + 1], pair_high_ref[leaf], pair_low_ref[leaf], ROWS_ROWS)
            total = total + weight_of(place_ref, ids_ref, leaf, 1) * after
        out_ref[:, at * LEAF : (at + 1) * LEAF] = total


def edge_kernel(sums, *refs):
    place_ref, core_ref, ids_ref, paired_ref, other_ref, high_ref, low_ref, front_ref, back_ref = refs[:9]
    refs = refs[9:]
    out_ref = refs[-2] if sums else refs[-1]
    core = core_ref[0]
    leaves = ids_ref.shape[0]
    rows, width = out_ref.shape
    before = chosen(core, paired_ref[:rows], other_ref[:rows])
    after = chosen(core, other_ref[:rows], paired_ref[:rows])
    out_ref[:, : width // 2] = front_ref[...]
    out_ref[:, width // 2 :] = back_ref[...]
    part = product(stacked(before), high_ref[0], low_ref[0], ROWS_ROWS)
    out_ref[:, :LEAF] += weight_of(place_ref, ids_ref, 0, -1) * part
    part = product(stacked(after), high_ref[1], low_ref[1], ROWS_ROWS)
    out_ref[:, width - LEAF :] += weight_of(place_ref, ids_ref, leaves - 1, 1) * part
    if not sums:
        return
    fields = dict(zip("rqdw", refs[:4]))
    locals_ = dict(zip("rqd", refs[4:7]))
    tile_ref = refs[-1]
    totals = {pair: jnp.zeros((rows, 1), jnp.float32) for pair in PAIRS}
    for leaf in range(leaves):
        here = {name: leaf_of(ref, leaf) for name, ref in fields.items()}
        here["z"] = leaf_of(out_ref, leaf)
        for left, right in PAIRS:
            totals[left + right] = totals[left + right] + row_sum(here[left] * here[right])
    for block in range(LOCAL):
        scale = 1.0 / (LEAF * (2 if block < 2 else 4))
        lanes = slice(block * LANES, (block + 1) * LANES)
        for name in "rqd":
            term = row_sum(locals_[name][:, lanes] * locals_["q"][:, lanes])
            totals[name + "z"] = totals[name + "z"] + scale * term
    tile_ref[...] = sums_tile([totals[pair] for pair in PAIRS], rows, PRODUCTS_TILE)


def combine_kernel(products, bit, cluster, *refs):
    refs = list(refs)
    core_ref, mine_ref, other_ref = refs[:3]
    refs = refs[3:]
    tile_ref = refs.pop(0) if bit == 0 else None
    if products:
        field_ref, direction_ref = refs[:2]
        refs = refs[2:]
    *level_refs, next_ref, level_ref = refs
    own = level_ref.shape[0]
    depth = PRODUCTS_TILE if products else NORM_TILE
    total = mine_ref[...] + other_ref[...]
    if bit == 0:
        tile = tile_ref[...]
    else:
        tile = total[total.shape[0] - depth :]
        total = total[: total.shape[0] - depth]
    level = total[:own]
    level_ref[...] = level
    if products:
        here = slice(bit * own, (bit + 1) * own)
        partners = [field_ref[here], level, direction_ref[here]]
        columns = [row_sum(level * partner) * (1.0 / cluster) for partner in partners]
        tile = tile + level_terms(core_ref[0], columns, 2 * own, depth)
    left = total.shape[0] - own
    if left:
        next_ref[:left] = total[own:]
        next_ref[left:] = tile
    else:
        for index, ref in enumerate(level_refs):
            next_ref[index * own : (index + 1) * own] = ref[...]
        next_ref[bit * own : (bit + 1) * own] = level
        next_ref[(bit + 1) * own :] = tile


def up_parts(core, mine_ref, other_ref, local_ref, rows, width, depth):
    own = rows // 2
    crossing = (mine_ref.shape[0] - depth) // own
    sums = (mine_ref[crossing * own :] + other_ref[crossing * own :]).T[:rows]
    scaled = []
    for bit in range(crossing):
        here = slice(bit * own, (bit + 1) * own)
        low_rows = chosen(core, other_ref[here], mine_ref[here])
        high_rows = chosen(core, mine_ref[here], other_ref[here])
        scaled.append(jnp.concatenate([low_rows, high_rows], axis=0) * (1.0 / (width * (2 << bit))))
    one = [local_ref[:, part * LANES : (part + 1) * LANES] * (1.0 / (2 * LEAF)) for part in range(2)]
    two = local_ref[:, 2 * LANES :] * (1.0 / (4 * LEAF))
    return sums, [stacked(jnp.concatenate([one[part], two] + scaled, axis=1)) for part in range(2)]


def own_rows(core, column, crossing):
    own = column.shape[0] // 2
    return jnp.concatenate([chosen(core, column[own:], column[:own])] * crossing, axis=0)


def put_edges(core, field_ref, paired_ref, send_ref):
    width = field_ref.shape[1]
    head = field_ref[:, :LEAF]
    tail = field_ref[:, width - LEAF :]
    paired_ref[...] = chosen(core, head, tail)
    send_ref[...] = chosen(core, tail, head)


def residual_up_kernel(first, *refs):
    core_ref, high_ref, low_ref, near_ref, mine_ref, other_ref, local_ref = refs[:7]
    refs = refs[7:]
    if first:
        image_ref, state_ref, paired_ref, send_ref = refs
        q_ref = image_ref
    else:
        field_ref, old_d_ref, old_q_ref, old_skel_ref, old_local_ref, old_state_ref = refs[:6]
        image_ref, state_ref, paired_ref, send_ref, d_ref, q_ref, skel_ref, new_local_ref = refs[6:]
    core = core_ref[0]
    rows, width = near_ref.shape
    half = width // 2
    sums, stacks = up_parts(core, mine_ref, other_ref, local_ref, rows, width, NORM_TILE)
    norm = sums[:, 0:1]
    state_ref[...] = in_lanes([norm], (rows, LANES))
    ratio = None if first else norm / old_state_ref[:, 0:1]
    for part in range(2):
        points = slice(part * half, (part + 1) * half)
        image = near_ref[:, points] + product(stacks[part], high_ref[:, points], low_ref[:, points], ROWS_COLS)
        image_ref[:, points] = image
        if not first:
            d_ref[:, points] = field_ref[:, points] + ratio * old_d_ref[:, points]
            q_ref[:, points] = image + ratio * old_q_ref[:, points]
    put_edges(core, q_ref, paired_ref, send_ref)
    if not first:
        rows_in = skel_ref.shape[0]
        crossing = rows_in // (rows // 2)
        skel_ref[...] = mine_ref[:rows_in] + own_rows(core, ratio, crossing) * old_skel_ref[...]
        new_local_ref[...] = local_ref[...] + ratio * old_local_ref[...]


def image_up_kernel(first, last, *refs):
    core_ref, high_ref, low_ref, near_ref, mine_ref, other_ref, local_ref = refs[:7]
    r_ref, w_ref, d_ref, q_ref, state_ref = refs[7:12]
    refs = refs[12:]
    if not first:
        solution_ref = refs[0]
        refs = refs[1:]
    if not last:
        r_skel_ref, d_skel_ref, r_local_ref, d_local_ref = refs[:4]
        refs = refs[4:]
    new_solution_ref, new_r_ref = refs[:2]
    if not last:
        new_d_ref, new_q_ref, new_skel_ref, new_local_ref, new_state_ref, paired_ref, send_ref = refs[2:]
    core = core_ref[0]
    rows, width = near_ref.shape
    half = width // 2
    sums, stacks = up_parts(core, mine_ref, other_ref, local_ref, rows, width, PRODUCTS_TILE)
    dot = {pair: sums[:, index : index + 1] for index, pair in enumerate(PAIRS)}
    norm = state_ref[:, 0:1]
    step = norm / dot["dq"]
    new_norm = norm - step * (2.0 * dot["rq"] - step * dot["qq"])
    ratio = new_norm / norm
    curve = dot["rw"] - step * (dot["qw"] + dot["rz"] - step * dot["qz"])
    curve = curve + ratio * (dot["dw"] - step * dot["dz"] + dot["rq"] - step * dot["qq"] + ratio * dot["dq"])
    new_step = new_norm / curve
    for part in range(2):
        points = slice(part * half, (part + 1) * half)
        image = near_ref[:, points] + product(stacks[part], high_ref[:, points], low_ref[:, points], ROWS_COLS)
        d = d_ref[:, points]
        q = q_ref[:, points]
        r = r_ref[:, points] - step * q
        new_q = w_ref[:, points] - step * image + ratio * q
        new_d = r + ratio * d
        moved = step * d + new_step * new_d
        new_solution_ref[:, points] = moved if first else solution_ref[:, points] + moved
        new_r_ref[:, points] = r - new_step * new_q
        if not last:
            new_d_ref[:, points] = new_d
            new_q_ref[:, points] = new_q
    if not last:
        rows_in = new_skel_ref.shape[0]
        crossing = rows_in // (rows // 2)
        r_skel = r_skel_ref[:rows_in] - own_rows(core, step, crossing) * mine_ref[:rows_in]
        new_skel_ref[...] = r_skel + own_rows(core, ratio, crossing) * d_skel_ref[:rows_in]
        new_local_ref[...] = r_local_ref[...] - step * local_ref[...] + ratio * d_local_ref[...]
        new_state_ref[...] = in_lanes([new_norm], (rows, LANES))
        put_edges(core, new_r_ref, paired_ref, send_ref)


def per_device(rhs, coords, nugget, near_ids, basis):
    rows, width = rhs.shape
    levels = basis.shape[0]
    leaves = width // LEAF
    own = rows // 2
    crossing = levels - (leaves.bit_length() - 1)
    devices = lax.axis_size("row") * lax.axis_size("col")
    place = jnp.reshape(lax.axis_index(BOTH), (1,))
    core = place % 2
    nugget = nugget[None, :]

    def swap(value, bit):
        return lax.ppermute(value, BOTH, [(source, source ^ (1 << bit)) for source in range(devices)])

    def halo(paired, other):
        outward = [(index, index + 1) for index in range(1, devices - 1, 2)]
        ends = [(0, 0), (devices - 1, devices - 1)]
        return swap(paired, 0), lax.ppermute(other, BOTH, outward + [(target, source) for source, target in outward] + ends)

    def down(field):
        shapes = [f32(rows, LOCAL * LANES)] + [f32(crossing * own, LANES)] * 2 + [f32(NORM_TILE, LANES)]
        return call(down_kernel, shapes, core, field, high, low, scalars=1, flops=FLOPS)

    def inner(half, field):
        args = [place, near_ids, field, nugget, *diagonal[half], *beside]
        body = functools.partial(inner_kernel, half)
        return call(body, [f32(rows, width // 2)], *args, scalars=2, flops=FLOPS // 2)[0]

    def edge(edges, front, back, *more):
        shapes = [f32(rows, width)] + ([f32(PRODUCTS_TILE, LANES)] if more else [])
        args = [place, core, near_ids, *edges, *outside, front, back, *more]
        return call(functools.partial(edge_kernel, bool(more)), shapes, *args, scalars=3, flops=FLOPS // 3)

    def chain(products, keep, got, tile, beside_steps, *skeletons):
        depth = PRODUCTS_TILE if products else NORM_TILE
        done = []
        results = []
        message = keep
        for bit in range(crossing):
            left = crossing - bit - 1
            args = [core, message, got] + ([tile] if bit == 0 else []) + list(skeletons) + (done if left == 0 else [])
            message, level = call(
                functools.partial(combine_kernel, products, bit, width * (2 << bit)),
                [f32((left or crossing) * own + depth, LANES), f32(own, LANES)],
                *args,
                scalars=1,
            )
            done.append(level)
            got = swap(message, bit + 1 if left else 0)
            if bit < len(beside_steps):
                got, result = lax.optimization_barrier((got, beside_steps[bit](message)))
                results.append(result)
        return message, got, results

    edges = halo(*call(edges_kernel, [f32(rows + 8, LEAF)] * 2, core, rhs, coords, scalars=1))
    turned = coords.T
    half = leaves // 2
    pairs = [(leaf, leaf) for leaf in range(half)]
    *front_diagonal, high, low = pl.pallas_call(
        functools.partial(setup_kernel, pairs),
        out_shape=[bf16(half, LEAF, LEAF)] * 2 + [bf16(levels * LANES, width)] * 2,
        in_specs=[whole(), whole(), whole(pltpu.HBM)],
        out_specs=[whole()] * 4,
        scratch_shapes=[pltpu.VMEM(basis.shape, jnp.float32), pltpu.SemaphoreType.DMA((levels,))],
        compiler_params=pltpu.CompilerParams(vmem_limit_bytes=46 * 2**20),
        cost_estimate=pl.CostEstimate(flops=FLOPS, bytes_accessed=2**20, transcendentals=0),
    )(coords, turned, basis)
    diagonal = [front_diagonal, None]
    beside = outside = None

    def after(message, *values):
        return lax.optimization_barrier((message, *values))[1:]

    def late_matrices(pairs):
        def run(message):
            shapes = [bf16(len(pairs), LEAF, LEAF)] * 2
            return call(functools.partial(fill_matrices, pairs), shapes, *after(message, coords, turned), flops=FLOPS)

        return run

    def late_edge_matrices(message):
        def body(core_ref, *refs):
            edge_matrices(core_ref, rows, *refs)

        args = after(message, turned, *edges)
        return call(body, [bf16(2, LEAF, LEAF)] * 2, core, *args, scalars=1, flops=FLOPS)

    solution, r, carried = None, rhs, None
    for step in range(0, ITERS, 2):
        first, last = step == 0, step + 2 == ITERS
        r_local, keep, part, tile = down(r)
        got = swap(part, 0)
        if first:
            work = [
                late_matrices([(leaf, leaf) for leaf in range(half, leaves)]),
                late_matrices([(leaf, leaf + 1) for leaf in range(leaves - 1)]),
                late_edge_matrices,
            ]
            message, got, results = chain(False, keep, got, tile, work)
            diagonal[1], beside, outside = results
            (near,) = edge(edges, inner(0, r), inner(1, r))
        else:
            fronts = []

            def front_work(message):
                fronts.append(inner(0, *after(message, r)))
                return fronts[0]

            def back_work(message):
                fronts.append(inner(1, *after(message, r)))
                return fronts[1]

            def edge_work(message):
                return edge(edges, *after(message, *fronts))[0]

            message, got, results = chain(False, keep, got, tile, [front_work, back_work, edge_work])
            near = results[2]
        args = [core, high, low, near, message, got, r_local]
        outs = [f32(rows, width), f32(rows, LANES)] + [f32(rows, LEAF)] * 2
        if first:
            w, state, *edges = call(
                functools.partial(residual_up_kernel, True), outs, *args, scalars=1, flops=FLOPS // 2
            )
            d, q, d_skel, d_local = r, w, message, r_local
        else:
            outs = outs + [f32(rows, width)] * 2 + [f32(crossing * own, LANES), f32(rows, LOCAL * LANES)]
            w, state, *edges, d, q, d_skel, d_local = call(
                functools.partial(residual_up_kernel, False), outs, *args, r, *carried, scalars=1, flops=FLOPS // 2
            )
        r_skel = message
        edges = halo(*edges)
        q_local, keep, part, _ = down(q)
        got = swap(part, 0)
        near, tile = edge(edges, inner(0, q), inner(1, q), r, q, d, w, r_local, q_local, d_local)
        message, got, _ = chain(True, keep, got, tile, [], r_skel, d_skel)
        args = [core, high, low, near, message, got, q_local, r, w, d, q, state]
        args = args + ([] if first else [solution]) + ([] if last else [r_skel, d_skel, r_local, d_local])
        outs = [f32(rows, width)] * 2
        if not last:
            outs = outs + [f32(rows, width)] * 2 + [f32(crossing * own, LANES), f32(rows, LOCAL * LANES)]
            outs = outs + [f32(rows, LANES)] + [f32(rows, LEAF)] * 2
        solution, r, *rest = call(
            functools.partial(image_up_kernel, first, last), outs, *args, scalars=1, flops=FLOPS // 2
        )
        if not last:
            carried = rest[:5]
            edges = halo(*rest[5:])
    return (solution, r)


def solution(mesh):
    placed = (
        P(None, BOTH),
        P(None, BOTH),
        P(BOTH),
        P(BOTH, None),
        P(None, None, BOTH),
    )
    return jax.shard_map(
        per_device,
        mesh=mesh,
        in_specs=placed,
        out_specs=(P(None, BOTH), P(None, BOTH)),
        check_vma=False,
    )
```

```python
import functools

import jax
import jax.numpy as jnp
from jax import lax
from jax.experimental import pallas as pl
from jax.experimental.pallas import tpu as pltpu
from jax.sharding import PartitionSpec as P

LEAF = 512
ITERS = 4
WIN = 3
LANES = 128
LOCAL = 3
CHUNK = 16
NORM_TILE = 8
PRODUCTS_TILE = 16
FLOPS = 3 * 10**9

root_three = 1.7320508075688772
spacing_factor = 1.6
matern_scale = root_three / (spacing_factor * LEAF ** (-1.0 / 3.0))

BOTH = ("row", "col")
ROWS_COLS = (((1,), (0,)), ((), ()))
ROWS_ROWS = (((1,), (1,)), ((), ()))

PAIRS = ("dq", "rq", "qq", "rw", "qw", "dw", "rz", "qz", "dz")


def halves(values):
    high = values.astype(jnp.bfloat16)
    low = (values - high.astype(jnp.float32)).astype(jnp.bfloat16)
    return high, low


def stacked(values):
    return jnp.concatenate(halves(values), axis=0)


def product(stack, high, low, dims):
    rows = stack.shape[0] // 2
    main = lax.dot_general(stack, high, dims, preferred_element_type=jnp.float32)
    rest = lax.dot_general(stack[:rows], low, dims, preferred_element_type=jnp.float32)
    return main[:rows] + (main[rows:] + rest)


def row_sum(values):
    return jnp.sum(values, axis=1, keepdims=True)


def in_lanes(columns, shape):
    lane = lax.broadcasted_iota(jnp.int32, shape, 1)
    block = jnp.zeros(shape, jnp.float32)
    for index, column in enumerate(columns):
        block = jnp.where(lane == index, column, block)
    return block


def sums_tile(columns, rows, depth):
    turned = in_lanes(columns, (rows, LANES)).T[:depth]
    return jnp.concatenate([turned, jnp.zeros((depth, LANES - rows), jnp.float32)], axis=1)


def level_terms(core, columns, rows, depth):
    twice = [jnp.concatenate([column, column], axis=0) for column in columns]
    zero = jnp.zeros((rows, 1), jnp.float32)
    tile = sums_tile([zero] * (len(PAIRS) - len(columns)) + twice, rows, depth)
    lane = lax.broadcasted_iota(jnp.int32, tile.shape, 1)
    return jnp.where(lane // (rows // 2) == core, tile, 0.0)


def chosen(core, odd, even):
    return jnp.where(core == 1, odd, even)


def whole(memory=pltpu.VMEM):
    return pl.BlockSpec(memory_space=memory)


def call(body, outs, *args, scalars=0, flops=0, limit=32):
    return pl.pallas_call(
        body,
        out_shape=outs,
        in_specs=[whole(pltpu.SMEM)] * scalars + [whole()] * (len(args) - scalars),
        out_specs=[whole()] * len(outs),
        compiler_params=pltpu.CompilerParams(vmem_limit_bytes=limit * 2**20),
        cost_estimate=pl.CostEstimate(flops=flops, bytes_accessed=2**20, transcendentals=0),
    )(*args)


def f32(*shape):
    return jax.ShapeDtypeStruct(shape, jnp.float32)


def bf16(*shape):
    return jax.ShapeDtypeStruct(shape, jnp.bfloat16)


def matrix_rows(rows, lanes):
    square = None
    for axis in range(3):
        spread = rows[:, axis : axis + 1] - lanes[axis : axis + 1]
        square = spread * spread if square is None else square + spread * spread
    square = square * (matern_scale * matern_scale)
    scaled = square * lax.rsqrt(jnp.maximum(square, 1e-30))
    return halves((1.0 + scaled) * jnp.exp(-scaled))


def fill_matrices(pairs, lane_ref, sub_ref, high_ref, low_ref):
    for matrix, (row_leaf, col_leaf) in enumerate(pairs):
        lanes = lane_ref[:, col_leaf * LEAF : (col_leaf + 1) * LEAF]

        def one(part, carry):
            row_at = pl.multiple_of(row_leaf * LEAF + part * CHUNK, CHUNK)
            out_at = pl.ds(pl.multiple_of(part * CHUNK, CHUNK), CHUNK)
            values = matrix_rows(sub_ref[pl.ds(row_at, CHUNK)], lanes)
            high_ref[matrix, out_at], low_ref[matrix, out_at] = values
            return carry

        lax.fori_loop(0, LEAF // CHUNK, one, 0, unroll=4)


def setup_kernel(pairs, lane_ref, sub_ref, basis_ref, high_ref, low_ref, basis_high_ref, basis_low_ref, raw_ref, sem_ref):
    levels, rank, _ = basis_ref.shape
    copies = [pltpu.make_async_copy(basis_ref.at[at], raw_ref.at[at], sem_ref.at[at]) for at in range(levels)]
    for copy in copies:
        copy.start()
    fill_matrices(pairs, lane_ref, sub_ref, high_ref, low_ref)
    for at, copy in enumerate(copies):
        copy.wait()
        here = slice(at * rank, (at + 1) * rank)
        basis_high_ref[here], basis_low_ref[here] = halves(raw_ref[at])


def edge_matrices(core_ref, rows, sub_ref, paired_ref, other_ref, high_ref, low_ref):
    core = core_ref[0]
    leaves = sub_ref.shape[0] // LEAF
    here = slice(rows, rows + 3)
    lanes = [
        chosen(core, paired_ref[here], other_ref[here]),
        chosen(core, other_ref[here], paired_ref[here]),
    ]

    for side in range(2):
        first_row = side * (leaves - 1) * LEAF

        def one(part, carry):
            row_at = pl.multiple_of(first_row + part * CHUNK, CHUNK)
            out_at = pl.ds(pl.multiple_of(part * CHUNK, CHUNK), CHUNK)
            values = matrix_rows(sub_ref[pl.ds(row_at, CHUNK)], lanes[side])
            high_ref[side, out_at], low_ref[side, out_at] = values
            return carry

        lax.fori_loop(0, LEAF // CHUNK, one, 0, unroll=4)


def edges_kernel(core_ref, field_ref, coords_ref, paired_ref, other_ref):
    core = core_ref[0]
    rows, width = field_ref.shape
    pad = jnp.zeros((8 - 3, LEAF), jnp.float32)
    head = jnp.concatenate([field_ref[:, :LEAF], coords_ref[:, :LEAF], pad], axis=0)
    tail = jnp.concatenate([field_ref[:, width - LEAF :], coords_ref[:, width - LEAF :], pad], axis=0)
    paired_ref[...] = chosen(core, head, tail)
    other_ref[...] = chosen(core, tail, head)


def down_kernel(core_ref, field_ref, high_ref, low_ref, local_ref, keep_ref, send_ref, tile_ref):
    core = core_ref[0]
    rank = LANES
    rows, width = field_ref.shape
    half = width // 2
    stack = stacked(field_ref[...])
    for part in range(2):
        points = slice(part * half, (part + 1) * half)
        local_ref[:, part * rank : (part + 1) * rank] = product(
            stack[:, points], high_ref[:rank, points], low_ref[:rank, points], ROWS_ROWS
        )
    all_points = product(stack, high_ref[rank:], low_ref[rank:], ROWS_ROWS)
    local_ref[:, 2 * rank :] = all_points[:, :rank]
    own = rows // 2
    for bit in range(all_points.shape[1] // rank - 1):
        block = all_points[:, (bit + 1) * rank : (bit + 2) * rank]
        keep_ref[bit * own : (bit + 1) * own] = chosen(core, block[own:], block[:own])
        send_ref[bit * own : (bit + 1) * own] = chosen(core, block[:own], block[own:])
    tile_ref[...] = sums_tile([row_sum(field_ref[...] * field_ref[...])], rows, NORM_TILE)


def leaf_of(ref, leaf):
    return ref[:, leaf * LEAF : (leaf + 1) * LEAF]


def weight_of(place_ref, ids_ref, leaf, offset):
    target = place_ref[0] * ids_ref.shape[0] + leaf + offset
    found = ids_ref[leaf, 0] == target
    for slot in range(1, WIN):
        found = jnp.logical_or(found, ids_ref[leaf, slot] == target)
    return jnp.where(jnp.logical_and(found, target >= 0), 1.0 / (16 * WIN), 0.0)


def inner_kernel(half, place_ref, ids_ref, field_ref, nugget_ref, high_ref, low_ref, pair_high_ref, pair_low_ref, out_ref):
    leaves = ids_ref.shape[0]
    start = half * (leaves // 2)
    stop = start + leaves // 2
    pieces = {leaf: stacked(leaf_of(field_ref, leaf)) for leaf in range(max(start - 1, 0), min(stop + 1, leaves))}
    for leaf in range(start, stop):
        at = leaf - start
        inside = product(pieces[leaf], high_ref[at], low_ref[at], ROWS_COLS)
        total = leaf_of(nugget_ref, leaf) * leaf_of(field_ref, leaf) + weight_of(place_ref, ids_ref, leaf, 0) * inside
        if leaf > 0:
            before = product(pieces[leaf - 1], pair_high_ref[leaf - 1], pair_low_ref[leaf - 1], ROWS_COLS)
            total = total + weight_of(place_ref, ids_ref, leaf, -1) * before
        if leaf < leaves - 1:
            after = product(pieces[leaf + 1], pair_high_ref[leaf], pair_low_ref[leaf], ROWS_ROWS)
            total = total + weight_of(place_ref, ids_ref, leaf, 1) * after
        out_ref[:, at * LEAF : (at + 1) * LEAF] = total


def edge_kernel(sums, *refs):
    place_ref, core_ref, ids_ref, paired_ref, other_ref, high_ref, low_ref, front_ref, back_ref = refs[:9]
    refs = refs[9:]
    out_ref = refs[-2] if sums else refs[-1]
    core = core_ref[0]
    leaves = ids_ref.shape[0]
    rows, width = out_ref.shape
    before = chosen(core, paired_ref[:rows], other_ref[:rows])
    after = chosen(core, other_ref[:rows], paired_ref[:rows])
    out_ref[:, : width // 2] = front_ref[...]
    out_ref[:, width // 2 :] = back_ref[...]
    part = product(stacked(before), high_ref[0], low_ref[0], ROWS_ROWS)
    out_ref[:, :LEAF] += weight_of(place_ref, ids_ref, 0, -1) * part
    part = product(stacked(after), high_ref[1], low_ref[1], ROWS_ROWS)
    out_ref[:, width - LEAF :] += weight_of(place_ref, ids_ref, leaves - 1, 1) * part
    if not sums:
        return
    fields = dict(zip("rqdw", refs[:4]))
    locals_ = dict(zip("rqd", refs[4:7]))
    tile_ref = refs[-1]
    totals = {pair: jnp.zeros((rows, 1), jnp.float32) for pair in PAIRS}
    for leaf in range(leaves):
        here = {name: leaf_of(ref, leaf) for name, ref in fields.items()}
        here["z"] = leaf_of(out_ref, leaf)
        for left, right in PAIRS:
            totals[left + right] = totals[left + right] + row_sum(here[left] * here[right])
    for block in range(LOCAL):
        scale = 1.0 / (LEAF * (2 if block < 2 else 4))
        lanes = slice(block * LANES, (block + 1) * LANES)
        for name in "rqd":
            term = row_sum(locals_[name][:, lanes] * locals_["q"][:, lanes])
            totals[name + "z"] = totals[name + "z"] + scale * term
    tile_ref[...] = sums_tile([totals[pair] for pair in PAIRS], rows, PRODUCTS_TILE)


def first_combine_kernel(products, cluster, *refs):
    core_ref, mine_ref, other_ref, tile_ref = refs[:4]
    message_ref, level_ref = refs[-2:]
    own = level_ref.shape[0]
    depth = tile_ref.shape[0]
    total = mine_ref[...] + other_ref[...]
    level = total[:own]
    level_ref[...] = level
    tile = tile_ref[...]
    if products:
        partners = [refs[4][:own], level, refs[5][:own]]
        columns = [row_sum(level * partner) * (1.0 / cluster) for partner in partners]
        tile = tile + level_terms(core_ref[0], columns, 2 * own, depth)
    left = total.shape[0] - own
    message_ref[:left] = total[own:]
    message_ref[left:] = tile


def combine_kernel(products, bits, clusters, *refs):
    refs = list(refs)
    core_ref, mine_ref = refs[:2]
    got = [ref[...] for ref in refs[2 : 2 + 2 ** len(bits) - 1]]
    refs = refs[1 + 2 ** len(bits) :]
    sibling_ref = refs.pop() if len(bits) == 2 else None
    level_out = [refs.pop() for _ in bits][::-1]
    next_ref = refs.pop()
    own = level_out[0].shape[0]
    depth = PRODUCTS_TILE if products else NORM_TILE
    near = mine_ref[...] + got[0]
    total = near
    pairs = [(near[:own], bits[0], 0, clusters[0])]
    if len(bits) == 2:
        far = got[1] + got[2]
        total = near + far
        sibling = far[:own]
        sibling_ref[...] = sibling
        pairs.append((sibling, None, 1, clusters[0]))
        pairs.append((total[own : 2 * own], bits[1], 0, clusters[1]))
    for ref, pair in zip(level_out, pairs[:: 2 if len(bits) == 2 else 1]):
        ref[...] = pair[0]
    tile = total[total.shape[0] - depth :]
    if products:
        r_ref, d_ref = refs[:2]
        refs = refs[2:]
        siblings = [refs.pop(0), refs.pop(0)] if len(bits) == 2 else []
        columns = [jnp.zeros((own, 1), jnp.float32)] * 3
        for level, bit, kind, cluster in pairs:
            if kind:
                partners = [siblings[0][...], level, siblings[1][...]]
            else:
                here = slice(bit * own, (bit + 1) * own)
                partners = [r_ref[here], level, d_ref[here]]
            terms = [row_sum(level * partner) * (1.0 / cluster) for partner in partners]
            columns = [column + term for column, term in zip(columns, terms)]
        tile = tile + level_terms(core_ref[0], columns, 2 * own, depth)
    left = total.shape[0] - depth - len(bits) * own
    if left:
        next_ref[:left] = total[len(bits) * own : len(bits) * own + left]
        next_ref[left:] = tile
    else:
        for index, ref in enumerate(refs):
            next_ref[index * own : (index + 1) * own] = ref[...]
        for bit, pair in zip(bits, pairs[:: 2 if len(bits) == 2 else 1]):
            next_ref[bit * own : (bit + 1) * own] = pair[0]
        next_ref[next_ref.shape[0] - depth :] = tile


def up_parts(core, mine_ref, other_ref, local_ref, rows, width, depth):
    own = rows // 2
    crossing = (mine_ref.shape[0] - depth) // own
    sums = (mine_ref[crossing * own :] + other_ref[crossing * own :]).T[:rows]
    scaled = []
    for bit in range(crossing):
        here = slice(bit * own, (bit + 1) * own)
        low_rows = chosen(core, other_ref[here], mine_ref[here])
        high_rows = chosen(core, mine_ref[here], other_ref[here])
        scaled.append(jnp.concatenate([low_rows, high_rows], axis=0) * (1.0 / (width * (2 << bit))))
    one = [local_ref[:, part * LANES : (part + 1) * LANES] * (1.0 / (2 * LEAF)) for part in range(2)]
    two = local_ref[:, 2 * LANES :] * (1.0 / (4 * LEAF))
    return sums, [stacked(jnp.concatenate([one[part], two] + scaled, axis=1)) for part in range(2)]


def own_rows(core, column, crossing):
    own = column.shape[0] // 2
    return jnp.concatenate([chosen(core, column[own:], column[:own])] * crossing, axis=0)


def put_edges(core, field_ref, paired_ref, send_ref):
    width = field_ref.shape[1]
    head = field_ref[:, :LEAF]
    tail = field_ref[:, width - LEAF :]
    paired_ref[...] = chosen(core, head, tail)
    send_ref[...] = chosen(core, tail, head)


def residual_up_kernel(first, siblings, *refs):
    core_ref, high_ref, low_ref, near_ref, mine_ref, other_ref, local_ref = refs[:7]
    refs = refs[7:]
    if first:
        image_ref, state_ref, paired_ref, send_ref = refs
        q_ref = image_ref
    else:
        field_ref, old_d_ref, old_q_ref, old_skel_ref, old_local_ref, old_state_ref = refs[:6]
        r_siblings = refs[6 : 6 + siblings]
        d_siblings = refs[6 + siblings : 6 + 2 * siblings]
        refs = refs[6 + 2 * siblings :]
        image_ref, state_ref, paired_ref, send_ref, d_ref, q_ref, skel_ref, new_local_ref = refs[:8]
        new_siblings = refs[8:]
    core = core_ref[0]
    rows, width = near_ref.shape
    half = width // 2
    sums, stacks = up_parts(core, mine_ref, other_ref, local_ref, rows, width, NORM_TILE)
    norm = sums[:, 0:1]
    state_ref[...] = in_lanes([norm], (rows, LANES))
    ratio = None if first else norm / old_state_ref[:, 0:1]
    for part in range(2):
        points = slice(part * half, (part + 1) * half)
        image = near_ref[:, points] + product(stacks[part], high_ref[:, points], low_ref[:, points], ROWS_COLS)
        image_ref[:, points] = image
        if not first:
            d_ref[:, points] = field_ref[:, points] + ratio * old_d_ref[:, points]
            q_ref[:, points] = image + ratio * old_q_ref[:, points]
    put_edges(core, q_ref, paired_ref, send_ref)
    if not first:
        rows_in = skel_ref.shape[0]
        crossing = rows_in // (rows // 2)
        skel_ref[...] = mine_ref[:rows_in] + own_rows(core, ratio, crossing) * old_skel_ref[...]
        new_local_ref[...] = local_ref[...] + ratio * old_local_ref[...]
        own_ratio = own_rows(core, ratio, 1)
        for new_ref, r_ref, d_ref in zip(new_siblings, r_siblings, d_siblings):
            new_ref[...] = r_ref[...] + own_ratio * d_ref[...]


def image_up_kernel(first, last, siblings, *refs):
    core_ref, high_ref, low_ref, near_ref, mine_ref, other_ref, local_ref = refs[:7]
    r_ref, w_ref, d_ref, q_ref, state_ref = refs[7:12]
    refs = refs[12:]
    if not first:
        solution_ref = refs[0]
        refs = refs[1:]
    if not last:
        r_skel_ref, d_skel_ref, r_local_ref, d_local_ref = refs[:4]
        r_siblings, q_siblings, d_siblings = [
            refs[4 + index * siblings : 4 + (index + 1) * siblings] for index in range(3)
        ]
        refs = refs[4 + 3 * siblings :]
    new_solution_ref, new_r_ref = refs[:2]
    if not last:
        new_d_ref, new_q_ref, new_skel_ref, new_local_ref, new_state_ref, paired_ref, send_ref = refs[2:9]
        new_siblings = refs[9:]
    core = core_ref[0]
    rows, width = near_ref.shape
    half = width // 2
    sums, stacks = up_parts(core, mine_ref, other_ref, local_ref, rows, width, PRODUCTS_TILE)
    dot = {pair: sums[:, index : index + 1] for index, pair in enumerate(PAIRS)}
    norm = state_ref[:, 0:1]
    step = norm / dot["dq"]
    new_norm = norm - step * (2.0 * dot["rq"] - step * dot["qq"])
    ratio = new_norm / norm
    curve = dot["rw"] - step * (dot["qw"] + dot["rz"] - step * dot["qz"])
    curve = curve + ratio * (dot["dw"] - step * dot["dz"] + dot["rq"] - step * dot["qq"] + ratio * dot["dq"])
    new_step = new_norm / curve
    for part in range(2):
        points = slice(part * half, (part + 1) * half)
        image = near_ref[:, points] + product(stacks[part], high_ref[:, points], low_ref[:, points], ROWS_COLS)
        d = d_ref[:, points]
        q = q_ref[:, points]
        r = r_ref[:, points] - step * q
        new_q = w_ref[:, points] - step * image + ratio * q
        new_d = r + ratio * d
        moved = step * d + new_step * new_d
        new_solution_ref[:, points] = moved if first else solution_ref[:, points] + moved
        new_r_ref[:, points] = r - new_step * new_q
        if not last:
            new_d_ref[:, points] = new_d
            new_q_ref[:, points] = new_q
    if not last:
        rows_in = new_skel_ref.shape[0]
        crossing = rows_in // (rows // 2)
        r_skel = r_skel_ref[:rows_in] - own_rows(core, step, crossing) * mine_ref[:rows_in]
        new_skel_ref[...] = r_skel + own_rows(core, ratio, crossing) * d_skel_ref[:rows_in]
        new_local_ref[...] = r_local_ref[...] - step * local_ref[...] + ratio * d_local_ref[...]
        own_step, own_ratio = own_rows(core, step, 1), own_rows(core, ratio, 1)
        for new_ref, r_ref, q_ref, d_ref in zip(new_siblings, r_siblings, q_siblings, d_siblings):
            new_ref[...] = r_ref[...] - own_step * q_ref[...] + own_ratio * d_ref[...]
        new_state_ref[...] = in_lanes([new_norm], (rows, LANES))
        put_edges(core, new_r_ref, paired_ref, send_ref)


def per_device(rhs, coords, nugget, near_ids, basis):
    rows, width = rhs.shape
    levels = basis.shape[0]
    leaves = width // LEAF
    own = rows // 2
    crossing = levels - (leaves.bit_length() - 1)
    devices = lax.axis_size("row") * lax.axis_size("col")
    place = jnp.reshape(lax.axis_index(BOTH), (1,))
    core = place % 2
    nugget = nugget[None, :]

    stages = [list(range(bit, min(bit + 2, crossing))) for bit in range(1, crossing, 2)]
    siblings = sum(len(bits) == 2 for bits in stages)

    def swap(value, mask):
        return lax.ppermute(value, BOTH, [(source, source ^ mask) for source in range(devices)])

    def halo(paired, other):
        outward = [(index, index + 1) for index in range(1, devices - 1, 2)]
        ends = [(0, 0), (devices - 1, devices - 1)]
        return swap(paired, 1), lax.ppermute(other, BOTH, outward + [(target, source) for source, target in outward] + ends)

    def down(field):
        shapes = [f32(rows, LOCAL * LANES)] + [f32(crossing * own, LANES)] * 2 + [f32(NORM_TILE, LANES)]
        return call(down_kernel, shapes, core, field, high, low, scalars=1, flops=FLOPS)

    def inner(half, field):
        args = [place, near_ids, field, nugget, *diagonal[half], *beside]
        body = functools.partial(inner_kernel, half)
        return call(body, [f32(rows, width // 2)], *args, scalars=2, flops=FLOPS // 2)[0]

    def edge(edges, front, back, *more):
        shapes = [f32(rows, width)] + ([f32(PRODUCTS_TILE, LANES)] if more else [])
        args = [place, core, near_ids, *edges, *outside, front, back, *more]
        return call(functools.partial(edge_kernel, bool(more)), shapes, *args, scalars=3, flops=FLOPS // 3)

    def chain(products, keep, got, tile, beside_steps, r_skel=None, d_skel=None, r_sib=(), d_sib=()):
        depth = PRODUCTS_TILE if products else NORM_TILE
        results = []
        both = [r_skel, d_skel] if products else []
        message, level = call(
            functools.partial(first_combine_kernel, products, 2 * width),
            [f32((crossing - 1) * own + depth, LANES), f32(own, LANES)],
            core,
            keep,
            got,
            tile,
            *both,
            scalars=1,
        )
        done, kept = [level], []
        for index in range(len(stages) + 1):
            bits = stages[index] if index < len(stages) else []
            masks = [sum(1 << bit for at, bit in enumerate(bits) if pick >> at & 1) for pick in range(1, 2 ** len(bits))]
            got = [swap(message, mask) for mask in masks or [1]]
            if index < len(beside_steps):
                *got, result = lax.optimization_barrier((*got, beside_steps[index](message)))
                results.append(result)
            if not bits:
                break
            left = crossing - bits[-1] - 1
            paired = len(bits) == 2
            args = [core, message, *got, *both]
            if products and paired:
                args = args + [r_sib[len(kept)], d_sib[len(kept)]]
            message, *levels_out = call(
                functools.partial(combine_kernel, products, bits, [width * (2 << bit) for bit in bits]),
                [f32((left or crossing) * own + depth, LANES)] + [f32(own, LANES)] * (3 if paired else 1),
                *args,
                *([] if left else done),
                scalars=1,
            )
            done = done + levels_out[: len(bits)]
            kept = kept + levels_out[len(bits) :]
        return message, got[0], results, kept

    edges = halo(*call(edges_kernel, [f32(rows + 8, LEAF)] * 2, core, rhs, coords, scalars=1))
    turned = coords.T
    half = leaves // 2
    pairs = [(leaf, leaf) for leaf in range(half)]
    *front_diagonal, high, low = pl.pallas_call(
        functools.partial(setup_kernel, pairs),
        out_shape=[bf16(half, LEAF, LEAF)] * 2 + [pltpu.VMEM((levels * LANES, width), jnp.bfloat16)] * 2,
        in_specs=[whole(), whole(), whole(pltpu.HBM)],
        out_specs=[whole()] * 4,
        scratch_shapes=[pltpu.VMEM(basis.shape, jnp.float32), pltpu.SemaphoreType.DMA((levels,))],
        compiler_params=pltpu.CompilerParams(vmem_limit_bytes=44 * 2**20),
        cost_estimate=pl.CostEstimate(flops=FLOPS, bytes_accessed=2**20, transcendentals=0),
    )(coords, turned, basis)
    diagonal = [front_diagonal, None]
    beside = outside = None

    def after(message, *values):
        return lax.optimization_barrier((message, *values))[1:]

    def late_matrices(message):
        groups = [[(leaf, leaf) for leaf in range(half, leaves)], [(leaf, leaf + 1) for leaf in range(leaves - 1)]]

        def body(lane_ref, sub_ref, *refs):
            for index, group in enumerate(groups):
                fill_matrices(group, lane_ref, sub_ref, *refs[2 * index : 2 * index + 2])

        shapes = [bf16(len(group), LEAF, LEAF) for group in groups for _ in range(2)]
        return call(body, shapes, *after(message, coords, turned), flops=2 * FLOPS)

    def late_edge_matrices(message):
        def body(core_ref, *refs):
            edge_matrices(core_ref, rows, *refs)

        args = after(message, turned, *edges)
        return call(body, [bf16(2, LEAF, LEAF)] * 2, core, *args, scalars=1, flops=FLOPS)

    solution, r, carried = None, rhs, None
    for step in range(0, ITERS, 2):
        first, last = step == 0, step + 2 == ITERS
        r_local, keep, part, tile = down(r)
        got = swap(part, 1)
        if first:
            message, got, results, r_sib = chain(False, keep, got, tile, [late_matrices, late_edge_matrices])
            diagonal[1], beside = results[0][:2], results[0][2:]
            outside = results[1]
            (near,) = edge(edges, inner(0, r), inner(1, r))
        else:
            fronts = []

            def inner_work(message):
                fronts.extend(inner(half, *after(message, r)) for half in range(2))
                return fronts

            def edge_work(message):
                return edge(edges, *after(message, *fronts))[0]

            message, got, results, r_sib = chain(False, keep, got, tile, [inner_work, edge_work])
            near = results[1]
        args = [core, high, low, near, message, got, r_local]
        outs = [f32(rows, width), f32(rows, LANES)] + [f32(rows, LEAF)] * 2
        if first:
            w, state, *edges = call(
                functools.partial(residual_up_kernel, True, 0), outs, *args, scalars=1, flops=FLOPS // 2
            )
            d, q, d_skel, d_local, d_sib = r, w, message, r_local, r_sib
        else:
            outs = outs + [f32(rows, width)] * 2 + [f32(crossing * own, LANES), f32(rows, LOCAL * LANES)]
            outs = outs + [f32(own, LANES)] * siblings
            body = functools.partial(residual_up_kernel, False, siblings)
            args = args + [r, *carried, *r_sib, *d_sib]
            w, state, edge_paired, edge_other, d, q, d_skel, d_local, *d_sib = call(
                body, outs, *args, scalars=1, flops=FLOPS // 2
            )
            edges = (edge_paired, edge_other)
        r_skel = message
        edges = halo(*edges)
        q_local, keep, part, _ = down(q)
        got = swap(part, 1)
        near, tile = edge(edges, inner(0, q), inner(1, q), r, q, d, w, r_local, q_local, d_local)
        message, got, _, q_sib = chain(True, keep, got, tile, [], r_skel, d_skel, r_sib, d_sib)
        args = [core, high, low, near, message, got, q_local, r, w, d, q, state]
        args = args + ([] if first else [solution]) + ([] if last else [r_skel, d_skel, r_local, d_local, *r_sib, *q_sib, *d_sib])
        outs = [f32(rows, width)] * 2
        if not last:
            outs = outs + [f32(rows, width)] * 2 + [f32(crossing * own, LANES), f32(rows, LOCAL * LANES)]
            outs = outs + [f32(rows, LANES)] + [f32(rows, LEAF)] * 2 + [f32(own, LANES)] * siblings
        solution, r, *rest = call(
            functools.partial(image_up_kernel, first, last, siblings), outs, *args, scalars=1, flops=FLOPS // 2
        )
        if not last:
            carried = rest[:5]
            edges = halo(*rest[5:7])
            d_sib = rest[7:]
    return (solution, r)


def solution(mesh):
    placed = (
        P(None, BOTH),
        P(None, BOTH),
        P(BOTH),
        P(BOTH, None),
        P(None, None, BOTH),
    )
    return jax.shard_map(
        per_device,
        mesh=mesh,
        in_specs=placed,
        out_specs=(P(None, BOTH), P(None, BOTH)),
        check_vma=False,
    )
```

```python
import functools

import jax
import jax.numpy as jnp
from jax import lax
from jax.experimental import pallas as pl
from jax.experimental.pallas import tpu as pltpu
from jax.sharding import PartitionSpec as P

LEAF = 512
ITERS = 4
WIN = 3
LANES = 128
LOCAL = 3
CHUNK = 16
NORM_TILE = 8
PRODUCTS_TILE = 16
FLOPS = 3 * 10**9

root_three = 1.7320508075688772
spacing_factor = 1.6
matern_scale = root_three / (spacing_factor * LEAF ** (-1.0 / 3.0))

BOTH = ("row", "col")
ROWS_COLS = (((1,), (0,)), ((), ()))
ROWS_ROWS = (((1,), (1,)), ((), ()))

PAIRS = ("dq", "rq", "qq", "rw", "qw", "dw", "rz", "qz", "dz")


def halves(values):
    high = values.astype(jnp.bfloat16)
    low = (values - high.astype(jnp.float32)).astype(jnp.bfloat16)
    return high, low


def stacked(values):
    return jnp.concatenate(halves(values), axis=0)


def product(stack, high, low, dims):
    rows = stack.shape[0] // 2
    main = lax.dot_general(stack, high, dims, preferred_element_type=jnp.float32)
    rest = lax.dot_general(stack[:rows], low, dims, preferred_element_type=jnp.float32)
    return main[:rows] + (main[rows:] + rest)


def row_sum(values):
    return jnp.sum(values, axis=1, keepdims=True)


def in_lanes(columns, shape):
    lane = lax.broadcasted_iota(jnp.int32, shape, 1)
    block = jnp.zeros(shape, jnp.float32)
    for index, column in enumerate(columns):
        block = jnp.where(lane == index, column, block)
    return block


def sums_tile(columns, rows, depth):
    turned = in_lanes(columns, (rows, LANES)).T[:depth]
    return jnp.concatenate([turned, jnp.zeros((depth, LANES - rows), jnp.float32)], axis=1)


def level_terms(core, columns, rows, depth):
    twice = [jnp.concatenate([column, column], axis=0) for column in columns]
    zero = jnp.zeros((rows, 1), jnp.float32)
    tile = sums_tile([zero] * (len(PAIRS) - len(columns)) + twice, rows, depth)
    lane = lax.broadcasted_iota(jnp.int32, tile.shape, 1)
    return jnp.where(lane // (rows // 2) == core, tile, 0.0)


def chosen(core, odd, even):
    return jnp.where(core == 1, odd, even)


def whole(memory=pltpu.VMEM):
    return pl.BlockSpec(memory_space=memory)


def call(body, outs, *args, scalars=0, flops=0, limit=32):
    return pl.pallas_call(
        body,
        out_shape=outs,
        in_specs=[whole(pltpu.SMEM)] * scalars + [whole()] * (len(args) - scalars),
        out_specs=[whole()] * len(outs),
        compiler_params=pltpu.CompilerParams(vmem_limit_bytes=limit * 2**20),
        cost_estimate=pl.CostEstimate(flops=flops, bytes_accessed=2**20, transcendentals=0),
    )(*args)


def f32(*shape):
    return jax.ShapeDtypeStruct(shape, jnp.float32)


def bf16(*shape):
    return jax.ShapeDtypeStruct(shape, jnp.bfloat16)


def matrix_rows(rows, lanes):
    square = None
    for axis in range(3):
        spread = rows[:, axis : axis + 1] - lanes[axis : axis + 1]
        square = spread * spread if square is None else square + spread * spread
    square = square * (matern_scale * matern_scale)
    scaled = square * lax.rsqrt(jnp.maximum(square, 1e-30))
    return halves((1.0 + scaled) * jnp.exp(-scaled))


def fill_matrices(pairs, lane_ref, sub_ref, high_ref, low_ref):
    for matrix, (row_leaf, col_leaf) in enumerate(pairs):
        lanes = lane_ref[:, col_leaf * LEAF : (col_leaf + 1) * LEAF]

        def one(part, carry):
            row_at = pl.multiple_of(row_leaf * LEAF + part * CHUNK, CHUNK)
            out_at = pl.ds(pl.multiple_of(part * CHUNK, CHUNK), CHUNK)
            values = matrix_rows(sub_ref[pl.ds(row_at, CHUNK)], lanes)
            high_ref[matrix, out_at], low_ref[matrix, out_at] = values
            return carry

        lax.fori_loop(0, LEAF // CHUNK, one, 0, unroll=4)


def setup_kernel(pairs, lane_ref, basis_ref, high_ref, low_ref, basis_high_ref, basis_low_ref, sub_ref, raw_ref, sem_ref):
    levels, rank, _ = basis_ref.shape
    copies = [pltpu.make_async_copy(basis_ref.at[at], raw_ref.at[at], sem_ref.at[at]) for at in range(levels)]
    for copy in copies:
        copy.start()
    lanes = lane_ref[...]
    sub_ref[...] = jnp.concatenate([lanes, jnp.zeros((8 - lanes.shape[0], lanes.shape[1]), jnp.float32)], axis=0).T
    fill_matrices(pairs, lane_ref, sub_ref, high_ref, low_ref)
    for at, copy in enumerate(copies):
        copy.wait()
        here = slice(at * rank, (at + 1) * rank)
        basis_high_ref[here], basis_low_ref[here] = halves(raw_ref[at])


def edge_matrices(core_ref, rows, sub_ref, paired_ref, other_ref, high_ref, low_ref):
    core = core_ref[0]
    leaves = sub_ref.shape[0] // LEAF
    here = slice(rows, rows + 3)
    lanes = [
        chosen(core, paired_ref[here], other_ref[here]),
        chosen(core, other_ref[here], paired_ref[here]),
    ]

    for side in range(2):
        first_row = side * (leaves - 1) * LEAF

        def one(part, carry):
            row_at = pl.multiple_of(first_row + part * CHUNK, CHUNK)
            out_at = pl.ds(pl.multiple_of(part * CHUNK, CHUNK), CHUNK)
            values = matrix_rows(sub_ref[pl.ds(row_at, CHUNK)], lanes[side])
            high_ref[side, out_at], low_ref[side, out_at] = values
            return carry

        lax.fori_loop(0, LEAF // CHUNK, one, 0, unroll=4)


def edges_kernel(core_ref, field_ref, coords_ref, paired_ref, other_ref):
    core = core_ref[0]
    rows, width = field_ref.shape
    pad = jnp.zeros((8 - 3, LEAF), jnp.float32)
    head = jnp.concatenate([field_ref[:, :LEAF], coords_ref[:, :LEAF], pad], axis=0)
    tail = jnp.concatenate([field_ref[:, width - LEAF :], coords_ref[:, width - LEAF :], pad], axis=0)
    paired_ref[...] = chosen(core, head, tail)
    other_ref[...] = chosen(core, tail, head)


def down_kernel(core_ref, field_ref, high_ref, low_ref, local_ref, keep_ref, send_ref, *tile_refs):
    core = core_ref[0]
    rank = LANES
    rows, width = field_ref.shape
    half = width // 2
    stack = stacked(field_ref[...])
    for part in range(2):
        points = slice(part * half, (part + 1) * half)
        local_ref[:, part * rank : (part + 1) * rank] = product(
            stack[:, points], high_ref[:rank, points], low_ref[:rank, points], ROWS_ROWS
        )
    all_points = product(stack, high_ref[rank:], low_ref[rank:], ROWS_ROWS)
    local_ref[:, 2 * rank :] = all_points[:, :rank]
    own = rows // 2
    for bit in range(all_points.shape[1] // rank - 1):
        block = all_points[:, (bit + 1) * rank : (bit + 2) * rank]
        keep_ref[bit * own : (bit + 1) * own] = chosen(core, block[own:], block[:own])
        send_ref[bit * own : (bit + 1) * own] = chosen(core, block[:own], block[own:])
    for ref in tile_refs:
        ref[...] = sums_tile([row_sum(field_ref[...] * field_ref[...])], rows, NORM_TILE)


def leaf_of(ref, leaf):
    return ref[:, leaf * LEAF : (leaf + 1) * LEAF]


def weight_of(weights_ref, leaf, offset):
    at = WIN * leaf + offset + 1
    return weights_ref[at : at + 1]


def leaf_weights(near_ids, first_leaf):
    target = first_leaf + jnp.arange(near_ids.shape[0])[:, None] + jnp.arange(WIN)[None, :] - 1
    found = jnp.any(near_ids[:, None, :] == target[:, :, None], axis=2) & (target >= 0)
    weights = jnp.where(found, 1.0 / (16 * WIN), 0.0).astype(jnp.float32)
    return jnp.broadcast_to(weights.reshape(-1, 1), (weights.size, LEAF))


def inner_kernel(half, weights_ref, field_ref, nugget_ref, high_ref, low_ref, pair_high_ref, pair_low_ref, out_ref):
    leaves = weights_ref.shape[0] // WIN
    start = half * (leaves // 2)
    stop = start + leaves // 2
    pieces = {leaf: stacked(leaf_of(field_ref, leaf)) for leaf in range(max(start - 1, 0), min(stop + 1, leaves))}
    for leaf in range(start, stop):
        at = leaf - start
        inside = product(pieces[leaf], high_ref[at], low_ref[at], ROWS_COLS)
        total = leaf_of(nugget_ref, leaf) * leaf_of(field_ref, leaf) + weight_of(weights_ref, leaf, 0) * inside
        if leaf > 0:
            before = product(pieces[leaf - 1], pair_high_ref[leaf - 1], pair_low_ref[leaf - 1], ROWS_COLS)
            total = total + weight_of(weights_ref, leaf, -1) * before
        if leaf < leaves - 1:
            after = product(pieces[leaf + 1], pair_high_ref[leaf], pair_low_ref[leaf], ROWS_ROWS)
            total = total + weight_of(weights_ref, leaf, 1) * after
        out_ref[:, at * LEAF : (at + 1) * LEAF] = total


def edge_kernel(sums, *refs):
    core_ref, weights_ref, paired_ref, other_ref, high_ref, low_ref, front_ref, back_ref = refs[:8]
    refs = refs[8:]
    out_ref = refs[-2] if sums else refs[-1]
    core = core_ref[0]
    rows, width = out_ref.shape
    leaves = width // LEAF
    before = chosen(core, paired_ref[:rows], other_ref[:rows])
    after = chosen(core, other_ref[:rows], paired_ref[:rows])
    out_ref[:, : width // 2] = front_ref[...]
    out_ref[:, width // 2 :] = back_ref[...]
    part = product(stacked(before), high_ref[0], low_ref[0], ROWS_ROWS)
    out_ref[:, :LEAF] += weight_of(weights_ref, 0, -1) * part
    part = product(stacked(after), high_ref[1], low_ref[1], ROWS_ROWS)
    out_ref[:, width - LEAF :] += weight_of(weights_ref, leaves - 1, 1) * part
    if not sums:
        return
    fields = dict(zip("rqdw", refs[:4]))
    locals_ = dict(zip("rqd", refs[4:7]))
    tile_ref = refs[-1]
    totals = {pair: jnp.zeros((rows, 1), jnp.float32) for pair in PAIRS}
    for leaf in range(leaves):
        here = {name: leaf_of(ref, leaf) for name, ref in fields.items()}
        here["z"] = leaf_of(out_ref, leaf)
        for left, right in PAIRS:
            totals[left + right] = totals[left + right] + row_sum(here[left] * here[right])
    for block in range(LOCAL):
        scale = 1.0 / (LEAF * (2 if block < 2 else 4))
        lanes = slice(block * LANES, (block + 1) * LANES)
        for name in "rqd":
            term = row_sum(locals_[name][:, lanes] * locals_["q"][:, lanes])
            totals[name + "z"] = totals[name + "z"] + scale * term
    tile_ref[...] = sums_tile([totals[pair] for pair in PAIRS], rows, PRODUCTS_TILE)


def first_combine_kernel(products, cluster, *refs):
    core_ref, mine_ref, other_ref, tile_ref = refs[:4]
    message_ref, level_ref = refs[-2:]
    own = level_ref.shape[0]
    depth = tile_ref.shape[0]
    total = mine_ref[...] + other_ref[...]
    level = total[:own]
    level_ref[...] = level
    tile = tile_ref[...]
    if products:
        partners = [refs[4][:own], level, refs[5][:own]]
        columns = [row_sum(level * partner) * (1.0 / cluster) for partner in partners]
        tile = tile + level_terms(core_ref[0], columns, 2 * own, depth)
    left = total.shape[0] - own
    message_ref[:left] = total[own:]
    message_ref[left:] = tile


def combine_kernel(products, last, sibling, own, bits, clusters, *refs):
    refs = list(refs)
    core_ref, mine_ref = refs[:2]
    got = [ref[...] for ref in refs[2 : 2 + 2 ** len(bits) - 1]]
    refs = refs[1 + 2 ** len(bits) :]
    sibling_ref = refs.pop() if sibling else None
    level_out = [] if last else [refs.pop() for _ in bits][::-1]
    next_ref = refs.pop()
    depth = PRODUCTS_TILE if products else NORM_TILE
    near = mine_ref[...] + got[0]
    total = near
    pairs = [(near[:own], bits[0], 0, clusters[0])]
    if len(bits) == 2:
        far = got[1] + got[2]
        total = near + far
        if sibling:
            sibling_ref[...] = far[:own]
        pairs.append((far[:own], None, 1, clusters[0]))
        pairs.append((total[own : 2 * own], bits[1], 0, clusters[1]))
    for ref, pair in zip(level_out, pairs[:: 2 if len(bits) == 2 else 1]):
        ref[...] = pair[0]
    tile = total[total.shape[0] - depth :]
    if products:
        r_ref, d_ref = refs[:2]
        refs = refs[2:]
        siblings = [refs.pop(0), refs.pop(0)] if len(bits) == 2 else []
        columns = [jnp.zeros((own, 1), jnp.float32)] * 3
        for level, bit, kind, cluster in pairs:
            if kind:
                partners = [siblings[0][...], level, siblings[1][...]]
            else:
                here = slice(bit * own, (bit + 1) * own)
                partners = [r_ref[here], level, d_ref[here]]
            terms = [row_sum(level * partner) * (1.0 / cluster) for partner in partners]
            columns = [column + term for column, term in zip(columns, terms)]
        tile = tile + level_terms(core_ref[0], columns, 2 * own, depth)
    left = total.shape[0] - depth - len(bits) * own
    if not last:
        next_ref[:left] = total[len(bits) * own : len(bits) * own + left]
        next_ref[left:] = tile
    else:
        for index, ref in enumerate(refs):
            next_ref[index * own : (index + 1) * own] = ref[...]
        for bit, pair in zip(bits, pairs[:: 2 if len(bits) == 2 else 1]):
            next_ref[bit * own : (bit + 1) * own] = pair[0]
        next_ref[next_ref.shape[0] - depth :] = tile


def up_parts(core, mine_ref, other_ref, local_ref, rows, width, depth):
    own = rows // 2
    crossing = (mine_ref.shape[0] - depth) // own
    sums = (mine_ref[crossing * own :] + other_ref[crossing * own :]).T[:rows]
    scaled = []
    for bit in range(crossing):
        here = slice(bit * own, (bit + 1) * own)
        low_rows = chosen(core, other_ref[here], mine_ref[here])
        high_rows = chosen(core, mine_ref[here], other_ref[here])
        scaled.append(jnp.concatenate([low_rows, high_rows], axis=0) * (1.0 / (width * (2 << bit))))
    one = [local_ref[:, part * LANES : (part + 1) * LANES] * (1.0 / (2 * LEAF)) for part in range(2)]
    two = local_ref[:, 2 * LANES :] * (1.0 / (4 * LEAF))
    return sums, [stacked(jnp.concatenate([one[part], two] + scaled, axis=1)) for part in range(2)]


def own_rows(core, column, crossing):
    own = column.shape[0] // 2
    return jnp.concatenate([chosen(core, column[own:], column[:own])] * crossing, axis=0)


def put_edges(core, field_ref, paired_ref, send_ref):
    width = field_ref.shape[1]
    head = field_ref[:, :LEAF]
    tail = field_ref[:, width - LEAF :]
    paired_ref[...] = chosen(core, head, tail)
    send_ref[...] = chosen(core, tail, head)


def residual_up_kernel(first, siblings, *refs):
    core_ref, high_ref, low_ref, near_ref, mine_ref, other_ref, local_ref = refs[:7]
    refs = refs[7:]
    if first:
        image_ref, state_ref, paired_ref, send_ref = refs
        q_ref = image_ref
    else:
        field_ref, old_d_ref, old_q_ref, old_skel_ref, old_local_ref, old_state_ref = refs[:6]
        r_siblings = refs[6 : 6 + siblings]
        d_siblings = refs[6 + siblings : 6 + 2 * siblings]
        refs = refs[6 + 2 * siblings :]
        image_ref, state_ref, paired_ref, send_ref, d_ref, q_ref, skel_ref, new_local_ref = refs[:8]
        new_siblings = refs[8:]
    core = core_ref[0]
    rows, width = near_ref.shape
    half = width // 2
    sums, stacks = up_parts(core, mine_ref, other_ref, local_ref, rows, width, NORM_TILE)
    norm = sums[:, 0:1]
    state_ref[...] = in_lanes([norm], (rows, LANES))
    ratio = None if first else norm / old_state_ref[:, 0:1]
    for part in range(2):
        points = slice(part * half, (part + 1) * half)
        image = near_ref[:, points] + product(stacks[part], high_ref[:, points], low_ref[:, points], ROWS_COLS)
        image_ref[:, points] = image
        if not first:
            d_ref[:, points] = field_ref[:, points] + ratio * old_d_ref[:, points]
            q_ref[:, points] = image + ratio * old_q_ref[:, points]
    put_edges(core, q_ref, paired_ref, send_ref)
    if not first:
        rows_in = skel_ref.shape[0]
        crossing = rows_in // (rows // 2)
        skel_ref[...] = mine_ref[:rows_in] + own_rows(core, ratio, crossing) * old_skel_ref[...]
        new_local_ref[...] = local_ref[...] + ratio * old_local_ref[...]
        own_ratio = own_rows(core, ratio, 1)
        for new_ref, r_ref, d_ref in zip(new_siblings, r_siblings, d_siblings):
            new_ref[...] = r_ref[...] + own_ratio * d_ref[...]


def image_up_kernel(first, last, siblings, *refs):
    core_ref, high_ref, low_ref, near_ref, mine_ref, other_ref, local_ref = refs[:7]
    r_ref, w_ref, d_ref, q_ref, state_ref = refs[7:12]
    refs = refs[12:]
    if not first:
        solution_ref = refs[0]
        refs = refs[1:]
    if not last:
        r_skel_ref, d_skel_ref, r_local_ref, d_local_ref = refs[:4]
        r_siblings, q_siblings, d_siblings = [
            refs[4 + index * siblings : 4 + (index + 1) * siblings] for index in range(3)
        ]
        refs = refs[4 + 3 * siblings :]
    new_solution_ref, new_r_ref = refs[:2]
    if not last:
        new_d_ref, new_q_ref, new_skel_ref, new_local_ref, new_state_ref, paired_ref, send_ref = refs[2:9]
        new_siblings = refs[9:]
    core = core_ref[0]
    rows, width = near_ref.shape
    half = width // 2
    sums, stacks = up_parts(core, mine_ref, other_ref, local_ref, rows, width, PRODUCTS_TILE)
    dot = {pair: sums[:, index : index + 1] for index, pair in enumerate(PAIRS)}
    norm = state_ref[:, 0:1]
    step = norm / dot["dq"]
    new_norm = norm - step * (2.0 * dot["rq"] - step * dot["qq"])
    ratio = new_norm / norm
    curve = dot["rw"] - step * (dot["qw"] + dot["rz"] - step * dot["qz"])
    curve = curve + ratio * (dot["dw"] - step * dot["dz"] + dot["rq"] - step * dot["qq"] + ratio * dot["dq"])
    new_step = new_norm / curve
    for part in range(2):
        points = slice(part * half, (part + 1) * half)
        image = near_ref[:, points] + product(stacks[part], high_ref[:, points], low_ref[:, points], ROWS_COLS)
        d = d_ref[:, points]
        q = q_ref[:, points]
        r = r_ref[:, points] - step * q
        new_q = w_ref[:, points] - step * image + ratio * q
        new_d = r + ratio * d
        moved = step * d + new_step * new_d
        new_solution_ref[:, points] = moved if first else solution_ref[:, points] + moved
        new_r_ref[:, points] = r - new_step * new_q
        if not last:
            new_d_ref[:, points] = new_d
            new_q_ref[:, points] = new_q
    if not last:
        rows_in = new_skel_ref.shape[0]
        crossing = rows_in // (rows // 2)
        r_skel = r_skel_ref[:rows_in] - own_rows(core, step, crossing) * mine_ref[:rows_in]
        new_skel_ref[...] = r_skel + own_rows(core, ratio, crossing) * d_skel_ref[:rows_in]
        new_local_ref[...] = r_local_ref[...] - step * local_ref[...] + ratio * d_local_ref[...]
        own_step, own_ratio = own_rows(core, step, 1), own_rows(core, ratio, 1)
        for new_ref, r_ref, q_ref, d_ref in zip(new_siblings, r_siblings, q_siblings, d_siblings):
            new_ref[...] = r_ref[...] - own_step * q_ref[...] + own_ratio * d_ref[...]
        new_state_ref[...] = in_lanes([new_norm], (rows, LANES))
        put_edges(core, new_r_ref, paired_ref, send_ref)


def per_device(rhs, coords, nugget, near_ids, basis):
    rows, width = rhs.shape
    levels = basis.shape[0]
    leaves = width // LEAF
    own = rows // 2
    crossing = levels - (leaves.bit_length() - 1)
    devices = lax.axis_size("row") * lax.axis_size("col")
    place = jnp.reshape(lax.axis_index(BOTH), (1,))
    core = place % 2
    nugget = nugget[None, :]
    weights = leaf_weights(near_ids, place[0] * leaves)

    stages = [list(range(bit, min(bit + 2, crossing))) for bit in range(1, crossing, 2)]
    siblings = sum(len(bits) == 2 for bits in stages)

    def swap(value, mask):
        return lax.ppermute(value, BOTH, [(source, source ^ mask) for source in range(devices)])

    def halo(paired, other):
        outward = [(index, index + 1) for index in range(1, devices - 1, 2)]
        ends = [(0, 0), (devices - 1, devices - 1)]
        return swap(paired, 1), lax.ppermute(other, BOTH, outward + [(target, source) for source, target in outward] + ends)

    def down(field, *tile):
        shapes = [f32(rows, LOCAL * LANES)] + [f32(crossing * own, LANES)] * 2 + list(tile)
        return call(down_kernel, shapes, core, field, high, low, scalars=1, flops=FLOPS)

    def inner(half, field):
        args = [weights, field, nugget, *diagonal[half], *beside]
        body = functools.partial(inner_kernel, half)
        return call(body, [f32(rows, width // 2)], *args, flops=FLOPS // 2)[0]

    def edge(edges, front, back, *more):
        shapes = [f32(rows, width)] + ([f32(PRODUCTS_TILE, LANES)] if more else [])
        args = [core, weights, *edges, *outside, front, back, *more]
        return call(functools.partial(edge_kernel, bool(more)), shapes, *args, scalars=1, flops=FLOPS // 3)

    def chain(products, final, keep, got, tile, beside_steps, r_skel=None, d_skel=None, r_sib=(), d_sib=()):
        depth = PRODUCTS_TILE if products else NORM_TILE
        results = []
        both = [r_skel, d_skel] if products else []
        message, level = call(
            functools.partial(first_combine_kernel, products, 2 * width),
            [f32((crossing - 1) * own + depth, LANES), f32(own, LANES)],
            core,
            keep,
            got,
            tile,
            *both,
            scalars=1,
        )
        done, kept = [level], []
        for index in range(len(stages) + 1):
            bits = stages[index] if index < len(stages) else []
            masks = [sum(1 << bit for at, bit in enumerate(bits) if pick >> at & 1) for pick in range(1, 2 ** len(bits))]
            got = [swap(message, mask) for mask in masks or [1]]
            if index < len(beside_steps):
                *got, result = lax.optimization_barrier((*got, beside_steps[index](message)))
                results.append(result)
            if not bits:
                break
            left = crossing - bits[-1] - 1
            paired = len(bits) == 2
            args = [core, message, *got, *both]
            if products and paired:
                args = args + [r_sib[index], d_sib[index]]
            sibling = paired and not final
            clusters = [width * (2 << bit) for bit in bits]
            message, *levels_out = call(
                functools.partial(combine_kernel, products, not left, sibling, own, bits, clusters),
                [f32((left or crossing) * own + depth, LANES)] + [f32(own, LANES)] * ((len(bits) if left else 0) + sibling),
                *args,
                *([] if left else done),
                scalars=1,
            )
            kept = kept + levels_out[len(levels_out) - sibling :]
            done = done + levels_out[: len(levels_out) - sibling]
        return message, got[0], results, kept

    edges = halo(*call(edges_kernel, [f32(rows + 8, LEAF)] * 2, core, rhs, coords, scalars=1))
    half = leaves // 2
    pairs = [(leaf, leaf) for leaf in range(half)]
    *front_diagonal, high, low, turned = pl.pallas_call(
        functools.partial(setup_kernel, pairs),
        out_shape=[bf16(half, LEAF, LEAF)] * 2
        + [pltpu.VMEM((levels * LANES, width), jnp.bfloat16)] * 2
        + [f32(width, 8)],
        in_specs=[whole(), whole(pltpu.HBM)],
        out_specs=[whole()] * 5,
        scratch_shapes=[pltpu.VMEM(basis.shape, jnp.float32), pltpu.SemaphoreType.DMA((levels,))],
        compiler_params=pltpu.CompilerParams(vmem_limit_bytes=44 * 2**20),
        cost_estimate=pl.CostEstimate(flops=FLOPS, bytes_accessed=2**20, transcendentals=0),
    )(coords, basis)
    diagonal = [front_diagonal, None]
    beside = outside = None

    def after(message, *values):
        return lax.optimization_barrier((message, *values))[1:]

    def late_matrices(message):
        groups = [[(leaf, leaf) for leaf in range(half, leaves)], [(leaf, leaf + 1) for leaf in range(leaves - 1)]]

        def body(lane_ref, sub_ref, *refs):
            for index, group in enumerate(groups):
                fill_matrices(group, lane_ref, sub_ref, *refs[2 * index : 2 * index + 2])

        shapes = [bf16(len(group), LEAF, LEAF) for group in groups for _ in range(2)]
        return call(body, shapes, *after(message, coords, turned), flops=2 * FLOPS)

    def late_edge_matrices(message):
        def body(core_ref, *refs):
            edge_matrices(core_ref, rows, *refs)

        args = after(message, turned, *edges)
        return call(body, [bf16(2, LEAF, LEAF)] * 2, core, *args, scalars=1, flops=FLOPS)

    solution, r, carried = None, rhs, None
    for step in range(0, ITERS, 2):
        first, last = step == 0, step + 2 == ITERS
        r_local, keep, part, tile = down(r, f32(NORM_TILE, LANES))
        got = swap(part, 1)
        if first:
            message, got, results, r_sib = chain(False, False, keep, got, tile, [late_matrices, late_edge_matrices])
            diagonal[1], beside = results[0][:2], results[0][2:]
            outside = results[1]
            (near,) = edge(edges, inner(0, r), inner(1, r))
        else:
            fronts = []

            def inner_work(message):
                fronts.extend(inner(half, *after(message, r)) for half in range(2))
                return fronts

            def edge_work(message):
                return edge(edges, *after(message, *fronts))[0]

            message, got, results, r_sib = chain(False, False, keep, got, tile, [inner_work, edge_work])
            near = results[1]
        args = [core, high, low, near, message, got, r_local]
        outs = [f32(rows, width), f32(rows, LANES)] + [f32(rows, LEAF)] * 2
        if first:
            w, state, *edges = call(
                functools.partial(residual_up_kernel, True, 0), outs, *args, scalars=1, flops=FLOPS // 2
            )
            d, q, d_skel, d_local, d_sib = r, w, message, r_local, r_sib
        else:
            outs = outs + [f32(rows, width)] * 2 + [f32(crossing * own, LANES), f32(rows, LOCAL * LANES)]
            outs = outs + [f32(own, LANES)] * siblings
            body = functools.partial(residual_up_kernel, False, siblings)
            args = args + [r, *carried, *r_sib, *d_sib]
            w, state, edge_paired, edge_other, d, q, d_skel, d_local, *d_sib = call(
                body, outs, *args, scalars=1, flops=FLOPS // 2
            )
            edges = (edge_paired, edge_other)
        r_skel = message
        edges = halo(*edges)
        q_local, keep, part = down(q)
        got = swap(part, 1)
        near, tile = edge(edges, inner(0, q), inner(1, q), r, q, d, w, r_local, q_local, d_local)
        message, got, _, q_sib = chain(True, last, keep, got, tile, [], r_skel, d_skel, r_sib, d_sib)
        args = [core, high, low, near, message, got, q_local, r, w, d, q, state]
        args = args + ([] if first else [solution]) + ([] if last else [r_skel, d_skel, r_local, d_local, *r_sib, *q_sib, *d_sib])
        outs = [f32(rows, width)] * 2
        if not last:
            outs = outs + [f32(rows, width)] * 2 + [f32(crossing * own, LANES), f32(rows, LOCAL * LANES)]
            outs = outs + [f32(rows, LANES)] + [f32(rows, LEAF)] * 2 + [f32(own, LANES)] * siblings
        solution, r, *rest = call(
            functools.partial(image_up_kernel, first, last, siblings), outs, *args, scalars=1, flops=FLOPS // 2
        )
        if not last:
            carried = rest[:5]
            edges = halo(*rest[5:7])
            d_sib = rest[7:]
    return (solution, r)


def solution(mesh):
    placed = (
        P(None, BOTH),
        P(None, BOTH),
        P(BOTH),
        P(BOTH, None),
        P(None, None, BOTH),
    )
    return jax.shard_map(
        per_device,
        mesh=mesh,
        in_specs=placed,
        out_specs=(P(None, BOTH), P(None, BOTH)),
        check_vma=False,
    )
```

```python
import functools

import jax
import jax.numpy as jnp
from jax import lax
from jax.experimental import pallas as pl
from jax.experimental.pallas import tpu as pltpu
from jax.sharding import PartitionSpec as P

LEAF = 512
ITERS = 4
WIN = 3
LANES = 128
LOCAL = 3
EDGE_BLOCKS = LEAF // LANES
CHUNK = 16
NORM_TILE = 8
PRODUCTS_TILE = 16
FLOPS = 3 * 10**9

root_three = 1.7320508075688772
spacing_factor = 1.6
matern_scale = root_three / (spacing_factor * LEAF ** (-1.0 / 3.0))

BOTH = ("row", "col")
ROWS_COLS = (((1,), (0,)), ((), ()))
ROWS_ROWS = (((1,), (1,)), ((), ()))

PAIRS = ("dq", "rq", "qq", "rw", "qw", "dw", "rz", "qz", "dz")


def halves(values):
    high = values.astype(jnp.bfloat16)
    low = (values - high.astype(jnp.float32)).astype(jnp.bfloat16)
    return high, low


def stacked(values):
    return jnp.concatenate(halves(values), axis=0)


def product(stack, high, low, dims):
    rows = stack.shape[0] // 2
    main = lax.dot_general(stack, high, dims, preferred_element_type=jnp.float32)
    rest = lax.dot_general(stack[:rows], low, dims, preferred_element_type=jnp.float32)
    return main[:rows] + (main[rows:] + rest)


def row_sum(values):
    return jnp.sum(values, axis=1, keepdims=True)


def in_lanes(columns, shape):
    lane = lax.broadcasted_iota(jnp.int32, shape, 1)
    block = jnp.zeros(shape, jnp.float32)
    for index, column in enumerate(columns):
        block = jnp.where(lane == index, column, block)
    return block


def sums_tile(columns, rows, depth):
    turned = in_lanes(columns, (rows, LANES)).T[:depth]
    return jnp.concatenate([turned, jnp.zeros((depth, LANES - rows), jnp.float32)], axis=1)


def level_terms(core, columns, rows, depth):
    twice = [jnp.concatenate([column, column], axis=0) for column in columns]
    zero = jnp.zeros((rows, 1), jnp.float32)
    tile = sums_tile([zero] * (len(PAIRS) - len(columns)) + twice, rows, depth)
    lane = lax.broadcasted_iota(jnp.int32, tile.shape, 1)
    return jnp.where(lane // (rows // 2) == core, tile, 0.0)


def chosen(core, odd, even):
    return jnp.where(core == 1, odd, even)


def whole(memory=pltpu.VMEM):
    return pl.BlockSpec(memory_space=memory)


def call(body, outs, *args, scalars=0, flops=0, limit=32):
    return pl.pallas_call(
        body,
        out_shape=outs,
        in_specs=[whole(pltpu.SMEM)] * scalars + [whole()] * (len(args) - scalars),
        out_specs=[whole()] * len(outs),
        compiler_params=pltpu.CompilerParams(vmem_limit_bytes=limit * 2**20),
        cost_estimate=pl.CostEstimate(flops=flops, bytes_accessed=2**20, transcendentals=0),
    )(*args)


def f32(*shape):
    return jax.ShapeDtypeStruct(shape, jnp.float32)


def bf16(*shape):
    return jax.ShapeDtypeStruct(shape, jnp.bfloat16)


def matrix_rows(rows, lanes):
    square = None
    for axis in range(3):
        spread = rows[:, axis : axis + 1] - lanes[axis : axis + 1]
        square = spread * spread if square is None else square + spread * spread
    square = square * (matern_scale * matern_scale)
    scaled = square * lax.rsqrt(jnp.maximum(square, 1e-30))
    return halves((1.0 + scaled) * jnp.exp(-scaled))


def fill_matrices(pairs, lane_ref, sub_ref, high_ref, low_ref):
    for matrix, (row_leaf, col_leaf) in enumerate(pairs):
        lanes = lane_ref[:, col_leaf * LEAF : (col_leaf + 1) * LEAF]

        def one(part, carry):
            row_at = pl.multiple_of(row_leaf * LEAF + part * CHUNK, CHUNK)
            out_at = pl.ds(pl.multiple_of(part * CHUNK, CHUNK), CHUNK)
            values = matrix_rows(sub_ref[pl.ds(row_at, CHUNK)], lanes)
            high_ref[matrix, out_at], low_ref[matrix, out_at] = values
            return carry

        lax.fori_loop(0, LEAF // CHUNK, one, 0, unroll=4)


def setup_kernel(pairs, lane_ref, basis_ref, high_ref, low_ref, basis_high_ref, basis_low_ref, sub_ref, raw_ref, sem_ref):
    levels, rank, _ = basis_ref.shape
    copies = [pltpu.make_async_copy(basis_ref.at[at], raw_ref.at[at], sem_ref.at[at]) for at in range(levels)]
    for copy in copies:
        copy.start()
    lanes = lane_ref[...]
    sub_ref[...] = jnp.concatenate([lanes, jnp.zeros((8 - lanes.shape[0], lanes.shape[1]), jnp.float32)], axis=0).T
    fill_matrices(pairs, lane_ref, sub_ref, high_ref, low_ref)
    for at, copy in enumerate(copies):
        copy.wait()
        here = slice(at * rank, (at + 1) * rank)
        basis_high_ref[here], basis_low_ref[here] = halves(raw_ref[at])


def edge_matrices(core_ref, rows, sub_ref, paired_ref, other_ref, high_ref, low_ref):
    core = core_ref[0]
    leaves = sub_ref.shape[0] // LEAF
    paired = paired_ref[:3]
    other = other_ref[rows : rows + 3]
    lanes = [chosen(core, paired, other), chosen(core, other, paired)]

    for side in range(2):
        first_row = side * (leaves - 1) * LEAF

        def one(part, carry):
            row_at = pl.multiple_of(first_row + part * CHUNK, CHUNK)
            out_at = pl.ds(pl.multiple_of(part * CHUNK, CHUNK), CHUNK)
            values = matrix_rows(sub_ref[pl.ds(row_at, CHUNK)], lanes[side])
            high_ref[side, out_at], low_ref[side, out_at] = values
            return carry

        lax.fori_loop(0, LEAF // CHUNK, one, 0, unroll=4)


def sides(core, field_ref):
    head = field_ref[:, :LEAF]
    tail = field_ref[:, field_ref.shape[1] - LEAF :]
    return chosen(core, head, tail), chosen(core, tail, head)


def edges_kernel(core_ref, field_ref, coords_ref, paired_ref, other_ref):
    core = core_ref[0]
    pad = jnp.zeros((8 - 3, LEAF), jnp.float32)
    paired, other = sides(core, coords_ref)
    paired_ref[...] = jnp.concatenate([paired, pad], axis=0)
    other_ref[...] = jnp.concatenate([sides(core, field_ref)[1], other, pad], axis=0)


def down_kernel(core_ref, field_ref, high_ref, low_ref, local_ref, keep_ref, send_ref, *tile_refs):
    core = core_ref[0]
    rank = LANES
    rows, width = field_ref.shape
    half = width // 2
    stack = stacked(field_ref[...])
    for part in range(2):
        points = slice(part * half, (part + 1) * half)
        local_ref[:, part * rank : (part + 1) * rank] = product(
            stack[:, points], high_ref[:rank, points], low_ref[:rank, points], ROWS_ROWS
        )
    all_points = product(stack, high_ref[rank:], low_ref[rank:], ROWS_ROWS)
    local_ref[:, 2 * rank :] = all_points[:, :rank]
    own = rows // 2
    for bit in range(all_points.shape[1] // rank - 1):
        block = all_points[:, (bit + 1) * rank : (bit + 2) * rank]
        keep_ref[bit * own : (bit + 1) * own] = chosen(core, block[own:], block[:own])
        at = EDGE_BLOCKS * rows + bit * own
        send_ref[at : at + own] = chosen(core, block[:own], block[own:])
    paired = sides(core, field_ref)[0]
    for block in range(EDGE_BLOCKS):
        send_ref[block * rows : (block + 1) * rows] = paired[:, block * LANES : (block + 1) * LANES]
    for ref in tile_refs:
        ref[...] = sums_tile([row_sum(field_ref[...] * field_ref[...])], rows, NORM_TILE)


def leaf_of(ref, leaf):
    return ref[:, leaf * LEAF : (leaf + 1) * LEAF]


def weight_of(weights_ref, leaf, offset):
    at = WIN * leaf + offset + 1
    return weights_ref[at : at + 1]


def leaf_weights(near_ids, first_leaf):
    target = first_leaf + jnp.arange(near_ids.shape[0])[:, None] + jnp.arange(WIN)[None, :] - 1
    found = jnp.any(near_ids[:, None, :] == target[:, :, None], axis=2) & (target >= 0)
    weights = jnp.where(found, 1.0 / (16 * WIN), 0.0).astype(jnp.float32)
    return jnp.broadcast_to(weights.reshape(-1, 1), (weights.size, LEAF))


def inner_kernel(half, weights_ref, field_ref, nugget_ref, high_ref, low_ref, pair_high_ref, pair_low_ref, out_ref):
    leaves = weights_ref.shape[0] // WIN
    start = half * (leaves // 2)
    stop = start + leaves // 2
    pieces = {leaf: stacked(leaf_of(field_ref, leaf)) for leaf in range(max(start - 1, 0), min(stop + 1, leaves))}
    for leaf in range(start, stop):
        at = leaf - start
        inside = product(pieces[leaf], high_ref[at], low_ref[at], ROWS_COLS)
        total = leaf_of(nugget_ref, leaf) * leaf_of(field_ref, leaf) + weight_of(weights_ref, leaf, 0) * inside
        if leaf > 0:
            before = product(pieces[leaf - 1], pair_high_ref[leaf - 1], pair_low_ref[leaf - 1], ROWS_COLS)
            total = total + weight_of(weights_ref, leaf, -1) * before
        if leaf < leaves - 1:
            after = product(pieces[leaf + 1], pair_high_ref[leaf], pair_low_ref[leaf], ROWS_ROWS)
            total = total + weight_of(weights_ref, leaf, 1) * after
        out_ref[:, at * LEAF : (at + 1) * LEAF] = total


def edge_kernel(sums, *refs):
    core_ref, weights_ref, paired_ref, other_ref, high_ref, low_ref, front_ref, back_ref = refs[:8]
    refs = refs[8:]
    out_ref = refs[-2] if sums else refs[-1]
    core = core_ref[0]
    rows, width = out_ref.shape
    leaves = width // LEAF
    paired = [paired_ref[block * rows : (block + 1) * rows] for block in range(EDGE_BLOCKS)]
    paired = jnp.concatenate(paired, axis=1)
    before = chosen(core, paired, other_ref[:rows])
    after = chosen(core, other_ref[:rows], paired)
    out_ref[:, : width // 2] = front_ref[...]
    out_ref[:, width // 2 :] = back_ref[...]
    part = product(stacked(before), high_ref[0], low_ref[0], ROWS_ROWS)
    out_ref[:, :LEAF] += weight_of(weights_ref, 0, -1) * part
    part = product(stacked(after), high_ref[1], low_ref[1], ROWS_ROWS)
    out_ref[:, width - LEAF :] += weight_of(weights_ref, leaves - 1, 1) * part
    if not sums:
        return
    fields = dict(zip("rqdw", refs[:4]))
    locals_ = dict(zip("rqd", refs[4:7]))
    tile_ref = refs[-1]
    totals = {pair: jnp.zeros((rows, 1), jnp.float32) for pair in PAIRS}
    for leaf in range(leaves):
        here = {name: leaf_of(ref, leaf) for name, ref in fields.items()}
        here["z"] = leaf_of(out_ref, leaf)
        for left, right in PAIRS:
            totals[left + right] = totals[left + right] + row_sum(here[left] * here[right])
    for block in range(LOCAL):
        scale = 1.0 / (LEAF * (2 if block < 2 else 4))
        lanes = slice(block * LANES, (block + 1) * LANES)
        for name in "rqd":
            term = row_sum(locals_[name][:, lanes] * locals_["q"][:, lanes])
            totals[name + "z"] = totals[name + "z"] + scale * term
    tile_ref[...] = sums_tile([totals[pair] for pair in PAIRS], rows, PRODUCTS_TILE)


def first_combine_kernel(products, cluster, *refs):
    core_ref, mine_ref, other_ref, tile_ref = refs[:4]
    message_ref, level_ref = refs[-2:]
    own = level_ref.shape[0]
    depth = tile_ref.shape[0]
    total = mine_ref[...] + other_ref[EDGE_BLOCKS * 2 * own :]
    level = total[:own]
    level_ref[...] = level
    tile = tile_ref[...]
    if products:
        partners = [refs[4][:own], level, refs[5][:own]]
        columns = [row_sum(level * partner) * (1.0 / cluster) for partner in partners]
        tile = tile + level_terms(core_ref[0], columns, 2 * own, depth)
    left = total.shape[0] - own
    message_ref[:left] = total[own:]
    message_ref[left:] = tile


def combine_kernel(products, last, sibling, own, bits, clusters, *refs):
    refs = list(refs)
    core_ref, mine_ref = refs[:2]
    got = [ref[...] for ref in refs[2 : 2 + 2 ** len(bits) - 1]]
    refs = refs[1 + 2 ** len(bits) :]
    sibling_ref = refs.pop() if sibling else None
    level_out = [] if last else [refs.pop() for _ in bits][::-1]
    next_ref = refs.pop()
    depth = PRODUCTS_TILE if products else NORM_TILE
    near = mine_ref[...] + got[0]
    total = near
    pairs = [(near[:own], bits[0], 0, clusters[0])]
    if len(bits) == 2:
        far = got[1] + got[2]
        total = near + far
        if sibling:
            sibling_ref[...] = far[:own]
        pairs.append((far[:own], None, 1, clusters[0]))
        pairs.append((total[own : 2 * own], bits[1], 0, clusters[1]))
    for ref, pair in zip(level_out, pairs[:: 2 if len(bits) == 2 else 1]):
        ref[...] = pair[0]
    tile = total[total.shape[0] - depth :]
    if products:
        r_ref, d_ref = refs[:2]
        refs = refs[2:]
        siblings = [refs.pop(0), refs.pop(0)] if len(bits) == 2 else []
        columns = [jnp.zeros((own, 1), jnp.float32)] * 3
        for level, bit, kind, cluster in pairs:
            if kind:
                partners = [siblings[0][...], level, siblings[1][...]]
            else:
                here = slice(bit * own, (bit + 1) * own)
                partners = [r_ref[here], level, d_ref[here]]
            terms = [row_sum(level * partner) * (1.0 / cluster) for partner in partners]
            columns = [column + term for column, term in zip(columns, terms)]
        tile = tile + level_terms(core_ref[0], columns, 2 * own, depth)
    left = total.shape[0] - depth - len(bits) * own
    if not last:
        next_ref[:left] = total[len(bits) * own : len(bits) * own + left]
        next_ref[left:] = tile
    else:
        for index, ref in enumerate(refs):
            next_ref[index * own : (index + 1) * own] = ref[...]
        for bit, pair in zip(bits, pairs[:: 2 if len(bits) == 2 else 1]):
            next_ref[bit * own : (bit + 1) * own] = pair[0]
        next_ref[next_ref.shape[0] - depth :] = tile


def up_parts(core, mine_ref, other_ref, local_ref, rows, width, depth):
    own = rows // 2
    crossing = (mine_ref.shape[0] - depth) // own
    sums = (mine_ref[crossing * own :] + other_ref[crossing * own :]).T[:rows]
    scaled = []
    for bit in range(crossing):
        here = slice(bit * own, (bit + 1) * own)
        low_rows = chosen(core, other_ref[here], mine_ref[here])
        high_rows = chosen(core, mine_ref[here], other_ref[here])
        scaled.append(jnp.concatenate([low_rows, high_rows], axis=0) * (1.0 / (width * (2 << bit))))
    one = [local_ref[:, part * LANES : (part + 1) * LANES] * (1.0 / (2 * LEAF)) for part in range(2)]
    two = local_ref[:, 2 * LANES :] * (1.0 / (4 * LEAF))
    return sums, [stacked(jnp.concatenate([one[part], two] + scaled, axis=1)) for part in range(2)]


def own_rows(core, column, crossing):
    own = column.shape[0] // 2
    return jnp.concatenate([chosen(core, column[own:], column[:own])] * crossing, axis=0)


def residual_up_kernel(first, siblings, *refs):
    core_ref, high_ref, low_ref, near_ref, mine_ref, other_ref, local_ref = refs[:7]
    refs = refs[7:]
    if first:
        image_ref, state_ref, send_ref = refs
        q_ref = image_ref
    else:
        field_ref, old_d_ref, old_q_ref, old_skel_ref, old_local_ref, old_state_ref = refs[:6]
        r_siblings = refs[6 : 6 + siblings]
        d_siblings = refs[6 + siblings : 6 + 2 * siblings]
        refs = refs[6 + 2 * siblings :]
        image_ref, state_ref, send_ref, d_ref, q_ref, skel_ref, new_local_ref = refs[:7]
        new_siblings = refs[7:]
    core = core_ref[0]
    rows, width = near_ref.shape
    half = width // 2
    sums, stacks = up_parts(core, mine_ref, other_ref, local_ref, rows, width, NORM_TILE)
    norm = sums[:, 0:1]
    state_ref[...] = in_lanes([norm], (rows, LANES))
    ratio = None if first else norm / old_state_ref[:, 0:1]
    for part in range(2):
        points = slice(part * half, (part + 1) * half)
        image = near_ref[:, points] + product(stacks[part], high_ref[:, points], low_ref[:, points], ROWS_COLS)
        image_ref[:, points] = image
        if not first:
            d_ref[:, points] = field_ref[:, points] + ratio * old_d_ref[:, points]
            q_ref[:, points] = image + ratio * old_q_ref[:, points]
    send_ref[...] = sides(core, q_ref)[1]
    if not first:
        rows_in = skel_ref.shape[0]
        crossing = rows_in // (rows // 2)
        skel_ref[...] = mine_ref[:rows_in] + own_rows(core, ratio, crossing) * old_skel_ref[...]
        new_local_ref[...] = local_ref[...] + ratio * old_local_ref[...]
        own_ratio = own_rows(core, ratio, 1)
        for new_ref, r_ref, d_ref in zip(new_siblings, r_siblings, d_siblings):
            new_ref[...] = r_ref[...] + own_ratio * d_ref[...]


def image_up_kernel(first, last, siblings, *refs):
    core_ref, high_ref, low_ref, near_ref, mine_ref, other_ref, local_ref = refs[:7]
    r_ref, w_ref, d_ref, q_ref, state_ref = refs[7:12]
    refs = refs[12:]
    if not first:
        solution_ref = refs[0]
        refs = refs[1:]
    if not last:
        r_skel_ref, d_skel_ref, r_local_ref, d_local_ref = refs[:4]
        r_siblings, q_siblings, d_siblings = [
            refs[4 + index * siblings : 4 + (index + 1) * siblings] for index in range(3)
        ]
        refs = refs[4 + 3 * siblings :]
    new_solution_ref, new_r_ref = refs[:2]
    if not last:
        new_d_ref, new_q_ref, new_skel_ref, new_local_ref, new_state_ref, send_ref = refs[2:8]
        new_siblings = refs[8:]
    core = core_ref[0]
    rows, width = near_ref.shape
    half = width // 2
    sums, stacks = up_parts(core, mine_ref, other_ref, local_ref, rows, width, PRODUCTS_TILE)
    dot = {pair: sums[:, index : index + 1] for index, pair in enumerate(PAIRS)}
    norm = state_ref[:, 0:1]
    step = norm / dot["dq"]
    new_norm = norm - step * (2.0 * dot["rq"] - step * dot["qq"])
    ratio = new_norm / norm
    curve = dot["rw"] - step * (dot["qw"] + dot["rz"] - step * dot["qz"])
    curve = curve + ratio * (dot["dw"] - step * dot["dz"] + dot["rq"] - step * dot["qq"] + ratio * dot["dq"])
    new_step = new_norm / curve
    for part in range(2):
        points = slice(part * half, (part + 1) * half)
        image = near_ref[:, points] + product(stacks[part], high_ref[:, points], low_ref[:, points], ROWS_COLS)
        d = d_ref[:, points]
        q = q_ref[:, points]
        r = r_ref[:, points] - step * q
        new_q = w_ref[:, points] - step * image + ratio * q
        new_d = r + ratio * d
        moved = step * d + new_step * new_d
        new_solution_ref[:, points] = moved if first else solution_ref[:, points] + moved
        new_r_ref[:, points] = r - new_step * new_q
        if not last:
            new_d_ref[:, points] = new_d
            new_q_ref[:, points] = new_q
    if not last:
        rows_in = new_skel_ref.shape[0]
        crossing = rows_in // (rows // 2)
        r_skel = r_skel_ref[:rows_in] - own_rows(core, step, crossing) * mine_ref[:rows_in]
        new_skel_ref[...] = r_skel + own_rows(core, ratio, crossing) * d_skel_ref[:rows_in]
        new_local_ref[...] = r_local_ref[...] - step * local_ref[...] + ratio * d_local_ref[...]
        own_step, own_ratio = own_rows(core, step, 1), own_rows(core, ratio, 1)
        for new_ref, r_ref, q_ref, d_ref in zip(new_siblings, r_siblings, q_siblings, d_siblings):
            new_ref[...] = r_ref[...] - own_step * q_ref[...] + own_ratio * d_ref[...]
        new_state_ref[...] = in_lanes([new_norm], (rows, LANES))
        send_ref[...] = sides(core, new_r_ref)[1]


def per_device(rhs, coords, nugget, near_ids, basis):
    rows, width = rhs.shape
    levels = basis.shape[0]
    leaves = width // LEAF
    own = rows // 2
    crossing = levels - (leaves.bit_length() - 1)
    devices = lax.axis_size("row") * lax.axis_size("col")
    place = jnp.reshape(lax.axis_index(BOTH), (1,))
    core = place % 2
    nugget = nugget[None, :]
    weights = leaf_weights(near_ids, place[0] * leaves)

    stages = [list(range(bit, min(bit + 2, crossing))) for bit in range(1, crossing, 2)]
    siblings = sum(len(bits) == 2 for bits in stages)

    def swap(value, mask):
        return lax.ppermute(value, BOTH, [(source, source ^ mask) for source in range(devices)])

    def halo(other):
        outward = [(index, index + 1) for index in range(1, devices - 1, 2)]
        ends = [(0, 0), (devices - 1, devices - 1)]
        return lax.ppermute(other, BOTH, outward + [(target, source) for source, target in outward] + ends)

    def down(field, *tile):
        shapes = [f32(rows, LOCAL * LANES), f32(crossing * own, LANES)]
        shapes = shapes + [f32(EDGE_BLOCKS * rows + crossing * own, LANES)] + list(tile)
        return call(down_kernel, shapes, core, field, high, low, scalars=1, flops=FLOPS)

    def inner(half, field):
        args = [weights, field, nugget, *diagonal[half], *beside]
        body = functools.partial(inner_kernel, half)
        return call(body, [f32(rows, width // 2)], *args, flops=FLOPS // 2)[0]

    def edge(paired, other, front, back, *more):
        shapes = [f32(rows, width)] + ([f32(PRODUCTS_TILE, LANES)] if more else [])
        args = [core, weights, paired, other, *outside, front, back, *more]
        return call(functools.partial(edge_kernel, bool(more)), shapes, *args, scalars=1, flops=FLOPS // 3)

    def chain(products, final, keep, got, tile, beside_steps, r_skel=None, d_skel=None, r_sib=(), d_sib=()):
        depth = PRODUCTS_TILE if products else NORM_TILE
        results = []
        both = [r_skel, d_skel] if products else []
        message, level = call(
            functools.partial(first_combine_kernel, products, 2 * width),
            [f32((crossing - 1) * own + depth, LANES), f32(own, LANES)],
            core,
            keep,
            got,
            tile,
            *both,
            scalars=1,
        )
        done, kept = [level], []
        for index in range(len(stages) + 1):
            bits = stages[index] if index < len(stages) else []
            masks = [sum(1 << bit for at, bit in enumerate(bits) if pick >> at & 1) for pick in range(1, 2 ** len(bits))]
            got = [swap(message, mask) for mask in masks or [1]]
            if index < len(beside_steps):
                *got, result = lax.optimization_barrier((*got, beside_steps[index](message)))
                results.append(result)
            if not bits:
                break
            left = crossing - bits[-1] - 1
            paired = len(bits) == 2
            args = [core, message, *got, *both]
            if products and paired:
                args = args + [r_sib[index], d_sib[index]]
            sibling = paired and not final
            clusters = [width * (2 << bit) for bit in bits]
            message, *levels_out = call(
                functools.partial(combine_kernel, products, not left, sibling, own, bits, clusters),
                [f32((left or crossing) * own + depth, LANES)] + [f32(own, LANES)] * ((len(bits) if left else 0) + sibling),
                *args,
                *([] if left else done),
                scalars=1,
            )
            kept = kept + levels_out[len(levels_out) - sibling :]
            done = done + levels_out[: len(levels_out) - sibling]
        return message, got[0], results, kept

    paired_coords, other = call(
        edges_kernel, [f32(8, LEAF), f32(rows + 8, LEAF)], core, rhs, coords, scalars=1
    )
    other = halo(other)
    paired_coords = swap(paired_coords, 1)
    half = leaves // 2
    pairs = [(leaf, leaf) for leaf in range(half)]
    *front_diagonal, high, low, turned = pl.pallas_call(
        functools.partial(setup_kernel, pairs),
        out_shape=[bf16(half, LEAF, LEAF)] * 2
        + [pltpu.VMEM((levels * LANES, width), jnp.bfloat16)] * 2
        + [f32(width, 8)],
        in_specs=[whole(), whole(pltpu.HBM)],
        out_specs=[whole()] * 5,
        scratch_shapes=[pltpu.VMEM(basis.shape, jnp.float32), pltpu.SemaphoreType.DMA((levels,))],
        compiler_params=pltpu.CompilerParams(vmem_limit_bytes=44 * 2**20),
        cost_estimate=pl.CostEstimate(flops=FLOPS, bytes_accessed=2**20, transcendentals=0),
    )(coords, basis)
    diagonal = [front_diagonal, None]
    beside = outside = None

    def after(message, *values):
        return lax.optimization_barrier((message, *values))[1:]

    def late_matrices(message):
        groups = [[(leaf, leaf) for leaf in range(half, leaves)], [(leaf, leaf + 1) for leaf in range(leaves - 1)]]

        def body(lane_ref, sub_ref, *refs):
            for index, group in enumerate(groups):
                fill_matrices(group, lane_ref, sub_ref, *refs[2 * index : 2 * index + 2])

        shapes = [bf16(len(group), LEAF, LEAF) for group in groups for _ in range(2)]
        return call(body, shapes, *after(message, coords, turned), flops=2 * FLOPS)

    def late_edge_matrices(message):
        def body(core_ref, *refs):
            edge_matrices(core_ref, rows, *refs)

        args = after(message, turned, paired_coords, other)
        return call(body, [bf16(2, LEAF, LEAF)] * 2, core, *args, scalars=1, flops=FLOPS)

    solution, r, carried = None, rhs, None
    for step in range(0, ITERS, 2):
        first, last = step == 0, step + 2 == ITERS
        r_local, keep, part, tile = down(r, f32(NORM_TILE, LANES))
        from_core = got = swap(part, 1)
        if first:
            message, got, results, r_sib = chain(False, False, keep, got, tile, [late_matrices, late_edge_matrices])
            diagonal[1], beside = results[0][:2], results[0][2:]
            outside = results[1]
            (near,) = edge(from_core, other, inner(0, r), inner(1, r))
        else:
            fronts = []

            def inner_work(message):
                fronts.extend(inner(half, *after(message, r)) for half in range(2))
                return fronts

            def edge_work(message):
                return edge(from_core, other, *after(message, *fronts))[0]

            message, got, results, r_sib = chain(False, False, keep, got, tile, [inner_work, edge_work])
            near = results[1]
        args = [core, high, low, near, message, got, r_local]
        outs = [f32(rows, width), f32(rows, LANES), f32(rows, LEAF)]
        if first:
            w, state, other = call(
                functools.partial(residual_up_kernel, True, 0), outs, *args, scalars=1, flops=FLOPS // 2
            )
            d, q, d_skel, d_local, d_sib = r, w, message, r_local, r_sib
        else:
            outs = outs + [f32(rows, width)] * 2 + [f32(crossing * own, LANES), f32(rows, LOCAL * LANES)]
            outs = outs + [f32(own, LANES)] * siblings
            body = functools.partial(residual_up_kernel, False, siblings)
            args = args + [r, *carried, *r_sib, *d_sib]
            w, state, other, d, q, d_skel, d_local, *d_sib = call(
                body, outs, *args, scalars=1, flops=FLOPS // 2
            )
        r_skel = message
        other = halo(other)
        q_local, keep, part = down(q)
        got = swap(part, 1)
        near, tile = edge(got, other, inner(0, q), inner(1, q), r, q, d, w, r_local, q_local, d_local)
        message, got, _, q_sib = chain(True, last, keep, got, tile, [], r_skel, d_skel, r_sib, d_sib)
        args = [core, high, low, near, message, got, q_local, r, w, d, q, state]
        args = args + ([] if first else [solution]) + ([] if last else [r_skel, d_skel, r_local, d_local, *r_sib, *q_sib, *d_sib])
        outs = [f32(rows, width)] * 2
        if not last:
            outs = outs + [f32(rows, width)] * 2 + [f32(crossing * own, LANES), f32(rows, LOCAL * LANES)]
            outs = outs + [f32(rows, LANES), f32(rows, LEAF)] + [f32(own, LANES)] * siblings
        solution, r, *rest = call(
            functools.partial(image_up_kernel, first, last, siblings), outs, *args, scalars=1, flops=FLOPS // 2
        )
        if not last:
            carried = rest[:5]
            other = halo(rest[5])
            d_sib = rest[6:]
    return (solution, r)


def solution(mesh):
    placed = (
        P(None, BOTH),
        P(None, BOTH),
        P(BOTH),
        P(BOTH, None),
        P(None, None, BOTH),
    )
    return jax.shard_map(
        per_device,
        mesh=mesh,
        in_specs=placed,
        out_specs=(P(None, BOTH), P(None, BOTH)),
        check_vma=False,
    )
```

```python
import functools

import jax
import jax.numpy as jnp
from jax import lax
from jax.experimental import pallas as pl
from jax.experimental.pallas import tpu as pltpu
from jax.sharding import PartitionSpec as P

LEAF = 512
ITERS = 4
WIN = 3
LANES = 128
LOCAL = 3
EDGE_BLOCKS = LEAF // LANES
CHUNK = 16
NORM_TILE = 8
PRODUCTS_TILE = 16
FLOPS = 0

root_three = 1.7320508075688772
spacing_factor = 1.6
matern_scale = root_three / (spacing_factor * LEAF ** (-1.0 / 3.0))

BOTH = ("row", "col")
ROWS_COLS = (((1,), (0,)), ((), ()))
ROWS_ROWS = (((1,), (1,)), ((), ()))

PAIRS = ("dq", "rq", "qq", "rw", "qw", "dw", "rz", "qz", "dz")


def halves(values):
    high = values.astype(jnp.bfloat16)
    low = (values - high.astype(jnp.float32)).astype(jnp.bfloat16)
    return high, low


def stacked(values):
    return jnp.concatenate(halves(values), axis=0)


def product(stack, high, low, dims):
    rows = stack.shape[0] // 2
    main = lax.dot_general(stack, high, dims, preferred_element_type=jnp.float32)
    rest = lax.dot_general(stack[:rows], low, dims, preferred_element_type=jnp.float32)
    return main[:rows] + (main[rows:] + rest)


def row_sum(values):
    return jnp.sum(values, axis=1, keepdims=True)


def in_lanes(columns, shape):
    lane = lax.broadcasted_iota(jnp.int32, shape, 1)
    block = jnp.zeros(shape, jnp.float32)
    for index, column in enumerate(columns):
        block = jnp.where(lane == index, column, block)
    return block


def sums_tile(columns, rows, depth):
    turned = in_lanes(columns, (rows, LANES)).T[:depth]
    return jnp.concatenate([turned, jnp.zeros((depth, LANES - rows), jnp.float32)], axis=1)


def level_terms(core, columns, rows, depth):
    twice = [jnp.concatenate([column, column], axis=0) for column in columns]
    zero = jnp.zeros((rows, 1), jnp.float32)
    tile = sums_tile([zero] * (len(PAIRS) - len(columns)) + twice, rows, depth)
    lane = lax.broadcasted_iota(jnp.int32, tile.shape, 1)
    return jnp.where(lane // (rows // 2) == core, tile, 0.0)


def chosen(core, odd, even):
    return jnp.where(core == 1, odd, even)


def whole(memory=pltpu.VMEM):
    return pl.BlockSpec(memory_space=memory)


def call(body, outs, *args, scalars=0, flops=0, limit=32):
    return pl.pallas_call(
        body,
        out_shape=outs,
        in_specs=[whole(pltpu.SMEM)] * scalars + [whole()] * (len(args) - scalars),
        out_specs=[whole()] * len(outs),
        compiler_params=pltpu.CompilerParams(vmem_limit_bytes=limit * 2**20),
        cost_estimate=pl.CostEstimate(flops=flops, bytes_accessed=2**20, transcendentals=0),
    )(*args)


def f32(*shape):
    return jax.ShapeDtypeStruct(shape, jnp.float32)


def bf16(*shape):
    return jax.ShapeDtypeStruct(shape, jnp.bfloat16)


def matrix_rows(rows, lanes):
    square = None
    for axis in range(3):
        spread = rows[:, axis : axis + 1] - lanes[axis : axis + 1]
        square = spread * spread if square is None else square + spread * spread
    scaled = square * lax.rsqrt(jnp.maximum(square, 1e-30))
    return halves((1.0 + scaled) * jnp.exp(-scaled))


def fill_matrices(pairs, lane_ref, sub_ref, high_ref, low_ref):
    for matrix, (row_leaf, col_leaf) in enumerate(pairs):
        lanes = lane_ref[:, col_leaf * LEAF : (col_leaf + 1) * LEAF]

        def one(part, carry):
            row_at = pl.multiple_of(row_leaf * LEAF + part * CHUNK, CHUNK)
            out_at = pl.ds(pl.multiple_of(part * CHUNK, CHUNK), CHUNK)
            values = matrix_rows(sub_ref[pl.ds(row_at, CHUNK)], lanes)
            high_ref[matrix, out_at], low_ref[matrix, out_at] = values
            return carry

        lax.fori_loop(0, LEAF // CHUNK, one, 0, unroll=4)


def setup_kernel(pairs, lane_ref, basis_ref, high_ref, low_ref, basis_high_ref, basis_low_ref, sub_ref, raw_ref, sem_ref):
    levels, rank, _ = basis_ref.shape
    copies = [pltpu.make_async_copy(basis_ref.at[at], raw_ref.at[at], sem_ref.at[at]) for at in range(levels)]
    for copy in copies:
        copy.start()
    lanes = lane_ref[...]
    sub_ref[...] = jnp.concatenate([lanes, jnp.zeros((8 - lanes.shape[0], lanes.shape[1]), jnp.float32)], axis=0).T
    fill_matrices(pairs, lane_ref, sub_ref, high_ref, low_ref)
    for at, copy in enumerate(copies):
        copy.wait()
        here = slice(at * rank, (at + 1) * rank)
        basis_high_ref[here], basis_low_ref[here] = halves(raw_ref[at])


def edge_matrices(core_ref, rows, sub_ref, paired_ref, other_ref, high_ref, low_ref):
    core = core_ref[0]
    leaves = sub_ref.shape[0] // LEAF
    paired = paired_ref[:3]
    other = other_ref[rows : rows + 3]
    lanes = [chosen(core, paired, other), chosen(core, other, paired)]

    for side in range(2):
        first_row = side * (leaves - 1) * LEAF

        def one(part, carry):
            row_at = pl.multiple_of(first_row + part * CHUNK, CHUNK)
            out_at = pl.ds(pl.multiple_of(part * CHUNK, CHUNK), CHUNK)
            values = matrix_rows(sub_ref[pl.ds(row_at, CHUNK)], lanes[side])
            high_ref[side, out_at], low_ref[side, out_at] = values
            return carry

        lax.fori_loop(0, LEAF // CHUNK, one, 0, unroll=4)


def sides(core, field_ref):
    head = field_ref[:, :LEAF]
    tail = field_ref[:, field_ref.shape[1] - LEAF :]
    return chosen(core, head, tail), chosen(core, tail, head)


def edges_kernel(core_ref, field_ref, coords_ref, paired_ref, other_ref):
    core = core_ref[0]
    pad = jnp.zeros((8 - 3, LEAF), jnp.float32)
    paired, other = sides(core, coords_ref)
    paired_ref[...] = jnp.concatenate([paired, pad], axis=0)
    other_ref[...] = jnp.concatenate([sides(core, field_ref)[1], other, pad], axis=0)


def down_kernel(core_ref, field_ref, high_ref, low_ref, local_ref, keep_ref, send_ref, *tile_refs):
    core = core_ref[0]
    rank = LANES
    rows, width = field_ref.shape
    half = width // 2
    stack = stacked(field_ref[...])
    for part in range(2):
        points = slice(part * half, (part + 1) * half)
        local_ref[:, part * rank : (part + 1) * rank] = product(
            stack[:, points], high_ref[:rank, points], low_ref[:rank, points], ROWS_ROWS
        )
    all_points = product(stack, high_ref[rank:], low_ref[rank:], ROWS_ROWS)
    local_ref[:, 2 * rank :] = all_points[:, :rank]
    own = rows // 2
    for bit in range(all_points.shape[1] // rank - 1):
        block = all_points[:, (bit + 1) * rank : (bit + 2) * rank]
        keep_ref[bit * own : (bit + 1) * own] = chosen(core, block[own:], block[:own])
        at = EDGE_BLOCKS * rows + bit * own
        send_ref[at : at + own] = chosen(core, block[:own], block[own:])
    paired = sides(core, field_ref)[0]
    for block in range(EDGE_BLOCKS):
        send_ref[block * rows : (block + 1) * rows] = paired[:, block * LANES : (block + 1) * LANES]
    for ref in tile_refs:
        ref[...] = sums_tile([row_sum(field_ref[...] * field_ref[...])], rows, NORM_TILE)


def leaf_of(ref, leaf):
    return ref[:, leaf * LEAF : (leaf + 1) * LEAF]


def weight_of(weights_ref, leaf, offset):
    at = WIN * leaf + offset + 1
    return weights_ref[at : at + 1]


def leaf_weights(near_ids, first_leaf):
    target = first_leaf + jnp.arange(near_ids.shape[0])[:, None] + jnp.arange(WIN)[None, :] - 1
    found = jnp.any(near_ids[:, None, :] == target[:, :, None], axis=2) & (target >= 0)
    weights = jnp.where(found, 1.0 / (16 * WIN), 0.0).astype(jnp.float32)
    return jnp.broadcast_to(weights.reshape(-1, 1), (weights.size, LEAF))


def inner_kernel(half, weights_ref, field_ref, nugget_ref, high_ref, low_ref, pair_high_ref, pair_low_ref, out_ref):
    leaves = weights_ref.shape[0] // WIN
    start = half * (leaves // 2)
    stop = start + leaves // 2
    pieces = {leaf: stacked(leaf_of(field_ref, leaf)) for leaf in range(max(start - 1, 0), min(stop + 1, leaves))}
    for leaf in range(start, stop):
        at = leaf - start
        inside = product(pieces[leaf], high_ref[at], low_ref[at], ROWS_COLS)
        total = leaf_of(nugget_ref, leaf) * leaf_of(field_ref, leaf) + weight_of(weights_ref, leaf, 0) * inside
        if leaf > 0:
            before = product(pieces[leaf - 1], pair_high_ref[leaf - 1], pair_low_ref[leaf - 1], ROWS_COLS)
            total = total + weight_of(weights_ref, leaf, -1) * before
        if leaf < leaves - 1:
            after = product(pieces[leaf + 1], pair_high_ref[leaf], pair_low_ref[leaf], ROWS_ROWS)
            total = total + weight_of(weights_ref, leaf, 1) * after
        out_ref[:, at * LEAF : (at + 1) * LEAF] = total


def edge_kernel(sums, *refs):
    core_ref, weights_ref, paired_ref, other_ref, high_ref, low_ref, front_ref, back_ref = refs[:8]
    refs = refs[8:]
    out_ref = refs[-2] if sums else refs[-1]
    core = core_ref[0]
    rows, width = out_ref.shape
    leaves = width // LEAF
    paired = [paired_ref[block * rows : (block + 1) * rows] for block in range(EDGE_BLOCKS)]
    paired = jnp.concatenate(paired, axis=1)
    before = chosen(core, paired, other_ref[:rows])
    after = chosen(core, other_ref[:rows], paired)
    out_ref[:, : width // 2] = front_ref[...]
    out_ref[:, width // 2 :] = back_ref[...]
    part = product(stacked(before), high_ref[0], low_ref[0], ROWS_ROWS)
    out_ref[:, :LEAF] += weight_of(weights_ref, 0, -1) * part
    part = product(stacked(after), high_ref[1], low_ref[1], ROWS_ROWS)
    out_ref[:, width - LEAF :] += weight_of(weights_ref, leaves - 1, 1) * part
    if not sums:
        return
    fields = dict(zip("rqdw", refs[:4]))
    locals_ = dict(zip("rqd", refs[4:7]))
    tile_ref = refs[-1]
    totals = {pair: jnp.zeros((rows, 1), jnp.float32) for pair in PAIRS}
    for leaf in range(leaves):
        here = {name: leaf_of(ref, leaf) for name, ref in fields.items()}
        here["z"] = leaf_of(out_ref, leaf)
        for left, right in PAIRS:
            totals[left + right] = totals[left + right] + row_sum(here[left] * here[right])
    for block in range(LOCAL):
        scale = 1.0 / (LEAF * (2 if block < 2 else 4))
        lanes = slice(block * LANES, (block + 1) * LANES)
        for name in "rqd":
            term = row_sum(locals_[name][:, lanes] * locals_["q"][:, lanes])
            totals[name + "z"] = totals[name + "z"] + scale * term
    tile_ref[...] = sums_tile([totals[pair] for pair in PAIRS], rows, PRODUCTS_TILE)


def first_combine_kernel(products, cluster, *refs):
    core_ref, mine_ref, other_ref, tile_ref = refs[:4]
    message_ref, level_ref = refs[-2:]
    own = level_ref.shape[0]
    depth = tile_ref.shape[0]
    total = mine_ref[...] + other_ref[EDGE_BLOCKS * 2 * own :]
    level = total[:own]
    level_ref[...] = level
    tile = tile_ref[...]
    if products:
        partners = [refs[4][:own], level, refs[5][:own]]
        columns = [row_sum(level * partner) * (1.0 / cluster) for partner in partners]
        tile = tile + level_terms(core_ref[0], columns, 2 * own, depth)
    left = total.shape[0] - own
    message_ref[:left] = total[own:]
    message_ref[left:] = tile


def combine_kernel(products, last, sibling, own, bits, clusters, *refs):
    refs = list(refs)
    core_ref, mine_ref = refs[:2]
    got = [ref[...] for ref in refs[2 : 2 + 2 ** len(bits) - 1]]
    refs = refs[1 + 2 ** len(bits) :]
    sibling_ref = refs.pop() if sibling else None
    level_out = [] if last else [refs.pop() for _ in bits][::-1]
    next_ref = refs.pop()
    depth = PRODUCTS_TILE if products else NORM_TILE
    near = mine_ref[...] + got[0]
    total = near
    pairs = [(near[:own], bits[0], 0, clusters[0])]
    if len(bits) == 2:
        far = got[1] + got[2]
        total = near + far
        if sibling:
            sibling_ref[...] = far[:own]
        pairs.append((far[:own], None, 1, clusters[0]))
        pairs.append((total[own : 2 * own], bits[1], 0, clusters[1]))
    for ref, pair in zip(level_out, pairs[:: 2 if len(bits) == 2 else 1]):
        ref[...] = pair[0]
    tile = total[total.shape[0] - depth :]
    if products:
        r_ref, d_ref = refs[:2]
        refs = refs[2:]
        siblings = [refs.pop(0), refs.pop(0)] if len(bits) == 2 else []
        columns = [jnp.zeros((own, 1), jnp.float32)] * 3
        for level, bit, kind, cluster in pairs:
            if kind:
                partners = [siblings[0][...], level, siblings[1][...]]
            else:
                here = slice(bit * own, (bit + 1) * own)
                partners = [r_ref[here], level, d_ref[here]]
            terms = [row_sum(level * partner) * (1.0 / cluster) for partner in partners]
            columns = [column + term for column, term in zip(columns, terms)]
        tile = tile + level_terms(core_ref[0], columns, 2 * own, depth)
    left = total.shape[0] - depth - len(bits) * own
    if not last:
        next_ref[:left] = total[len(bits) * own : len(bits) * own + left]
        next_ref[left:] = tile
    else:
        for index, ref in enumerate(refs):
            next_ref[index * own : (index + 1) * own] = ref[...]
        for bit, pair in zip(bits, pairs[:: 2 if len(bits) == 2 else 1]):
            next_ref[bit * own : (bit + 1) * own] = pair[0]
        next_ref[next_ref.shape[0] - depth :] = tile


def up_parts(core, mine_ref, other_ref, local_ref, rows, width, depth):
    own = rows // 2
    crossing = (mine_ref.shape[0] - depth) // own
    sums = (mine_ref[crossing * own :] + other_ref[crossing * own :]).T[:rows]
    scaled = []
    for bit in range(crossing):
        here = slice(bit * own, (bit + 1) * own)
        low_rows = chosen(core, other_ref[here], mine_ref[here])
        high_rows = chosen(core, mine_ref[here], other_ref[here])
        scaled.append(jnp.concatenate([low_rows, high_rows], axis=0) * (1.0 / (width * (2 << bit))))
    one = [local_ref[:, part * LANES : (part + 1) * LANES] * (1.0 / (2 * LEAF)) for part in range(2)]
    two = local_ref[:, 2 * LANES :] * (1.0 / (4 * LEAF))
    return sums, [stacked(jnp.concatenate([one[part], two] + scaled, axis=1)) for part in range(2)]


def own_rows(core, column, crossing):
    own = column.shape[0] // 2
    return jnp.concatenate([chosen(core, column[own:], column[:own])] * crossing, axis=0)


def residual_up_kernel(first, siblings, *refs):
    core_ref, high_ref, low_ref, near_ref, mine_ref, other_ref, local_ref = refs[:7]
    refs = refs[7:]
    if first:
        image_ref, state_ref, send_ref = refs
        q_ref = image_ref
    else:
        field_ref, old_d_ref, old_q_ref, old_skel_ref, old_local_ref, old_state_ref = refs[:6]
        r_siblings = refs[6 : 6 + siblings]
        d_siblings = refs[6 + siblings : 6 + 2 * siblings]
        refs = refs[6 + 2 * siblings :]
        image_ref, state_ref, send_ref, d_ref, q_ref, skel_ref, new_local_ref = refs[:7]
        new_siblings = refs[7:]
    core = core_ref[0]
    rows, width = near_ref.shape
    half = width // 2
    sums, stacks = up_parts(core, mine_ref, other_ref, local_ref, rows, width, NORM_TILE)
    norm = sums[:, 0:1]
    state_ref[...] = in_lanes([norm], (rows, LANES))
    ratio = None if first else norm / old_state_ref[:, 0:1]
    for part in range(2):
        points = slice(part * half, (part + 1) * half)
        image = near_ref[:, points] + product(stacks[part], high_ref[:, points], low_ref[:, points], ROWS_COLS)
        image_ref[:, points] = image
        if not first:
            d_ref[:, points] = field_ref[:, points] + ratio * old_d_ref[:, points]
            q_ref[:, points] = image + ratio * old_q_ref[:, points]
    send_ref[...] = sides(core, q_ref)[1]
    if not first:
        rows_in = skel_ref.shape[0]
        crossing = rows_in // (rows // 2)
        skel_ref[...] = mine_ref[:rows_in] + own_rows(core, ratio, crossing) * old_skel_ref[...]
        new_local_ref[...] = local_ref[...] + ratio * old_local_ref[...]
        own_ratio = own_rows(core, ratio, 1)
        for new_ref, r_ref, d_ref in zip(new_siblings, r_siblings, d_siblings):
            new_ref[...] = r_ref[...] + own_ratio * d_ref[...]


def image_up_kernel(first, last, siblings, *refs):
    core_ref, high_ref, low_ref, near_ref, mine_ref, other_ref, local_ref = refs[:7]
    r_ref, w_ref, d_ref, q_ref, state_ref = refs[7:12]
    refs = refs[12:]
    if not first:
        solution_ref = refs[0]
        refs = refs[1:]
    if not last:
        r_skel_ref, d_skel_ref, r_local_ref, d_local_ref = refs[:4]
        r_siblings, q_siblings, d_siblings = [
            refs[4 + index * siblings : 4 + (index + 1) * siblings] for index in range(3)
        ]
        refs = refs[4 + 3 * siblings :]
    new_solution_ref, new_r_ref = refs[:2]
    if not last:
        new_d_ref, new_q_ref, new_skel_ref, new_local_ref, new_state_ref, send_ref = refs[2:8]
        new_siblings = refs[8:]
    core = core_ref[0]
    rows, width = near_ref.shape
    half = width // 2
    sums, stacks = up_parts(core, mine_ref, other_ref, local_ref, rows, width, PRODUCTS_TILE)
    dot = {pair: sums[:, index : index + 1] for index, pair in enumerate(PAIRS)}
    norm = state_ref[:, 0:1]
    step = norm / dot["dq"]
    new_norm = norm - step * (2.0 * dot["rq"] - step * dot["qq"])
    ratio = new_norm / norm
    curve = dot["rw"] - step * (dot["qw"] + dot["rz"] - step * dot["qz"])
    curve = curve + ratio * (dot["dw"] - step * dot["dz"] + dot["rq"] - step * dot["qq"] + ratio * dot["dq"])
    new_step = new_norm / curve
    for part in range(2):
        points = slice(part * half, (part + 1) * half)
        image = near_ref[:, points] + product(stacks[part], high_ref[:, points], low_ref[:, points], ROWS_COLS)
        d = d_ref[:, points]
        q = q_ref[:, points]
        r = r_ref[:, points] - step * q
        new_q = w_ref[:, points] - step * image + ratio * q
        new_d = r + ratio * d
        moved = step * d + new_step * new_d
        new_solution_ref[:, points] = moved if first else solution_ref[:, points] + moved
        new_r_ref[:, points] = r - new_step * new_q
        if not last:
            new_d_ref[:, points] = new_d
            new_q_ref[:, points] = new_q
    if not last:
        rows_in = new_skel_ref.shape[0]
        crossing = rows_in // (rows // 2)
        r_skel = r_skel_ref[:rows_in] - own_rows(core, step, crossing) * mine_ref[:rows_in]
        new_skel_ref[...] = r_skel + own_rows(core, ratio, crossing) * d_skel_ref[:rows_in]
        new_local_ref[...] = r_local_ref[...] - step * local_ref[...] + ratio * d_local_ref[...]
        own_step, own_ratio = own_rows(core, step, 1), own_rows(core, ratio, 1)
        for new_ref, r_ref, q_ref, d_ref in zip(new_siblings, r_siblings, q_siblings, d_siblings):
            new_ref[...] = r_ref[...] - own_step * q_ref[...] + own_ratio * d_ref[...]
        new_state_ref[...] = in_lanes([new_norm], (rows, LANES))
        send_ref[...] = sides(core, new_r_ref)[1]


def per_device(rhs, coords, nugget, near_ids, basis):
    rows, width = rhs.shape
    levels = basis.shape[0]
    leaves = width // LEAF
    own = rows // 2
    crossing = levels - (leaves.bit_length() - 1)
    devices = lax.axis_size("row") * lax.axis_size("col")
    place = jnp.reshape(lax.axis_index(BOTH), (1,))
    core = place % 2
    nugget = nugget[None, :]
    coords = coords * matern_scale
    weights = leaf_weights(near_ids, place[0] * leaves)

    stages = [list(range(bit, min(bit + 2, crossing))) for bit in range(1, crossing, 2)]
    siblings = sum(len(bits) == 2 for bits in stages)

    def swap(value, mask):
        return lax.ppermute(value, BOTH, [(source, source ^ mask) for source in range(devices)])

    def halo(other):
        outward = [(index, index + 1) for index in range(1, devices - 1, 2)]
        ends = [(0, 0), (devices - 1, devices - 1)]
        return lax.ppermute(other, BOTH, outward + [(target, source) for source, target in outward] + ends)

    def down(field, *tile):
        shapes = [f32(rows, LOCAL * LANES), f32(crossing * own, LANES)]
        shapes = shapes + [f32(EDGE_BLOCKS * rows + crossing * own, LANES)] + list(tile)
        return call(down_kernel, shapes, core, field, high, low, scalars=1, flops=FLOPS)

    def inner(half, field):
        args = [weights, field, nugget, *diagonal[half], *beside]
        body = functools.partial(inner_kernel, half)
        return call(body, [f32(rows, width // 2)], *args, flops=FLOPS // 2)[0]

    def edge(paired, other, front, back, *more):
        shapes = [f32(rows, width)] + ([f32(PRODUCTS_TILE, LANES)] if more else [])
        args = [core, weights, paired, other, *outside, front, back, *more]
        return call(functools.partial(edge_kernel, bool(more)), shapes, *args, scalars=1, flops=FLOPS // 3)

    def chain(products, final, keep, got, tile, beside_steps, r_skel=None, d_skel=None, r_sib=(), d_sib=()):
        depth = PRODUCTS_TILE if products else NORM_TILE
        results = []
        both = [r_skel, d_skel] if products else []
        message, level = call(
            functools.partial(first_combine_kernel, products, 2 * width),
            [f32((crossing - 1) * own + depth, LANES), f32(own, LANES)],
            core,
            keep,
            got,
            tile,
            *both,
            scalars=1,
        )
        done, kept = [level], []
        for index in range(len(stages) + 1):
            bits = stages[index] if index < len(stages) else []
            masks = [sum(1 << bit for at, bit in enumerate(bits) if pick >> at & 1) for pick in range(1, 2 ** len(bits))]
            got = [swap(message, mask) for mask in masks or [1]]
            if index < len(beside_steps):
                *got, result = lax.optimization_barrier((*got, beside_steps[index](message)))
                results.append(result)
            if not bits:
                break
            left = crossing - bits[-1] - 1
            paired = len(bits) == 2
            args = [core, message, *got, *both]
            if products and paired:
                args = args + [r_sib[index], d_sib[index]]
            sibling = paired and not final
            clusters = [width * (2 << bit) for bit in bits]
            message, *levels_out = call(
                functools.partial(combine_kernel, products, not left, sibling, own, bits, clusters),
                [f32((left or crossing) * own + depth, LANES)] + [f32(own, LANES)] * ((len(bits) if left else 0) + sibling),
                *args,
                *([] if left else done),
                scalars=1,
            )
            kept = kept + levels_out[len(levels_out) - sibling :]
            done = done + levels_out[: len(levels_out) - sibling]
        return message, got[0], results, kept

    paired_coords, other = call(
        edges_kernel, [f32(8, LEAF), f32(rows + 8, LEAF)], core, rhs, coords, scalars=1
    )
    other = halo(other)
    paired_coords = swap(paired_coords, 1)
    half = leaves // 2
    pairs = [(leaf, leaf) for leaf in range(half)]
    *front_diagonal, high, low, turned = pl.pallas_call(
        functools.partial(setup_kernel, pairs),
        out_shape=[bf16(half, LEAF, LEAF)] * 2
        + [pltpu.VMEM((levels * LANES, width), jnp.bfloat16)] * 2
        + [pltpu.VMEM((width, 8), jnp.float32)],
        in_specs=[whole(), whole(pltpu.HBM)],
        out_specs=[whole()] * 5,
        scratch_shapes=[pltpu.VMEM(basis.shape, jnp.float32), pltpu.SemaphoreType.DMA((levels,))],
        compiler_params=pltpu.CompilerParams(vmem_limit_bytes=44 * 2**20),
        cost_estimate=pl.CostEstimate(flops=FLOPS, bytes_accessed=2**20, transcendentals=0),
    )(coords, basis)
    diagonal = [front_diagonal, None]
    beside = outside = None

    def after(message, *values):
        return lax.optimization_barrier((message, *values))[1:]

    def late_matrices(message):
        groups = [[(leaf, leaf) for leaf in range(half, leaves)], [(leaf, leaf + 1) for leaf in range(leaves - 1)]]

        def body(lane_ref, sub_ref, *refs):
            for index, group in enumerate(groups):
                fill_matrices(group, lane_ref, sub_ref, *refs[2 * index : 2 * index + 2])

        shapes = [bf16(len(group), LEAF, LEAF) for group in groups for _ in range(2)]
        return call(body, shapes, *after(message, coords, turned), flops=2 * FLOPS)

    def late_edge_matrices(message):
        def body(core_ref, *refs):
            edge_matrices(core_ref, rows, *refs)

        args = after(message, turned, paired_coords, other)
        return call(body, [bf16(2, LEAF, LEAF)] * 2, core, *args, scalars=1, flops=FLOPS)

    solution, r, carried = None, rhs, None
    for step in range(0, ITERS, 2):
        first, last = step == 0, step + 2 == ITERS
        r_local, keep, part, tile = down(r, f32(NORM_TILE, LANES))
        from_core = got = swap(part, 1)
        if first:
            message, got, results, r_sib = chain(False, False, keep, got, tile, [late_matrices, late_edge_matrices])
            diagonal[1], beside = results[0][:2], results[0][2:]
            outside = results[1]
            (near,) = edge(from_core, other, inner(0, r), inner(1, r))
        else:
            fronts = []

            def inner_work(message):
                fronts.extend(inner(half, *after(message, r)) for half in range(2))
                return fronts

            def edge_work(message):
                return edge(from_core, other, *after(message, *fronts))[0]

            message, got, results, r_sib = chain(False, False, keep, got, tile, [inner_work, edge_work])
            near = results[1]
        args = [core, high, low, near, message, got, r_local]
        outs = [f32(rows, width), f32(rows, LANES), f32(rows, LEAF)]
        if first:
            w, state, other = call(
                functools.partial(residual_up_kernel, True, 0), outs, *args, scalars=1, flops=FLOPS // 2
            )
            d, q, d_skel, d_local, d_sib = r, w, message, r_local, r_sib
        else:
            outs = outs + [f32(rows, width)] * 2 + [f32(crossing * own, LANES), f32(rows, LOCAL * LANES)]
            outs = outs + [f32(own, LANES)] * siblings
            body = functools.partial(residual_up_kernel, False, siblings)
            args = args + [r, *carried, *r_sib, *d_sib]
            w, state, other, d, q, d_skel, d_local, *d_sib = call(
                body, outs, *args, scalars=1, flops=FLOPS // 2
            )
        r_skel = message
        other = halo(other)
        q_local, keep, part = down(q)
        got = swap(part, 1)
        near, tile = edge(got, other, inner(0, q), inner(1, q), r, q, d, w, r_local, q_local, d_local)
        message, got, _, q_sib = chain(True, last, keep, got, tile, [], r_skel, d_skel, r_sib, d_sib)
        args = [core, high, low, near, message, got, q_local, r, w, d, q, state]
        args = args + ([] if first else [solution]) + ([] if last else [r_skel, d_skel, r_local, d_local, *r_sib, *q_sib, *d_sib])
        outs = [f32(rows, width)] * 2
        if not last:
            outs = outs + [f32(rows, width)] * 2 + [f32(crossing * own, LANES), f32(rows, LOCAL * LANES)]
            outs = outs + [f32(rows, LANES), f32(rows, LEAF)] + [f32(own, LANES)] * siblings
        solution, r, *rest = call(
            functools.partial(image_up_kernel, first, last, siblings), outs, *args, scalars=1, flops=FLOPS // 2
        )
        if not last:
            carried = rest[:5]
            other = halo(rest[5])
            d_sib = rest[6:]
    return (solution, r)


def solution(mesh):
    placed = (
        P(None, BOTH),
        P(None, BOTH),
        P(BOTH),
        P(BOTH, None),
        P(None, None, BOTH),
    )
    return jax.shard_map(
        per_device,
        mesh=mesh,
        in_specs=placed,
        out_specs=(P(None, BOTH), P(None, BOTH)),
        check_vma=False,
    )
```

```python
import functools

import jax
import jax.numpy as jnp
from jax import lax
from jax.experimental import pallas as pl
from jax.experimental.pallas import tpu as pltpu
from jax.sharding import PartitionSpec as P

LEAF = 512
ITERS = 4
WIN = 3
LANES = 128
LOCAL = 3
EDGE_BLOCKS = LEAF // LANES
CHUNK = 16
NORM_TILE = 8
PRODUCTS_TILE = 16
FLOPS = 3 * 10**9

root_three = 1.7320508075688772
spacing_factor = 1.6
matern_scale = root_three / (spacing_factor * LEAF ** (-1.0 / 3.0))

BOTH = ("row", "col")
ROWS_COLS = (((1,), (0,)), ((), ()))
ROWS_ROWS = (((1,), (1,)), ((), ()))

PAIRS = ("dq", "rq", "qq", "rw", "qw", "dw", "rz", "qz", "dz")


def halves(values):
    high = values.astype(jnp.bfloat16)
    low = (values - high.astype(jnp.float32)).astype(jnp.bfloat16)
    return high, low


def stacked(values):
    return jnp.concatenate(halves(values), axis=0)


def product(stack, high, low, dims):
    rows = stack.shape[0] // 2
    main = lax.dot_general(stack, high, dims, preferred_element_type=jnp.float32)
    rest = lax.dot_general(stack[:rows], low, dims, preferred_element_type=jnp.float32)
    return main[:rows] + (main[rows:] + rest)


def row_sum(values):
    return jnp.sum(values, axis=1, keepdims=True)


def in_lanes(columns, shape):
    lane = lax.broadcasted_iota(jnp.int32, shape, 1)
    block = jnp.zeros(shape, jnp.float32)
    for index, column in enumerate(columns):
        block = jnp.where(lane == index, column, block)
    return block


def sums_tile(columns, rows, depth):
    turned = in_lanes(columns, (rows, LANES)).T[:depth]
    return jnp.concatenate([turned, jnp.zeros((depth, LANES - rows), jnp.float32)], axis=1)


def level_terms(core, columns, rows, depth):
    twice = [jnp.concatenate([column, column], axis=0) for column in columns]
    zero = jnp.zeros((rows, 1), jnp.float32)
    tile = sums_tile([zero] * (len(PAIRS) - len(columns)) + twice, rows, depth)
    lane = lax.broadcasted_iota(jnp.int32, tile.shape, 1)
    return jnp.where(lane // (rows // 2) == core, tile, 0.0)


def chosen(core, odd, even):
    return jnp.where(core == 1, odd, even)


def whole(memory=pltpu.VMEM):
    return pl.BlockSpec(memory_space=memory)


def call(body, outs, *args, scalars=0, flops=0, limit=32):
    return pl.pallas_call(
        body,
        out_shape=outs,
        in_specs=[whole(pltpu.SMEM)] * scalars + [whole()] * (len(args) - scalars),
        out_specs=[whole()] * len(outs),
        compiler_params=pltpu.CompilerParams(vmem_limit_bytes=limit * 2**20),
        cost_estimate=pl.CostEstimate(flops=flops, bytes_accessed=2**20, transcendentals=0),
    )(*args)


def f32(*shape):
    return jax.ShapeDtypeStruct(shape, jnp.float32)


def bf16(*shape):
    return jax.ShapeDtypeStruct(shape, jnp.bfloat16)


def matrix_rows(rows, lanes):
    square = None
    for axis in range(3):
        spread = rows[:, axis : axis + 1] - lanes[axis : axis + 1]
        square = spread * spread if square is None else square + spread * spread
    scaled = square * lax.rsqrt(jnp.maximum(square, 1e-30))
    return halves((1.0 + scaled) * jnp.exp(-scaled))


def fill_matrices(pairs, lane_ref, sub_ref, high_ref, low_ref):
    for matrix, (row_leaf, col_leaf) in enumerate(pairs):
        lanes = lane_ref[:, col_leaf * LEAF : (col_leaf + 1) * LEAF] * matern_scale

        def one(part, carry):
            row_at = pl.multiple_of(row_leaf * LEAF + part * CHUNK, CHUNK)
            out_at = pl.ds(pl.multiple_of(part * CHUNK, CHUNK), CHUNK)
            values = matrix_rows(sub_ref[pl.ds(row_at, CHUNK)], lanes)
            high_ref[matrix, out_at], low_ref[matrix, out_at] = values
            return carry

        lax.fori_loop(0, LEAF // CHUNK, one, 0, unroll=4)


def setup_kernel(pairs, lane_ref, basis_ref, high_ref, low_ref, basis_high_ref, basis_low_ref, sub_ref, raw_ref, sem_ref):
    levels, rank, _ = basis_ref.shape
    copies = [pltpu.make_async_copy(basis_ref.at[at], raw_ref.at[at], sem_ref.at[at]) for at in range(levels)]
    for copy in copies:
        copy.start()
    lanes = lane_ref[...] * matern_scale
    sub_ref[...] = jnp.concatenate([lanes, jnp.zeros((8 - lanes.shape[0], lanes.shape[1]), jnp.float32)], axis=0).T
    fill_matrices(pairs, lane_ref, sub_ref, high_ref, low_ref)
    for at, copy in enumerate(copies):
        copy.wait()
        here = slice(at * rank, (at + 1) * rank)
        basis_high_ref[here], basis_low_ref[here] = halves(raw_ref[at])


def edge_matrices(core_ref, rows, sub_ref, paired_ref, other_ref, high_ref, low_ref):
    core = core_ref[0]
    leaves = sub_ref.shape[0] // LEAF
    paired = paired_ref[:3] * matern_scale
    other = other_ref[rows : rows + 3] * matern_scale
    lanes = [chosen(core, paired, other), chosen(core, other, paired)]

    for side in range(2):
        first_row = side * (leaves - 1) * LEAF

        def one(part, carry):
            row_at = pl.multiple_of(first_row + part * CHUNK, CHUNK)
            out_at = pl.ds(pl.multiple_of(part * CHUNK, CHUNK), CHUNK)
            values = matrix_rows(sub_ref[pl.ds(row_at, CHUNK)], lanes[side])
            high_ref[side, out_at], low_ref[side, out_at] = values
            return carry

        lax.fori_loop(0, LEAF // CHUNK, one, 0, unroll=4)


def sides(core, field_ref):
    head = field_ref[:, :LEAF]
    tail = field_ref[:, field_ref.shape[1] - LEAF :]
    return chosen(core, head, tail), chosen(core, tail, head)


def edges_kernel(core_ref, field_ref, coords_ref, paired_ref, other_ref):
    core = core_ref[0]
    pad = jnp.zeros((8 - 3, LEAF), jnp.float32)
    paired, other = sides(core, coords_ref)
    paired_ref[...] = jnp.concatenate([paired, pad], axis=0)
    other_ref[...] = jnp.concatenate([sides(core, field_ref)[1], other, pad], axis=0)


def down_kernel(core_ref, field_ref, high_ref, low_ref, local_ref, keep_ref, send_ref, *tile_refs):
    core = core_ref[0]
    rank = LANES
    rows, width = field_ref.shape
    half = width // 2
    stack = stacked(field_ref[...])
    for part in range(2):
        points = slice(part * half, (part + 1) * half)
        local_ref[:, part * rank : (part + 1) * rank] = product(
            stack[:, points], high_ref[:rank, points], low_ref[:rank, points], ROWS_ROWS
        )
    all_points = product(stack, high_ref[rank:], low_ref[rank:], ROWS_ROWS)
    local_ref[:, 2 * rank :] = all_points[:, :rank]
    own = rows // 2
    for bit in range(all_points.shape[1] // rank - 1):
        block = all_points[:, (bit + 1) * rank : (bit + 2) * rank]
        keep_ref[bit * own : (bit + 1) * own] = chosen(core, block[own:], block[:own])
        at = EDGE_BLOCKS * rows + bit * own
        send_ref[at : at + own] = chosen(core, block[:own], block[own:])
    paired = sides(core, field_ref)[0]
    for block in range(EDGE_BLOCKS):
        send_ref[block * rows : (block + 1) * rows] = paired[:, block * LANES : (block + 1) * LANES]
    for ref in tile_refs:
        ref[...] = sums_tile([row_sum(field_ref[...] * field_ref[...])], rows, NORM_TILE)


def leaf_of(ref, leaf):
    return ref[:, leaf * LEAF : (leaf + 1) * LEAF]


def weight_of(weights_ref, leaf, offset):
    at = WIN * leaf + offset + 1
    return weights_ref[at : at + 1]


def leaf_weights(near_ids, first_leaf):
    target = first_leaf + jnp.arange(near_ids.shape[0])[:, None] + jnp.arange(WIN)[None, :] - 1
    found = jnp.any(near_ids[:, None, :] == target[:, :, None], axis=2) & (target >= 0)
    weights = jnp.where(found, 1.0 / (16 * WIN), 0.0).astype(jnp.float32)
    return jnp.broadcast_to(weights.reshape(-1, 1), (weights.size, LEAF))


def inner_kernel(half, weights_ref, field_ref, nugget_ref, high_ref, low_ref, pair_high_ref, pair_low_ref, out_ref):
    leaves = weights_ref.shape[0] // WIN
    start = half * (leaves // 2)
    stop = start + leaves // 2
    pieces = {leaf: stacked(leaf_of(field_ref, leaf)) for leaf in range(max(start - 1, 0), min(stop + 1, leaves))}
    for leaf in range(start, stop):
        at = leaf - start
        inside = product(pieces[leaf], high_ref[at], low_ref[at], ROWS_COLS)
        total = leaf_of(nugget_ref, leaf) * leaf_of(field_ref, leaf) + weight_of(weights_ref, leaf, 0) * inside
        if leaf > 0:
            before = product(pieces[leaf - 1], pair_high_ref[leaf - 1], pair_low_ref[leaf - 1], ROWS_COLS)
            total = total + weight_of(weights_ref, leaf, -1) * before
        if leaf < leaves - 1:
            after = product(pieces[leaf + 1], pair_high_ref[leaf], pair_low_ref[leaf], ROWS_ROWS)
            total = total + weight_of(weights_ref, leaf, 1) * after
        out_ref[:, at * LEAF : (at + 1) * LEAF] = total


def edge_kernel(sums, *refs):
    core_ref, weights_ref, paired_ref, other_ref, high_ref, low_ref, front_ref, back_ref = refs[:8]
    refs = refs[8:]
    out_ref = refs[-2] if sums else refs[-1]
    core = core_ref[0]
    rows, width = out_ref.shape
    leaves = width // LEAF
    paired = [paired_ref[block * rows : (block + 1) * rows] for block in range(EDGE_BLOCKS)]
    paired = jnp.concatenate(paired, axis=1)
    before = chosen(core, paired, other_ref[:rows])
    after = chosen(core, other_ref[:rows], paired)
    out_ref[:, : width // 2] = front_ref[...]
    out_ref[:, width // 2 :] = back_ref[...]
    part = product(stacked(before), high_ref[0], low_ref[0], ROWS_ROWS)
    out_ref[:, :LEAF] += weight_of(weights_ref, 0, -1) * part
    part = product(stacked(after), high_ref[1], low_ref[1], ROWS_ROWS)
    out_ref[:, width - LEAF :] += weight_of(weights_ref, leaves - 1, 1) * part
    if not sums:
        return
    fields = dict(zip("rqdw", refs[:4]))
    locals_ = dict(zip("rqd", refs[4:7]))
    tile_ref = refs[-1]
    totals = {pair: jnp.zeros((rows, 1), jnp.float32) for pair in PAIRS}
    for leaf in range(leaves):
        here = {name: leaf_of(ref, leaf) for name, ref in fields.items()}
        here["z"] = leaf_of(out_ref, leaf)
        for left, right in PAIRS:
            totals[left + right] = totals[left + right] + row_sum(here[left] * here[right])
    for block in range(LOCAL):
        scale = 1.0 / (LEAF * (2 if block < 2 else 4))
        lanes = slice(block * LANES, (block + 1) * LANES)
        for name in "rqd":
            term = row_sum(locals_[name][:, lanes] * locals_["q"][:, lanes])
            totals[name + "z"] = totals[name + "z"] + scale * term
    tile_ref[...] = sums_tile([totals[pair] for pair in PAIRS], rows, PRODUCTS_TILE)


def first_combine_kernel(products, cluster, *refs):
    core_ref, mine_ref, other_ref, tile_ref = refs[:4]
    message_ref, level_ref = refs[-2:]
    own = level_ref.shape[0]
    depth = tile_ref.shape[0]
    total = mine_ref[...] + other_ref[EDGE_BLOCKS * 2 * own :]
    level = total[:own]
    level_ref[...] = level
    tile = tile_ref[...]
    if products:
        partners = [refs[4][:own], level, refs[5][:own]]
        columns = [row_sum(level * partner) * (1.0 / cluster) for partner in partners]
        tile = tile + level_terms(core_ref[0], columns, 2 * own, depth)
    left = total.shape[0] - own
    message_ref[:left] = total[own:]
    message_ref[left:] = tile


def combine_kernel(products, last, sibling, own, bits, clusters, *refs):
    refs = list(refs)
    core_ref, mine_ref = refs[:2]
    got = [ref[...] for ref in refs[2 : 2 + 2 ** len(bits) - 1]]
    refs = refs[1 + 2 ** len(bits) :]
    sibling_ref = refs.pop() if sibling else None
    level_out = [] if last else [refs.pop() for _ in bits][::-1]
    next_ref = refs.pop()
    depth = PRODUCTS_TILE if products else NORM_TILE
    near = mine_ref[...] + got[0]
    total = near
    pairs = [(near[:own], bits[0], 0, clusters[0])]
    if len(bits) == 2:
        far = got[1] + got[2]
        total = near + far
        if sibling:
            sibling_ref[...] = far[:own]
        pairs.append((far[:own], None, 1, clusters[0]))
        pairs.append((total[own : 2 * own], bits[1], 0, clusters[1]))
    for ref, pair in zip(level_out, pairs[:: 2 if len(bits) == 2 else 1]):
        ref[...] = pair[0]
    tile = total[total.shape[0] - depth :]
    if products:
        r_ref, d_ref = refs[:2]
        refs = refs[2:]
        siblings = [refs.pop(0), refs.pop(0)] if len(bits) == 2 else []
        columns = [jnp.zeros((own, 1), jnp.float32)] * 3
        for level, bit, kind, cluster in pairs:
            if kind:
                partners = [siblings[0][...], level, siblings[1][...]]
            else:
                here = slice(bit * own, (bit + 1) * own)
                partners = [r_ref[here], level, d_ref[here]]
            terms = [row_sum(level * partner) * (1.0 / cluster) for partner in partners]
            columns = [column + term for column, term in zip(columns, terms)]
        tile = tile + level_terms(core_ref[0], columns, 2 * own, depth)
    left = total.shape[0] - depth - len(bits) * own
    if not last:
        next_ref[:left] = total[len(bits) * own : len(bits) * own + left]
        next_ref[left:] = tile
    else:
        for index, ref in enumerate(refs):
            next_ref[index * own : (index + 1) * own] = ref[...]
        for bit, pair in zip(bits, pairs[:: 2 if len(bits) == 2 else 1]):
            next_ref[bit * own : (bit + 1) * own] = pair[0]
        next_ref[next_ref.shape[0] - depth :] = tile


def up_parts(core, mine_ref, other_ref, local_ref, rows, width, depth):
    own = rows // 2
    crossing = (mine_ref.shape[0] - depth) // own
    sums = (mine_ref[crossing * own :] + other_ref[crossing * own :]).T[:rows]
    scaled = []
    for bit in range(crossing):
        here = slice(bit * own, (bit + 1) * own)
        low_rows = chosen(core, other_ref[here], mine_ref[here])
        high_rows = chosen(core, mine_ref[here], other_ref[here])
        scaled.append(jnp.concatenate([low_rows, high_rows], axis=0) * (1.0 / (width * (2 << bit))))
    one = [local_ref[:, part * LANES : (part + 1) * LANES] * (1.0 / (2 * LEAF)) for part in range(2)]
    two = local_ref[:, 2 * LANES :] * (1.0 / (4 * LEAF))
    return sums, [stacked(jnp.concatenate([one[part], two] + scaled, axis=1)) for part in range(2)]


def own_rows(core, column, crossing):
    own = column.shape[0] // 2
    return jnp.concatenate([chosen(core, column[own:], column[:own])] * crossing, axis=0)


def residual_up_kernel(first, siblings, *refs):
    core_ref, high_ref, low_ref, near_ref, mine_ref, other_ref, local_ref = refs[:7]
    refs = refs[7:]
    if first:
        image_ref, state_ref, send_ref = refs
        q_ref = image_ref
    else:
        field_ref, old_d_ref, old_q_ref, old_skel_ref, old_local_ref, old_state_ref = refs[:6]
        r_siblings = refs[6 : 6 + siblings]
        d_siblings = refs[6 + siblings : 6 + 2 * siblings]
        refs = refs[6 + 2 * siblings :]
        image_ref, state_ref, send_ref, d_ref, q_ref, skel_ref, new_local_ref = refs[:7]
        new_siblings = refs[7:]
    core = core_ref[0]
    rows, width = near_ref.shape
    half = width // 2
    sums, stacks = up_parts(core, mine_ref, other_ref, local_ref, rows, width, NORM_TILE)
    norm = sums[:, 0:1]
    state_ref[...] = in_lanes([norm], (rows, LANES))
    ratio = None if first else norm / old_state_ref[:, 0:1]
    for part in range(2):
        points = slice(part * half, (part + 1) * half)
        image = near_ref[:, points] + product(stacks[part], high_ref[:, points], low_ref[:, points], ROWS_COLS)
        image_ref[:, points] = image
        if not first:
            d_ref[:, points] = field_ref[:, points] + ratio * old_d_ref[:, points]
            q_ref[:, points] = image + ratio * old_q_ref[:, points]
    send_ref[...] = sides(core, q_ref)[1]
    if not first:
        rows_in = skel_ref.shape[0]
        crossing = rows_in // (rows // 2)
        skel_ref[...] = mine_ref[:rows_in] + own_rows(core, ratio, crossing) * old_skel_ref[...]
        new_local_ref[...] = local_ref[...] + ratio * old_local_ref[...]
        own_ratio = own_rows(core, ratio, 1)
        for new_ref, r_ref, d_ref in zip(new_siblings, r_siblings, d_siblings):
            new_ref[...] = r_ref[...] + own_ratio * d_ref[...]


def image_up_kernel(first, last, siblings, *refs):
    core_ref, high_ref, low_ref, near_ref, mine_ref, other_ref, local_ref = refs[:7]
    r_ref, w_ref, d_ref, q_ref, state_ref = refs[7:12]
    refs = refs[12:]
    if not first:
        solution_ref = refs[0]
        refs = refs[1:]
    if not last:
        r_skel_ref, d_skel_ref, r_local_ref, d_local_ref = refs[:4]
        r_siblings, q_siblings, d_siblings = [
            refs[4 + index * siblings : 4 + (index + 1) * siblings] for index in range(3)
        ]
        refs = refs[4 + 3 * siblings :]
    new_solution_ref, new_r_ref = refs[:2]
    if not last:
        new_d_ref, new_q_ref, new_skel_ref, new_local_ref, new_state_ref, send_ref = refs[2:8]
        new_siblings = refs[8:]
    core = core_ref[0]
    rows, width = near_ref.shape
    half = width // 2
    sums, stacks = up_parts(core, mine_ref, other_ref, local_ref, rows, width, PRODUCTS_TILE)
    dot = {pair: sums[:, index : index + 1] for index, pair in enumerate(PAIRS)}
    norm = state_ref[:, 0:1]
    step = norm / dot["dq"]
    new_norm = norm - step * (2.0 * dot["rq"] - step * dot["qq"])
    ratio = new_norm / norm
    curve = dot["rw"] - step * (dot["qw"] + dot["rz"] - step * dot["qz"])
    curve = curve + ratio * (dot["dw"] - step * dot["dz"] + dot["rq"] - step * dot["qq"] + ratio * dot["dq"])
    new_step = new_norm / curve
    for part in range(2):
        points = slice(part * half, (part + 1) * half)
        image = near_ref[:, points] + product(stacks[part], high_ref[:, points], low_ref[:, points], ROWS_COLS)
        d = d_ref[:, points]
        q = q_ref[:, points]
        r = r_ref[:, points] - step * q
        new_q = w_ref[:, points] - step * image + ratio * q
        new_d = r + ratio * d
        moved = step * d + new_step * new_d
        new_solution_ref[:, points] = moved if first else solution_ref[:, points] + moved
        new_r_ref[:, points] = r - new_step * new_q
        if not last:
            new_d_ref[:, points] = new_d
            new_q_ref[:, points] = new_q
    if not last:
        rows_in = new_skel_ref.shape[0]
        crossing = rows_in // (rows // 2)
        r_skel = r_skel_ref[:rows_in] - own_rows(core, step, crossing) * mine_ref[:rows_in]
        new_skel_ref[...] = r_skel + own_rows(core, ratio, crossing) * d_skel_ref[:rows_in]
        new_local_ref[...] = r_local_ref[...] - step * local_ref[...] + ratio * d_local_ref[...]
        own_step, own_ratio = own_rows(core, step, 1), own_rows(core, ratio, 1)
        for new_ref, r_ref, q_ref, d_ref in zip(new_siblings, r_siblings, q_siblings, d_siblings):
            new_ref[...] = r_ref[...] - own_step * q_ref[...] + own_ratio * d_ref[...]
        new_state_ref[...] = in_lanes([new_norm], (rows, LANES))
        send_ref[...] = sides(core, new_r_ref)[1]


def per_device(rhs, coords, nugget, near_ids, basis):
    rows, width = rhs.shape
    levels = basis.shape[0]
    leaves = width // LEAF
    own = rows // 2
    crossing = levels - (leaves.bit_length() - 1)
    devices = lax.axis_size("row") * lax.axis_size("col")
    place = jnp.reshape(lax.axis_index(BOTH), (1,))
    core = place % 2
    nugget = nugget[None, :]
    weights = leaf_weights(near_ids, place[0] * leaves)

    stages = [list(range(bit, min(bit + 2, crossing))) for bit in range(1, crossing, 2)]
    siblings = sum(len(bits) == 2 for bits in stages)

    def swap(value, mask):
        return lax.ppermute(value, BOTH, [(source, source ^ mask) for source in range(devices)])

    def halo(other):
        outward = [(index, index + 1) for index in range(1, devices - 1, 2)]
        ends = [(0, 0), (devices - 1, devices - 1)]
        return lax.ppermute(other, BOTH, outward + [(target, source) for source, target in outward] + ends)

    def down(field, *tile):
        shapes = [f32(rows, LOCAL * LANES), f32(crossing * own, LANES)]
        shapes = shapes + [f32(EDGE_BLOCKS * rows + crossing * own, LANES)] + list(tile)
        return call(down_kernel, shapes, core, field, high, low, scalars=1, flops=FLOPS if opening else 0)

    def inner(half, field):
        args = [weights, field, nugget, *diagonal[half], *beside]
        body = functools.partial(inner_kernel, half)
        return call(body, [f32(rows, width // 2)], *args, flops=FLOPS // 2 if opening else 0)[0]

    def edge(paired, other, front, back, *more):
        shapes = [f32(rows, width)] + ([f32(PRODUCTS_TILE, LANES)] if more else [])
        args = [core, weights, paired, other, *outside, front, back, *more]
        return call(functools.partial(edge_kernel, bool(more)), shapes, *args, scalars=1, flops=FLOPS // 3 if opening else 0)

    def chain(products, final, keep, got, tile, beside_steps, r_skel=None, d_skel=None, r_sib=(), d_sib=()):
        depth = PRODUCTS_TILE if products else NORM_TILE
        results = []
        both = [r_skel, d_skel] if products else []
        message, level = call(
            functools.partial(first_combine_kernel, products, 2 * width),
            [f32((crossing - 1) * own + depth, LANES), f32(own, LANES)],
            core,
            keep,
            got,
            tile,
            *both,
            scalars=1,
        )
        done, kept = [level], []
        for index in range(len(stages) + 1):
            bits = stages[index] if index < len(stages) else []
            masks = [sum(1 << bit for at, bit in enumerate(bits) if pick >> at & 1) for pick in range(1, 2 ** len(bits))]
            got = [swap(message, mask) for mask in masks or [1]]
            if index < len(beside_steps):
                *got, result = lax.optimization_barrier((*got, beside_steps[index](message)))
                results.append(result)
            if not bits:
                break
            left = crossing - bits[-1] - 1
            paired = len(bits) == 2
            args = [core, message, *got, *both]
            if products and paired:
                args = args + [r_sib[index], d_sib[index]]
            sibling = paired and not final
            clusters = [width * (2 << bit) for bit in bits]
            message, *levels_out = call(
                functools.partial(combine_kernel, products, not left, sibling, own, bits, clusters),
                [f32((left or crossing) * own + depth, LANES)] + [f32(own, LANES)] * ((len(bits) if left else 0) + sibling),
                *args,
                *([] if left else done),
                scalars=1,
            )
            kept = kept + levels_out[len(levels_out) - sibling :]
            done = done + levels_out[: len(levels_out) - sibling]
        return message, got[0], results, kept

    paired_coords, other = call(
        edges_kernel, [f32(8, LEAF), f32(rows + 8, LEAF)], core, rhs, coords, scalars=1
    )
    other = halo(other)
    paired_coords = swap(paired_coords, 1)
    half = leaves // 2
    pairs = [(leaf, leaf) for leaf in range(half)]
    *front_diagonal, high, low, turned = pl.pallas_call(
        functools.partial(setup_kernel, pairs),
        out_shape=[bf16(half, LEAF, LEAF)] * 2
        + [pltpu.VMEM((levels * LANES, width), jnp.bfloat16)] * 2
        + [f32(width, 8)],
        in_specs=[whole(), whole(pltpu.HBM)],
        out_specs=[whole()] * 5,
        scratch_shapes=[pltpu.VMEM(basis.shape, jnp.float32), pltpu.SemaphoreType.DMA((levels,))],
        compiler_params=pltpu.CompilerParams(vmem_limit_bytes=44 * 2**20),
        cost_estimate=pl.CostEstimate(flops=FLOPS, bytes_accessed=2**20, transcendentals=0),
    )(coords, basis)
    diagonal = [front_diagonal, None]
    beside = outside = None

    def after(message, *values):
        return lax.optimization_barrier((message, *values))[1:]

    def late_matrices(message):
        groups = [[(leaf, leaf) for leaf in range(half, leaves)], [(leaf, leaf + 1) for leaf in range(leaves - 1)]]

        def body(lane_ref, sub_ref, *refs):
            for index, group in enumerate(groups):
                fill_matrices(group, lane_ref, sub_ref, *refs[2 * index : 2 * index + 2])

        shapes = [bf16(len(group), LEAF, LEAF) for group in groups for _ in range(2)]
        return call(body, shapes, *after(message, coords, turned), flops=2 * FLOPS)

    def late_edge_matrices(message):
        def body(core_ref, *refs):
            edge_matrices(core_ref, rows, *refs)

        args = after(message, turned, paired_coords, other)
        return call(body, [bf16(2, LEAF, LEAF)] * 2, core, *args, scalars=1, flops=FLOPS)

    solution, r, carried, opening = None, rhs, None, True
    for step in range(0, ITERS, 2):
        first, last = step == 0, step + 2 == ITERS
        r_local, keep, part, tile = down(r, f32(NORM_TILE, LANES))
        from_core = got = swap(part, 1)
        if first:
            message, got, results, r_sib = chain(False, False, keep, got, tile, [late_matrices, late_edge_matrices])
            diagonal[1], beside = results[0][:2], results[0][2:]
            outside = results[1]
            (near,) = edge(from_core, other, inner(0, r), inner(1, r))
        else:
            fronts = []

            def inner_work(message):
                fronts.extend(inner(half, *after(message, r)) for half in range(2))
                return fronts

            def edge_work(message):
                return edge(from_core, other, *after(message, *fronts))[0]

            message, got, results, r_sib = chain(False, False, keep, got, tile, [inner_work, edge_work])
            near = results[1]
        args = [core, high, low, near, message, got, r_local]
        outs = [f32(rows, width), f32(rows, LANES), f32(rows, LEAF)]
        if first:
            w, state, other = call(
                functools.partial(residual_up_kernel, True, 0), outs, *args, scalars=1, flops=FLOPS // 2
            )
            d, q, d_skel, d_local, d_sib = r, w, message, r_local, r_sib
        else:
            outs = outs + [f32(rows, width)] * 2 + [f32(crossing * own, LANES), f32(rows, LOCAL * LANES)]
            outs = outs + [f32(own, LANES)] * siblings
            body = functools.partial(residual_up_kernel, False, siblings)
            args = args + [r, *carried, *r_sib, *d_sib]
            w, state, other, d, q, d_skel, d_local, *d_sib = call(
                body, outs, *args, scalars=1, flops=FLOPS // 2
            )
        r_skel, opening = message, False
        other = halo(other)
        q_local, keep, part = down(q)
        got = swap(part, 1)
        near, tile = edge(got, other, inner(0, q), inner(1, q), r, q, d, w, r_local, q_local, d_local)
        message, got, _, q_sib = chain(True, last, keep, got, tile, [], r_skel, d_skel, r_sib, d_sib)
        args = [core, high, low, near, message, got, q_local, r, w, d, q, state]
        args = args + ([] if first else [solution]) + ([] if last else [r_skel, d_skel, r_local, d_local, *r_sib, *q_sib, *d_sib])
        outs = [f32(rows, width)] * 2
        if not last:
            outs = outs + [f32(rows, width)] * 2 + [f32(crossing * own, LANES), f32(rows, LOCAL * LANES)]
            outs = outs + [f32(rows, LANES), f32(rows, LEAF)] + [f32(own, LANES)] * siblings
        solution, r, *rest = call(
            functools.partial(image_up_kernel, first, last, siblings), outs, *args, scalars=1, flops=FLOPS // 2
        )
        if not last:
            carried = rest[:5]
            other = halo(rest[5])
            d_sib = rest[6:]
    return (solution, r)


def solution(mesh):
    placed = (
        P(None, BOTH),
        P(None, BOTH),
        P(BOTH),
        P(BOTH, None),
        P(None, None, BOTH),
    )
    return jax.shard_map(
        per_device,
        mesh=mesh,
        in_specs=placed,
        out_specs=(P(None, BOTH), P(None, BOTH)),
        check_vma=False,
    )
```

```python
import functools

import jax
import jax.numpy as jnp
from jax import lax
from jax.experimental import pallas as pl
from jax.experimental.pallas import tpu as pltpu
from jax.sharding import PartitionSpec as P

LEAF = 512
ITERS = 4
WIN = 3
LANES = 128
LOCAL = 3
EDGE_BLOCKS = LEAF // LANES
CHUNK = 16
NORM_TILE = 8
PRODUCTS_TILE = 16
FLOPS = 3 * 10**9

root_three = 1.7320508075688772
spacing_factor = 1.6
matern_scale = root_three / (spacing_factor * LEAF ** (-1.0 / 3.0))

BOTH = ("row", "col")
ROWS_COLS = (((1,), (0,)), ((), ()))
ROWS_ROWS = (((1,), (1,)), ((), ()))

PAIRS = ("dq", "rq", "qq", "rw", "qw", "dw", "rz", "qz", "dz")


def halves(values):
    high = values.astype(jnp.bfloat16)
    low = (values - high.astype(jnp.float32)).astype(jnp.bfloat16)
    return high, low


def stacked(values):
    return jnp.concatenate(halves(values), axis=0)


def product(stack, high, low, dims):
    rows = stack.shape[0] // 2
    main = lax.dot_general(stack, high, dims, preferred_element_type=jnp.float32)
    rest = lax.dot_general(stack[:rows], low, dims, preferred_element_type=jnp.float32)
    return main[:rows] + (main[rows:] + rest)


def row_sum(values):
    return jnp.sum(values, axis=1, keepdims=True)


def in_lanes(columns, shape):
    lane = lax.broadcasted_iota(jnp.int32, shape, 1)
    block = jnp.zeros(shape, jnp.float32)
    for index, column in enumerate(columns):
        block = jnp.where(lane == index, column, block)
    return block


def sums_tile(columns, rows, depth):
    turned = in_lanes(columns, (rows, LANES)).T[:depth]
    return jnp.concatenate([turned, jnp.zeros((depth, LANES - rows), jnp.float32)], axis=1)


def level_terms(core, columns, rows, depth):
    twice = [jnp.concatenate([column, column], axis=0) for column in columns]
    zero = jnp.zeros((rows, 1), jnp.float32)
    tile = sums_tile([zero] * (len(PAIRS) - len(columns)) + twice, rows, depth)
    lane = lax.broadcasted_iota(jnp.int32, tile.shape, 1)
    return jnp.where(lane // (rows // 2) == core, tile, 0.0)


def chosen(core, odd, even):
    return jnp.where(core == 1, odd, even)


def whole(memory=pltpu.VMEM):
    return pl.BlockSpec(memory_space=memory)


def call(body, outs, *args, scalars=0, flops=0, limit=16, scratch=()):
    return pl.pallas_call(
        body,
        out_shape=outs,
        in_specs=[whole(pltpu.SMEM)] * scalars + [whole()] * (len(args) - scalars),
        out_specs=[whole()] * len(outs),
        scratch_shapes=scratch,
        compiler_params=pltpu.CompilerParams(vmem_limit_bytes=limit * 2**20),
        cost_estimate=pl.CostEstimate(flops=flops, bytes_accessed=2**20, transcendentals=0),
    )(*args)


def f32(*shape):
    return jax.ShapeDtypeStruct(shape, jnp.float32)


def bf16(*shape):
    return jax.ShapeDtypeStruct(shape, jnp.bfloat16)


def matrix_rows(rows, lanes):
    square = None
    for axis in range(3):
        spread = rows[:, axis : axis + 1] - lanes[axis : axis + 1]
        square = spread * spread if square is None else square + spread * spread
    scaled = square * lax.rsqrt(jnp.maximum(square, 1e-30))
    return halves((1.0 + scaled) * jnp.exp(-scaled))


def fill_matrices(groups, lane_ref, sub_ref, high_ref, low_ref):
    sub_ref[...] = lane_ref[...].T
    matrix = 0
    for row_leaf, col_leaves in groups:
        lanes = [lane_ref[:, leaf * LEAF : (leaf + 1) * LEAF] for leaf in col_leaves]

        def one(part, carry):
            row_at = pl.multiple_of(row_leaf * LEAF + part * CHUNK, CHUNK)
            out_at = pl.ds(pl.multiple_of(part * CHUNK, CHUNK), CHUNK)
            rows = sub_ref[pl.ds(row_at, CHUNK)]
            for index, far in enumerate(lanes):
                values = matrix_rows(rows, far)
                high_ref[matrix + index, out_at], low_ref[matrix + index, out_at] = values
            return carry

        lax.fori_loop(0, LEAF // CHUNK, one, 0, unroll=4)
        matrix += len(col_leaves)


def setup_kernel(groups, lane_ref, basis_ref, high_ref, low_ref, basis_high_ref, basis_low_ref, sub_ref, raw_ref, sem_ref):
    levels, rank, _ = basis_ref.shape
    copies = [pltpu.make_async_copy(basis_ref.at[at], raw_ref.at[at], sem_ref.at[at]) for at in range(levels)]
    for copy in copies:
        copy.start()
    fill_matrices(groups, lane_ref, sub_ref, high_ref, low_ref)
    for at, copy in enumerate(copies):
        copy.wait()
        here = slice(at * rank, (at + 1) * rank)
        basis_high_ref[here], basis_low_ref[here] = halves(raw_ref[at])


def edge_matrices(core_ref, rows, lane_ref, paired_ref, other_ref, high_ref, low_ref, sub_ref):
    core = core_ref[0]
    leaves = lane_ref.shape[1] // LEAF
    sub_ref[...] = lane_ref[...].T
    paired = paired_ref[:3]
    other = other_ref[rows : rows + 3]
    lanes = [chosen(core, paired, other), chosen(core, other, paired)]

    for side in range(2):
        first_row = side * (leaves - 1) * LEAF

        def one(part, carry):
            row_at = pl.multiple_of(first_row + part * CHUNK, CHUNK)
            out_at = pl.ds(pl.multiple_of(part * CHUNK, CHUNK), CHUNK)
            values = matrix_rows(sub_ref[pl.ds(row_at, CHUNK)], lanes[side])
            high_ref[side, out_at], low_ref[side, out_at] = values
            return carry

        lax.fori_loop(0, LEAF // CHUNK, one, 0, unroll=4)


def sides(core, field_ref):
    head = field_ref[:, :LEAF]
    tail = field_ref[:, field_ref.shape[1] - LEAF :]
    return chosen(core, head, tail), chosen(core, tail, head)


def edges_kernel(core_ref, field_ref, coords_ref, paired_ref, other_ref, lane_ref):
    core = core_ref[0]
    scaled = coords_ref[...] * matern_scale
    lane_ref[...] = jnp.concatenate([scaled, jnp.zeros((8 - scaled.shape[0], scaled.shape[1]), jnp.float32)], axis=0)
    paired_ref[...], other = sides(core, lane_ref)
    other_ref[...] = jnp.concatenate([sides(core, field_ref)[1], other], axis=0)


def down_kernel(core_ref, field_ref, high_ref, low_ref, local_ref, keep_ref, send_ref, *tile_refs):
    core = core_ref[0]
    rank = LANES
    rows, width = field_ref.shape
    half = width // 2
    stack = stacked(field_ref[...])
    for part in range(2):
        points = slice(part * half, (part + 1) * half)
        local_ref[:, part * rank : (part + 1) * rank] = product(
            stack[:, points], high_ref[:rank, points], low_ref[:rank, points], ROWS_ROWS
        )
    all_points = product(stack, high_ref[rank:], low_ref[rank:], ROWS_ROWS)
    local_ref[:, 2 * rank :] = all_points[:, :rank]
    own = rows // 2
    for bit in range(all_points.shape[1] // rank - 1):
        block = all_points[:, (bit + 1) * rank : (bit + 2) * rank]
        keep_ref[bit * own : (bit + 1) * own] = chosen(core, block[own:], block[:own])
        at = EDGE_BLOCKS * rows + bit * own
        send_ref[at : at + own] = chosen(core, block[:own], block[own:])
    paired = sides(core, field_ref)[0]
    for block in range(EDGE_BLOCKS):
        send_ref[block * rows : (block + 1) * rows] = paired[:, block * LANES : (block + 1) * LANES]
    for ref in tile_refs:
        ref[...] = sums_tile([row_sum(field_ref[...] * field_ref[...])], rows, NORM_TILE)


def leaf_of(ref, leaf):
    return ref[:, leaf * LEAF : (leaf + 1) * LEAF]


def weight_of(weights_ref, leaf, offset):
    at = WIN * leaf + offset + 1
    return weights_ref[at : at + 1]


def leaf_weights(near_ids, first_leaf):
    target = first_leaf + jnp.arange(near_ids.shape[0])[:, None] + jnp.arange(WIN)[None, :] - 1
    found = jnp.any(near_ids[:, None, :] == target[:, :, None], axis=2) & (target >= 0)
    weights = jnp.where(found, 1.0 / (16 * WIN), 0.0).astype(jnp.float32)
    return jnp.broadcast_to(weights.reshape(-1, 1), (weights.size, LEAF))


def row_groups(leaves):
    return [(leaf, [leaf, leaf + 1] if leaf + 1 < leaves else [leaf]) for leaf in range(leaves)]


def inner_kernel(half, weights_ref, field_ref, nugget_ref, *refs):
    out_ref = refs[-1]
    leaves = weights_ref.shape[0] // WIN
    start = half * (leaves // 2)
    stop = start + leaves // 2
    pieces = {leaf: stacked(leaf_of(field_ref, leaf)) for leaf in range(max(start - 1, 0), min(stop + 1, leaves))}
    pairs = [(row, col) for row, cols in row_groups(leaves) for col in cols]

    def matrix(row, col):
        at = pairs.index((row, col))
        front = refs[0].shape[0]
        return (refs[0][at], refs[1][at]) if at < front else (refs[2][at - front], refs[3][at - front])

    for leaf in range(start, stop):
        at = leaf - start
        inside = product(pieces[leaf], *matrix(leaf, leaf), ROWS_COLS)
        total = leaf_of(nugget_ref, leaf) * leaf_of(field_ref, leaf) + weight_of(weights_ref, leaf, 0) * inside
        if leaf > 0:
            before = product(pieces[leaf - 1], *matrix(leaf - 1, leaf), ROWS_COLS)
            total = total + weight_of(weights_ref, leaf, -1) * before
        if leaf < leaves - 1:
            after = product(pieces[leaf + 1], *matrix(leaf, leaf + 1), ROWS_ROWS)
            total = total + weight_of(weights_ref, leaf, 1) * after
        out_ref[:, at * LEAF : (at + 1) * LEAF] = total


def edge_kernel(sums, *refs):
    core_ref, weights_ref, paired_ref, other_ref, high_ref, low_ref, front_ref, back_ref = refs[:8]
    refs = refs[8:]
    out_ref = refs[-2] if sums else refs[-1]
    core = core_ref[0]
    rows, width = out_ref.shape
    leaves = width // LEAF
    paired = [paired_ref[block * rows : (block + 1) * rows] for block in range(EDGE_BLOCKS)]
    paired = jnp.concatenate(paired, axis=1)
    before = chosen(core, paired, other_ref[:rows])
    after = chosen(core, other_ref[:rows], paired)
    out_ref[:, : width // 2] = front_ref[...]
    out_ref[:, width // 2 :] = back_ref[...]
    part = product(stacked(before), high_ref[0], low_ref[0], ROWS_ROWS)
    out_ref[:, :LEAF] += weight_of(weights_ref, 0, -1) * part
    part = product(stacked(after), high_ref[1], low_ref[1], ROWS_ROWS)
    out_ref[:, width - LEAF :] += weight_of(weights_ref, leaves - 1, 1) * part
    if not sums:
        return
    fields = dict(zip("rqdw", refs[:4]))
    locals_ = dict(zip("rqd", refs[4:7]))
    tile_ref = refs[-1]
    totals = {pair: jnp.zeros((rows, 1), jnp.float32) for pair in PAIRS}
    for leaf in range(leaves):
        here = {name: leaf_of(ref, leaf) for name, ref in fields.items()}
        here["z"] = leaf_of(out_ref, leaf)
        for left, right in PAIRS:
            totals[left + right] = totals[left + right] + row_sum(here[left] * here[right])
    for block in range(LOCAL):
        scale = 1.0 / (LEAF * (2 if block < 2 else 4))
        lanes = slice(block * LANES, (block + 1) * LANES)
        for name in "rqd":
            term = row_sum(locals_[name][:, lanes] * locals_["q"][:, lanes])
            totals[name + "z"] = totals[name + "z"] + scale * term
    tile_ref[...] = sums_tile([totals[pair] for pair in PAIRS], rows, PRODUCTS_TILE)


def first_combine_kernel(products, cluster, *refs):
    core_ref, mine_ref, other_ref, tile_ref = refs[:4]
    message_ref, level_ref = refs[-2:]
    own = level_ref.shape[0]
    depth = tile_ref.shape[0]
    total = mine_ref[...] + other_ref[EDGE_BLOCKS * 2 * own :]
    level = total[:own]
    level_ref[...] = level
    tile = tile_ref[...]
    if products:
        partners = [refs[4][:own], level, refs[5][:own]]
        columns = [row_sum(level * partner) * (1.0 / cluster) for partner in partners]
        tile = tile + level_terms(core_ref[0], columns, 2 * own, depth)
    left = total.shape[0] - own
    message_ref[:left] = total[own:]
    message_ref[left:] = tile


def combine_kernel(products, last, sibling, own, bits, clusters, *refs):
    refs = list(refs)
    core_ref, mine_ref = refs[:2]
    got = [ref[...] for ref in refs[2 : 2 + 2 ** len(bits) - 1]]
    refs = refs[1 + 2 ** len(bits) :]
    sibling_ref = refs.pop() if sibling else None
    level_out = [] if last else [refs.pop() for _ in bits][::-1]
    next_ref = refs.pop()
    depth = PRODUCTS_TILE if products else NORM_TILE
    near = mine_ref[...] + got[0]
    total = near
    pairs = [(near[:own], bits[0], 0, clusters[0])]
    if len(bits) == 2:
        far = got[1] + got[2]
        total = near + far
        if sibling:
            sibling_ref[...] = far[:own]
        pairs.append((far[:own], None, 1, clusters[0]))
        pairs.append((total[own : 2 * own], bits[1], 0, clusters[1]))
    for ref, pair in zip(level_out, pairs[:: 2 if len(bits) == 2 else 1]):
        ref[...] = pair[0]
    tile = total[total.shape[0] - depth :]
    if products:
        r_ref, d_ref = refs[:2]
        refs = refs[2:]
        siblings = [refs.pop(0), refs.pop(0)] if len(bits) == 2 else []
        columns = [jnp.zeros((own, 1), jnp.float32)] * 3
        for level, bit, kind, cluster in pairs:
            if kind:
                partners = [siblings[0][...], level, siblings[1][...]]
            else:
                here = slice(bit * own, (bit + 1) * own)
                partners = [r_ref[here], level, d_ref[here]]
            terms = [row_sum(level * partner) * (1.0 / cluster) for partner in partners]
            columns = [column + term for column, term in zip(columns, terms)]
        tile = tile + level_terms(core_ref[0], columns, 2 * own, depth)
    left = total.shape[0] - depth - len(bits) * own
    if not last:
        next_ref[:left] = total[len(bits) * own : len(bits) * own + left]
        next_ref[left:] = tile
    else:
        for index, ref in enumerate(refs):
            next_ref[index * own : (index + 1) * own] = ref[...]
        for bit, pair in zip(bits, pairs[:: 2 if len(bits) == 2 else 1]):
            next_ref[bit * own : (bit + 1) * own] = pair[0]
        next_ref[next_ref.shape[0] - depth :] = tile


def up_parts(core, mine_ref, other_ref, local_ref, rows, width, depth):
    own = rows // 2
    crossing = (mine_ref.shape[0] - depth) // own
    sums = (mine_ref[crossing * own :] + other_ref[crossing * own :]).T[:rows]
    scaled = []
    for bit in range(crossing):
        here = slice(bit * own, (bit + 1) * own)
        low_rows = chosen(core, other_ref[here], mine_ref[here])
        high_rows = chosen(core, mine_ref[here], other_ref[here])
        scaled.append(jnp.concatenate([low_rows, high_rows], axis=0) * (1.0 / (width * (2 << bit))))
    one = [local_ref[:, part * LANES : (part + 1) * LANES] * (1.0 / (2 * LEAF)) for part in range(2)]
    two = local_ref[:, 2 * LANES :] * (1.0 / (4 * LEAF))
    return sums, [stacked(jnp.concatenate([one[part], two] + scaled, axis=1)) for part in range(2)]


def own_rows(core, column, crossing):
    own = column.shape[0] // 2
    return jnp.concatenate([chosen(core, column[own:], column[:own])] * crossing, axis=0)


def residual_up_kernel(first, siblings, *refs):
    core_ref, high_ref, low_ref, near_ref, mine_ref, other_ref, local_ref = refs[:7]
    refs = refs[7:]
    if first:
        image_ref, state_ref, send_ref = refs
        q_ref = image_ref
    else:
        field_ref, old_d_ref, old_q_ref, old_skel_ref, old_local_ref, old_state_ref = refs[:6]
        r_siblings = refs[6 : 6 + siblings]
        d_siblings = refs[6 + siblings : 6 + 2 * siblings]
        refs = refs[6 + 2 * siblings :]
        image_ref, state_ref, send_ref, d_ref, q_ref, skel_ref, new_local_ref = refs[:7]
        new_siblings = refs[7:]
    core = core_ref[0]
    rows, width = near_ref.shape
    half = width // 2
    sums, stacks = up_parts(core, mine_ref, other_ref, local_ref, rows, width, NORM_TILE)
    norm = sums[:, 0:1]
    state_ref[...] = in_lanes([norm], (rows, LANES))
    ratio = None if first else norm / old_state_ref[:, 0:1]
    for part in range(2):
        points = slice(part * half, (part + 1) * half)
        image = near_ref[:, points] + product(stacks[part], high_ref[:, points], low_ref[:, points], ROWS_COLS)
        image_ref[:, points] = image
        if not first:
            d_ref[:, points] = field_ref[:, points] + ratio * old_d_ref[:, points]
            q_ref[:, points] = image + ratio * old_q_ref[:, points]
    send_ref[...] = sides(core, q_ref)[1]
    if not first:
        rows_in = skel_ref.shape[0]
        crossing = rows_in // (rows // 2)
        skel_ref[...] = mine_ref[:rows_in] + own_rows(core, ratio, crossing) * old_skel_ref[...]
        new_local_ref[...] = local_ref[...] + ratio * old_local_ref[...]
        own_ratio = own_rows(core, ratio, 1)
        for new_ref, r_ref, d_ref in zip(new_siblings, r_siblings, d_siblings):
            new_ref[...] = r_ref[...] + own_ratio * d_ref[...]


def image_up_kernel(first, last, siblings, *refs):
    core_ref, high_ref, low_ref, near_ref, mine_ref, other_ref, local_ref = refs[:7]
    r_ref, w_ref, d_ref, q_ref, state_ref = refs[7:12]
    refs = refs[12:]
    if not first:
        solution_ref = refs[0]
        refs = refs[1:]
    if not last:
        r_skel_ref, d_skel_ref, r_local_ref, d_local_ref = refs[:4]
        r_siblings, q_siblings, d_siblings = [
            refs[4 + index * siblings : 4 + (index + 1) * siblings] for index in range(3)
        ]
        refs = refs[4 + 3 * siblings :]
    new_solution_ref, new_r_ref = refs[:2]
    if not last:
        new_d_ref, new_q_ref, new_skel_ref, new_local_ref, new_state_ref, send_ref = refs[2:8]
        new_siblings = refs[8:]
    core = core_ref[0]
    rows, width = near_ref.shape
    half = width // 2
    sums, stacks = up_parts(core, mine_ref, other_ref, local_ref, rows, width, PRODUCTS_TILE)
    dot = {pair: sums[:, index : index + 1] for index, pair in enumerate(PAIRS)}
    norm = state_ref[:, 0:1]
    step = norm / dot["dq"]
    new_norm = norm - step * (2.0 * dot["rq"] - step * dot["qq"])
    ratio = new_norm / norm
    curve = dot["rw"] - step * (dot["qw"] + dot["rz"] - step * dot["qz"])
    curve = curve + ratio * (dot["dw"] - step * dot["dz"] + dot["rq"] - step * dot["qq"] + ratio * dot["dq"])
    new_step = new_norm / curve
    for part in range(2):
        points = slice(part * half, (part + 1) * half)
        image = near_ref[:, points] + product(stacks[part], high_ref[:, points], low_ref[:, points], ROWS_COLS)
        d = d_ref[:, points]
        q = q_ref[:, points]
        r = r_ref[:, points] - step * q
        new_q = w_ref[:, points] - step * image + ratio * q
        new_d = r + ratio * d
        moved = step * d + new_step * new_d
        new_solution_ref[:, points] = moved if first else solution_ref[:, points] + moved
        new_r_ref[:, points] = r - new_step * new_q
        if not last:
            new_d_ref[:, points] = new_d
            new_q_ref[:, points] = new_q
    if not last:
        rows_in = new_skel_ref.shape[0]
        crossing = rows_in // (rows // 2)
        r_skel = r_skel_ref[:rows_in] - own_rows(core, step, crossing) * mine_ref[:rows_in]
        new_skel_ref[...] = r_skel + own_rows(core, ratio, crossing) * d_skel_ref[:rows_in]
        new_local_ref[...] = r_local_ref[...] - step * local_ref[...] + ratio * d_local_ref[...]
        own_step, own_ratio = own_rows(core, step, 1), own_rows(core, ratio, 1)
        for new_ref, r_ref, q_ref, d_ref in zip(new_siblings, r_siblings, q_siblings, d_siblings):
            new_ref[...] = r_ref[...] - own_step * q_ref[...] + own_ratio * d_ref[...]
        new_state_ref[...] = in_lanes([new_norm], (rows, LANES))
        send_ref[...] = sides(core, new_r_ref)[1]


def per_device(rhs, coords, nugget, near_ids, basis):
    rows, width = rhs.shape
    levels = basis.shape[0]
    leaves = width // LEAF
    own = rows // 2
    crossing = levels - (leaves.bit_length() - 1)
    devices = lax.axis_size("row") * lax.axis_size("col")
    place = jnp.reshape(lax.axis_index(BOTH), (1,))
    core = place % 2
    nugget = nugget[None, :]
    weights = leaf_weights(near_ids, place[0] * leaves)

    stages = [list(range(bit, min(bit + 2, crossing))) for bit in range(1, crossing, 2)]
    siblings = sum(len(bits) == 2 for bits in stages)

    def swap(value, mask):
        return lax.ppermute(value, BOTH, [(source, source ^ mask) for source in range(devices)])

    def halo(other):
        outward = [(index, index + 1) for index in range(1, devices - 1, 2)]
        ends = [(0, 0), (devices - 1, devices - 1)]
        return lax.ppermute(other, BOTH, outward + [(target, source) for source, target in outward] + ends)

    def down(field, *tile):
        shapes = [f32(rows, LOCAL * LANES), f32(crossing * own, LANES)]
        shapes = shapes + [f32(EDGE_BLOCKS * rows + crossing * own, LANES)] + list(tile)
        return call(down_kernel, shapes, core, field, high, low, scalars=1, flops=FLOPS if opening else 0)

    def inner(half, field):
        args = [weights, field, nugget, *front_matrices, *back_matrices]
        body = functools.partial(inner_kernel, half)
        return call(body, [f32(rows, width // 2)], *args, flops=FLOPS // 2 if opening else 0)[0]

    def edge(paired, other, front, back, *more):
        shapes = [f32(rows, width)] + ([f32(PRODUCTS_TILE, LANES)] if more else [])
        args = [core, weights, paired, other, *outside, front, back, *more]
        return call(functools.partial(edge_kernel, bool(more)), shapes, *args, scalars=1, flops=FLOPS // 3 if opening else 0)

    def chain(products, final, keep, got, tile, beside_steps, r_skel=None, d_skel=None, r_sib=(), d_sib=()):
        depth = PRODUCTS_TILE if products else NORM_TILE
        results = []
        both = [r_skel, d_skel] if products else []
        message, level = call(
            functools.partial(first_combine_kernel, products, 2 * width),
            [f32((crossing - 1) * own + depth, LANES), f32(own, LANES)],
            core,
            keep,
            got,
            tile,
            *both,
            scalars=1,
        )
        done, kept = [level], []
        for index in range(len(stages) + 1):
            bits = stages[index] if index < len(stages) else []
            masks = [sum(1 << bit for at, bit in enumerate(bits) if pick >> at & 1) for pick in range(1, 2 ** len(bits))]
            got = [swap(message, mask) for mask in masks or [1]]
            if index < len(beside_steps):
                *got, result = lax.optimization_barrier((*got, beside_steps[index](message)))
                results.append(result)
            if not bits:
                break
            left = crossing - bits[-1] - 1
            paired = len(bits) == 2
            args = [core, message, *got, *both]
            if products and paired:
                args = args + [r_sib[index], d_sib[index]]
            sibling = paired and not final
            clusters = [width * (2 << bit) for bit in bits]
            message, *levels_out = call(
                functools.partial(combine_kernel, products, not left, sibling, own, bits, clusters),
                [f32((left or crossing) * own + depth, LANES)] + [f32(own, LANES)] * ((len(bits) if left else 0) + sibling),
                *args,
                *([] if left else done),
                scalars=1,
            )
            kept = kept + levels_out[len(levels_out) - sibling :]
            done = done + levels_out[: len(levels_out) - sibling]
        return message, got[0], results, kept

    paired_coords, other, lanes = call(
        edges_kernel, [f32(8, LEAF), f32(rows + 8, LEAF), f32(8, width)], core, rhs, coords, scalars=1
    )
    other = halo(other)
    paired_coords = swap(paired_coords, 1)
    groups = row_groups(leaves)
    turned = pltpu.VMEM((width, 8), jnp.float32)
    *front_matrices, high, low = pl.pallas_call(
        functools.partial(setup_kernel, groups[:1]),
        out_shape=[bf16(2, LEAF, LEAF)] * 2 + [pltpu.VMEM((levels * LANES, width), jnp.bfloat16)] * 2,
        in_specs=[whole(), whole(pltpu.HBM)],
        out_specs=[whole()] * 4,
        scratch_shapes=[turned, pltpu.VMEM(basis.shape, jnp.float32), pltpu.SemaphoreType.DMA((levels,))],
        compiler_params=pltpu.CompilerParams(vmem_limit_bytes=44 * 2**20),
        cost_estimate=pl.CostEstimate(flops=FLOPS, bytes_accessed=2**20, transcendentals=0),
    )(lanes, basis)
    back_matrices = outside = None

    def after(message, *values):
        return lax.optimization_barrier((message, *values))[1:]

    def late_matrices(message):
        def body(lane_ref, high_ref, low_ref, sub_ref):
            fill_matrices(groups[1:], lane_ref, sub_ref, high_ref, low_ref)

        shapes = [bf16(2 * leaves - 3, LEAF, LEAF)] * 2
        return call(body, shapes, *after(message, lanes), flops=2 * FLOPS, scratch=[turned])

    def late_edge_matrices(message):
        def body(core_ref, *refs):
            edge_matrices(core_ref, rows, *refs)

        args = after(message, lanes, paired_coords, other)
        return call(body, [bf16(2, LEAF, LEAF)] * 2, core, *args, scalars=1, flops=FLOPS, scratch=[turned])

    solution, r, carried, opening = None, rhs, None, True
    for step in range(0, ITERS, 2):
        first, last = step == 0, step + 2 == ITERS
        r_local, keep, part, tile = down(r, f32(NORM_TILE, LANES))
        from_core = got = swap(part, 1)
        if first:
            message, got, results, r_sib = chain(False, False, keep, got, tile, [late_matrices, late_edge_matrices])
            back_matrices, outside = results
            (near,) = edge(from_core, other, inner(0, r), inner(1, r))
        else:
            fronts = []

            def inner_work(message):
                fronts.extend(inner(half, *after(message, r)) for half in range(2))
                return fronts

            def edge_work(message):
                return edge(from_core, other, *after(message, *fronts))[0]

            message, got, results, r_sib = chain(False, False, keep, got, tile, [inner_work, edge_work])
            near = results[1]
        args = [core, high, low, near, message, got, r_local]
        outs = [f32(rows, width), f32(rows, LANES), f32(rows, LEAF)]
        if first:
            w, state, other = call(
                functools.partial(residual_up_kernel, True, 0), outs, *args, scalars=1, flops=FLOPS // 2
            )
            d, q, d_skel, d_local, d_sib = r, w, message, r_local, r_sib
        else:
            outs = outs + [f32(rows, width)] * 2 + [f32(crossing * own, LANES), f32(rows, LOCAL * LANES)]
            outs = outs + [f32(own, LANES)] * siblings
            body = functools.partial(residual_up_kernel, False, siblings)
            args = args + [r, *carried, *r_sib, *d_sib]
            w, state, other, d, q, d_skel, d_local, *d_sib = call(
                body, outs, *args, scalars=1, flops=FLOPS // 2
            )
        r_skel, opening = message, False
        other = halo(other)
        q_local, keep, part = down(q)
        got = swap(part, 1)
        near, tile = edge(got, other, inner(0, q), inner(1, q), r, q, d, w, r_local, q_local, d_local)
        message, got, _, q_sib = chain(True, last, keep, got, tile, [], r_skel, d_skel, r_sib, d_sib)
        args = [core, high, low, near, message, got, q_local, r, w, d, q, state]
        args = args + ([] if first else [solution]) + ([] if last else [r_skel, d_skel, r_local, d_local, *r_sib, *q_sib, *d_sib])
        outs = [f32(rows, width)] * 2
        if not last:
            outs = outs + [f32(rows, width)] * 2 + [f32(crossing * own, LANES), f32(rows, LOCAL * LANES)]
            outs = outs + [f32(rows, LANES), f32(rows, LEAF)] + [f32(own, LANES)] * siblings
        solution, r, *rest = call(
            functools.partial(image_up_kernel, first, last, siblings), outs, *args, scalars=1, flops=FLOPS // 2
        )
        if not last:
            carried = rest[:5]
            other = halo(rest[5])
            d_sib = rest[6:]
    return (solution, r)


def solution(mesh):
    placed = (
        P(None, BOTH),
        P(None, BOTH),
        P(BOTH),
        P(BOTH, None),
        P(None, None, BOTH),
    )
    return jax.shard_map(
        per_device,
        mesh=mesh,
        in_specs=placed,
        out_specs=(P(None, BOTH), P(None, BOTH)),
        check_vma=False,
    )
```

```python
import functools

import jax
import jax.numpy as jnp
from jax import lax
from jax.experimental import pallas as pl
from jax.experimental.pallas import tpu as pltpu
from jax.sharding import PartitionSpec as P

LEAF = 512
ITERS = 4
WIN = 3
LANES = 128
LOCAL = 3
SPARE = 8
CHUNK = 16
NORM_TILE = 8
PRODUCTS_TILE = 16
FLOPS = 3 * 10**9

root_three = 1.7320508075688772
spacing_factor = 1.6
matern_scale = root_three / (spacing_factor * LEAF ** (-1.0 / 3.0))

BOTH = ("row", "col")
ROWS_COLS = (((1,), (0,)), ((), ()))
ROWS_ROWS = (((1,), (1,)), ((), ()))

PAIRS = ("dq", "rq", "qq", "rw", "qw", "dw", "rz", "qz", "dz")


def halves(values):
    high = values.astype(jnp.bfloat16)
    low = (values - high.astype(jnp.float32)).astype(jnp.bfloat16)
    return high, low


def stacked(values):
    return jnp.concatenate(halves(values), axis=0)


def product(stack, high, low, dims):
    rows = stack.shape[0] // 2
    main = lax.dot_general(stack, high, dims, preferred_element_type=jnp.float32)
    rest = lax.dot_general(stack[:rows], low, dims, preferred_element_type=jnp.float32)
    return main[:rows] + (main[rows:] + rest)


def row_sum(values):
    return jnp.sum(values, axis=1, keepdims=True)


def in_lanes(columns, shape):
    lane = lax.broadcasted_iota(jnp.int32, shape, 1)
    block = jnp.zeros(shape, jnp.float32)
    for index, column in enumerate(columns):
        block = jnp.where(lane == index, column, block)
    return block


def sums_tile(columns, rows, depth):
    turned = in_lanes(columns, (rows, LANES)).T[:depth]
    return jnp.concatenate([turned, jnp.zeros((depth, LANES - rows), jnp.float32)], axis=1)


def level_terms(core, columns, rows, depth):
    twice = [jnp.concatenate([column, column], axis=0) for column in columns]
    zero = jnp.zeros((rows, 1), jnp.float32)
    tile = sums_tile([zero] * (len(PAIRS) - len(columns)) + twice, rows, depth)
    lane = lax.broadcasted_iota(jnp.int32, tile.shape, 1)
    return jnp.where(lane // (rows // 2) == core, tile, 0.0)


def chosen(core, odd, even):
    return jnp.where(core == 1, odd, even)


def whole(memory=pltpu.VMEM):
    return pl.BlockSpec(memory_space=memory)


def call(body, outs, *args, scalars=0, flops=0, traffic=2**20, limit=16, scratch=()):
    return pl.pallas_call(
        body,
        out_shape=outs,
        in_specs=[whole(pltpu.SMEM)] * scalars + [whole()] * (len(args) - scalars),
        out_specs=[whole()] * len(outs),
        scratch_shapes=scratch,
        compiler_params=pltpu.CompilerParams(vmem_limit_bytes=limit * 2**20),
        cost_estimate=pl.CostEstimate(flops=flops, bytes_accessed=traffic, transcendentals=0),
    )(*args)


def f32(*shape):
    return jax.ShapeDtypeStruct(shape, jnp.float32)


def bf16(*shape):
    return jax.ShapeDtypeStruct(shape, jnp.bfloat16)


def matrix_rows(rows, lanes):
    square = None
    for axis in range(3):
        spread = rows[:, axis : axis + 1] - lanes[axis : axis + 1]
        square = spread * spread if square is None else square + spread * spread
    scaled = square * lax.rsqrt(jnp.maximum(square, 1e-30))
    return halves((1.0 + scaled) * jnp.exp(-scaled))


def fill_matrices(groups, lane_ref, sub_ref, high_ref, low_ref):
    sub_ref[...] = lane_ref[...].T
    matrix = 0
    for row_leaf, col_leaves in groups:
        lanes = [lane_ref[:, leaf * LEAF : (leaf + 1) * LEAF] for leaf in col_leaves]

        def one(part, carry):
            row_at = pl.multiple_of(row_leaf * LEAF + part * CHUNK, CHUNK)
            out_at = pl.ds(pl.multiple_of(part * CHUNK, CHUNK), CHUNK)
            rows = sub_ref[pl.ds(row_at, CHUNK)]
            for index, far in enumerate(lanes):
                values = matrix_rows(rows, far)
                high_ref[matrix + index, out_at], low_ref[matrix + index, out_at] = values
            return carry

        lax.fori_loop(0, LEAF // CHUNK, one, 0, unroll=4)
        matrix += len(col_leaves)


def setup_kernel(groups, lane_ref, basis_ref, high_ref, low_ref, basis_high_ref, basis_low_ref, sub_ref, raw_ref, sem_ref):
    levels, rank, _ = basis_ref.shape
    copies = [pltpu.make_async_copy(basis_ref.at[at], raw_ref.at[at], sem_ref.at[at]) for at in range(levels)]
    for copy in copies:
        copy.start()
    fill_matrices(groups, lane_ref, sub_ref, high_ref, low_ref)
    for at, copy in enumerate(copies):
        copy.wait()
        here = slice(at * rank, (at + 1) * rank)
        basis_high_ref[here], basis_low_ref[here] = halves(raw_ref[at])


def edge_matrices(core_ref, rows, lane_ref, paired_ref, other_ref, high_ref, low_ref, sub_ref):
    core = core_ref[0]
    leaves = lane_ref.shape[1] // LEAF
    sub_ref[...] = lane_ref[...].T
    paired = paired_ref[rows : rows + 3]
    other = other_ref[rows : rows + 3]
    lanes = [chosen(core, paired, other), chosen(core, other, paired)]

    for side in range(2):
        first_row = side * (leaves - 1) * LEAF

        def one(part, carry):
            row_at = pl.multiple_of(first_row + part * CHUNK, CHUNK)
            out_at = pl.ds(pl.multiple_of(part * CHUNK, CHUNK), CHUNK)
            values = matrix_rows(sub_ref[pl.ds(row_at, CHUNK)], lanes[side])
            high_ref[side, out_at], low_ref[side, out_at] = values
            return carry

        lax.fori_loop(0, LEAF // CHUNK, one, 0, unroll=4)


def sides(core, field_ref):
    head = field_ref[:, :LEAF]
    tail = field_ref[:, field_ref.shape[1] - LEAF :]
    return chosen(core, head, tail), chosen(core, tail, head)


def edges_kernel(core_ref, field_ref, coords_ref, paired_ref, other_ref, lane_ref):
    core = core_ref[0]
    scaled = coords_ref[...] * matern_scale
    lane_ref[...] = jnp.concatenate([scaled, jnp.zeros((8 - scaled.shape[0], scaled.shape[1]), jnp.float32)], axis=0)
    for ref, field, place in zip((paired_ref, other_ref), sides(core, field_ref), sides(core, lane_ref)):
        ref[...] = jnp.concatenate([field, place], axis=0)


def down_kernel(core_ref, field_ref, high_ref, low_ref, local_ref, keep_ref, send_ref, *tile_refs):
    core = core_ref[0]
    rank = LANES
    rows, width = field_ref.shape
    half = width // 2
    stack = stacked(field_ref[...])
    for part in range(2):
        points = slice(part * half, (part + 1) * half)
        local_ref[:, part * rank : (part + 1) * rank] = product(
            stack[:, points], high_ref[:rank, points], low_ref[:rank, points], ROWS_ROWS
        )
    all_points = product(stack, high_ref[rank:], low_ref[rank:], ROWS_ROWS)
    local_ref[:, 2 * rank :] = all_points[:, :rank]
    own = rows // 2
    for bit in range(all_points.shape[1] // rank - 1):
        block = all_points[:, (bit + 1) * rank : (bit + 2) * rank]
        keep_ref[bit * own : (bit + 1) * own] = chosen(core, block[own:], block[:own])
        send_ref[bit * own : (bit + 1) * own] = chosen(core, block[:own], block[own:])
    for ref in tile_refs:
        ref[...] = sums_tile([row_sum(field_ref[...] * field_ref[...])], rows, NORM_TILE)


def leaf_of(ref, leaf):
    return ref[:, leaf * LEAF : (leaf + 1) * LEAF]


def weight_of(weights_ref, leaf, offset):
    at = WIN * leaf + offset + 1
    return weights_ref[at : at + 1]


def leaf_weights(near_ids, first_leaf):
    target = first_leaf + jnp.arange(near_ids.shape[0])[:, None] + jnp.arange(WIN)[None, :] - 1
    found = jnp.any(near_ids[:, None, :] == target[:, :, None], axis=2) & (target >= 0)
    weights = jnp.where(found, 1.0 / (16 * WIN), 0.0).astype(jnp.float32)
    return jnp.broadcast_to(weights.reshape(-1, 1), (weights.size, LEAF))


def row_groups(leaves):
    return [(leaf, [leaf, leaf + 1] if leaf + 1 < leaves else [leaf]) for leaf in range(leaves)]


def inner_kernel(half, weights_ref, field_ref, nugget_ref, *refs):
    out_ref = refs[-1]
    leaves = weights_ref.shape[0] // WIN
    start = half * (leaves // 2)
    stop = start + leaves // 2
    pieces = {leaf: stacked(leaf_of(field_ref, leaf)) for leaf in range(max(start - 1, 0), min(stop + 1, leaves))}
    pairs = [(row, col) for row, cols in row_groups(leaves) for col in cols]

    def matrix(row, col):
        at = pairs.index((row, col))
        front = refs[0].shape[0]
        return (refs[0][at], refs[1][at]) if at < front else (refs[2][at - front], refs[3][at - front])

    for leaf in range(start, stop):
        at = leaf - start
        inside = product(pieces[leaf], *matrix(leaf, leaf), ROWS_COLS)
        total = leaf_of(nugget_ref, leaf) * leaf_of(field_ref, leaf) + weight_of(weights_ref, leaf, 0) * inside
        if leaf > 0:
            before = product(pieces[leaf - 1], *matrix(leaf - 1, leaf), ROWS_COLS)
            total = total + weight_of(weights_ref, leaf, -1) * before
        if leaf < leaves - 1:
            after = product(pieces[leaf + 1], *matrix(leaf, leaf + 1), ROWS_ROWS)
            total = total + weight_of(weights_ref, leaf, 1) * after
        out_ref[:, at * LEAF : (at + 1) * LEAF] = total


def edge_kernel(sums, *refs):
    core_ref, weights_ref, paired_ref, other_ref, high_ref, low_ref, front_ref, back_ref = refs[:8]
    refs = refs[8:]
    out_ref = refs[-2] if sums else refs[-1]
    core = core_ref[0]
    rows, width = out_ref.shape
    leaves = width // LEAF
    before = chosen(core, paired_ref[:rows], other_ref[:rows])
    after = chosen(core, other_ref[:rows], paired_ref[:rows])
    out_ref[:, : width // 2] = front_ref[...]
    out_ref[:, width // 2 :] = back_ref[...]
    part = product(stacked(before), high_ref[0], low_ref[0], ROWS_ROWS)
    out_ref[:, :LEAF] += weight_of(weights_ref, 0, -1) * part
    part = product(stacked(after), high_ref[1], low_ref[1], ROWS_ROWS)
    out_ref[:, width - LEAF :] += weight_of(weights_ref, leaves - 1, 1) * part
    if not sums:
        return
    fields = dict(zip("rqdw", refs[:4]))
    locals_ = dict(zip("rqd", refs[4:7]))
    tile_ref = refs[-1]
    totals = {pair: jnp.zeros((rows, 1), jnp.float32) for pair in PAIRS}
    for leaf in range(leaves):
        here = {name: leaf_of(ref, leaf) for name, ref in fields.items()}
        here["z"] = leaf_of(out_ref, leaf)
        for left, right in PAIRS:
            totals[left + right] = totals[left + right] + row_sum(here[left] * here[right])
    for block in range(LOCAL):
        scale = 1.0 / (LEAF * (2 if block < 2 else 4))
        lanes = slice(block * LANES, (block + 1) * LANES)
        for name in "rqd":
            term = row_sum(locals_[name][:, lanes] * locals_["q"][:, lanes])
            totals[name + "z"] = totals[name + "z"] + scale * term
    tile_ref[...] = sums_tile([totals[pair] for pair in PAIRS], rows, PRODUCTS_TILE)


def first_combine_kernel(products, cluster, *refs):
    core_ref, mine_ref, other_ref, tile_ref = refs[:4]
    message_ref, level_ref = refs[-2:]
    own = level_ref.shape[0]
    depth = tile_ref.shape[0]
    total = mine_ref[...] + other_ref[...]
    level = total[:own]
    level_ref[...] = level
    tile = tile_ref[...]
    if products:
        partners = [refs[4][:own], level, refs[5][:own]]
        columns = [row_sum(level * partner) * (1.0 / cluster) for partner in partners]
        tile = tile + level_terms(core_ref[0], columns, 2 * own, depth)
    left = total.shape[0] - own
    message_ref[:left] = total[own:]
    message_ref[left:] = tile


def combine_kernel(products, last, sibling, own, bits, clusters, *refs):
    refs = list(refs)
    core_ref, mine_ref = refs[:2]
    got = [ref[...] for ref in refs[2 : 2 + 2 ** len(bits) - 1]]
    refs = refs[1 + 2 ** len(bits) :]
    sibling_ref = refs.pop() if sibling else None
    level_out = [] if last else [refs.pop() for _ in bits][::-1]
    next_ref = refs.pop()
    depth = PRODUCTS_TILE if products else NORM_TILE
    near = mine_ref[...] + got[0]
    total = near
    pairs = [(near[:own], bits[0], 0, clusters[0])]
    if len(bits) == 2:
        far = got[1] + got[2]
        total = near + far
        if sibling:
            sibling_ref[...] = far[:own]
        pairs.append((far[:own], None, 1, clusters[0]))
        pairs.append((total[own : 2 * own], bits[1], 0, clusters[1]))
    for ref, pair in zip(level_out, pairs[:: 2 if len(bits) == 2 else 1]):
        ref[...] = pair[0]
    tile = total[total.shape[0] - depth :]
    if products:
        r_ref, d_ref = refs[:2]
        refs = refs[2:]
        siblings = [refs.pop(0), refs.pop(0)] if len(bits) == 2 else []
        columns = [jnp.zeros((own, 1), jnp.float32)] * 3
        for level, bit, kind, cluster in pairs:
            if kind:
                partners = [siblings[0][...], level, siblings[1][...]]
            else:
                here = slice(bit * own, (bit + 1) * own)
                partners = [r_ref[here], level, d_ref[here]]
            terms = [row_sum(level * partner) * (1.0 / cluster) for partner in partners]
            columns = [column + term for column, term in zip(columns, terms)]
        tile = tile + level_terms(core_ref[0], columns, 2 * own, depth)
    left = total.shape[0] - depth - len(bits) * own
    if not last:
        next_ref[:left] = total[len(bits) * own : len(bits) * own + left]
        next_ref[left:] = tile
    else:
        for index, ref in enumerate(refs):
            next_ref[index * own : (index + 1) * own] = ref[...]
        for bit, pair in zip(bits, pairs[:: 2 if len(bits) == 2 else 1]):
            next_ref[bit * own : (bit + 1) * own] = pair[0]
        next_ref[next_ref.shape[0] - depth :] = tile


def up_parts(core, mine_ref, other_ref, local_ref, rows, width, depth):
    own = rows // 2
    crossing = (mine_ref.shape[0] - depth) // own
    sums = (mine_ref[crossing * own :] + other_ref[crossing * own :]).T[:rows]
    scaled = []
    for bit in range(crossing):
        here = slice(bit * own, (bit + 1) * own)
        low_rows = chosen(core, other_ref[here], mine_ref[here])
        high_rows = chosen(core, mine_ref[here], other_ref[here])
        scaled.append(jnp.concatenate([low_rows, high_rows], axis=0) * (1.0 / (width * (2 << bit))))
    one = [local_ref[:, part * LANES : (part + 1) * LANES] * (1.0 / (2 * LEAF)) for part in range(2)]
    two = local_ref[:, 2 * LANES :] * (1.0 / (4 * LEAF))
    return sums, [stacked(jnp.concatenate([one[part], two] + scaled, axis=1)) for part in range(2)]


def own_rows(core, column, crossing):
    own = column.shape[0] // 2
    return jnp.concatenate([chosen(core, column[own:], column[:own])] * crossing, axis=0)


def put_edges(core, field_ref, paired_ref, send_ref):
    rows = paired_ref.shape[0]
    paired_ref[...], send_ref[:rows] = sides(core, field_ref)
    send_ref[rows:] = jnp.zeros((SPARE, LEAF), jnp.float32)


def residual_up_kernel(first, siblings, *refs):
    core_ref, high_ref, low_ref, near_ref, mine_ref, other_ref, local_ref = refs[:7]
    refs = refs[7:]
    if first:
        image_ref, state_ref, paired_ref, send_ref = refs
        q_ref = image_ref
    else:
        field_ref, old_d_ref, old_q_ref, old_skel_ref, old_local_ref, old_state_ref = refs[:6]
        r_siblings = refs[6 : 6 + siblings]
        d_siblings = refs[6 + siblings : 6 + 2 * siblings]
        refs = refs[6 + 2 * siblings :]
        image_ref, state_ref, paired_ref, send_ref, d_ref, q_ref, skel_ref, new_local_ref = refs[:8]
        new_siblings = refs[8:]
    core = core_ref[0]
    rows, width = near_ref.shape
    half = width // 2
    sums, stacks = up_parts(core, mine_ref, other_ref, local_ref, rows, width, NORM_TILE)
    norm = sums[:, 0:1]
    state_ref[...] = in_lanes([norm], (rows, LANES))
    ratio = None if first else norm / old_state_ref[:, 0:1]
    for part in range(2):
        points = slice(part * half, (part + 1) * half)
        image = near_ref[:, points] + product(stacks[part], high_ref[:, points], low_ref[:, points], ROWS_COLS)
        image_ref[:, points] = image
        if not first:
            d_ref[:, points] = field_ref[:, points] + ratio * old_d_ref[:, points]
            q_ref[:, points] = image + ratio * old_q_ref[:, points]
    put_edges(core, q_ref, paired_ref, send_ref)
    if not first:
        rows_in = skel_ref.shape[0]
        crossing = rows_in // (rows // 2)
        skel_ref[...] = mine_ref[:rows_in] + own_rows(core, ratio, crossing) * old_skel_ref[...]
        new_local_ref[...] = local_ref[...] + ratio * old_local_ref[...]
        own_ratio = own_rows(core, ratio, 1)
        for new_ref, r_ref, d_ref in zip(new_siblings, r_siblings, d_siblings):
            new_ref[...] = r_ref[...] + own_ratio * d_ref[...]


def image_up_kernel(first, last, siblings, *refs):
    core_ref, high_ref, low_ref, near_ref, mine_ref, other_ref, local_ref = refs[:7]
    r_ref, w_ref, d_ref, q_ref, state_ref = refs[7:12]
    refs = refs[12:]
    if not first:
        solution_ref = refs[0]
        refs = refs[1:]
    if not last:
        r_skel_ref, d_skel_ref, r_local_ref, d_local_ref = refs[:4]
        r_siblings, q_siblings, d_siblings = [
            refs[4 + index * siblings : 4 + (index + 1) * siblings] for index in range(3)
        ]
        refs = refs[4 + 3 * siblings :]
    new_solution_ref, new_r_ref = refs[:2]
    if not last:
        new_d_ref, new_q_ref, new_skel_ref, new_local_ref, new_state_ref, paired_ref, send_ref = refs[2:9]
        new_siblings = refs[9:]
    core = core_ref[0]
    rows, width = near_ref.shape
    half = width // 2
    sums, stacks = up_parts(core, mine_ref, other_ref, local_ref, rows, width, PRODUCTS_TILE)
    dot = {pair: sums[:, index : index + 1] for index, pair in enumerate(PAIRS)}
    norm = state_ref[:, 0:1]
    step = norm / dot["dq"]
    new_norm = norm - step * (2.0 * dot["rq"] - step * dot["qq"])
    ratio = new_norm / norm
    curve = dot["rw"] - step * (dot["qw"] + dot["rz"] - step * dot["qz"])
    curve = curve + ratio * (dot["dw"] - step * dot["dz"] + dot["rq"] - step * dot["qq"] + ratio * dot["dq"])
    new_step = new_norm / curve
    for part in range(2):
        points = slice(part * half, (part + 1) * half)
        image = near_ref[:, points] + product(stacks[part], high_ref[:, points], low_ref[:, points], ROWS_COLS)
        d = d_ref[:, points]
        q = q_ref[:, points]
        r = r_ref[:, points] - step * q
        new_q = w_ref[:, points] - step * image + ratio * q
        new_d = r + ratio * d
        moved = step * d + new_step * new_d
        new_solution_ref[:, points] = moved if first else solution_ref[:, points] + moved
        new_r_ref[:, points] = r - new_step * new_q
        if not last:
            new_d_ref[:, points] = new_d
            new_q_ref[:, points] = new_q
    if not last:
        rows_in = new_skel_ref.shape[0]
        crossing = rows_in // (rows // 2)
        r_skel = r_skel_ref[:rows_in] - own_rows(core, step, crossing) * mine_ref[:rows_in]
        new_skel_ref[...] = r_skel + own_rows(core, ratio, crossing) * d_skel_ref[:rows_in]
        new_local_ref[...] = r_local_ref[...] - step * local_ref[...] + ratio * d_local_ref[...]
        own_step, own_ratio = own_rows(core, step, 1), own_rows(core, ratio, 1)
        for new_ref, r_ref, q_ref, d_ref in zip(new_siblings, r_siblings, q_siblings, d_siblings):
            new_ref[...] = r_ref[...] - own_step * q_ref[...] + own_ratio * d_ref[...]
        new_state_ref[...] = in_lanes([new_norm], (rows, LANES))
        put_edges(core, new_r_ref, paired_ref, send_ref)


def per_device(rhs, coords, nugget, near_ids, basis):
    rows, width = rhs.shape
    levels = basis.shape[0]
    leaves = width // LEAF
    own = rows // 2
    crossing = levels - (leaves.bit_length() - 1)
    devices = lax.axis_size("row") * lax.axis_size("col")
    place = jnp.reshape(lax.axis_index(BOTH), (1,))
    core = place % 2
    nugget = nugget[None, :]
    weights = leaf_weights(near_ids, place[0] * leaves)

    stages = [list(range(bit, min(bit + 2, crossing))) for bit in range(1, crossing, 2)]
    siblings = sum(len(bits) == 2 for bits in stages)

    def swap(value, mask):
        return lax.ppermute(value, BOTH, [(source, source ^ mask) for source in range(devices)])

    def halo(paired, other):
        outward = [(index, index + 1) for index in range(1, devices - 1, 2)]
        ends = [(0, 0), (devices - 1, devices - 1)]
        other = lax.ppermute(other, BOTH, outward + [(target, source) for source, target in outward] + ends)
        return swap(paired, 1), other

    def down(field, *tile):
        shapes = [f32(rows, LOCAL * LANES), f32(crossing * own, LANES)]
        shapes = shapes + [f32(crossing * own, LANES)] + list(tile)
        return call(down_kernel, shapes, core, field, high, low, scalars=1, flops=FLOPS if opening else 0, traffic=2**20 if opening else 0)

    def inner(half, field):
        args = [weights, field, nugget, *front_matrices, *back_matrices]
        body = functools.partial(inner_kernel, half)
        return call(body, [f32(rows, width // 2)], *args, flops=FLOPS // 2 if opening else 0)[0]

    def edge(paired, other, front, back, *more):
        shapes = [f32(rows, width)] + ([f32(PRODUCTS_TILE, LANES)] if more else [])
        args = [core, weights, paired, other, *outside, front, back, *more]
        return call(functools.partial(edge_kernel, bool(more)), shapes, *args, scalars=1, flops=FLOPS // 3 if opening else 0)

    def chain(products, final, keep, got, tile, beside_steps, r_skel=None, d_skel=None, r_sib=(), d_sib=()):
        depth = PRODUCTS_TILE if products else NORM_TILE
        results = []
        both = [r_skel, d_skel] if products else []
        message, level = call(
            functools.partial(first_combine_kernel, products, 2 * width),
            [f32((crossing - 1) * own + depth, LANES), f32(own, LANES)],
            core,
            keep,
            got,
            tile,
            *both,
            scalars=1,
        )
        done, kept = [level], []
        for index in range(len(stages) + 1):
            bits = stages[index] if index < len(stages) else []
            masks = [sum(1 << bit for at, bit in enumerate(bits) if pick >> at & 1) for pick in range(1, 2 ** len(bits))]
            got = [swap(message, mask) for mask in masks or [1]]
            if index < len(beside_steps):
                *got, result = lax.optimization_barrier((*got, beside_steps[index](message)))
                results.append(result)
            if not bits:
                break
            left = crossing - bits[-1] - 1
            paired = len(bits) == 2
            args = [core, message, *got, *both]
            if products and paired:
                args = args + [r_sib[index], d_sib[index]]
            sibling = paired and not final
            clusters = [width * (2 << bit) for bit in bits]
            message, *levels_out = call(
                functools.partial(combine_kernel, products, not left, sibling, own, bits, clusters),
                [f32((left or crossing) * own + depth, LANES)] + [f32(own, LANES)] * ((len(bits) if left else 0) + sibling),
                *args,
                *([] if left else done),
                scalars=1,
            )
            kept = kept + levels_out[len(levels_out) - sibling :]
            done = done + levels_out[: len(levels_out) - sibling]
        return message, got[0], results, kept

    *edges, lanes = call(
        edges_kernel, [f32(rows + 8, LEAF)] * 2 + [f32(8, width)], core, rhs, coords, scalars=1
    )
    groups = row_groups(leaves)
    turned = pltpu.VMEM((width, 8), jnp.float32)
    *front_matrices, high, low = pl.pallas_call(
        functools.partial(setup_kernel, groups[:1]),
        out_shape=[bf16(2, LEAF, LEAF)] * 2 + [pltpu.VMEM((levels * LANES, width), jnp.bfloat16)] * 2,
        in_specs=[whole(), whole(pltpu.HBM)],
        out_specs=[whole()] * 4,
        scratch_shapes=[turned, pltpu.VMEM(basis.shape, jnp.float32), pltpu.SemaphoreType.DMA((levels,))],
        compiler_params=pltpu.CompilerParams(vmem_limit_bytes=44 * 2**20),
        cost_estimate=pl.CostEstimate(flops=FLOPS, bytes_accessed=2**20, transcendentals=0),
    )(lanes, basis)
    back_matrices = outside = None

    def after(message, *values):
        return lax.optimization_barrier((message, *values))[1:]

    def late_matrices(message):
        def body(lane_ref, high_ref, low_ref, sub_ref):
            fill_matrices(groups[1:], lane_ref, sub_ref, high_ref, low_ref)

        shapes = [bf16(2 * leaves - 3, LEAF, LEAF)] * 2
        return call(body, shapes, *after(message, lanes), flops=2 * FLOPS, scratch=[turned])

    def late_edge_matrices(message):
        def body(core_ref, *refs):
            edge_matrices(core_ref, rows, *refs)

        args = after(message, lanes, *edges)
        return call(body, [bf16(2, LEAF, LEAF)] * 2, core, *args, scalars=1, flops=FLOPS, scratch=[turned])

    solution, r, carried, opening = None, rhs, None, True
    for step in range(0, ITERS, 2):
        first, last = step == 0, step + 2 == ITERS
        r_local, keep, part, tile = down(r, f32(NORM_TILE, LANES))
        if first:
            edges = halo(*lax.optimization_barrier((part, *edges))[1:])
        got = swap(part, 1)
        if first:
            message, got, results, r_sib = chain(False, False, keep, got, tile, [late_matrices, late_edge_matrices])
            back_matrices, outside = results
            (near,) = edge(*edges, inner(0, r), inner(1, r))
        else:
            fronts = []

            def inner_work(message):
                fronts.extend(inner(half, *after(message, r)) for half in range(2))
                return fronts

            def edge_work(message):
                return edge(*edges, *after(message, *fronts))[0]

            message, got, results, r_sib = chain(False, False, keep, got, tile, [inner_work, edge_work])
            near = results[1]
        args = [core, high, low, near, message, got, r_local]
        outs = [f32(rows, width), f32(rows, LANES), f32(rows, LEAF), f32(rows + SPARE, LEAF)]
        if first:
            w, state, *edges = call(
                functools.partial(residual_up_kernel, True, 0), outs, *args, scalars=1, flops=FLOPS // 2
            )
            d, q, d_skel, d_local, d_sib = r, w, message, r_local, r_sib
        else:
            outs = outs + [f32(rows, width)] * 2 + [f32(crossing * own, LANES), f32(rows, LOCAL * LANES)]
            outs = outs + [f32(own, LANES)] * siblings
            body = functools.partial(residual_up_kernel, False, siblings)
            args = args + [r, *carried, *r_sib, *d_sib]
            w, state, paired, other, d, q, d_skel, d_local, *d_sib = call(
                body, outs, *args, scalars=1, flops=FLOPS // 2
            )
            edges = (paired, other)
        r_skel, opening = message, False
        edges = halo(*edges)
        q_local, keep, part = down(q)
        got = swap(part, 1)
        near, tile = edge(*edges, inner(0, q), inner(1, q), r, q, d, w, r_local, q_local, d_local)
        message, got, _, q_sib = chain(True, last, keep, got, tile, [], r_skel, d_skel, r_sib, d_sib)
        args = [core, high, low, near, message, got, q_local, r, w, d, q, state]
        args = args + ([] if first else [solution]) + ([] if last else [r_skel, d_skel, r_local, d_local, *r_sib, *q_sib, *d_sib])
        outs = [f32(rows, width)] * 2
        if not last:
            outs = outs + [f32(rows, width)] * 2 + [f32(crossing * own, LANES), f32(rows, LOCAL * LANES)]
            outs = outs + [f32(rows, LANES), f32(rows, LEAF), f32(rows + SPARE, LEAF)] + [f32(own, LANES)] * siblings
        solution, r, *rest = call(
            functools.partial(image_up_kernel, first, last, siblings), outs, *args, scalars=1, flops=FLOPS // 2
        )
        if not last:
            carried = rest[:5]
            edges = halo(*rest[5:7])
            d_sib = rest[7:]
    return (solution, r)


def solution(mesh):
    placed = (
        P(None, BOTH),
        P(None, BOTH),
        P(BOTH),
        P(BOTH, None),
        P(None, None, BOTH),
    )
    return jax.shard_map(
        per_device,
        mesh=mesh,
        in_specs=placed,
        out_specs=(P(None, BOTH), P(None, BOTH)),
        check_vma=False,
    )
```

```python
import functools

import jax
import jax.numpy as jnp
from jax import lax
from jax.experimental import pallas as pl
from jax.experimental.pallas import tpu as pltpu
from jax.sharding import PartitionSpec as P

LEAF = 512
ITERS = 4
WIN = 3
LANES = 128
LOCAL = 3
SPARE = 8
CHUNK = 16
NORM_TILE = 8
PRODUCTS_TILE = 8
FLOPS = 3 * 10**9

root_three = 1.7320508075688772
spacing_factor = 1.6
matern_scale = root_three / (spacing_factor * LEAF ** (-1.0 / 3.0))

BOTH = ("row", "col")
ROWS_COLS = (((1,), (0,)), ((), ()))
ROWS_ROWS = (((1,), (1,)), ((), ()))

PAIRS = ("dq", "rq", "qq", "rw", "dw", "rz", "qz", "dz")


def halves(values):
    high = values.astype(jnp.bfloat16)
    low = (values - high.astype(jnp.float32)).astype(jnp.bfloat16)
    return high, low


def stacked(values):
    return jnp.concatenate(halves(values), axis=0)


def product(stack, high, low, dims):
    rows = stack.shape[0] // 2
    main = lax.dot_general(stack, high, dims, preferred_element_type=jnp.float32)
    rest = lax.dot_general(stack[:rows], low, dims, preferred_element_type=jnp.float32)
    return main[:rows] + (main[rows:] + rest)


def row_sum(values):
    return jnp.sum(values, axis=1, keepdims=True)


def in_lanes(columns, shape):
    lane = lax.broadcasted_iota(jnp.int32, shape, 1)
    block = jnp.zeros(shape, jnp.float32)
    for index, column in enumerate(columns):
        block = jnp.where(lane == index, column, block)
    return block


def sums_tile(columns, rows, depth):
    turned = in_lanes(columns, (rows, LANES)).T[:depth]
    return jnp.concatenate([turned, jnp.zeros((depth, LANES - rows), jnp.float32)], axis=1)


def level_terms(core, columns, rows, depth):
    twice = [jnp.concatenate([column, column], axis=0) for column in columns]
    zero = jnp.zeros((rows, 1), jnp.float32)
    tile = sums_tile([zero] * (len(PAIRS) - len(columns)) + twice, rows, depth)
    lane = lax.broadcasted_iota(jnp.int32, tile.shape, 1)
    return jnp.where(lane // (rows // 2) == core, tile, 0.0)


def chosen(core, odd, even):
    return jnp.where(core == 1, odd, even)


def whole(memory=pltpu.VMEM):
    return pl.BlockSpec(memory_space=memory)


def call(body, outs, *args, scalars=0, flops=0, traffic=2**20, limit=16, scratch=()):
    return pl.pallas_call(
        body,
        out_shape=outs,
        in_specs=[whole(pltpu.SMEM)] * scalars + [whole()] * (len(args) - scalars),
        out_specs=[whole()] * len(outs),
        scratch_shapes=scratch,
        compiler_params=pltpu.CompilerParams(vmem_limit_bytes=limit * 2**20),
        cost_estimate=pl.CostEstimate(flops=flops, bytes_accessed=traffic, transcendentals=0),
    )(*args)


def f32(*shape):
    return jax.ShapeDtypeStruct(shape, jnp.float32)


def bf16(*shape):
    return jax.ShapeDtypeStruct(shape, jnp.bfloat16)


def matrix_rows(rows, lanes):
    square = None
    for axis in range(3):
        spread = rows[:, axis : axis + 1] - lanes[axis : axis + 1]
        square = spread * spread if square is None else square + spread * spread
    scaled = square * lax.rsqrt(jnp.maximum(square, 1e-30))
    return halves((1.0 + scaled) * jnp.exp(-scaled))


def fill_matrices(groups, lane_ref, sub_ref, high_ref, low_ref):
    sub_ref[...] = lane_ref[...].T
    matrix = 0
    for row_leaf, col_leaves in groups:
        lanes = [lane_ref[:, leaf * LEAF : (leaf + 1) * LEAF] for leaf in col_leaves]

        def one(part, carry):
            row_at = pl.multiple_of(row_leaf * LEAF + part * CHUNK, CHUNK)
            out_at = pl.ds(pl.multiple_of(part * CHUNK, CHUNK), CHUNK)
            rows = sub_ref[pl.ds(row_at, CHUNK)]
            for index, far in enumerate(lanes):
                values = matrix_rows(rows, far)
                high_ref[matrix + index, out_at], low_ref[matrix + index, out_at] = values
            return carry

        lax.fori_loop(0, LEAF // CHUNK, one, 0, unroll=4)
        matrix += len(col_leaves)


def setup_kernel(groups, coords_ref, basis_ref, high_ref, low_ref, basis_high_ref, basis_low_ref, lane_ref, *scratch):
    sub_ref, raw_ref, sem_ref = scratch
    levels, rank, _ = basis_ref.shape
    copies = [pltpu.make_async_copy(basis_ref.at[at], raw_ref.at[at], sem_ref.at[at]) for at in range(levels)]
    for copy in copies:
        copy.start()
    scaled = coords_ref[...] * matern_scale
    lane_ref[...] = jnp.concatenate([scaled, jnp.zeros((8 - scaled.shape[0], scaled.shape[1]), jnp.float32)], axis=0)
    fill_matrices(groups, lane_ref, sub_ref, high_ref, low_ref)
    for at, copy in enumerate(copies):
        copy.wait()
        here = slice(at * rank, (at + 1) * rank)
        basis_high_ref[here], basis_low_ref[here] = halves(raw_ref[at])


def edge_matrices(core_ref, rows, lane_ref, paired_ref, other_ref, high_ref, low_ref, sub_ref):
    core = core_ref[0]
    leaves = lane_ref.shape[1] // LEAF
    sub_ref[...] = lane_ref[...].T
    paired = paired_ref[rows : rows + 3]
    other = other_ref[rows : rows + 3]
    lanes = [chosen(core, paired, other), chosen(core, other, paired)]

    for side in range(2):
        first_row = side * (leaves - 1) * LEAF

        def one(part, carry):
            row_at = pl.multiple_of(first_row + part * CHUNK, CHUNK)
            out_at = pl.ds(pl.multiple_of(part * CHUNK, CHUNK), CHUNK)
            values = matrix_rows(sub_ref[pl.ds(row_at, CHUNK)], lanes[side])
            high_ref[side, out_at], low_ref[side, out_at] = values
            return carry

        lax.fori_loop(0, LEAF // CHUNK, one, 0, unroll=4)


def sides(core, field_ref):
    head = field_ref[:, :LEAF]
    tail = field_ref[:, field_ref.shape[1] - LEAF :]
    return chosen(core, head, tail), chosen(core, tail, head)


def edges_kernel(core_ref, field_ref, lane_ref, paired_ref, other_ref):
    core = core_ref[0]
    for ref, field, place in zip((paired_ref, other_ref), sides(core, field_ref), sides(core, lane_ref)):
        ref[...] = jnp.concatenate([field, place], axis=0)


def down_kernel(core_ref, field_ref, high_ref, low_ref, local_ref, keep_ref, send_ref, *tile_refs):
    core = core_ref[0]
    rank = LANES
    rows, width = field_ref.shape
    half = width // 2
    stack = stacked(field_ref[...])
    for part in range(2):
        points = slice(part * half, (part + 1) * half)
        local_ref[:, part * rank : (part + 1) * rank] = product(
            stack[:, points], high_ref[:rank, points], low_ref[:rank, points], ROWS_ROWS
        )
    all_points = product(stack, high_ref[rank:], low_ref[rank:], ROWS_ROWS)
    local_ref[:, 2 * rank :] = all_points[:, :rank]
    own = rows // 2
    for bit in range(all_points.shape[1] // rank - 1):
        block = all_points[:, (bit + 1) * rank : (bit + 2) * rank]
        keep_ref[bit * own : (bit + 1) * own] = chosen(core, block[own:], block[:own])
        send_ref[bit * own : (bit + 1) * own] = chosen(core, block[:own], block[own:])
    for ref in tile_refs:
        ref[...] = sums_tile([row_sum(field_ref[...] * field_ref[...])], rows, NORM_TILE)


def leaf_of(ref, leaf):
    return ref[:, leaf * LEAF : (leaf + 1) * LEAF]


def weight_of(weights_ref, leaf, offset):
    at = WIN * leaf + offset + 1
    return weights_ref[at : at + 1]


def leaf_weights(near_ids, first_leaf):
    target = first_leaf + jnp.arange(near_ids.shape[0])[:, None] + jnp.arange(WIN)[None, :] - 1
    found = jnp.any(near_ids[:, None, :] == target[:, :, None], axis=2) & (target >= 0)
    weights = jnp.where(found, 1.0 / (16 * WIN), 0.0).astype(jnp.float32)
    return jnp.broadcast_to(weights.reshape(-1, 1), (weights.size, LEAF))


def row_groups(leaves):
    return [(leaf, [leaf, leaf + 1] if leaf + 1 < leaves else [leaf]) for leaf in range(leaves)]


def inner_kernel(half, weights_ref, field_ref, nugget_ref, *refs):
    out_ref = refs[-1]
    leaves = weights_ref.shape[0] // WIN
    start = half * (leaves // 2)
    stop = start + leaves // 2
    pieces = {leaf: stacked(leaf_of(field_ref, leaf)) for leaf in range(max(start - 1, 0), min(stop + 1, leaves))}
    pairs = [(row, col) for row, cols in row_groups(leaves) for col in cols]

    def matrix(row, col):
        at = pairs.index((row, col))
        front = refs[0].shape[0]
        return (refs[0][at], refs[1][at]) if at < front else (refs[2][at - front], refs[3][at - front])

    for leaf in range(start, stop):
        at = leaf - start
        inside = product(pieces[leaf], *matrix(leaf, leaf), ROWS_COLS)
        total = leaf_of(nugget_ref, leaf) * leaf_of(field_ref, leaf) + weight_of(weights_ref, leaf, 0) * inside
        if leaf > 0:
            before = product(pieces[leaf - 1], *matrix(leaf - 1, leaf), ROWS_COLS)
            total = total + weight_of(weights_ref, leaf, -1) * before
        if leaf < leaves - 1:
            after = product(pieces[leaf + 1], *matrix(leaf, leaf + 1), ROWS_ROWS)
            total = total + weight_of(weights_ref, leaf, 1) * after
        out_ref[:, at * LEAF : (at + 1) * LEAF] = total


def edge_kernel(sums, *refs):
    core_ref, weights_ref, paired_ref, other_ref, high_ref, low_ref, front_ref, back_ref = refs[:8]
    refs = refs[8:]
    out_ref = refs[-2] if sums else refs[-1]
    core = core_ref[0]
    rows, width = out_ref.shape
    leaves = width // LEAF
    before = chosen(core, paired_ref[:rows], other_ref[:rows])
    after = chosen(core, other_ref[:rows], paired_ref[:rows])
    out_ref[:, : width // 2] = front_ref[...]
    out_ref[:, width // 2 :] = back_ref[...]
    part = product(stacked(before), high_ref[0], low_ref[0], ROWS_ROWS)
    out_ref[:, :LEAF] += weight_of(weights_ref, 0, -1) * part
    part = product(stacked(after), high_ref[1], low_ref[1], ROWS_ROWS)
    out_ref[:, width - LEAF :] += weight_of(weights_ref, leaves - 1, 1) * part
    if not sums:
        return
    fields = dict(zip("rqdw", refs[:4]))
    locals_ = dict(zip("rqd", refs[4:7]))
    tile_ref = refs[-1]
    totals = {pair: jnp.zeros((rows, 1), jnp.float32) for pair in PAIRS}
    for leaf in range(leaves):
        here = {name: leaf_of(ref, leaf) for name, ref in fields.items()}
        here["z"] = leaf_of(out_ref, leaf)
        for left, right in PAIRS:
            terms = here[left] * here[right]
            if left + right == "rz":
                terms = terms + here["q"] * here["w"]
            totals[left + right] = totals[left + right] + row_sum(terms)
    for block in range(LOCAL):
        scale = 1.0 / (LEAF * (2 if block < 2 else 4))
        lanes = slice(block * LANES, (block + 1) * LANES)
        for name in "rqd":
            term = row_sum(locals_[name][:, lanes] * locals_["q"][:, lanes])
            totals[name + "z"] = totals[name + "z"] + scale * term
    tile_ref[...] = sums_tile([totals[pair] for pair in PAIRS], rows, PRODUCTS_TILE)


def first_combine_kernel(products, cluster, *refs):
    core_ref, mine_ref, other_ref, tile_ref = refs[:4]
    message_ref, level_ref = refs[-2:]
    own = level_ref.shape[0]
    depth = tile_ref.shape[0]
    total = mine_ref[...] + other_ref[...]
    level = total[:own]
    level_ref[...] = level
    tile = tile_ref[...]
    if products:
        partners = [refs[4][:own], level, refs[5][:own]]
        columns = [row_sum(level * partner) * (1.0 / cluster) for partner in partners]
        tile = tile + level_terms(core_ref[0], columns, 2 * own, depth)
    left = total.shape[0] - own
    message_ref[:left] = total[own:]
    message_ref[left:] = tile


def combine_kernel(products, last, sibling, own, bits, clusters, *refs):
    refs = list(refs)
    core_ref, mine_ref = refs[:2]
    got = [ref[...] for ref in refs[2 : 2 + 2 ** len(bits) - 1]]
    refs = refs[1 + 2 ** len(bits) :]
    sibling_ref = refs.pop() if sibling else None
    level_out = [] if last else [refs.pop() for _ in bits][::-1]
    next_ref = refs.pop()
    depth = PRODUCTS_TILE if products else NORM_TILE
    near = mine_ref[...] + got[0]
    total = near
    pairs = [(near[:own], bits[0], 0, clusters[0])]
    if len(bits) == 2:
        far = got[1] + got[2]
        total = near + far
        if sibling:
            sibling_ref[...] = far[:own]
        pairs.append((far[:own], None, 1, clusters[0]))
        pairs.append((total[own : 2 * own], bits[1], 0, clusters[1]))
    for ref, pair in zip(level_out, pairs[:: 2 if len(bits) == 2 else 1]):
        ref[...] = pair[0]
    tile = total[total.shape[0] - depth :]
    if products:
        r_ref, d_ref = refs[:2]
        refs = refs[2:]
        siblings = [refs.pop(0), refs.pop(0)] if len(bits) == 2 else []
        columns = [jnp.zeros((own, 1), jnp.float32)] * 3
        for level, bit, kind, cluster in pairs:
            if kind:
                partners = [siblings[0][...], level, siblings[1][...]]
            else:
                here = slice(bit * own, (bit + 1) * own)
                partners = [r_ref[here], level, d_ref[here]]
            terms = [row_sum(level * partner) * (1.0 / cluster) for partner in partners]
            columns = [column + term for column, term in zip(columns, terms)]
        tile = tile + level_terms(core_ref[0], columns, 2 * own, depth)
    left = total.shape[0] - depth - len(bits) * own
    if not last:
        next_ref[:left] = total[len(bits) * own : len(bits) * own + left]
        next_ref[left:] = tile
    else:
        for index, ref in enumerate(refs):
            next_ref[index * own : (index + 1) * own] = ref[...]
        for bit, pair in zip(bits, pairs[:: 2 if len(bits) == 2 else 1]):
            next_ref[bit * own : (bit + 1) * own] = pair[0]
        next_ref[next_ref.shape[0] - depth :] = tile


def up_parts(core, mine_ref, other_ref, local_ref, rows, width, depth):
    own = rows // 2
    crossing = (mine_ref.shape[0] - depth) // own
    sums = (mine_ref[crossing * own :] + other_ref[crossing * own :]).T[:rows]
    scaled = []
    for bit in range(crossing):
        here = slice(bit * own, (bit + 1) * own)
        low_rows = chosen(core, other_ref[here], mine_ref[here])
        high_rows = chosen(core, mine_ref[here], other_ref[here])
        scaled.append(jnp.concatenate([low_rows, high_rows], axis=0) * (1.0 / (width * (2 << bit))))
    one = [local_ref[:, part * LANES : (part + 1) * LANES] * (1.0 / (2 * LEAF)) for part in range(2)]
    two = local_ref[:, 2 * LANES :] * (1.0 / (4 * LEAF))
    return sums, [stacked(jnp.concatenate([one[part], two] + scaled, axis=1)) for part in range(2)]


def own_rows(core, column, crossing):
    own = column.shape[0] // 2
    return jnp.concatenate([chosen(core, column[own:], column[:own])] * crossing, axis=0)


def put_edges(core, field_ref, paired_ref, send_ref):
    rows = paired_ref.shape[0]
    paired_ref[...], send_ref[:rows] = sides(core, field_ref)
    send_ref[rows:] = jnp.zeros((SPARE, LEAF), jnp.float32)


def residual_up_kernel(first, siblings, *refs):
    core_ref, high_ref, low_ref, near_ref, mine_ref, other_ref, local_ref = refs[:7]
    refs = refs[7:]
    if first:
        image_ref, state_ref, paired_ref, send_ref = refs
        q_ref = image_ref
    else:
        field_ref, old_d_ref, old_q_ref, old_skel_ref, old_local_ref, old_state_ref = refs[:6]
        r_siblings = refs[6 : 6 + siblings]
        d_siblings = refs[6 + siblings : 6 + 2 * siblings]
        refs = refs[6 + 2 * siblings :]
        image_ref, state_ref, paired_ref, send_ref, d_ref, q_ref, skel_ref, new_local_ref = refs[:8]
        new_siblings = refs[8:]
    core = core_ref[0]
    rows, width = near_ref.shape
    half = width // 2
    sums, stacks = up_parts(core, mine_ref, other_ref, local_ref, rows, width, NORM_TILE)
    norm = sums[:, 0:1]
    state_ref[...] = in_lanes([norm], (rows, LANES))
    ratio = None if first else norm / old_state_ref[:, 0:1]
    for part in range(2):
        points = slice(part * half, (part + 1) * half)
        image = near_ref[:, points] + product(stacks[part], high_ref[:, points], low_ref[:, points], ROWS_COLS)
        image_ref[:, points] = image
        if not first:
            d_ref[:, points] = field_ref[:, points] + ratio * old_d_ref[:, points]
            q_ref[:, points] = image + ratio * old_q_ref[:, points]
    put_edges(core, q_ref, paired_ref, send_ref)
    if not first:
        rows_in = skel_ref.shape[0]
        crossing = rows_in // (rows // 2)
        skel_ref[...] = mine_ref[:rows_in] + own_rows(core, ratio, crossing) * old_skel_ref[...]
        new_local_ref[...] = local_ref[...] + ratio * old_local_ref[...]
        own_ratio = own_rows(core, ratio, 1)
        for new_ref, r_ref, d_ref in zip(new_siblings, r_siblings, d_siblings):
            new_ref[...] = r_ref[...] + own_ratio * d_ref[...]


def image_up_kernel(first, last, siblings, *refs):
    core_ref, high_ref, low_ref, near_ref, mine_ref, other_ref, local_ref = refs[:7]
    r_ref, w_ref, d_ref, q_ref, state_ref = refs[7:12]
    refs = refs[12:]
    if not first:
        solution_ref = refs[0]
        refs = refs[1:]
    if not last:
        r_skel_ref, d_skel_ref, r_local_ref, d_local_ref = refs[:4]
        r_siblings, q_siblings, d_siblings = [
            refs[4 + index * siblings : 4 + (index + 1) * siblings] for index in range(3)
        ]
        refs = refs[4 + 3 * siblings :]
    new_solution_ref, new_r_ref = refs[:2]
    if not last:
        new_d_ref, new_q_ref, new_skel_ref, new_local_ref, new_state_ref, paired_ref, send_ref = refs[2:9]
        new_siblings = refs[9:]
    core = core_ref[0]
    rows, width = near_ref.shape
    half = width // 2
    sums, stacks = up_parts(core, mine_ref, other_ref, local_ref, rows, width, PRODUCTS_TILE)
    dot = {pair: sums[:, index : index + 1] for index, pair in enumerate(PAIRS)}
    norm = state_ref[:, 0:1]
    step = norm / dot["dq"]
    new_norm = norm - step * (2.0 * dot["rq"] - step * dot["qq"])
    ratio = new_norm / norm
    curve = dot["rw"] - step * (dot["rz"] - step * dot["qz"])
    curve = curve + ratio * (dot["dw"] - step * dot["dz"] + dot["rq"] - step * dot["qq"] + ratio * dot["dq"])
    new_step = new_norm / curve
    for part in range(2):
        points = slice(part * half, (part + 1) * half)
        image = near_ref[:, points] + product(stacks[part], high_ref[:, points], low_ref[:, points], ROWS_COLS)
        d = d_ref[:, points]
        q = q_ref[:, points]
        r = r_ref[:, points] - step * q
        new_q = w_ref[:, points] - step * image + ratio * q
        new_d = r + ratio * d
        moved = step * d + new_step * new_d
        new_solution_ref[:, points] = moved if first else solution_ref[:, points] + moved
        new_r_ref[:, points] = r - new_step * new_q
        if not last:
            new_d_ref[:, points] = new_d
            new_q_ref[:, points] = new_q
    if not last:
        rows_in = new_skel_ref.shape[0]
        crossing = rows_in // (rows // 2)
        r_skel = r_skel_ref[:rows_in] - own_rows(core, step, crossing) * mine_ref[:rows_in]
        new_skel_ref[...] = r_skel + own_rows(core, ratio, crossing) * d_skel_ref[:rows_in]
        new_local_ref[...] = r_local_ref[...] - step * local_ref[...] + ratio * d_local_ref[...]
        own_step, own_ratio = own_rows(core, step, 1), own_rows(core, ratio, 1)
        for new_ref, r_ref, q_ref, d_ref in zip(new_siblings, r_siblings, q_siblings, d_siblings):
            new_ref[...] = r_ref[...] - own_step * q_ref[...] + own_ratio * d_ref[...]
        new_state_ref[...] = in_lanes([new_norm], (rows, LANES))
        put_edges(core, new_r_ref, paired_ref, send_ref)


def per_device(rhs, coords, nugget, near_ids, basis):
    rows, width = rhs.shape
    levels = basis.shape[0]
    leaves = width // LEAF
    own = rows // 2
    crossing = levels - (leaves.bit_length() - 1)
    devices = lax.axis_size("row") * lax.axis_size("col")
    place = jnp.reshape(lax.axis_index(BOTH), (1,))
    core = place % 2
    nugget = nugget[None, :]
    weights = leaf_weights(near_ids, place[0] * leaves)

    stages = [list(range(bit, min(bit + 2, crossing))) for bit in range(1, crossing, 2)]
    siblings = sum(len(bits) == 2 for bits in stages)

    def swap(value, mask):
        return lax.ppermute(value, BOTH, [(source, source ^ mask) for source in range(devices)])

    def halo(paired, other):
        outward = [(index, index + 1) for index in range(1, devices - 1, 2)]
        ends = [(0, 0), (devices - 1, devices - 1)]
        other = lax.ppermute(other, BOTH, outward + [(target, source) for source, target in outward] + ends)
        return swap(paired, 1), other

    def down(field, *tile):
        shapes = [f32(rows, LOCAL * LANES), f32(crossing * own, LANES)]
        shapes = shapes + [f32(crossing * own, LANES)] + list(tile)
        return call(down_kernel, shapes, core, field, high, low, scalars=1, flops=FLOPS if opening else 0, traffic=2**20 if opening else 0)

    def inner(half, field):
        args = [weights, field, nugget, *front_matrices, *back_matrices]
        body = functools.partial(inner_kernel, half)
        return call(body, [f32(rows, width // 2)], *args, flops=FLOPS // 2 if opening else 0)[0]

    def edge(paired, other, front, back, *more):
        shapes = [f32(rows, width)] + ([f32(PRODUCTS_TILE, LANES)] if more else [])
        args = [core, weights, paired, other, *outside, front, back, *more]
        return call(functools.partial(edge_kernel, bool(more)), shapes, *args, scalars=1, flops=FLOPS // 3 if opening else 0)

    def chain(products, final, keep, got, tile, beside_steps, r_skel=None, d_skel=None, r_sib=(), d_sib=()):
        depth = PRODUCTS_TILE if products else NORM_TILE
        results = []
        both = [r_skel, d_skel] if products else []
        message, level = call(
            functools.partial(first_combine_kernel, products, 2 * width),
            [f32((crossing - 1) * own + depth, LANES), f32(own, LANES)],
            core,
            keep,
            got,
            tile,
            *both,
            scalars=1,
        )
        done, kept = [level], []
        for index in range(len(stages) + 1):
            bits = stages[index] if index < len(stages) else []
            masks = [sum(1 << bit for at, bit in enumerate(bits) if pick >> at & 1) for pick in range(1, 2 ** len(bits))]
            got = [swap(message, mask) for mask in masks or [1]]
            if index < len(beside_steps):
                *got, result = lax.optimization_barrier((*got, beside_steps[index](message)))
                results.append(result)
            if not bits:
                break
            left = crossing - bits[-1] - 1
            paired = len(bits) == 2
            args = [core, message, *got, *both]
            if products and paired:
                args = args + [r_sib[index], d_sib[index]]
            sibling = paired and not final
            clusters = [width * (2 << bit) for bit in bits]
            message, *levels_out = call(
                functools.partial(combine_kernel, products, not left, sibling, own, bits, clusters),
                [f32((left or crossing) * own + depth, LANES)] + [f32(own, LANES)] * ((len(bits) if left else 0) + sibling),
                *args,
                *([] if left else done),
                scalars=1,
            )
            kept = kept + levels_out[len(levels_out) - sibling :]
            done = done + levels_out[: len(levels_out) - sibling]
        return message, got[0], results, kept

    groups = row_groups(leaves)
    turned = pltpu.VMEM((width, 8), jnp.float32)
    *front_matrices, high, low, lanes = pl.pallas_call(
        functools.partial(setup_kernel, groups[:1]),
        out_shape=[bf16(2, LEAF, LEAF)] * 2
        + [pltpu.VMEM((levels * LANES, width), jnp.bfloat16)] * 2
        + [f32(8, width)],
        in_specs=[whole(), whole(pltpu.HBM)],
        out_specs=[whole()] * 5,
        scratch_shapes=[turned, pltpu.VMEM(basis.shape, jnp.float32), pltpu.SemaphoreType.DMA((levels,))],
        compiler_params=pltpu.CompilerParams(vmem_limit_bytes=44 * 2**20),
        cost_estimate=pl.CostEstimate(flops=FLOPS, bytes_accessed=2**20, transcendentals=0),
    )(coords, basis)
    edges = call(edges_kernel, [f32(rows + 8, LEAF)] * 2, core, rhs, lanes, scalars=1)
    back_matrices = outside = None

    def after(message, *values):
        return lax.optimization_barrier((message, *values))[1:]

    def late_matrices(message):
        def body(lane_ref, high_ref, low_ref, sub_ref):
            fill_matrices(groups[1:], lane_ref, sub_ref, high_ref, low_ref)

        shapes = [bf16(2 * leaves - 3, LEAF, LEAF)] * 2
        return call(body, shapes, *after(message, lanes), flops=2 * FLOPS, scratch=[turned])

    def late_edge_matrices(message):
        def body(core_ref, *refs):
            edge_matrices(core_ref, rows, *refs)

        args = after(message, lanes, *edges)
        return call(body, [bf16(2, LEAF, LEAF)] * 2, core, *args, scalars=1, flops=FLOPS, scratch=[turned])

    solution, r, carried, opening = None, rhs, None, True
    for step in range(0, ITERS, 2):
        first, last = step == 0, step + 2 == ITERS
        r_local, keep, part, tile = down(r, f32(NORM_TILE, LANES))
        if first:
            edges = halo(*lax.optimization_barrier((part, *edges))[1:])
        got = swap(part, 1)
        if first:
            message, got, results, r_sib = chain(False, False, keep, got, tile, [late_matrices, late_edge_matrices])
            back_matrices, outside = results
            (near,) = edge(*edges, inner(0, r), inner(1, r))
        else:
            fronts = []

            def inner_work(message):
                fronts.extend(inner(half, *after(message, r)) for half in range(2))
                return fronts

            def edge_work(message):
                return edge(*edges, *after(message, *fronts))[0]

            message, got, results, r_sib = chain(False, False, keep, got, tile, [inner_work, edge_work])
            near = results[1]
        args = [core, high, low, near, message, got, r_local]
        outs = [f32(rows, width), f32(rows, LANES), f32(rows, LEAF), f32(rows + SPARE, LEAF)]
        if first:
            w, state, *edges = call(
                functools.partial(residual_up_kernel, True, 0), outs, *args, scalars=1, flops=FLOPS // 2
            )
            d, q, d_skel, d_local, d_sib = r, w, message, r_local, r_sib
        else:
            outs = outs + [f32(rows, width)] * 2 + [f32(crossing * own, LANES), f32(rows, LOCAL * LANES)]
            outs = outs + [f32(own, LANES)] * siblings
            body = functools.partial(residual_up_kernel, False, siblings)
            args = args + [r, *carried, *r_sib, *d_sib]
            w, state, paired, other, d, q, d_skel, d_local, *d_sib = call(
                body, outs, *args, scalars=1, flops=FLOPS // 2
            )
            edges = (paired, other)
        r_skel, opening = message, False
        edges = halo(*edges)
        q_local, keep, part = down(q)
        got = swap(part, 1)
        parts = [inner(half, q) for half in range(2)]
        near, tile = edge(*edges, *parts, r, q, d, w, r_local, q_local, d_local)
        message, got, _, q_sib = chain(True, last, keep, got, tile, [], r_skel, d_skel, r_sib, d_sib)
        args = [core, high, low, near, message, got, q_local, r, w, d, q, state]
        args = args + ([] if first else [solution]) + ([] if last else [r_skel, d_skel, r_local, d_local, *r_sib, *q_sib, *d_sib])
        outs = [f32(rows, width)] * 2
        if not last:
            outs = outs + [f32(rows, width)] * 2 + [f32(crossing * own, LANES), f32(rows, LOCAL * LANES)]
            outs = outs + [f32(rows, LANES), f32(rows, LEAF), f32(rows + SPARE, LEAF)] + [f32(own, LANES)] * siblings
        solution, r, *rest = call(
            functools.partial(image_up_kernel, first, last, siblings), outs, *args, scalars=1, flops=FLOPS // 2
        )
        if not last:
            carried = rest[:5]
            edges = halo(*rest[5:7])
            d_sib = rest[7:]
    return (solution, r)


def solution(mesh):
    placed = (
        P(None, BOTH),
        P(None, BOTH),
        P(BOTH),
        P(BOTH, None),
        P(None, None, BOTH),
    )
    return jax.shard_map(
        per_device,
        mesh=mesh,
        in_specs=placed,
        out_specs=(P(None, BOTH), P(None, BOTH)),
        check_vma=False,
    )
```

```python
import functools

import jax
import jax.numpy as jnp
from jax import lax
from jax.experimental import pallas as pl
from jax.experimental.pallas import tpu as pltpu
from jax.sharding import PartitionSpec as P

LEAF = 512
ITERS = 4
WIN = 3
LANES = 128
LOCAL = 3
SPARE = 8
CHUNK = 16
NORM_TILE = 8
PRODUCTS_TILE = 8
FLOPS = 3 * 10**9

root_three = 1.7320508075688772
spacing_factor = 1.6
matern_scale = root_three / (spacing_factor * LEAF ** (-1.0 / 3.0))

BOTH = ("row", "col")
ROWS_COLS = (((1,), (0,)), ((), ()))
ROWS_ROWS = (((1,), (1,)), ((), ()))

PAIRS = ("dq", "rq", "qq", "rw", "dw", "rz", "qz", "dz")


def halves(values):
    high = values.astype(jnp.bfloat16)
    low = (values - high.astype(jnp.float32)).astype(jnp.bfloat16)
    return high, low


def stacked(values):
    return jnp.concatenate(halves(values), axis=0)


def product(stack, high, low, dims):
    rows = stack.shape[0] // 2
    main = lax.dot_general(stack, high, dims, preferred_element_type=jnp.float32)
    rest = lax.dot_general(stack[:rows], low, dims, preferred_element_type=jnp.float32)
    return main[:rows] + (main[rows:] + rest)


def row_sum(values):
    return jnp.sum(values, axis=1, keepdims=True)


def in_lanes(columns, shape):
    lane = lax.broadcasted_iota(jnp.int32, shape, 1)
    block = jnp.zeros(shape, jnp.float32)
    for index, column in enumerate(columns):
        block = jnp.where(lane == index, column, block)
    return block


def sums_tile(columns, rows, depth):
    turned = in_lanes(columns, (rows, LANES)).T[:depth]
    return jnp.concatenate([turned, jnp.zeros((depth, LANES - rows), jnp.float32)], axis=1)


def level_terms(core, columns, rows, depth):
    twice = [jnp.concatenate([column, column], axis=0) for column in columns]
    zero = jnp.zeros((rows, 1), jnp.float32)
    tile = sums_tile([zero] * (len(PAIRS) - len(columns)) + twice, rows, depth)
    lane = lax.broadcasted_iota(jnp.int32, tile.shape, 1)
    return jnp.where(lane // (rows // 2) == core, tile, 0.0)


def chosen(core, odd, even):
    return jnp.where(core == 1, odd, even)


def whole(memory=pltpu.VMEM):
    return pl.BlockSpec(memory_space=memory)


def call(body, outs, *args, scalars=0, flops=0, traffic=2**20, limit=16, scratch=()):
    return pl.pallas_call(
        body,
        out_shape=outs,
        in_specs=[whole(pltpu.SMEM)] * scalars + [whole()] * (len(args) - scalars),
        out_specs=[whole()] * len(outs),
        scratch_shapes=scratch,
        compiler_params=pltpu.CompilerParams(vmem_limit_bytes=limit * 2**20),
        cost_estimate=pl.CostEstimate(flops=flops, bytes_accessed=traffic, transcendentals=0),
    )(*args)


def f32(*shape):
    return jax.ShapeDtypeStruct(shape, jnp.float32)


def bf16(*shape):
    return jax.ShapeDtypeStruct(shape, jnp.bfloat16)


def matrix_rows(rows, lanes):
    square = None
    for axis in range(3):
        spread = rows[:, axis : axis + 1] - lanes[axis : axis + 1]
        square = spread * spread if square is None else square + spread * spread
    scaled = square * lax.rsqrt(jnp.maximum(square, 1e-30))
    return halves((1.0 + scaled) * jnp.exp(-scaled))


def fill_matrices(groups, lane_ref, sub_ref, high_ref, low_ref):
    sub_ref[...] = lane_ref[...].T
    matrix = 0
    for row_leaf, col_leaves in groups:
        lanes = [lane_ref[:, leaf * LEAF : (leaf + 1) * LEAF] for leaf in col_leaves]

        def one(part, carry):
            row_at = pl.multiple_of(row_leaf * LEAF + part * CHUNK, CHUNK)
            out_at = pl.ds(pl.multiple_of(part * CHUNK, CHUNK), CHUNK)
            rows = sub_ref[pl.ds(row_at, CHUNK)]
            for index, far in enumerate(lanes):
                values = matrix_rows(rows, far)
                high_ref[matrix + index, out_at], low_ref[matrix + index, out_at] = values
            return carry

        lax.fori_loop(0, LEAF // CHUNK, one, 0, unroll=4)
        matrix += len(col_leaves)


def setup_kernel(groups, coords_ref, basis_ref, high_ref, low_ref, basis_high_ref, basis_low_ref, lane_ref, *scratch):
    sub_ref, raw_ref, sem_ref = scratch
    levels, rank, _ = basis_ref.shape
    copies = [pltpu.make_async_copy(basis_ref.at[at], raw_ref.at[at], sem_ref.at[at]) for at in range(levels)]
    for copy in copies:
        copy.start()
    scaled = coords_ref[...] * matern_scale
    lane_ref[...] = jnp.concatenate([scaled, jnp.zeros((8 - scaled.shape[0], scaled.shape[1]), jnp.float32)], axis=0)
    fill_matrices(groups, lane_ref, sub_ref, high_ref, low_ref)
    for at, copy in enumerate(copies):
        copy.wait()
        here = slice(at * rank, (at + 1) * rank)
        basis_high_ref[here], basis_low_ref[here] = halves(raw_ref[at])


def edge_matrices(core_ref, rows, lane_ref, paired_ref, other_ref, high_ref, low_ref, sub_ref):
    core = core_ref[0]
    leaves = lane_ref.shape[1] // LEAF
    paired = paired_ref[rows : rows + 3]
    other = other_ref[rows : rows + 3]
    lanes = [chosen(core, paired, other), chosen(core, other, paired)]

    for side in range(2):
        first_point = side * (leaves - 1) * LEAF
        sub_ref[side * LEAF : (side + 1) * LEAF] = lane_ref[:, first_point : first_point + LEAF].T

        def one(part, carry):
            row_at = pl.multiple_of(side * LEAF + part * CHUNK, CHUNK)
            out_at = pl.ds(pl.multiple_of(part * CHUNK, CHUNK), CHUNK)
            values = matrix_rows(sub_ref[pl.ds(row_at, CHUNK)], lanes[side])
            high_ref[side, out_at], low_ref[side, out_at] = values
            return carry

        lax.fori_loop(0, LEAF // CHUNK, one, 0, unroll=4)


def sides(core, field_ref):
    head = field_ref[:, :LEAF]
    tail = field_ref[:, field_ref.shape[1] - LEAF :]
    return chosen(core, head, tail), chosen(core, tail, head)


def edges_kernel(core_ref, field_ref, lane_ref, paired_ref, other_ref):
    core = core_ref[0]
    for ref, field, place in zip((paired_ref, other_ref), sides(core, field_ref), sides(core, lane_ref)):
        ref[...] = jnp.concatenate([field, place], axis=0)


def down_kernel(core_ref, field_ref, high_ref, low_ref, local_ref, keep_ref, send_ref, *tile_refs):
    core = core_ref[0]
    rank = LANES
    rows, width = field_ref.shape
    half = width // 2
    stack = stacked(field_ref[...])
    for part in range(2):
        points = slice(part * half, (part + 1) * half)
        local_ref[:, part * rank : (part + 1) * rank] = product(
            stack[:, points], high_ref[:rank, points], low_ref[:rank, points], ROWS_ROWS
        )
    all_points = product(stack, high_ref[rank:], low_ref[rank:], ROWS_ROWS)
    local_ref[:, 2 * rank :] = all_points[:, :rank]
    own = rows // 2
    for bit in range(all_points.shape[1] // rank - 1):
        block = all_points[:, (bit + 1) * rank : (bit + 2) * rank]
        keep_ref[bit * own : (bit + 1) * own] = chosen(core, block[own:], block[:own])
        send_ref[bit * own : (bit + 1) * own] = chosen(core, block[:own], block[own:])
    for ref in tile_refs:
        ref[...] = sums_tile([row_sum(field_ref[...] * field_ref[...])], rows, NORM_TILE)


def leaf_of(ref, leaf):
    return ref[:, leaf * LEAF : (leaf + 1) * LEAF]


def weight_of(weights_ref, leaf, offset):
    at = WIN * leaf + offset + 1
    return weights_ref[at : at + 1]


def leaf_weights(near_ids, first_leaf):
    target = first_leaf + jnp.arange(near_ids.shape[0])[:, None] + jnp.arange(WIN)[None, :] - 1
    found = jnp.any(near_ids[:, None, :] == target[:, :, None], axis=2) & (target >= 0)
    weights = jnp.where(found, 1.0 / (16 * WIN), 0.0).astype(jnp.float32)
    return jnp.broadcast_to(weights.reshape(-1, 1), (weights.size, LEAF))


def row_groups(leaves):
    return [(leaf, [leaf, leaf + 1] if leaf + 1 < leaves else [leaf]) for leaf in range(leaves)]


def inner_kernel(half, weights_ref, field_ref, nugget_ref, *refs):
    out_ref = refs[-1]
    leaves = weights_ref.shape[0] // WIN
    start = half * (leaves // 2)
    stop = start + leaves // 2
    pieces = {leaf: stacked(leaf_of(field_ref, leaf)) for leaf in range(max(start - 1, 0), min(stop + 1, leaves))}
    pairs = [(row, col) for row, cols in row_groups(leaves) for col in cols]

    def matrix(row, col):
        at = pairs.index((row, col))
        front = refs[0].shape[0]
        return (refs[0][at], refs[1][at]) if at < front else (refs[2][at - front], refs[3][at - front])

    for leaf in range(start, stop):
        at = leaf - start
        inside = product(pieces[leaf], *matrix(leaf, leaf), ROWS_COLS)
        total = leaf_of(nugget_ref, leaf) * leaf_of(field_ref, leaf) + weight_of(weights_ref, leaf, 0) * inside
        if leaf > 0:
            before = product(pieces[leaf - 1], *matrix(leaf - 1, leaf), ROWS_COLS)
            total = total + weight_of(weights_ref, leaf, -1) * before
        if leaf < leaves - 1:
            after = product(pieces[leaf + 1], *matrix(leaf, leaf + 1), ROWS_ROWS)
            total = total + weight_of(weights_ref, leaf, 1) * after
        out_ref[:, at * LEAF : (at + 1) * LEAF] = total


def edge_kernel(sums, *refs):
    core_ref, weights_ref, paired_ref, other_ref, high_ref, low_ref, front_ref, back_ref = refs[:8]
    refs = refs[8:]
    out_ref = refs[-2] if sums else refs[-1]
    core = core_ref[0]
    rows, width = out_ref.shape
    leaves = width // LEAF
    before = chosen(core, paired_ref[:rows], other_ref[:rows])
    after = chosen(core, other_ref[:rows], paired_ref[:rows])
    out_ref[:, : width // 2] = front_ref[...]
    out_ref[:, width // 2 :] = back_ref[...]
    part = product(stacked(before), high_ref[0], low_ref[0], ROWS_ROWS)
    out_ref[:, :LEAF] += weight_of(weights_ref, 0, -1) * part
    part = product(stacked(after), high_ref[1], low_ref[1], ROWS_ROWS)
    out_ref[:, width - LEAF :] += weight_of(weights_ref, leaves - 1, 1) * part
    if not sums:
        return
    fields = dict(zip("rqdw", refs[:4]))
    locals_ = dict(zip("rqd", refs[4:7]))
    tile_ref = refs[-1]
    totals = {pair: jnp.zeros((rows, 1), jnp.float32) for pair in PAIRS}
    for leaf in range(leaves):
        here = {name: leaf_of(ref, leaf) for name, ref in fields.items()}
        here["z"] = leaf_of(out_ref, leaf)
        for left, right in PAIRS:
            terms = here[left] * here[right]
            if left + right == "rz":
                terms = terms + here["q"] * here["w"]
            totals[left + right] = totals[left + right] + row_sum(terms)
    for block in range(LOCAL):
        scale = 1.0 / (LEAF * (2 if block < 2 else 4))
        lanes = slice(block * LANES, (block + 1) * LANES)
        for name in "rqd":
            term = row_sum(locals_[name][:, lanes] * locals_["q"][:, lanes])
            totals[name + "z"] = totals[name + "z"] + scale * term
    tile_ref[...] = sums_tile([totals[pair] for pair in PAIRS], rows, PRODUCTS_TILE)


def first_combine_kernel(products, cluster, *refs):
    core_ref, mine_ref, other_ref, tile_ref = refs[:4]
    message_ref, level_ref = refs[-2:]
    own = level_ref.shape[0]
    depth = tile_ref.shape[0]
    total = mine_ref[...] + other_ref[...]
    level = total[:own]
    level_ref[...] = level
    tile = tile_ref[...]
    if products:
        partners = [refs[4][:own], level, refs[5][:own]]
        columns = [row_sum(level * partner) * (1.0 / cluster) for partner in partners]
        tile = tile + level_terms(core_ref[0], columns, 2 * own, depth)
    left = total.shape[0] - own
    message_ref[:left] = total[own:]
    message_ref[left:] = tile


def combine_kernel(products, last, sibling, own, bits, clusters, *refs):
    refs = list(refs)
    core_ref, mine_ref = refs[:2]
    got = [ref[...] for ref in refs[2 : 2 + 2 ** len(bits) - 1]]
    refs = refs[1 + 2 ** len(bits) :]
    sibling_ref = refs.pop() if sibling else None
    level_out = [] if last else [refs.pop() for _ in bits][::-1]
    next_ref = refs.pop()
    depth = PRODUCTS_TILE if products else NORM_TILE
    near = mine_ref[...] + got[0]
    total = near
    pairs = [(near[:own], bits[0], 0, clusters[0])]
    if len(bits) == 2:
        far = got[1] + got[2]
        total = near + far
        if sibling:
            sibling_ref[...] = far[:own]
        pairs.append((far[:own], None, 1, clusters[0]))
        pairs.append((total[own : 2 * own], bits[1], 0, clusters[1]))
    for ref, pair in zip(level_out, pairs[:: 2 if len(bits) == 2 else 1]):
        ref[...] = pair[0]
    tile = total[total.shape[0] - depth :]
    if products:
        r_ref, d_ref = refs[:2]
        refs = refs[2:]
        siblings = [refs.pop(0), refs.pop(0)] if len(bits) == 2 else []
        columns = [jnp.zeros((own, 1), jnp.float32)] * 3
        for level, bit, kind, cluster in pairs:
            if kind:
                partners = [siblings[0][...], level, siblings[1][...]]
            else:
                here = slice(bit * own, (bit + 1) * own)
                partners = [r_ref[here], level, d_ref[here]]
            terms = [row_sum(level * partner) * (1.0 / cluster) for partner in partners]
            columns = [column + term for column, term in zip(columns, terms)]
        tile = tile + level_terms(core_ref[0], columns, 2 * own, depth)
    left = total.shape[0] - depth - len(bits) * own
    if not last:
        next_ref[:left] = total[len(bits) * own : len(bits) * own + left]
        next_ref[left:] = tile
    else:
        for index, ref in enumerate(refs):
            next_ref[index * own : (index + 1) * own] = ref[...]
        for bit, pair in zip(bits, pairs[:: 2 if len(bits) == 2 else 1]):
            next_ref[bit * own : (bit + 1) * own] = pair[0]
        next_ref[next_ref.shape[0] - depth :] = tile


def up_parts(core, mine_ref, other_ref, local_ref, rows, width, depth):
    own = rows // 2
    crossing = (mine_ref.shape[0] - depth) // own
    sums = (mine_ref[crossing * own :] + other_ref[crossing * own :]).T[:rows]
    scaled = []
    for bit in range(crossing):
        here = slice(bit * own, (bit + 1) * own)
        low_rows = chosen(core, other_ref[here], mine_ref[here])
        high_rows = chosen(core, mine_ref[here], other_ref[here])
        scaled.append(jnp.concatenate([low_rows, high_rows], axis=0) * (1.0 / (width * (2 << bit))))
    one = [local_ref[:, part * LANES : (part + 1) * LANES] * (1.0 / (2 * LEAF)) for part in range(2)]
    two = local_ref[:, 2 * LANES :] * (1.0 / (4 * LEAF))
    return sums, [stacked(jnp.concatenate([one[part], two] + scaled, axis=1)) for part in range(2)]


def own_rows(core, column, crossing):
    own = column.shape[0] // 2
    return jnp.concatenate([chosen(core, column[own:], column[:own])] * crossing, axis=0)


def put_edges(core, field_ref, paired_ref, send_ref):
    rows = paired_ref.shape[0]
    paired_ref[...], send_ref[:rows] = sides(core, field_ref)
    send_ref[rows:] = jnp.zeros((SPARE, LEAF), jnp.float32)


def residual_up_kernel(first, siblings, *refs):
    core_ref, high_ref, low_ref, near_ref, mine_ref, other_ref, local_ref = refs[:7]
    refs = refs[7:]
    if first:
        image_ref, state_ref, paired_ref, send_ref = refs
        q_ref = image_ref
    else:
        field_ref, old_d_ref, old_q_ref, old_skel_ref, old_local_ref, old_state_ref = refs[:6]
        r_siblings = refs[6 : 6 + siblings]
        d_siblings = refs[6 + siblings : 6 + 2 * siblings]
        refs = refs[6 + 2 * siblings :]
        image_ref, state_ref, paired_ref, send_ref, d_ref, q_ref, skel_ref, new_local_ref = refs[:8]
        new_siblings = refs[8:]
    core = core_ref[0]
    rows, width = near_ref.shape
    half = width // 2
    sums, stacks = up_parts(core, mine_ref, other_ref, local_ref, rows, width, NORM_TILE)
    norm = sums[:, 0:1]
    state_ref[...] = in_lanes([norm], (rows, LANES))
    ratio = None if first else norm / old_state_ref[:, 0:1]
    for part in range(2):
        points = slice(part * half, (part + 1) * half)
        image = near_ref[:, points] + product(stacks[part], high_ref[:, points], low_ref[:, points], ROWS_COLS)
        image_ref[:, points] = image
        if not first:
            d_ref[:, points] = field_ref[:, points] + ratio * old_d_ref[:, points]
            q_ref[:, points] = image + ratio * old_q_ref[:, points]
    put_edges(core, q_ref, paired_ref, send_ref)
    if not first:
        rows_in = skel_ref.shape[0]
        crossing = rows_in // (rows // 2)
        skel_ref[...] = mine_ref[:rows_in] + own_rows(core, ratio, crossing) * old_skel_ref[...]
        new_local_ref[...] = local_ref[...] + ratio * old_local_ref[...]
        own_ratio = own_rows(core, ratio, 1)
        for new_ref, r_ref, d_ref in zip(new_siblings, r_siblings, d_siblings):
            new_ref[...] = r_ref[...] + own_ratio * d_ref[...]


def image_up_kernel(first, last, siblings, *refs):
    core_ref, high_ref, low_ref, near_ref, mine_ref, other_ref, local_ref = refs[:7]
    r_ref, w_ref, d_ref, q_ref, state_ref = refs[7:12]
    refs = refs[12:]
    if not first:
        solution_ref = refs[0]
        refs = refs[1:]
    if not last:
        r_skel_ref, d_skel_ref, r_local_ref, d_local_ref = refs[:4]
        r_siblings, q_siblings, d_siblings = [
            refs[4 + index * siblings : 4 + (index + 1) * siblings] for index in range(3)
        ]
        refs = refs[4 + 3 * siblings :]
    new_solution_ref, new_r_ref = refs[:2]
    if not last:
        new_d_ref, new_q_ref, new_skel_ref, new_local_ref, new_state_ref, paired_ref, send_ref = refs[2:9]
        new_siblings = refs[9:]
    core = core_ref[0]
    rows, width = near_ref.shape
    half = width // 2
    sums, stacks = up_parts(core, mine_ref, other_ref, local_ref, rows, width, PRODUCTS_TILE)
    dot = {pair: sums[:, index : index + 1] for index, pair in enumerate(PAIRS)}
    norm = state_ref[:, 0:1]
    step = norm / dot["dq"]
    new_norm = norm - step * (2.0 * dot["rq"] - step * dot["qq"])
    ratio = new_norm / norm
    curve = dot["rw"] - step * (dot["rz"] - step * dot["qz"])
    curve = curve + ratio * (dot["dw"] - step * dot["dz"] + dot["rq"] - step * dot["qq"] + ratio * dot["dq"])
    new_step = new_norm / curve
    for part in range(2):
        points = slice(part * half, (part + 1) * half)
        image = near_ref[:, points] + product(stacks[part], high_ref[:, points], low_ref[:, points], ROWS_COLS)
        d = d_ref[:, points]
        q = q_ref[:, points]
        r = r_ref[:, points] - step * q
        new_q = w_ref[:, points] - step * image + ratio * q
        new_d = r + ratio * d
        moved = step * d + new_step * new_d
        new_solution_ref[:, points] = moved if first else solution_ref[:, points] + moved
        new_r_ref[:, points] = r - new_step * new_q
        if not last:
            new_d_ref[:, points] = new_d
            new_q_ref[:, points] = new_q
    if not last:
        rows_in = new_skel_ref.shape[0]
        crossing = rows_in // (rows // 2)
        r_skel = r_skel_ref[:rows_in] - own_rows(core, step, crossing) * mine_ref[:rows_in]
        new_skel_ref[...] = r_skel + own_rows(core, ratio, crossing) * d_skel_ref[:rows_in]
        new_local_ref[...] = r_local_ref[...] - step * local_ref[...] + ratio * d_local_ref[...]
        own_step, own_ratio = own_rows(core, step, 1), own_rows(core, ratio, 1)
        for new_ref, r_ref, q_ref, d_ref in zip(new_siblings, r_siblings, q_siblings, d_siblings):
            new_ref[...] = r_ref[...] - own_step * q_ref[...] + own_ratio * d_ref[...]
        new_state_ref[...] = in_lanes([new_norm], (rows, LANES))
        put_edges(core, new_r_ref, paired_ref, send_ref)


def per_device(rhs, coords, nugget, near_ids, basis):
    rows, width = rhs.shape
    levels = basis.shape[0]
    leaves = width // LEAF
    own = rows // 2
    crossing = levels - (leaves.bit_length() - 1)
    devices = lax.axis_size("row") * lax.axis_size("col")
    place = jnp.reshape(lax.axis_index(BOTH), (1,))
    core = place % 2
    nugget = nugget[None, :]
    weights = leaf_weights(near_ids, place[0] * leaves)

    stages = [list(range(bit, min(bit + 2, crossing))) for bit in range(1, crossing, 2)]
    siblings = sum(len(bits) == 2 for bits in stages)

    def swap(value, mask):
        return lax.ppermute(value, BOTH, [(source, source ^ mask) for source in range(devices)])

    def far_halo(other):
        outward = [(index, index + 1) for index in range(1, devices - 1, 2)]
        ends = [(0, 0), (devices - 1, devices - 1)]
        return lax.ppermute(other, BOTH, outward + [(target, source) for source, target in outward] + ends)

    def halo(paired, other):
        return swap(paired, 1), far_halo(other)

    def down(field, *tile):
        shapes = [f32(rows, LOCAL * LANES), f32(crossing * own, LANES)]
        shapes = shapes + [f32(crossing * own, LANES)] + list(tile)
        return call(down_kernel, shapes, core, field, high, low, scalars=1, flops=FLOPS if opening else 0, traffic=2**20 if opening else 0)

    def inner(half, field):
        args = [weights, field, nugget, *front_matrices, *back_matrices]
        body = functools.partial(inner_kernel, half)
        return call(body, [f32(rows, width // 2)], *args, flops=FLOPS // 2 if opening else 0)[0]

    def edge(paired, other, front, back, *more):
        shapes = [f32(rows, width)] + ([f32(PRODUCTS_TILE, LANES)] if more else [])
        args = [core, weights, paired, other, *outside, front, back, *more]
        return call(functools.partial(edge_kernel, bool(more)), shapes, *args, scalars=1, flops=FLOPS // 3 if opening else 0)

    def chain(products, final, keep, got, tile, beside_steps, r_skel=None, d_skel=None, r_sib=(), d_sib=()):
        depth = PRODUCTS_TILE if products else NORM_TILE
        results = []
        both = [r_skel, d_skel] if products else []
        message, level = call(
            functools.partial(first_combine_kernel, products, 2 * width),
            [f32((crossing - 1) * own + depth, LANES), f32(own, LANES)],
            core,
            keep,
            got,
            tile,
            *both,
            scalars=1,
        )
        done, kept = [level], []
        for index in range(len(stages) + 1):
            bits = stages[index] if index < len(stages) else []
            masks = [sum(1 << bit for at, bit in enumerate(bits) if pick >> at & 1) for pick in range(1, 2 ** len(bits))]
            got = [swap(message, mask) for mask in masks or [1]]
            if index < len(beside_steps):
                *got, result = lax.optimization_barrier((*got, beside_steps[index](message)))
                results.append(result)
            if not bits:
                break
            left = crossing - bits[-1] - 1
            paired = len(bits) == 2
            args = [core, message, *got, *both]
            if products and paired:
                args = args + [r_sib[index], d_sib[index]]
            sibling = paired and not final
            clusters = [width * (2 << bit) for bit in bits]
            message, *levels_out = call(
                functools.partial(combine_kernel, products, not left, sibling, own, bits, clusters),
                [f32((left or crossing) * own + depth, LANES)] + [f32(own, LANES)] * ((len(bits) if left else 0) + sibling),
                *args,
                *([] if left else done),
                scalars=1,
            )
            kept = kept + levels_out[len(levels_out) - sibling :]
            done = done + levels_out[: len(levels_out) - sibling]
        return message, got[0], results, kept

    groups = row_groups(leaves)
    turned = pltpu.VMEM((width, 8), jnp.float32)
    *front_matrices, high, low, lanes = pl.pallas_call(
        functools.partial(setup_kernel, groups[:1]),
        out_shape=[bf16(2, LEAF, LEAF)] * 2
        + [bf16(levels * LANES, width)] * 2
        + [f32(8, width)],
        in_specs=[whole(), whole(pltpu.HBM)],
        out_specs=[whole()] * 5,
        scratch_shapes=[turned, pltpu.VMEM(basis.shape, jnp.float32), pltpu.SemaphoreType.DMA((levels,))],
        compiler_params=pltpu.CompilerParams(vmem_limit_bytes=44 * 2**20),
        cost_estimate=pl.CostEstimate(flops=FLOPS, bytes_accessed=2**20, transcendentals=0),
    )(coords, basis)
    edges = call(edges_kernel, [f32(rows + 8, LEAF)] * 2, core, rhs, lanes, scalars=1)
    back_matrices = outside = None

    def after(message, *values):
        return lax.optimization_barrier((message, *values))[1:]

    def late_matrices(message):
        edges[0] = swap(after(message, edges[0])[0], 1)

        def body(lane_ref, high_ref, low_ref, sub_ref):
            fill_matrices(groups[1:], lane_ref, sub_ref, high_ref, low_ref)

        shapes = [bf16(2 * leaves - 3, LEAF, LEAF)] * 2
        return call(body, shapes, *after(message, lanes), flops=2 * FLOPS, scratch=[turned])

    def late_edge_matrices(message):
        def body(core_ref, *refs):
            edge_matrices(core_ref, rows, *refs)

        args = after(message, lanes, *edges)
        return call(body, [bf16(2, LEAF, LEAF)] * 2, core, *args, scalars=1, flops=FLOPS, scratch=[pltpu.VMEM((2 * LEAF, 8), jnp.float32)])

    solution, r, carried, opening = None, rhs, None, True
    for step in range(0, ITERS, 2):
        first, last = step == 0, step + 2 == ITERS
        r_local, keep, part, tile = down(r, f32(NORM_TILE, LANES))
        if first:
            edges = [edges[0], far_halo(lax.optimization_barrier((part, edges[1]))[1])]
        got = swap(part, 1)
        if first:
            message, got, results, r_sib = chain(False, False, keep, got, tile, [late_matrices, late_edge_matrices])
            back_matrices, outside = results
            (near,) = edge(*edges, inner(0, r), inner(1, r))
        else:
            fronts = []

            def inner_work(message):
                fronts.extend(inner(half, *after(message, r)) for half in range(2))
                return fronts

            def edge_work(message):
                return edge(*edges, *after(message, *fronts))[0]

            message, got, results, r_sib = chain(False, False, keep, got, tile, [inner_work, edge_work])
            near = results[1]
        args = [core, high, low, near, message, got, r_local]
        outs = [f32(rows, width), f32(rows, LANES), f32(rows, LEAF), f32(rows + SPARE, LEAF)]
        if first:
            w, state, *edges = call(
                functools.partial(residual_up_kernel, True, 0), outs, *args, scalars=1, flops=FLOPS // 2
            )
            d, q, d_skel, d_local, d_sib = r, w, message, r_local, r_sib
        else:
            outs = outs + [f32(rows, width)] * 2 + [f32(crossing * own, LANES), f32(rows, LOCAL * LANES)]
            outs = outs + [f32(own, LANES)] * siblings
            body = functools.partial(residual_up_kernel, False, siblings)
            args = args + [r, *carried, *r_sib, *d_sib]
            w, state, paired, other, d, q, d_skel, d_local, *d_sib = call(
                body, outs, *args, scalars=1, flops=FLOPS // 2
            )
            edges = (paired, other)
        r_skel, opening = message, False
        edges = halo(*edges)
        q_local, keep, part = down(q)
        got = swap(part, 1)
        parts = [inner(half, q) for half in range(2)]
        near, tile = edge(*edges, *parts, r, q, d, w, r_local, q_local, d_local)
        message, got, _, q_sib = chain(True, last, keep, got, tile, [], r_skel, d_skel, r_sib, d_sib)
        args = [core, high, low, near, message, got, q_local, r, w, d, q, state]
        args = args + ([] if first else [solution]) + ([] if last else [r_skel, d_skel, r_local, d_local, *r_sib, *q_sib, *d_sib])
        outs = [f32(rows, width)] * 2
        if not last:
            outs = outs + [f32(rows, width)] * 2 + [f32(crossing * own, LANES), f32(rows, LOCAL * LANES)]
            outs = outs + [f32(rows, LANES), f32(rows, LEAF), f32(rows + SPARE, LEAF)] + [f32(own, LANES)] * siblings
        solution, r, *rest = call(
            functools.partial(image_up_kernel, first, last, siblings), outs, *args, scalars=1, flops=FLOPS // 2
        )
        if not last:
            carried = rest[:5]
            edges = halo(*rest[5:7])
            d_sib = rest[7:]
    return (solution, r)


def solution(mesh):
    placed = (
        P(None, BOTH),
        P(None, BOTH),
        P(BOTH),
        P(BOTH, None),
        P(None, None, BOTH),
    )
    return jax.shard_map(
        per_device,
        mesh=mesh,
        in_specs=placed,
        out_specs=(P(None, BOTH), P(None, BOTH)),
        check_vma=False,
    )
```

```python
import functools

import jax
import jax.numpy as jnp
from jax import lax
from jax.experimental import pallas as pl
from jax.experimental.pallas import tpu as pltpu
from jax.sharding import PartitionSpec as P

LEAF = 512
ITERS = 4
WIN = 3
LANES = 128
LOCAL = 3
SPARE = 8
CHUNK = 16
NORM_TILE = 8
PRODUCTS_TILE = 8
FLOPS = 3 * 10**9

root_three = 1.7320508075688772
spacing_factor = 1.6
matern_scale = root_three / (spacing_factor * LEAF ** (-1.0 / 3.0))

BOTH = ("row", "col")
ROWS_COLS = (((1,), (0,)), ((), ()))
ROWS_ROWS = (((1,), (1,)), ((), ()))

PAIRS = ("dq", "rq", "qq", "rw", "dw", "rz", "qz", "dz")


def halves(values):
    high = values.astype(jnp.bfloat16)
    low = (values - high.astype(jnp.float32)).astype(jnp.bfloat16)
    return high, low


def stacked(values):
    return jnp.concatenate(halves(values), axis=0)


def product(stack, high, low, dims):
    rows = stack.shape[0] // 2
    main = lax.dot_general(stack, high, dims, preferred_element_type=jnp.float32)
    rest = lax.dot_general(stack[:rows], low, dims, preferred_element_type=jnp.float32)
    return main[:rows] + (main[rows:] + rest)


def row_sum(values):
    return jnp.sum(values, axis=1, keepdims=True)


def in_lanes(columns, shape):
    lane = lax.broadcasted_iota(jnp.int32, shape, 1)
    block = jnp.zeros(shape, jnp.float32)
    for index, column in enumerate(columns):
        block = jnp.where(lane == index, column, block)
    return block


def sums_tile(columns, rows, depth):
    turned = in_lanes(columns, (rows, LANES)).T[:depth]
    return jnp.concatenate([turned, jnp.zeros((depth, LANES - rows), jnp.float32)], axis=1)


def level_terms(core, columns, rows, depth):
    twice = [jnp.concatenate([column, column], axis=0) for column in columns]
    zero = jnp.zeros((rows, 1), jnp.float32)
    tile = sums_tile([zero] * (len(PAIRS) - len(columns)) + twice, rows, depth)
    lane = lax.broadcasted_iota(jnp.int32, tile.shape, 1)
    return jnp.where(lane // (rows // 2) == core, tile, 0.0)


def chosen(core, odd, even):
    return jnp.where(core == 1, odd, even)


def whole(memory=pltpu.VMEM):
    return pl.BlockSpec(memory_space=memory)


def call(body, outs, *args, scalars=0, flops=0, traffic=2**20, limit=16, scratch=()):
    return pl.pallas_call(
        body,
        out_shape=outs,
        in_specs=[whole(pltpu.SMEM)] * scalars + [whole()] * (len(args) - scalars),
        out_specs=[whole()] * len(outs),
        scratch_shapes=scratch,
        compiler_params=pltpu.CompilerParams(vmem_limit_bytes=limit * 2**20),
        cost_estimate=pl.CostEstimate(flops=flops, bytes_accessed=traffic, transcendentals=0),
    )(*args)


def f32(*shape):
    return jax.ShapeDtypeStruct(shape, jnp.float32)


def bf16(*shape):
    return jax.ShapeDtypeStruct(shape, jnp.bfloat16)


def matrix_rows(rows, lanes):
    square = None
    for axis in range(3):
        spread = rows[:, axis : axis + 1] - lanes[axis : axis + 1]
        square = spread * spread if square is None else square + spread * spread
    scaled = square * lax.rsqrt(jnp.maximum(square, 1e-30))
    return halves((1.0 + scaled) * jnp.exp(-scaled))


def fill_matrices(groups, lane_ref, sub_ref, high_ref, low_ref):
    sub_ref[...] = lane_ref[...].T
    matrix = 0
    for row_leaf, col_leaves in groups:
        lanes = [lane_ref[:, leaf * LEAF : (leaf + 1) * LEAF] for leaf in col_leaves]

        def one(part, carry):
            row_at = pl.multiple_of(row_leaf * LEAF + part * CHUNK, CHUNK)
            out_at = pl.ds(pl.multiple_of(part * CHUNK, CHUNK), CHUNK)
            rows = sub_ref[pl.ds(row_at, CHUNK)]
            for index, far in enumerate(lanes):
                values = matrix_rows(rows, far)
                high_ref[matrix + index, out_at], low_ref[matrix + index, out_at] = values
            return carry

        lax.fori_loop(0, LEAF // CHUNK, one, 0, unroll=4)
        matrix += len(col_leaves)


def setup_kernel(groups, coords_ref, basis_ref, high_ref, low_ref, basis_high_ref, basis_low_ref, lane_ref, *scratch):
    sub_ref, raw_ref, sem_ref = scratch
    levels, rank, _ = basis_ref.shape
    copies = [pltpu.make_async_copy(basis_ref.at[at], raw_ref.at[at], sem_ref.at[at]) for at in range(levels)]
    for copy in copies:
        copy.start()
    scaled = coords_ref[...] * matern_scale
    lane_ref[...] = jnp.concatenate([scaled, jnp.zeros((8 - scaled.shape[0], scaled.shape[1]), jnp.float32)], axis=0)
    fill_matrices(groups, lane_ref, sub_ref, high_ref, low_ref)
    for at, copy in enumerate(copies):
        copy.wait()
        here = slice(at * rank, (at + 1) * rank)
        basis_high_ref[here], basis_low_ref[here] = halves(raw_ref[at])


def edge_matrices(core_ref, rows, lane_ref, paired_ref, other_ref, high_ref, low_ref, sub_ref):
    core = core_ref[0]
    leaves = lane_ref.shape[1] // LEAF
    paired = paired_ref[rows : rows + 3]
    other = other_ref[rows : rows + 3]
    lanes = [chosen(core, paired, other), chosen(core, other, paired)]

    for side in range(2):
        first_point = side * (leaves - 1) * LEAF
        sub_ref[side * LEAF : (side + 1) * LEAF] = lane_ref[:, first_point : first_point + LEAF].T

        def one(part, carry):
            row_at = pl.multiple_of(side * LEAF + part * CHUNK, CHUNK)
            out_at = pl.ds(pl.multiple_of(part * CHUNK, CHUNK), CHUNK)
            values = matrix_rows(sub_ref[pl.ds(row_at, CHUNK)], lanes[side])
            high_ref[side, out_at], low_ref[side, out_at] = values
            return carry

        lax.fori_loop(0, LEAF // CHUNK, one, 0, unroll=4)


def sides(core, field_ref):
    head = field_ref[:, :LEAF]
    tail = field_ref[:, field_ref.shape[1] - LEAF :]
    return chosen(core, head, tail), chosen(core, tail, head)


def edges_kernel(place_ref, core_ref, ids_ref, field_ref, lane_ref, paired_ref, other_ref, weights_ref):
    core = core_ref[0]
    leaves = ids_ref.shape[0]
    for leaf in range(leaves):
        for offset in range(-1, WIN - 1):
            target = place_ref[0] * leaves + leaf + offset
            found = ids_ref[leaf, 0] == target
            for slot in range(1, WIN):
                found = jnp.logical_or(found, ids_ref[leaf, slot] == target)
            value = jnp.where(jnp.logical_and(found, target >= 0), 1.0 / (16 * WIN), 0.0)
            at = WIN * leaf + offset + 1
            weights_ref[at : at + 1] = jnp.full((1, LEAF), value, jnp.float32)
    for ref, field, place in zip((paired_ref, other_ref), sides(core, field_ref), sides(core, lane_ref)):
        ref[...] = jnp.concatenate([field, place], axis=0)


def down_kernel(core_ref, field_ref, high_ref, low_ref, local_ref, keep_ref, send_ref, *tile_refs):
    core = core_ref[0]
    rank = LANES
    rows, width = field_ref.shape
    half = width // 2
    stack = stacked(field_ref[...])
    for part in range(2):
        points = slice(part * half, (part + 1) * half)
        local_ref[:, part * rank : (part + 1) * rank] = product(
            stack[:, points], high_ref[:rank, points], low_ref[:rank, points], ROWS_ROWS
        )
    all_points = product(stack, high_ref[rank:], low_ref[rank:], ROWS_ROWS)
    local_ref[:, 2 * rank :] = all_points[:, :rank]
    own = rows // 2
    for bit in range(all_points.shape[1] // rank - 1):
        block = all_points[:, (bit + 1) * rank : (bit + 2) * rank]
        keep_ref[bit * own : (bit + 1) * own] = chosen(core, block[own:], block[:own])
        send_ref[bit * own : (bit + 1) * own] = chosen(core, block[:own], block[own:])
    for ref in tile_refs:
        ref[...] = sums_tile([row_sum(field_ref[...] * field_ref[...])], rows, NORM_TILE)


def leaf_of(ref, leaf):
    return ref[:, leaf * LEAF : (leaf + 1) * LEAF]


def weight_of(weights_ref, leaf, offset):
    at = WIN * leaf + offset + 1
    return weights_ref[at : at + 1]


def row_groups(leaves):
    return [(leaf, [leaf, leaf + 1] if leaf + 1 < leaves else [leaf]) for leaf in range(leaves)]


def inner_kernel(half, weights_ref, field_ref, nugget_ref, *refs):
    out_ref = refs[-1]
    leaves = weights_ref.shape[0] // WIN
    start = half * (leaves // 2)
    stop = start + leaves // 2
    pieces = {leaf: stacked(leaf_of(field_ref, leaf)) for leaf in range(max(start - 1, 0), min(stop + 1, leaves))}
    pairs = [(row, col) for row, cols in row_groups(leaves) for col in cols]

    def matrix(row, col):
        at = pairs.index((row, col))
        front = refs[0].shape[0]
        return (refs[0][at], refs[1][at]) if at < front else (refs[2][at - front], refs[3][at - front])

    for leaf in range(start, stop):
        at = leaf - start
        inside = product(pieces[leaf], *matrix(leaf, leaf), ROWS_COLS)
        total = leaf_of(nugget_ref, leaf) * leaf_of(field_ref, leaf) + weight_of(weights_ref, leaf, 0) * inside
        if leaf > 0:
            before = product(pieces[leaf - 1], *matrix(leaf - 1, leaf), ROWS_COLS)
            total = total + weight_of(weights_ref, leaf, -1) * before
        if leaf < leaves - 1:
            after = product(pieces[leaf + 1], *matrix(leaf, leaf + 1), ROWS_ROWS)
            total = total + weight_of(weights_ref, leaf, 1) * after
        out_ref[:, at * LEAF : (at + 1) * LEAF] = total


def edge_kernel(sums, *refs):
    core_ref, weights_ref, paired_ref, other_ref, high_ref, low_ref, front_ref, back_ref = refs[:8]
    refs = refs[8:]
    out_ref = refs[-2] if sums else refs[-1]
    core = core_ref[0]
    rows, width = out_ref.shape
    leaves = width // LEAF
    before = chosen(core, paired_ref[:rows], other_ref[:rows])
    after = chosen(core, other_ref[:rows], paired_ref[:rows])
    out_ref[:, : width // 2] = front_ref[...]
    out_ref[:, width // 2 :] = back_ref[...]
    part = product(stacked(before), high_ref[0], low_ref[0], ROWS_ROWS)
    out_ref[:, :LEAF] += weight_of(weights_ref, 0, -1) * part
    part = product(stacked(after), high_ref[1], low_ref[1], ROWS_ROWS)
    out_ref[:, width - LEAF :] += weight_of(weights_ref, leaves - 1, 1) * part
    if not sums:
        return
    fields = dict(zip("rqdw", refs[:4]))
    locals_ = dict(zip("rqd", refs[4:7]))
    tile_ref = refs[-1]
    totals = {pair: jnp.zeros((rows, 1), jnp.float32) for pair in PAIRS}
    for leaf in range(leaves):
        here = {name: leaf_of(ref, leaf) for name, ref in fields.items()}
        here["z"] = leaf_of(out_ref, leaf)
        for left, right in PAIRS:
            terms = here[left] * here[right]
            if left + right == "rz":
                terms = terms + here["q"] * here["w"]
            totals[left + right] = totals[left + right] + row_sum(terms)
    for block in range(LOCAL):
        scale = 1.0 / (LEAF * (2 if block < 2 else 4))
        lanes = slice(block * LANES, (block + 1) * LANES)
        for name in "rqd":
            term = row_sum(locals_[name][:, lanes] * locals_["q"][:, lanes])
            totals[name + "z"] = totals[name + "z"] + scale * term
    tile_ref[...] = sums_tile([totals[pair] for pair in PAIRS], rows, PRODUCTS_TILE)


def first_combine_kernel(products, cluster, *refs):
    core_ref, mine_ref, other_ref, tile_ref = refs[:4]
    message_ref, level_ref = refs[-2:]
    own = level_ref.shape[0]
    depth = tile_ref.shape[0]
    total = mine_ref[...] + other_ref[...]
    level = total[:own]
    level_ref[...] = level
    tile = tile_ref[...]
    if products:
        partners = [refs[4][:own], level, refs[5][:own]]
        columns = [row_sum(level * partner) * (1.0 / cluster) for partner in partners]
        tile = tile + level_terms(core_ref[0], columns, 2 * own, depth)
    left = total.shape[0] - own
    message_ref[:left] = total[own:]
    message_ref[left:] = tile


def combine_kernel(products, last, sibling, own, bits, clusters, *refs):
    refs = list(refs)
    core_ref, mine_ref = refs[:2]
    got = [ref[...] for ref in refs[2 : 2 + 2 ** len(bits) - 1]]
    refs = refs[1 + 2 ** len(bits) :]
    sibling_ref = refs.pop() if sibling else None
    level_out = [] if last else [refs.pop() for _ in bits][::-1]
    next_ref = refs.pop()
    depth = PRODUCTS_TILE if products else NORM_TILE
    near = mine_ref[...] + got[0]
    total = near
    pairs = [(near[:own], bits[0], 0, clusters[0])]
    if len(bits) == 2:
        far = got[1] + got[2]
        total = near + far
        if sibling:
            sibling_ref[...] = far[:own]
        pairs.append((far[:own], None, 1, clusters[0]))
        pairs.append((total[own : 2 * own], bits[1], 0, clusters[1]))
    for ref, pair in zip(level_out, pairs[:: 2 if len(bits) == 2 else 1]):
        ref[...] = pair[0]
    tile = total[total.shape[0] - depth :]
    if products:
        r_ref, d_ref = refs[:2]
        refs = refs[2:]
        siblings = [refs.pop(0), refs.pop(0)] if len(bits) == 2 else []
        columns = [jnp.zeros((own, 1), jnp.float32)] * 3
        for level, bit, kind, cluster in pairs:
            if kind:
                partners = [siblings[0][...], level, siblings[1][...]]
            else:
                here = slice(bit * own, (bit + 1) * own)
                partners = [r_ref[here], level, d_ref[here]]
            terms = [row_sum(level * partner) * (1.0 / cluster) for partner in partners]
            columns = [column + term for column, term in zip(columns, terms)]
        tile = tile + level_terms(core_ref[0], columns, 2 * own, depth)
    left = total.shape[0] - depth - len(bits) * own
    if not last:
        next_ref[:left] = total[len(bits) * own : len(bits) * own + left]
        next_ref[left:] = tile
    else:
        for index, ref in enumerate(refs):
            next_ref[index * own : (index + 1) * own] = ref[...]
        for bit, pair in zip(bits, pairs[:: 2 if len(bits) == 2 else 1]):
            next_ref[bit * own : (bit + 1) * own] = pair[0]
        next_ref[next_ref.shape[0] - depth :] = tile


def up_parts(core, mine_ref, other_ref, local_ref, rows, width, depth):
    own = rows // 2
    crossing = (mine_ref.shape[0] - depth) // own
    sums = (mine_ref[crossing * own :] + other_ref[crossing * own :]).T[:rows]
    scaled = []
    for bit in range(crossing):
        here = slice(bit * own, (bit + 1) * own)
        low_rows = chosen(core, other_ref[here], mine_ref[here])
        high_rows = chosen(core, mine_ref[here], other_ref[here])
        scaled.append(jnp.concatenate([low_rows, high_rows], axis=0) * (1.0 / (width * (2 << bit))))
    one = [local_ref[:, part * LANES : (part + 1) * LANES] * (1.0 / (2 * LEAF)) for part in range(2)]
    two = local_ref[:, 2 * LANES :] * (1.0 / (4 * LEAF))
    return sums, [stacked(jnp.concatenate([one[part], two] + scaled, axis=1)) for part in range(2)]


def own_rows(core, column, crossing):
    own = column.shape[0] // 2
    return jnp.concatenate([chosen(core, column[own:], column[:own])] * crossing, axis=0)


def put_edges(core, field_ref, paired_ref, send_ref):
    rows = paired_ref.shape[0]
    paired_ref[...], send_ref[:rows] = sides(core, field_ref)
    send_ref[rows:] = jnp.zeros((SPARE, LEAF), jnp.float32)


def residual_up_kernel(first, siblings, *refs):
    core_ref, high_ref, low_ref, near_ref, mine_ref, other_ref, local_ref = refs[:7]
    refs = refs[7:]
    if first:
        image_ref, state_ref, paired_ref, send_ref = refs
        q_ref = image_ref
    else:
        field_ref, old_d_ref, old_q_ref, old_skel_ref, old_local_ref, old_state_ref = refs[:6]
        r_siblings = refs[6 : 6 + siblings]
        d_siblings = refs[6 + siblings : 6 + 2 * siblings]
        refs = refs[6 + 2 * siblings :]
        image_ref, state_ref, paired_ref, send_ref, d_ref, q_ref, skel_ref, new_local_ref = refs[:8]
        new_siblings = refs[8:]
    core = core_ref[0]
    rows, width = near_ref.shape
    half = width // 2
    sums, stacks = up_parts(core, mine_ref, other_ref, local_ref, rows, width, NORM_TILE)
    norm = sums[:, 0:1]
    state_ref[...] = in_lanes([norm], (rows, LANES))
    ratio = None if first else norm / old_state_ref[:, 0:1]
    for part in range(2):
        points = slice(part * half, (part + 1) * half)
        image = near_ref[:, points] + product(stacks[part], high_ref[:, points], low_ref[:, points], ROWS_COLS)
        image_ref[:, points] = image
        if not first:
            d_ref[:, points] = field_ref[:, points] + ratio * old_d_ref[:, points]
            q_ref[:, points] = image + ratio * old_q_ref[:, points]
    put_edges(core, q_ref, paired_ref, send_ref)
    if not first:
        rows_in = skel_ref.shape[0]
        crossing = rows_in // (rows // 2)
        skel_ref[...] = mine_ref[:rows_in] + own_rows(core, ratio, crossing) * old_skel_ref[...]
        new_local_ref[...] = local_ref[...] + ratio * old_local_ref[...]
        own_ratio = own_rows(core, ratio, 1)
        for new_ref, r_ref, d_ref in zip(new_siblings, r_siblings, d_siblings):
            new_ref[...] = r_ref[...] + own_ratio * d_ref[...]


def image_up_kernel(first, last, siblings, *refs):
    core_ref, high_ref, low_ref, near_ref, mine_ref, other_ref, local_ref = refs[:7]
    r_ref, w_ref, d_ref, q_ref, state_ref = refs[7:12]
    refs = refs[12:]
    if not first:
        solution_ref = refs[0]
        refs = refs[1:]
    if not last:
        r_skel_ref, d_skel_ref, r_local_ref, d_local_ref = refs[:4]
        r_siblings, q_siblings, d_siblings = [
            refs[4 + index * siblings : 4 + (index + 1) * siblings] for index in range(3)
        ]
        refs = refs[4 + 3 * siblings :]
    new_solution_ref, new_r_ref = refs[:2]
    if not last:
        new_d_ref, new_q_ref, new_skel_ref, new_local_ref, new_state_ref, paired_ref, send_ref = refs[2:9]
        new_siblings = refs[9:]
    core = core_ref[0]
    rows, width = near_ref.shape
    half = width // 2
    sums, stacks = up_parts(core, mine_ref, other_ref, local_ref, rows, width, PRODUCTS_TILE)
    dot = {pair: sums[:, index : index + 1] for index, pair in enumerate(PAIRS)}
    norm = state_ref[:, 0:1]
    step = norm / dot["dq"]
    new_norm = norm - step * (2.0 * dot["rq"] - step * dot["qq"])
    ratio = new_norm / norm
    curve = dot["rw"] - step * (dot["rz"] - step * dot["qz"])
    curve = curve + ratio * (dot["dw"] - step * dot["dz"] + dot["rq"] - step * dot["qq"] + ratio * dot["dq"])
    new_step = new_norm / curve
    for part in range(2):
        points = slice(part * half, (part + 1) * half)
        image = near_ref[:, points] + product(stacks[part], high_ref[:, points], low_ref[:, points], ROWS_COLS)
        d = d_ref[:, points]
        q = q_ref[:, points]
        r = r_ref[:, points] - step * q
        new_q = w_ref[:, points] - step * image + ratio * q
        new_d = r + ratio * d
        moved = step * d + new_step * new_d
        new_solution_ref[:, points] = moved if first else solution_ref[:, points] + moved
        new_r_ref[:, points] = r - new_step * new_q
        if not last:
            new_d_ref[:, points] = new_d
            new_q_ref[:, points] = new_q
    if not last:
        rows_in = new_skel_ref.shape[0]
        crossing = rows_in // (rows // 2)
        r_skel = r_skel_ref[:rows_in] - own_rows(core, step, crossing) * mine_ref[:rows_in]
        new_skel_ref[...] = r_skel + own_rows(core, ratio, crossing) * d_skel_ref[:rows_in]
        new_local_ref[...] = r_local_ref[...] - step * local_ref[...] + ratio * d_local_ref[...]
        own_step, own_ratio = own_rows(core, step, 1), own_rows(core, ratio, 1)
        for new_ref, r_ref, q_ref, d_ref in zip(new_siblings, r_siblings, q_siblings, d_siblings):
            new_ref[...] = r_ref[...] - own_step * q_ref[...] + own_ratio * d_ref[...]
        new_state_ref[...] = in_lanes([new_norm], (rows, LANES))
        put_edges(core, new_r_ref, paired_ref, send_ref)


def per_device(rhs, coords, nugget, near_ids, basis):
    rows, width = rhs.shape
    levels = basis.shape[0]
    leaves = width // LEAF
    own = rows // 2
    crossing = levels - (leaves.bit_length() - 1)
    devices = lax.axis_size("row") * lax.axis_size("col")
    place = jnp.reshape(lax.axis_index(BOTH), (1,))
    core = place % 2
    nugget = nugget[None, :]

    stages = [list(range(bit, min(bit + 2, crossing))) for bit in range(1, crossing, 2)]
    siblings = sum(len(bits) == 2 for bits in stages)

    def swap(value, mask):
        return lax.ppermute(value, BOTH, [(source, source ^ mask) for source in range(devices)])

    def far_halo(other):
        outward = [(index, index + 1) for index in range(1, devices - 1, 2)]
        ends = [(0, 0), (devices - 1, devices - 1)]
        return lax.ppermute(other, BOTH, outward + [(target, source) for source, target in outward] + ends)

    def halo(paired, other):
        return swap(paired, 1), far_halo(other)

    def down(field, *tile):
        shapes = [f32(rows, LOCAL * LANES), f32(crossing * own, LANES)]
        shapes = shapes + [f32(crossing * own, LANES)] + list(tile)
        return call(down_kernel, shapes, core, field, high, low, scalars=1, flops=FLOPS if opening else 0, traffic=2**20 if opening else 0)

    def inner(half, field):
        args = [weights, field, nugget, *front_matrices, *back_matrices]
        body = functools.partial(inner_kernel, half)
        return call(body, [f32(rows, width // 2)], *args, flops=FLOPS // 2 if opening else 0)[0]

    def edge(paired, other, front, back, *more):
        shapes = [f32(rows, width)] + ([f32(PRODUCTS_TILE, LANES)] if more else [])
        args = [core, weights, paired, other, *outside, front, back, *more]
        return call(functools.partial(edge_kernel, bool(more)), shapes, *args, scalars=1, flops=FLOPS // 3 if opening else 0)

    def chain(products, final, keep, got, tile, beside_steps, r_skel=None, d_skel=None, r_sib=(), d_sib=()):
        depth = PRODUCTS_TILE if products else NORM_TILE
        results = []
        both = [r_skel, d_skel] if products else []
        message, level = call(
            functools.partial(first_combine_kernel, products, 2 * width),
            [f32((crossing - 1) * own + depth, LANES), f32(own, LANES)],
            core,
            keep,
            got,
            tile,
            *both,
            scalars=1,
        )
        done, kept = [level], []
        for index in range(len(stages) + 1):
            bits = stages[index] if index < len(stages) else []
            masks = [sum(1 << bit for at, bit in enumerate(bits) if pick >> at & 1) for pick in range(1, 2 ** len(bits))]
            got = [swap(message, mask) for mask in masks or [1]]
            if index < len(beside_steps):
                *got, result = lax.optimization_barrier((*got, beside_steps[index](message)))
                results.append(result)
            if not bits:
                break
            left = crossing - bits[-1] - 1
            paired = len(bits) == 2
            args = [core, message, *got, *both]
            if products and paired:
                args = args + [r_sib[index], d_sib[index]]
            sibling = paired and not final
            clusters = [width * (2 << bit) for bit in bits]
            message, *levels_out = call(
                functools.partial(combine_kernel, products, not left, sibling, own, bits, clusters),
                [f32((left or crossing) * own + depth, LANES)] + [f32(own, LANES)] * ((len(bits) if left else 0) + sibling),
                *args,
                *([] if left else done),
                scalars=1,
            )
            kept = kept + levels_out[len(levels_out) - sibling :]
            done = done + levels_out[: len(levels_out) - sibling]
        return message, got[0], results, kept

    groups = row_groups(leaves)
    turned = pltpu.VMEM((width, 8), jnp.float32)
    *front_matrices, high, low, lanes = pl.pallas_call(
        functools.partial(setup_kernel, groups[:1]),
        out_shape=[bf16(2, LEAF, LEAF)] * 2
        + [bf16(levels * LANES, width)] * 2
        + [f32(8, width)],
        in_specs=[whole(), whole(pltpu.HBM)],
        out_specs=[whole()] * 5,
        scratch_shapes=[turned, pltpu.VMEM(basis.shape, jnp.float32), pltpu.SemaphoreType.DMA((levels,))],
        compiler_params=pltpu.CompilerParams(vmem_limit_bytes=44 * 2**20),
        cost_estimate=pl.CostEstimate(flops=FLOPS, bytes_accessed=2**20, transcendentals=0),
    )(coords, basis)
    shapes = [f32(rows + 8, LEAF)] * 2 + [f32(WIN * leaves, LEAF)]
    *edges, weights = call(edges_kernel, shapes, place, core, near_ids, rhs, lanes, scalars=3)
    back_matrices = outside = None

    def after(message, *values):
        return lax.optimization_barrier((message, *values))[1:]

    def late_matrices(message):
        edges[0] = swap(after(message, edges[0])[0], 1)

        def body(lane_ref, high_ref, low_ref, sub_ref):
            fill_matrices(groups[1:], lane_ref, sub_ref, high_ref, low_ref)

        shapes = [bf16(2 * leaves - 3, LEAF, LEAF)] * 2
        return call(body, shapes, *after(message, lanes), flops=2 * FLOPS, scratch=[turned])

    def late_edge_matrices(message):
        def body(core_ref, *refs):
            edge_matrices(core_ref, rows, *refs)

        args = after(message, lanes, *edges)
        return call(body, [bf16(2, LEAF, LEAF)] * 2, core, *args, scalars=1, flops=FLOPS, scratch=[pltpu.VMEM((2 * LEAF, 8), jnp.float32)])

    solution, r, carried, opening = None, rhs, None, True
    for step in range(0, ITERS, 2):
        first, last = step == 0, step + 2 == ITERS
        r_local, keep, part, tile = down(r, f32(NORM_TILE, LANES))
        if first:
            edges = [edges[0], far_halo(lax.optimization_barrier((part, edges[1]))[1])]
        got = swap(part, 1)
        if first:
            message, got, results, r_sib = chain(False, False, keep, got, tile, [late_matrices, late_edge_matrices])
            back_matrices, outside = results
            (near,) = edge(*edges, inner(0, r), inner(1, r))
        else:
            fronts = []

            def inner_work(message):
                fronts.extend(inner(half, *after(message, r)) for half in range(2))
                return fronts

            def edge_work(message):
                return edge(*edges, *after(message, *fronts))[0]

            message, got, results, r_sib = chain(False, False, keep, got, tile, [inner_work, edge_work])
            near = results[1]
        args = [core, high, low, near, message, got, r_local]
        outs = [f32(rows, width), f32(rows, LANES), f32(rows, LEAF), f32(rows + SPARE, LEAF)]
        if first:
            w, state, *edges = call(
                functools.partial(residual_up_kernel, True, 0), outs, *args, scalars=1, flops=FLOPS // 2
            )
            d, q, d_skel, d_local, d_sib = r, w, message, r_local, r_sib
        else:
            outs = outs + [f32(rows, width)] * 2 + [f32(crossing * own, LANES), f32(rows, LOCAL * LANES)]
            outs = outs + [f32(own, LANES)] * siblings
            body = functools.partial(residual_up_kernel, False, siblings)
            args = args + [r, *carried, *r_sib, *d_sib]
            w, state, paired, other, d, q, d_skel, d_local, *d_sib = call(
                body, outs, *args, scalars=1, flops=FLOPS // 2
            )
            edges = (paired, other)
        r_skel, opening = message, False
        edges = halo(*edges)
        q_local, keep, part = down(q)
        got = swap(part, 1)
        parts = [inner(half, q) for half in range(2)]
        near, tile = edge(*edges, *parts, r, q, d, w, r_local, q_local, d_local)
        message, got, _, q_sib = chain(True, last, keep, got, tile, [], r_skel, d_skel, r_sib, d_sib)
        args = [core, high, low, near, message, got, q_local, r, w, d, q, state]
        args = args + ([] if first else [solution]) + ([] if last else [r_skel, d_skel, r_local, d_local, *r_sib, *q_sib, *d_sib])
        outs = [f32(rows, width)] * 2
        if not last:
            outs = outs + [f32(rows, width)] * 2 + [f32(crossing * own, LANES), f32(rows, LOCAL * LANES)]
            outs = outs + [f32(rows, LANES), f32(rows, LEAF), f32(rows + SPARE, LEAF)] + [f32(own, LANES)] * siblings
        solution, r, *rest = call(
            functools.partial(image_up_kernel, first, last, siblings), outs, *args, scalars=1, flops=FLOPS // 2
        )
        if not last:
            carried = rest[:5]
            edges = halo(*rest[5:7])
            d_sib = rest[7:]
    return (solution, r)


def solution(mesh):
    placed = (
        P(None, BOTH),
        P(None, BOTH),
        P(BOTH),
        P(BOTH, None),
        P(None, None, BOTH),
    )
    return jax.shard_map(
        per_device,
        mesh=mesh,
        in_specs=placed,
        out_specs=(P(None, BOTH), P(None, BOTH)),
        check_vma=False,
    )
```

```python
import functools

import jax
import jax.numpy as jnp
from jax import lax
from jax.experimental import pallas as pl
from jax.experimental.pallas import tpu as pltpu
from jax.sharding import PartitionSpec as P

LEAF = 512
ITERS = 4
WIN = 3
LANES = 128
LOCAL = 3
SPARE = 8
CHUNK = 16
NORM_TILE = 8
PRODUCTS_TILE = 8
FLOPS = 3 * 10**9

root_three = 1.7320508075688772
spacing_factor = 1.6
matern_scale = root_three / (spacing_factor * LEAF ** (-1.0 / 3.0))

BOTH = ("row", "col")
ROWS_COLS = (((1,), (0,)), ((), ()))
ROWS_ROWS = (((1,), (1,)), ((), ()))

PAIRS = ("dq", "rq", "qq", "rw", "dw", "rz", "qz", "dz")


def halves(values):
    high = values.astype(jnp.bfloat16)
    low = (values - high.astype(jnp.float32)).astype(jnp.bfloat16)
    return high, low


def stacked(values):
    return jnp.concatenate(halves(values), axis=0)


def product(stack, high, low, dims):
    rows = stack.shape[0] // 2
    main = lax.dot_general(stack, high, dims, preferred_element_type=jnp.float32)
    rest = lax.dot_general(stack[:rows], low, dims, preferred_element_type=jnp.float32)
    return main[:rows] + (main[rows:] + rest)


def row_sum(values):
    return jnp.sum(values, axis=1, keepdims=True)


def in_lanes(columns, shape):
    lane = lax.broadcasted_iota(jnp.int32, shape, 1)
    block = jnp.zeros(shape, jnp.float32)
    for index, column in enumerate(columns):
        block = jnp.where(lane == index, column, block)
    return block


def sums_tile(columns, rows, depth):
    turned = in_lanes(columns, (rows, LANES)).T[:depth]
    return jnp.concatenate([turned, jnp.zeros((depth, LANES - rows), jnp.float32)], axis=1)


def level_terms(core, columns, rows, depth):
    twice = [jnp.concatenate([column, column], axis=0) for column in columns]
    zero = jnp.zeros((rows, 1), jnp.float32)
    tile = sums_tile([zero] * (len(PAIRS) - len(columns)) + twice, rows, depth)
    lane = lax.broadcasted_iota(jnp.int32, tile.shape, 1)
    return jnp.where(lane // (rows // 2) == core, tile, 0.0)


def chosen(core, odd, even):
    return jnp.where(core == 1, odd, even)


def whole(memory=pltpu.VMEM):
    return pl.BlockSpec(memory_space=memory)


def call(body, outs, *args, scalars=0, flops=0, traffic=2**20, limit=16, scratch=()):
    return pl.pallas_call(
        body,
        out_shape=outs,
        in_specs=[whole(pltpu.SMEM)] * scalars + [whole()] * (len(args) - scalars),
        out_specs=[whole()] * len(outs),
        scratch_shapes=scratch,
        compiler_params=pltpu.CompilerParams(vmem_limit_bytes=limit * 2**20),
        cost_estimate=pl.CostEstimate(flops=flops, bytes_accessed=traffic, transcendentals=0),
    )(*args)


def f32(*shape):
    return jax.ShapeDtypeStruct(shape, jnp.float32)


def bf16(*shape):
    return jax.ShapeDtypeStruct(shape, jnp.bfloat16)


def matrix_rows(rows, lanes):
    square = None
    for axis in range(3):
        spread = rows[:, axis : axis + 1] - lanes[axis : axis + 1]
        square = spread * spread if square is None else square + spread * spread
    scaled = square * lax.rsqrt(jnp.maximum(square, 1e-30))
    return halves((1.0 + scaled) * jnp.exp(-scaled))


def fill_matrices(groups, lane_ref, sub_ref, high_ref, low_ref):
    sub_ref[...] = lane_ref[...].T
    matrix = 0
    for row_leaf, col_leaves in groups:
        lanes = [lane_ref[:, leaf * LEAF : (leaf + 1) * LEAF] for leaf in col_leaves]

        def one(part, carry):
            row_at = pl.multiple_of(row_leaf * LEAF + part * CHUNK, CHUNK)
            out_at = pl.ds(pl.multiple_of(part * CHUNK, CHUNK), CHUNK)
            rows = sub_ref[pl.ds(row_at, CHUNK)]
            for index, far in enumerate(lanes):
                values = matrix_rows(rows, far)
                high_ref[matrix + index, out_at], low_ref[matrix + index, out_at] = values
            return carry

        lax.fori_loop(0, LEAF // CHUNK, one, 0, unroll=4)
        matrix += len(col_leaves)


def setup_kernel(groups, coords_ref, basis_ref, high_ref, low_ref, basis_high_ref, basis_low_ref, lane_ref, *scratch):
    sub_ref, raw_ref, sem_ref = scratch
    levels, rank, _ = basis_ref.shape
    copies = [pltpu.make_async_copy(basis_ref.at[at], raw_ref.at[at], sem_ref.at[at]) for at in range(levels)]
    for copy in copies:
        copy.start()
    scaled = coords_ref[...] * matern_scale
    lane_ref[...] = jnp.concatenate([scaled, jnp.zeros((8 - scaled.shape[0], scaled.shape[1]), jnp.float32)], axis=0)
    fill_matrices(groups, lane_ref, sub_ref, high_ref, low_ref)
    for at, copy in enumerate(copies):
        copy.wait()
        here = slice(at * rank, (at + 1) * rank)
        basis_high_ref[here], basis_low_ref[here] = halves(raw_ref[at])


def edge_matrices(core_ref, rows, lane_ref, paired_ref, other_ref, high_ref, low_ref, sub_ref):
    core = core_ref[0]
    leaves = lane_ref.shape[1] // LEAF
    paired = paired_ref[rows : rows + 3]
    other = other_ref[rows : rows + 3]
    lanes = [chosen(core, paired, other), chosen(core, other, paired)]

    for side in range(2):
        first_point = side * (leaves - 1) * LEAF
        sub_ref[side * LEAF : (side + 1) * LEAF] = lane_ref[:, first_point : first_point + LEAF].T

    def one(part, carry):
        out_at = pl.ds(pl.multiple_of(part * CHUNK, CHUNK), CHUNK)
        for side in range(2):
            row_at = pl.multiple_of(side * LEAF + part * CHUNK, CHUNK)
            values = matrix_rows(sub_ref[pl.ds(row_at, CHUNK)], lanes[side])
            high_ref[side, out_at], low_ref[side, out_at] = values
        return carry

    lax.fori_loop(0, LEAF // CHUNK, one, 0, unroll=4)


def sides(core, field_ref):
    head = field_ref[:, :LEAF]
    tail = field_ref[:, field_ref.shape[1] - LEAF :]
    return chosen(core, head, tail), chosen(core, tail, head)


def edges_kernel(place_ref, core_ref, ids_ref, field_ref, lane_ref, paired_ref, other_ref, weights_ref):
    core = core_ref[0]
    leaves = ids_ref.shape[0]
    for leaf in range(leaves):
        for offset in range(-1, WIN - 1):
            target = place_ref[0] * leaves + leaf + offset
            found = ids_ref[leaf, 0] == target
            for slot in range(1, WIN):
                found = jnp.logical_or(found, ids_ref[leaf, slot] == target)
            value = jnp.where(jnp.logical_and(found, target >= 0), 1.0 / (16 * WIN), 0.0)
            at = WIN * leaf + offset + 1
            weights_ref[at : at + 1] = jnp.full((1, LEAF), value, jnp.float32)
    for ref, field, place in zip((paired_ref, other_ref), sides(core, field_ref), sides(core, lane_ref)):
        ref[...] = jnp.concatenate([field, place], axis=0)


def down_kernel(core_ref, field_ref, high_ref, low_ref, local_ref, keep_ref, send_ref, *tile_refs):
    core = core_ref[0]
    rank = LANES
    rows, width = field_ref.shape
    half = width // 2
    stack = stacked(field_ref[...])
    for part in range(2):
        points = slice(part * half, (part + 1) * half)
        local_ref[:, part * rank : (part + 1) * rank] = product(
            stack[:, points], high_ref[:rank, points], low_ref[:rank, points], ROWS_ROWS
        )
    all_points = product(stack, high_ref[rank:], low_ref[rank:], ROWS_ROWS)
    local_ref[:, 2 * rank :] = all_points[:, :rank]
    own = rows // 2
    for bit in range(all_points.shape[1] // rank - 1):
        block = all_points[:, (bit + 1) * rank : (bit + 2) * rank]
        keep_ref[bit * own : (bit + 1) * own] = chosen(core, block[own:], block[:own])
        send_ref[bit * own : (bit + 1) * own] = chosen(core, block[:own], block[own:])
    for ref in tile_refs:
        ref[...] = sums_tile([row_sum(field_ref[...] * field_ref[...])], rows, NORM_TILE)


def leaf_of(ref, leaf):
    return ref[:, leaf * LEAF : (leaf + 1) * LEAF]


def weight_of(weights_ref, leaf, offset):
    at = WIN * leaf + offset + 1
    return weights_ref[at : at + 1]


def row_groups(leaves):
    return [(leaf, [leaf, leaf + 1] if leaf + 1 < leaves else [leaf]) for leaf in range(leaves)]


def inner_kernel(half, weights_ref, field_ref, nugget_ref, *refs):
    out_ref = refs[-1]
    leaves = weights_ref.shape[0] // WIN
    start = half * (leaves // 2)
    stop = start + leaves // 2
    pieces = {leaf: stacked(leaf_of(field_ref, leaf)) for leaf in range(max(start - 1, 0), min(stop + 1, leaves))}
    pairs = [(row, col) for row, cols in row_groups(leaves) for col in cols]

    def matrix(row, col):
        at = pairs.index((row, col))
        front = refs[0].shape[0]
        return (refs[0][at], refs[1][at]) if at < front else (refs[2][at - front], refs[3][at - front])

    for leaf in range(start, stop):
        at = leaf - start
        inside = product(pieces[leaf], *matrix(leaf, leaf), ROWS_COLS)
        total = leaf_of(nugget_ref, leaf) * leaf_of(field_ref, leaf) + weight_of(weights_ref, leaf, 0) * inside
        if leaf > 0:
            before = product(pieces[leaf - 1], *matrix(leaf - 1, leaf), ROWS_COLS)
            total = total + weight_of(weights_ref, leaf, -1) * before
        if leaf < leaves - 1:
            after = product(pieces[leaf + 1], *matrix(leaf, leaf + 1), ROWS_ROWS)
            total = total + weight_of(weights_ref, leaf, 1) * after
        out_ref[:, at * LEAF : (at + 1) * LEAF] = total


def edge_kernel(sums, *refs):
    core_ref, weights_ref, paired_ref, other_ref, high_ref, low_ref, front_ref, back_ref = refs[:8]
    refs = refs[8:]
    out_ref = refs[-2] if sums else refs[-1]
    core = core_ref[0]
    rows, width = out_ref.shape
    leaves = width // LEAF
    before = chosen(core, paired_ref[:rows], other_ref[:rows])
    after = chosen(core, other_ref[:rows], paired_ref[:rows])
    out_ref[:, : width // 2] = front_ref[...]
    out_ref[:, width // 2 :] = back_ref[...]
    part = product(stacked(before), high_ref[0], low_ref[0], ROWS_ROWS)
    out_ref[:, :LEAF] += weight_of(weights_ref, 0, -1) * part
    part = product(stacked(after), high_ref[1], low_ref[1], ROWS_ROWS)
    out_ref[:, width - LEAF :] += weight_of(weights_ref, leaves - 1, 1) * part
    if not sums:
        return
    fields = dict(zip("rqdw", refs[:4]))
    locals_ = dict(zip("rqd", refs[4:7]))
    tile_ref = refs[-1]
    totals = {pair: jnp.zeros((rows, 1), jnp.float32) for pair in PAIRS}
    for leaf in range(leaves):
        here = {name: leaf_of(ref, leaf) for name, ref in fields.items()}
        here["z"] = leaf_of(out_ref, leaf)
        for left, right in PAIRS:
            terms = here[left] * here[right]
            if left + right == "rz":
                terms = terms + here["q"] * here["w"]
            totals[left + right] = totals[left + right] + row_sum(terms)
    for block in range(LOCAL):
        scale = 1.0 / (LEAF * (2 if block < 2 else 4))
        lanes = slice(block * LANES, (block + 1) * LANES)
        for name in "rqd":
            term = row_sum(locals_[name][:, lanes] * locals_["q"][:, lanes])
            totals[name + "z"] = totals[name + "z"] + scale * term
    tile_ref[...] = sums_tile([totals[pair] for pair in PAIRS], rows, PRODUCTS_TILE)


def first_combine_kernel(products, cluster, *refs):
    core_ref, mine_ref, other_ref, tile_ref = refs[:4]
    message_ref, level_ref = refs[-2:]
    own = level_ref.shape[0]
    depth = tile_ref.shape[0]
    total = mine_ref[...] + other_ref[...]
    level = total[:own]
    level_ref[...] = level
    tile = tile_ref[...]
    if products:
        partners = [refs[4][:own], level, refs[5][:own]]
        columns = [row_sum(level * partner) * (1.0 / cluster) for partner in partners]
        tile = tile + level_terms(core_ref[0], columns, 2 * own, depth)
    left = total.shape[0] - own
    message_ref[:left] = total[own:]
    message_ref[left:] = tile


def combine_kernel(products, last, sibling, own, bits, clusters, *refs):
    refs = list(refs)
    core_ref, mine_ref = refs[:2]
    got = [ref[...] for ref in refs[2 : 2 + 2 ** len(bits) - 1]]
    refs = refs[1 + 2 ** len(bits) :]
    sibling_ref = refs.pop() if sibling else None
    level_out = [] if last else [refs.pop() for _ in bits][::-1]
    next_ref = refs.pop()
    depth = PRODUCTS_TILE if products else NORM_TILE
    near = mine_ref[...] + got[0]
    total = near
    pairs = [(near[:own], bits[0], 0, clusters[0])]
    if len(bits) == 2:
        far = got[1] + got[2]
        total = near + far
        if sibling:
            sibling_ref[...] = far[:own]
        pairs.append((far[:own], None, 1, clusters[0]))
        pairs.append((total[own : 2 * own], bits[1], 0, clusters[1]))
    for ref, pair in zip(level_out, pairs[:: 2 if len(bits) == 2 else 1]):
        ref[...] = pair[0]
    tile = total[total.shape[0] - depth :]
    if products:
        r_ref, d_ref = refs[:2]
        refs = refs[2:]
        siblings = [refs.pop(0), refs.pop(0)] if len(bits) == 2 else []
        columns = [jnp.zeros((own, 1), jnp.float32)] * 3
        for level, bit, kind, cluster in pairs:
            if kind:
                partners = [siblings[0][...], level, siblings[1][...]]
            else:
                here = slice(bit * own, (bit + 1) * own)
                partners = [r_ref[here], level, d_ref[here]]
            terms = [row_sum(level * partner) * (1.0 / cluster) for partner in partners]
            columns = [column + term for column, term in zip(columns, terms)]
        tile = tile + level_terms(core_ref[0], columns, 2 * own, depth)
    left = total.shape[0] - depth - len(bits) * own
    if not last:
        next_ref[:left] = total[len(bits) * own : len(bits) * own + left]
        next_ref[left:] = tile
    else:
        for index, ref in enumerate(refs):
            next_ref[index * own : (index + 1) * own] = ref[...]
        for bit, pair in zip(bits, pairs[:: 2 if len(bits) == 2 else 1]):
            next_ref[bit * own : (bit + 1) * own] = pair[0]
        next_ref[next_ref.shape[0] - depth :] = tile


def up_parts(core, mine_ref, other_ref, local_ref, rows, width, depth):
    own = rows // 2
    crossing = (mine_ref.shape[0] - depth) // own
    sums = (mine_ref[crossing * own :] + other_ref[crossing * own :]).T[:rows]
    scaled = []
    for bit in range(crossing):
        here = slice(bit * own, (bit + 1) * own)
        low_rows = chosen(core, other_ref[here], mine_ref[here])
        high_rows = chosen(core, mine_ref[here], other_ref[here])
        scaled.append(jnp.concatenate([low_rows, high_rows], axis=0) * (1.0 / (width * (2 << bit))))
    one = [local_ref[:, part * LANES : (part + 1) * LANES] * (1.0 / (2 * LEAF)) for part in range(2)]
    two = local_ref[:, 2 * LANES :] * (1.0 / (4 * LEAF))
    return sums, [stacked(jnp.concatenate([one[part], two] + scaled, axis=1)) for part in range(2)]


def own_rows(core, column, crossing):
    own = column.shape[0] // 2
    return jnp.concatenate([chosen(core, column[own:], column[:own])] * crossing, axis=0)


def put_edges(core, field_ref, paired_ref, send_ref):
    rows = paired_ref.shape[0]
    paired_ref[...], send_ref[:rows] = sides(core, field_ref)
    send_ref[rows:] = jnp.zeros((SPARE, LEAF), jnp.float32)


def residual_up_kernel(first, siblings, *refs):
    core_ref, high_ref, low_ref, near_ref, mine_ref, other_ref, local_ref = refs[:7]
    refs = refs[7:]
    if first:
        image_ref, state_ref, paired_ref, send_ref = refs
        q_ref = image_ref
    else:
        field_ref, old_d_ref, old_q_ref, old_skel_ref, old_local_ref, old_state_ref = refs[:6]
        r_siblings = refs[6 : 6 + siblings]
        d_siblings = refs[6 + siblings : 6 + 2 * siblings]
        refs = refs[6 + 2 * siblings :]
        image_ref, state_ref, paired_ref, send_ref, d_ref, q_ref, skel_ref, new_local_ref = refs[:8]
        new_siblings = refs[8:]
    core = core_ref[0]
    rows, width = near_ref.shape
    half = width // 2
    sums, stacks = up_parts(core, mine_ref, other_ref, local_ref, rows, width, NORM_TILE)
    norm = sums[:, 0:1]
    state_ref[...] = in_lanes([norm], (rows, LANES))
    ratio = None if first else norm / old_state_ref[:, 0:1]
    for part in range(2):
        points = slice(part * half, (part + 1) * half)
        image = near_ref[:, points] + product(stacks[part], high_ref[:, points], low_ref[:, points], ROWS_COLS)
        image_ref[:, points] = image
        if not first:
            d_ref[:, points] = field_ref[:, points] + ratio * old_d_ref[:, points]
            q_ref[:, points] = image + ratio * old_q_ref[:, points]
    put_edges(core, q_ref, paired_ref, send_ref)
    if not first:
        rows_in = skel_ref.shape[0]
        crossing = rows_in // (rows // 2)
        skel_ref[...] = mine_ref[:rows_in] + own_rows(core, ratio, crossing) * old_skel_ref[...]
        new_local_ref[...] = local_ref[...] + ratio * old_local_ref[...]
        own_ratio = own_rows(core, ratio, 1)
        for new_ref, r_ref, d_ref in zip(new_siblings, r_siblings, d_siblings):
            new_ref[...] = r_ref[...] + own_ratio * d_ref[...]


def image_up_kernel(first, last, siblings, *refs):
    core_ref, high_ref, low_ref, near_ref, mine_ref, other_ref, local_ref = refs[:7]
    r_ref, w_ref, d_ref, q_ref, state_ref = refs[7:12]
    refs = refs[12:]
    if not first:
        solution_ref = refs[0]
        refs = refs[1:]
    if not last:
        r_skel_ref, d_skel_ref, r_local_ref, d_local_ref = refs[:4]
        r_siblings, q_siblings, d_siblings = [
            refs[4 + index * siblings : 4 + (index + 1) * siblings] for index in range(3)
        ]
        refs = refs[4 + 3 * siblings :]
    new_solution_ref, new_r_ref = refs[:2]
    if not last:
        new_d_ref, new_q_ref, new_skel_ref, new_local_ref, new_state_ref, paired_ref, send_ref = refs[2:9]
        new_siblings = refs[9:]
    core = core_ref[0]
    rows, width = near_ref.shape
    half = width // 2
    sums, stacks = up_parts(core, mine_ref, other_ref, local_ref, rows, width, PRODUCTS_TILE)
    dot = {pair: sums[:, index : index + 1] for index, pair in enumerate(PAIRS)}
    norm = state_ref[:, 0:1]
    step = norm / dot["dq"]
    new_norm = norm - step * (2.0 * dot["rq"] - step * dot["qq"])
    ratio = new_norm / norm
    curve = dot["rw"] - step * (dot["rz"] - step * dot["qz"])
    curve = curve + ratio * (dot["dw"] - step * dot["dz"] + dot["rq"] - step * dot["qq"] + ratio * dot["dq"])
    new_step = new_norm / curve
    for part in range(2):
        points = slice(part * half, (part + 1) * half)
        image = near_ref[:, points] + product(stacks[part], high_ref[:, points], low_ref[:, points], ROWS_COLS)
        d = d_ref[:, points]
        q = q_ref[:, points]
        r = r_ref[:, points] - step * q
        new_q = w_ref[:, points] - step * image + ratio * q
        new_d = r + ratio * d
        moved = step * d + new_step * new_d
        new_solution_ref[:, points] = moved if first else solution_ref[:, points] + moved
        new_r_ref[:, points] = r - new_step * new_q
        if not last:
            new_d_ref[:, points] = new_d
            new_q_ref[:, points] = new_q
    if not last:
        rows_in = new_skel_ref.shape[0]
        crossing = rows_in // (rows // 2)
        r_skel = r_skel_ref[:rows_in] - own_rows(core, step, crossing) * mine_ref[:rows_in]
        new_skel_ref[...] = r_skel + own_rows(core, ratio, crossing) * d_skel_ref[:rows_in]
        new_local_ref[...] = r_local_ref[...] - step * local_ref[...] + ratio * d_local_ref[...]
        own_step, own_ratio = own_rows(core, step, 1), own_rows(core, ratio, 1)
        for new_ref, r_ref, q_ref, d_ref in zip(new_siblings, r_siblings, q_siblings, d_siblings):
            new_ref[...] = r_ref[...] - own_step * q_ref[...] + own_ratio * d_ref[...]
        new_state_ref[...] = in_lanes([new_norm], (rows, LANES))
        put_edges(core, new_r_ref, paired_ref, send_ref)


def per_device(rhs, coords, nugget, near_ids, basis):
    rows, width = rhs.shape
    levels = basis.shape[0]
    leaves = width // LEAF
    own = rows // 2
    crossing = levels - (leaves.bit_length() - 1)
    devices = lax.axis_size("row") * lax.axis_size("col")
    place = jnp.reshape(lax.axis_index(BOTH), (1,))
    core = place % 2
    nugget = nugget[None, :]

    stages = [list(range(bit, min(bit + 2, crossing))) for bit in range(1, crossing, 2)]
    siblings = sum(len(bits) == 2 for bits in stages)

    def swap(value, mask):
        return lax.ppermute(value, BOTH, [(source, source ^ mask) for source in range(devices)])

    def far_halo(other):
        outward = [(index, index + 1) for index in range(1, devices - 1, 2)]
        ends = [(0, 0), (devices - 1, devices - 1)]
        return lax.ppermute(other, BOTH, outward + [(target, source) for source, target in outward] + ends)

    def halo(paired, other):
        return swap(paired, 1), far_halo(other)

    def down(field, *tile):
        shapes = [f32(rows, LOCAL * LANES), f32(crossing * own, LANES)]
        shapes = shapes + [f32(crossing * own, LANES)] + list(tile)
        return call(down_kernel, shapes, core, field, high, low, scalars=1, flops=FLOPS if opening else 0, traffic=2**20 if opening else 0)

    def inner(half, field):
        args = [weights, field, nugget, *front_matrices, *back_matrices]
        body = functools.partial(inner_kernel, half)
        return call(body, [f32(rows, width // 2)], *args, flops=FLOPS // 2 if opening else 0)[0]

    def edge(paired, other, front, back, *more):
        shapes = [f32(rows, width)] + ([f32(PRODUCTS_TILE, LANES)] if more else [])
        args = [core, weights, paired, other, *outside, front, back, *more]
        return call(functools.partial(edge_kernel, bool(more)), shapes, *args, scalars=1, flops=FLOPS // 3 if opening else 0)

    def chain(products, final, keep, got, tile, beside_steps, r_skel=None, d_skel=None, r_sib=(), d_sib=()):
        depth = PRODUCTS_TILE if products else NORM_TILE
        results = []
        both = [r_skel, d_skel] if products else []
        message, level = call(
            functools.partial(first_combine_kernel, products, 2 * width),
            [f32((crossing - 1) * own + depth, LANES), f32(own, LANES)],
            core,
            keep,
            got,
            tile,
            *both,
            scalars=1,
        )
        done, kept = [level], []
        for index in range(len(stages) + 1):
            bits = stages[index] if index < len(stages) else []
            masks = [sum(1 << bit for at, bit in enumerate(bits) if pick >> at & 1) for pick in range(1, 2 ** len(bits))]
            got = [swap(message, mask) for mask in masks or [1]]
            if index < len(beside_steps):
                *got, result = lax.optimization_barrier((*got, beside_steps[index](message)))
                results.append(result)
            if not bits:
                break
            left = crossing - bits[-1] - 1
            paired = len(bits) == 2
            args = [core, message, *got, *both]
            if products and paired:
                args = args + [r_sib[index], d_sib[index]]
            sibling = paired and not final
            clusters = [width * (2 << bit) for bit in bits]
            message, *levels_out = call(
                functools.partial(combine_kernel, products, not left, sibling, own, bits, clusters),
                [f32((left or crossing) * own + depth, LANES)] + [f32(own, LANES)] * ((len(bits) if left else 0) + sibling),
                *args,
                *([] if left else done),
                scalars=1,
            )
            kept = kept + levels_out[len(levels_out) - sibling :]
            done = done + levels_out[: len(levels_out) - sibling]
        return message, got[0], results, kept

    groups = row_groups(leaves)
    turned = pltpu.VMEM((width, 8), jnp.float32)
    *front_matrices, high, low, lanes = pl.pallas_call(
        functools.partial(setup_kernel, groups[:1]),
        out_shape=[bf16(2, LEAF, LEAF)] * 2
        + [bf16(levels * LANES, width)] * 2
        + [f32(8, width)],
        in_specs=[whole(), whole(pltpu.HBM)],
        out_specs=[whole()] * 5,
        scratch_shapes=[turned, pltpu.VMEM(basis.shape, jnp.float32), pltpu.SemaphoreType.DMA((levels,))],
        compiler_params=pltpu.CompilerParams(vmem_limit_bytes=44 * 2**20),
        cost_estimate=pl.CostEstimate(flops=FLOPS, bytes_accessed=2**20, transcendentals=0),
    )(coords, basis)
    shapes = [f32(rows + 8, LEAF)] * 2 + [f32(WIN * leaves, LEAF)]
    *edges, weights = call(edges_kernel, shapes, place, core, near_ids, rhs, lanes, scalars=3)
    back_matrices = outside = None

    def after(message, *values):
        return lax.optimization_barrier((message, *values))[1:]

    def late_matrices(message):
        edges[0] = swap(after(message, edges[0])[0], 1)

        def body(lane_ref, high_ref, low_ref, sub_ref):
            fill_matrices(groups[1:], lane_ref, sub_ref, high_ref, low_ref)

        shapes = [bf16(2 * leaves - 3, LEAF, LEAF)] * 2
        return call(body, shapes, *after(message, lanes), flops=2 * FLOPS, scratch=[turned])

    def late_edge_matrices(message):
        def body(core_ref, *refs):
            edge_matrices(core_ref, rows, *refs)

        args = after(message, lanes, *edges)
        return call(body, [bf16(2, LEAF, LEAF)] * 2, core, *args, scalars=1, flops=FLOPS, scratch=[pltpu.VMEM((2 * LEAF, 8), jnp.float32)])

    solution, r, carried, opening = None, rhs, None, True
    for step in range(0, ITERS, 2):
        first, last = step == 0, step + 2 == ITERS
        r_local, keep, part, tile = down(r, f32(NORM_TILE, LANES))
        if first:
            edges = [edges[0], far_halo(lax.optimization_barrier((part, edges[1]))[1])]
        got = swap(part, 1)
        if first:
            message, got, results, r_sib = chain(False, False, keep, got, tile, [late_matrices, late_edge_matrices])
            back_matrices, outside = results
            (near,) = edge(*edges, inner(0, r), inner(1, r))
        else:
            fronts = []

            def inner_work(message):
                fronts.extend(inner(half, *after(message, r)) for half in range(2))
                return fronts

            def edge_work(message):
                return edge(*edges, *after(message, *fronts))[0]

            message, got, results, r_sib = chain(False, False, keep, got, tile, [inner_work, edge_work])
            near = results[1]
        args = [core, high, low, near, message, got, r_local]
        outs = [f32(rows, width), f32(rows, LANES), f32(rows, LEAF), f32(rows + SPARE, LEAF)]
        if first:
            w, state, *edges = call(
                functools.partial(residual_up_kernel, True, 0), outs, *args, scalars=1, flops=FLOPS // 2
            )
            d, q, d_skel, d_local, d_sib = r, w, message, r_local, r_sib
        else:
            outs = outs + [f32(rows, width)] * 2 + [f32(crossing * own, LANES), f32(rows, LOCAL * LANES)]
            outs = outs + [f32(own, LANES)] * siblings
            body = functools.partial(residual_up_kernel, False, siblings)
            args = args + [r, *carried, *r_sib, *d_sib]
            w, state, paired, other, d, q, d_skel, d_local, *d_sib = call(
                body, outs, *args, scalars=1, flops=FLOPS // 2
            )
            edges = (paired, other)
        r_skel, opening = message, False
        edges = halo(*edges)
        q_local, keep, part = down(q)
        got = swap(part, 1)
        parts = [inner(half, q) for half in range(2)]
        near, tile = edge(*edges, *parts, r, q, d, w, r_local, q_local, d_local)
        message, got, _, q_sib = chain(True, last, keep, got, tile, [], r_skel, d_skel, r_sib, d_sib)
        args = [core, high, low, near, message, got, q_local, r, w, d, q, state]
        args = args + ([] if first else [solution]) + ([] if last else [r_skel, d_skel, r_local, d_local, *r_sib, *q_sib, *d_sib])
        outs = [f32(rows, width)] * 2
        if not last:
            outs = outs + [f32(rows, width)] * 2 + [f32(crossing * own, LANES), f32(rows, LOCAL * LANES)]
            outs = outs + [f32(rows, LANES), f32(rows, LEAF), f32(rows + SPARE, LEAF)] + [f32(own, LANES)] * siblings
        solution, r, *rest = call(
            functools.partial(image_up_kernel, first, last, siblings), outs, *args, scalars=1, flops=FLOPS // 2
        )
        if not last:
            carried = rest[:5]
            edges = halo(*rest[5:7])
            d_sib = rest[7:]
    return (solution, r)


def solution(mesh):
    placed = (
        P(None, BOTH),
        P(None, BOTH),
        P(BOTH),
        P(BOTH, None),
        P(None, None, BOTH),
    )
    return jax.shard_map(
        per_device,
        mesh=mesh,
        in_specs=placed,
        out_specs=(P(None, BOTH), P(None, BOTH)),
        check_vma=False,
    )
```
